32 devices in a mesh: rep: 8 (over y, x, core), ep: 4 (over z).
Axes of the slice: x: 2, y: 2, z: 4, core: 2. Of those that a mesh axis runs over, the one named last changes fastest.
Arguments:
- tokens: bfloat16 [16384, 2048], P(('rep', 'ep')), may hold values from -6 to 6
- teacher: bfloat16 [16384, 2048], P(('rep', 'ep')), may hold values from -6 to 6
- segment_ids: int32 [8, 2048], P('rep', 'ep'), may hold values from 0 to 4, as said below
- valid_mask: int32 [8, 2048], P('rep', 'ep'), may hold values from 0 to 1
- routes: int32 [16384, 2], P(('rep', 'ep')), may hold values from 0 to 3, all different within a row; in each aligned block of 512 rows (0 to 511, 512 to 1023, ...) at most 320 rows name the same one
- attn_gain: bfloat16 [2048], P(('rep', 'ep')), may hold values from 0.5 to 1.5
- q_gain: bfloat16 [2048], P(('rep', 'ep')), may hold values from 0.5 to 1.5
- k_gain: bfloat16 [2048], P(('rep', 'ep')), may hold values from 0.5 to 1.5
- moe_gain: bfloat16 [2048], P(('rep', 'ep')), may hold values from 0.5 to 1.5
- w_query: bfloat16 [2048, 2048], P(('rep', 'ep')), may hold values from -0.125 to 0.125
- w_key: bfloat16 [2048, 2048], P(('rep', 'ep')), may hold values from -0.125 to 0.125
- w_value: bfloat16 [2048, 2048], P(('rep', 'ep')), may hold values from -0.125 to 0.125
- w_out: bfloat16 [2048, 2048], P(('rep', 'ep')), may hold values from -2 to 2
- w_router: bfloat16 [2048, 4], P(('rep', 'ep')), may hold values from -0.0625 to 0.0625
- w_gate: bfloat16 [4, 2048, 1024], P('ep'), may hold values from -0.125 to 0.125
- w_up: bfloat16 [4, 2048, 1024], P('ep'), may hold values from -0.125 to 0.125
- w_down: bfloat16 [4, 1024, 2048], P('ep'), may hold values from -1.5 to 1.5
Outputs:
- output: bfloat16 [16384, 2048], P(('rep', 'ep'))
- loss: float32 [], replicated
- tokens_grad: float32 [16384, 2048], P(('rep', 'ep'))
- attn_gain_grad: float32 [2048], P(('rep', 'ep'))
- q_gain_grad: float32 [2048], P(('rep', 'ep'))
- k_gain_grad: float32 [2048], P(('rep', 'ep'))
- moe_gain_grad: float32 [2048], P(('rep', 'ep'))
- query_grad: float32 [2048, 2048], P(('rep', 'ep'))
- key_grad: float32 [2048, 2048], P(('rep', 'ep'))
- value_grad: float32 [2048, 2048], P(('rep', 'ep'))
- out_grad: float32 [2048, 2048], P(('rep', 'ep'))
- router_grad: float32 [2048, 4], P(('rep', 'ep'))
- gate_grad: float32 [4, 2048, 1024], P('ep', 'rep')
- up_grad: float32 [4, 2048, 1024], P('ep', 'rep')
- down_grad: float32 [4, 1024, 2048], P('ep', 'rep')
The draws below stay inside these ranges and needn't reach their ends.
Inputs may be any that keep to these rules, and one draw needn't show every extreme that they name: `routes`: each row names 2 different experts; within the rows of one device no expert is named by more than 320 rows. `segment_ids`: within each sequence the numbers start at 0 and never fall.
All inputs are finite; a program needn't handle non-finite values.
Results may differ from the reference program's by a relative error of at most 0.012.
The reference program's roundings to bfloat16 on the way count: a program that leaves them out, or rounds other values in their place, can miss the bound.
Values may be sent and summed in bfloat16 or wider, within the bound.
No kernel may reach another device: no remote copies, remote signals or barrier semaphores. Data moves between devices by JAX's collectives and lax.ppermute only.
A program may use at most 320 MiB of HBM per device.

```python
import math
import jax
import jax.numpy as jnp
import numpy as np
from jax import lax

D = 2048
HEADS = 16
HEAD_DIM = 128
FF = 1024
TOK_DEV = 512
WINDOW = 1024
TOP = 2
EXPERTS = 4
CAP = 320
SEQ = 2048
TOKENS = 16384


def draw_segment_ids(key, part):
    key = jax.random.fold_in(key, 5)
    sequences = TOKENS // SEQ
    halfway = TOK_DEV // 2
    streams = jax.random.split(key, 4)
    first = jax.random.randint(streams[0], (sequences, 1), 1, halfway)
    second = jax.random.randint(streams[1], (sequences, 1), halfway, TOK_DEV)
    third = jax.random.randint(streams[2], (sequences, 1), SEQ - TOK_DEV, SEQ - halfway)
    fourth = jax.random.randint(streams[3], (sequences, 1), SEQ - halfway, SEQ)
    positions = jnp.arange(SEQ, dtype=jnp.int32)[None, :]
    numbers = (positions >= first).astype(jnp.int32) + (positions >= second).astype(jnp.int32)
    numbers = numbers + (positions >= third).astype(jnp.int32) + (positions >= fourth).astype(jnp.int32)
    return numbers


def draw_valid_mask(key, part):
    key = jax.random.fold_in(key, 9)
    sequences = TOKENS // SEQ
    rolls = jax.random.randint(key, (sequences, SEQ), 0, 1000)
    places = jnp.arange(sequences, dtype=jnp.int32)[:, None] * SEQ + jnp.arange(SEQ, dtype=jnp.int32)[None, :]
    bounds = 300 + 600 * places // TOKENS
    return (rolls < bounds).astype(jnp.int32)


def block_scale(rng, dims, pieces, smallest, largest):
    level, own = 1.0, jax.random.fold_in(rng, 6)
    for dim, parts in pieces:
        heights = jnp.exp(jax.random.uniform(jax.random.fold_in(own, dim), (parts,), jnp.float32, smallest / len(pieces), largest / len(pieces)))
        level = level * jnp.repeat(heights, dims[dim] // parts).reshape([-1 if axis == dim else 1 for axis in range(len(dims))])
    return level


def assign_block(rng, own, number, rows, amount, top, reach, skew):
    order = jax.random.permutation(rng, amount)
    crowded, usual = load_shares(amount, rows * top, reach, skew, True), load_shares(amount, rows * top, reach, skew, False)
    places = jnp.arange(amount)

    def named(sizes, rotation):
        used = int((sizes > 0).sum())
        fixed = max(1, used // 4)
        shifted = fixed + (places - fixed + rotation * (used - fixed)) % max(1, amount - fixed)
        return jnp.zeros((amount,), jnp.int32).at[order[jnp.where(places < fixed, places, shifted)]].set(jnp.asarray(sizes, jnp.int32))

    sizes = jnp.where(number % 4 == 0, named(crowded, number // 4), named(usual, number - number // 4 - 1))
    mixed = jax.random.permutation(jax.random.fold_in(own, 3), amount)
    giver, receiver = mixed[0:amount // 2 * 2:2], mixed[1:amount // 2 * 2:2]
    room = jnp.minimum(sizes[giver] - 1, reach - sizes[receiver]) // 2
    room = jnp.where((giver == order[0]) | (receiver == order[0]) | (sizes[receiver] == 0), 0, jnp.maximum(room, 0))
    shifted = jax.random.randint(jax.random.fold_in(own, 4), (amount // 2,), 0, 1 << 20) % (room + 1)
    sizes = sizes.at[giver].add(-shifted).at[receiver].add(shifted)
    labels = jnp.searchsorted(jnp.cumsum(sizes), jnp.arange(rows * top), side="right").astype(jnp.int32)
    table = labels.reshape(top, rows).T
    table = table[jax.random.permutation(jax.random.fold_in(own, 1), rows)]
    rotation = jax.random.randint(jax.random.fold_in(own, 2), (rows, 1), 0, top)
    return jnp.take_along_axis(table, (jnp.arange(top)[None, :] + rotation) % top, axis=1)


def load_shares(number_of, total, reach, lean, full):
    portions = [(1 << 20) // math.isqrt(standing ** lean) + 1 for standing in range(1, number_of + 1)]
    largest = reach if full else min(reach, max(-(-total // number_of), total * portions[0] // sum(portions)))
    least = 1 if total - largest >= number_of - 1 else 0
    holding, rest = [largest] + [least] * (number_of - 1), total - largest - least * (number_of - 1)
    while rest > 0:
        candidates = [i for i in range(1, number_of) if holding[i] < largest] or [i for i in range(1, number_of) if holding[i] < reach]
        pool, left = sum([portions[i] for i in candidates]), rest
        for i in candidates:
            extra = min(reach - holding[i], max(1, left * portions[i] // pool), rest)
            holding[i] = holding[i] + extra
            rest = rest - extra
    return np.array(holding)


def scatter_about(own_key, shape, spread, most, cuts=(), kind=jnp.bfloat16):
    values = spread * jax.random.normal(own_key, shape, jnp.float32)
    if cuts:
        values = values * block_scale(own_key, shape, cuts, -0.22, 0.18)
    return jnp.clip(values, -most, most).astype(kind)


def setup_inputs(seed: int = 0) -> dict:
    streams_of = jax.random.split(jax.random.key(seed), 18)
    tokens = scatter_about(streams_of[0], (TOKENS, D), 1.0, 6.0, ((0, 32),))
    teacher = scatter_about(streams_of[1], (TOKENS, D), 1.0, 6.0, ((0, 32),))
    segment_ids = draw_segment_ids(jax.random.fold_in(streams_of[17], 71), 0)
    valid_mask = draw_valid_mask(jax.random.fold_in(streams_of[17], 71), 0)
    routes_keys = jax.random.split(jax.random.fold_in(streams_of[4], 1), TOKENS // TOK_DEV)
    routes_turns = jax.random.permutation(jax.random.fold_in(streams_of[4], 3), TOKENS // TOK_DEV)
    routes = jax.vmap(lambda own, number: assign_block(jax.random.fold_in(streams_of[4], 2), own, number, TOK_DEV, EXPERTS, TOP, CAP, 2))(routes_keys, routes_turns).reshape((TOKENS, TOP))
    attn_gain = jnp.clip(1.0 + 0.1 * jax.random.normal(streams_of[5], (D,), jnp.float32), 0.5, 1.5).astype(jnp.bfloat16)
    q_gain = jnp.clip(1.0 + 0.1 * jax.random.normal(streams_of[6], (D,), jnp.float32), 0.5, 1.5).astype(jnp.bfloat16)
    k_gain = jnp.clip(1.0 + 0.1 * jax.random.normal(streams_of[7], (D,), jnp.float32), 0.5, 1.5).astype(jnp.bfloat16)
    moe_gain = jnp.clip(1.0 + 0.1 * jax.random.normal(streams_of[8], (D,), jnp.float32), 0.5, 1.5).astype(jnp.bfloat16)
    w_query = scatter_about(streams_of[9], (D, D), D ** -0.5, 0.125, ((0, 32),))
    w_key = scatter_about(streams_of[10], (D, D), D ** -0.5, 0.125, ((0, 32),))
    w_value = scatter_about(streams_of[11], (D, D), D ** -0.5, 0.125, ((0, 32),))
    w_out = scatter_about(streams_of[12], (D, D), (max(D // 256, 4)) ** -0.5, 2.0, ((0, 32),))
    w_router = scatter_about(streams_of[13], (D, EXPERTS), (4 * D) ** -0.5, 0.0625, ((0, 32),))
    w_gate = scatter_about(streams_of[14], (EXPERTS, D, FF), D ** -0.5, 0.125, ((0, 4),))
    w_up = scatter_about(streams_of[15], (EXPERTS, D, FF), D ** -0.5, 0.125, ((0, 4),))
    w_down = scatter_about(streams_of[16], (EXPERTS, FF, D), (max(FF // 64, 4)) ** -0.5, 1.5, ((0, 4),))
    return dict(tokens=tokens, teacher=teacher, segment_ids=segment_ids, valid_mask=valid_mask, routes=routes, attn_gain=attn_gain, q_gain=q_gain, k_gain=k_gain, moe_gain=moe_gain, w_query=w_query, w_key=w_key, w_value=w_value, w_out=w_out, w_router=w_router, w_gate=w_gate, w_up=w_up, w_down=w_down)


@jax.custom_vjp
def low(v):
    return lax.optimization_barrier(v.astype(jnp.bfloat16)).astype(jnp.float32)

@jax.custom_vjp
def low_back(v):
    return v

def low_keep(v):
    return (low(v), None)

def low_pass(kept, grad):
    return (grad,)

def back_keep(v):
    return (v, None)

def back_low(kept, grad):
    return (low(grad),)
low.defvjp(low_keep, low_pass)
low_back.defvjp(back_keep, back_low)
norm_eps = 1e-05
highest = lax.Precision.HIGHEST

def product(left, right):
    return jnp.dot(left, right, precision=highest)

def rms_norm(value, gain):
    return value * lax.rsqrt(lax.optimization_barrier(jnp.mean(value * value, axis=-1, keepdims=True)) + norm_eps) * gain

def rotary_tables(positions, head_size):
    half = head_size // 2
    frequency = 10000.0 ** (-jnp.arange(half, dtype=jnp.float32) * 2.0 / head_size)
    angles = positions[:, None].astype(jnp.float32) * frequency[None, :]
    cosine = jnp.cos(angles)
    sine = jnp.sin(angles)
    return (jnp.concatenate([cosine, cosine], -1)[:, None, :], jnp.concatenate([sine, sine], -1)[:, None, :])

def rotate(value, cosine, sine):
    half = value.shape[-1] // 2
    turned = jnp.concatenate([-value[..., half:], value[..., :half]], -1)
    return value * cosine + turned * sine

def attend(normed, segments, w_query, w_key, w_value, w_out, q_gain, k_gain):
    length = normed.shape[0]
    query_lin = rms_norm(low_back(product(normed, w_query)), q_gain)
    key_lin = rms_norm(low_back(product(normed, w_key)), k_gain)
    value_rows = low_back(low(product(normed, w_value))).reshape(length, HEADS, HEAD_DIM)
    positions = jnp.arange(length, dtype=jnp.int32)
    cosine, sine = rotary_tables(positions, HEAD_DIM)
    query_rows = low_back(low(rotate(query_lin.reshape(length, HEADS, HEAD_DIM), cosine, sine)))
    key_rows = low_back(low(rotate(key_lin.reshape(length, HEADS, HEAD_DIM), cosine, sine)))
    scores = low_back(jnp.einsum('qhd,khd->hqk', query_rows, key_rows, precision=highest) * HEAD_DIM ** (-0.5))
    distance = positions[:, None] - positions[None, :]
    allowed = (distance >= 0) & (distance < WINDOW) & (segments[:, None] == segments[None, :])
    scores = jnp.where(allowed[None], scores, -1e+30)
    weights = low(jax.nn.softmax(scores, axis=-1))
    mixed = jnp.einsum('hqk,khd->qhd', weights, value_rows, precision=highest)
    mixed = low_back(low(mixed)).reshape(length, HEADS * HEAD_DIM)
    return low_back(product(mixed, w_out))

def layer(tokens, segment_ids, routes, attn_gain, q_gain, k_gain, moe_gain, w_query, w_key, w_value, w_out, w_router, w_gate, w_up, w_down):
    normed = low(rms_norm(tokens, attn_gain))
    sequences = normed.reshape(TOKENS // SEQ, SEQ, D)
    attend_block = jax.checkpoint(attend)

    def one_sequence(carry, item):
        return (carry, attend_block(item[0], item[1], w_query, w_key, w_value, w_out, q_gain, k_gain))
    _, branch = lax.scan(one_sequence, jnp.zeros((), jnp.float32), (sequences, segment_ids))
    residual = tokens + branch.reshape(TOKENS, D)
    normed_moe = low(rms_norm(residual, moe_gain))
    router_probs = jax.nn.softmax(product(normed_moe, w_router), axis=-1)
    chosen = lax.optimization_barrier(jnp.sum((routes[:, :, None] == jnp.arange(EXPERTS, dtype=jnp.int32)[None, None, :]).astype(jnp.float32), axis=1))
    gates = router_probs * chosen

    def one_expert(total, item):
        gate_weight, up_weight, down_weight, column = item
        inputs = low_back(normed_moe)
        gate_pre = low_back(product(inputs, gate_weight))
        up_pre = low_back(product(inputs, up_weight))
        middle = low(jax.nn.silu(gate_pre) * up_pre)
        expert_out = low_back(low(product(middle, down_weight)))
        return (total + column[:, None] * expert_out, None)
    mixture, _ = lax.scan(jax.checkpoint(one_expert), jnp.zeros((TOKENS, D), jnp.float32), (w_gate, w_up, w_down, gates.T))
    return residual + mixture

def reference(tokens, teacher, segment_ids, valid_mask, routes, attn_gain, q_gain, k_gain, moe_gain, w_query, w_key, w_value, w_out, w_router, w_gate, w_up, w_down):
    floats = [value.astype(jnp.float32) for value in (tokens, attn_gain, q_gain, k_gain, moe_gain, w_query, w_key, w_value, w_out, w_router, w_gate, w_up, w_down)]
    valid = valid_mask.reshape(TOKENS).astype(jnp.float32)
    count = jnp.sum(valid)
    target = teacher.astype(jnp.float32)

    def objective(*values):
        result = layer(values[0], segment_ids, routes, *values[1:])
        squares = jnp.sum(valid[:, None] * (result - target) ** 2)
        return (squares * TOKENS / (2.0 * count), (result, squares / (2.0 * count * D)))
    _, pullback, extras = jax.vjp(objective, *floats, has_aux=True)
    gradients = pullback(jnp.ones((), jnp.float32))
    result, loss = extras
    return (result.astype(jnp.bfloat16), loss, gradients[0], gradients[1], gradients[2], gradients[3], gradients[4], gradients[5], gradients[6], gradients[7], gradients[8], gradients[9], gradients[10], gradients[11], gradients[12])
```

```python
import jax
import jax.numpy as jnp
from jax import lax
from jax.sharding import PartitionSpec as P

HEADS = 16
HEAD_DIM = 128
WINDOW = 1024
TOP = 2


norm_eps = 1e-05
highest = lax.Precision.HIGHEST


def from_behind(value, axis, steps):
    count = lax.axis_size(axis)
    leading, last = (max(0, -steps), min(count, count - steps))
    return lax.ppermute(value, axis, [(source, source + steps) for source in range(leading, last)])


def matmul(left, right):
    return jnp.dot(left, right, preferred_element_type=jnp.float32)


def rms_scale(value):
    return lax.rsqrt(jnp.mean(value * value, axis=-1, keepdims=True) + norm_eps)


def norm_back(value, scale, gain, grad):
    weighted = grad * gain
    inner = jnp.mean(weighted * value, axis=-1, keepdims=True)
    return (
        scale * weighted - value * (scale * scale * scale) * inner,
        jnp.sum(grad * value * scale, axis=0),
    )


def rounded(value):
    return lax.optimization_barrier(value.astype(jnp.bfloat16)).astype(jnp.float32)


def rotary_tables(positions, head_size):
    half = head_size // 2
    frequency = 10000.0 ** (-jnp.arange(half, dtype=jnp.float32) * 2.0 / head_size)
    angles = positions[:, None].astype(jnp.float32) * frequency[None, :]
    cosine = jnp.cos(angles)
    sine = jnp.sin(angles)
    return (
        jnp.concatenate([cosine, cosine], -1)[:, None, :],
        jnp.concatenate([sine, sine], -1)[:, None, :],
    )


def rotate(value, cosine, sine):
    half = value.shape[-1] // 2
    turned = jnp.concatenate([-value[..., half:], value[..., :half]], -1)
    return value * cosine + turned * sine


def rotate_back(grad, cosine, sine):
    half = grad.shape[-1] // 2
    scaled = grad * sine
    turned = jnp.concatenate([scaled[..., half:], -scaled[..., :half]], -1)
    return grad * cosine + turned


def unpack(everything):
    gains = [everything[index].astype(jnp.float32) for index in range(4)]
    return (gains, everything[4], everything[5], everything[6], everything[7], everything[8])


def body_plain(
    tokens,
    teacher,
    segment_ids,
    valid_mask,
    routes,
    attn_gain,
    q_gain,
    k_gain,
    moe_gain,
    w_query,
    w_key,
    w_value,
    w_out,
    w_router,
    w_gate,
    w_up,
    w_down,
):
    local_rows, width = tokens.shape
    experts = lax.axis_size("ep")
    pairs = local_rows * TOP
    capacity = 5 * pairs // (4 * experts)
    reach = min(-(-WINDOW // local_rows), experts - 1)
    group = min(HEADS, 4)
    score_scale = HEAD_DIM ** (-0.5)
    shard = lax.axis_index("ep")
    total_tokens = local_rows * lax.axis_size("rep") * experts
    everything = (
        lax.all_gather(attn_gain, ("rep", "ep"), axis=0, tiled=True),
        lax.all_gather(q_gain, ("rep", "ep"), axis=0, tiled=True),
        lax.all_gather(k_gain, ("rep", "ep"), axis=0, tiled=True),
        lax.all_gather(moe_gain, ("rep", "ep"), axis=0, tiled=True),
        lax.all_gather(w_query, ("rep", "ep"), axis=0, tiled=True),
        lax.all_gather(w_key, ("rep", "ep"), axis=0, tiled=True),
        lax.all_gather(w_value, ("rep", "ep"), axis=0, tiled=True),
        lax.all_gather(w_out, ("rep", "ep"), axis=0, tiled=True),
        lax.all_gather(w_router, ("rep", "ep"), axis=0, tiled=True),
    )
    gains, weight_query, weight_key, weight_value, weight_out, weight_router = unpack(everything)
    gain_attn, gain_query, gain_key, gain_moe = gains
    inputs = tokens.astype(jnp.float32)
    scale_attn = rms_scale(inputs)
    normed = (inputs * scale_attn * gain_attn).astype(jnp.bfloat16)
    query_lin = matmul(normed, weight_query)
    key_lin = matmul(normed, weight_key)
    value_rows = (
        matmul(normed, weight_value).astype(jnp.bfloat16).reshape(local_rows, HEADS, HEAD_DIM)
    )
    scale_query = rms_scale(query_lin)
    scale_key = rms_scale(key_lin)
    positions = shard * local_rows + jnp.arange(local_rows, dtype=jnp.int32)
    cosine, sine = rotary_tables(positions, HEAD_DIM)
    query_rows = rotate(
        (query_lin * scale_query * gain_query).reshape(local_rows, HEADS, HEAD_DIM), cosine, sine
    ).astype(jnp.bfloat16)
    key_rows = rotate(
        (key_lin * scale_key * gain_key).reshape(local_rows, HEADS, HEAD_DIM), cosine, sine
    ).astype(jnp.bfloat16)
    segments = segment_ids.reshape(local_rows)
    key_parts, value_parts, segment_parts = ([], [], [])
    for back in range(reach, 0, -1):
        moved = from_behind((key_rows, value_rows, segments.astype(jnp.bfloat16)), "ep", back)
        key_parts.append(moved[0])
        value_parts.append(moved[1])
        segment_parts.append(moved[2].astype(jnp.int32))
    all_keys = jnp.concatenate(key_parts + [key_rows], 0)
    all_values = jnp.concatenate(value_parts + [value_rows], 0)
    key_segments = jnp.concatenate(segment_parts + [segments], 0)
    key_positions = (shard - reach) * local_rows + jnp.arange(
        (reach + 1) * local_rows, dtype=jnp.int32
    )
    distance = positions[:, None] - key_positions[None, :]
    allowed = (
        (distance >= 0)
        & (distance < WINDOW)
        & (key_positions[None, :] >= 0)
        & (segments[:, None] == key_segments[None, :])
    )

    def by_group(value):
        return jnp.moveaxis(value.reshape(value.shape[0], HEADS // group, group, HEAD_DIM), 1, 0)

    def from_group(value):
        return jnp.moveaxis(value, 0, 1).reshape(value.shape[1], HEADS * HEAD_DIM)

    def scores_of(query_group, key_group):
        raw = (
            jnp.einsum("qhd,khd->hqk", query_group, key_group, preferred_element_type=jnp.float32)
            * score_scale
        )
        return jnp.where(allowed[None], raw, -1e30)

    def attend_forward(item):
        query_group, key_group, value_group = item
        scores = scores_of(query_group, key_group)
        peak = jnp.max(scores, axis=-1, keepdims=True)
        shifted = jnp.exp(scores - peak)
        total = jnp.sum(shifted, axis=-1, keepdims=True)
        weights = (shifted / total).astype(jnp.bfloat16)
        mixed = jnp.einsum("hqk,khd->qhd", weights, value_group, preferred_element_type=jnp.float32)
        return (mixed, peak, total)

    query_groups = by_group(query_rows)
    key_groups = by_group(all_keys)
    value_groups = by_group(all_values)
    mixed, peaks, totals = lax.map(attend_forward, (query_groups, key_groups, value_groups))
    mixed_rows = from_group(mixed).astype(jnp.bfloat16)
    residual = inputs + matmul(mixed_rows, weight_out)
    scale_moe = rms_scale(residual)
    normed_moe = (residual * scale_moe * gain_moe).astype(jnp.bfloat16)
    router_probs = jax.nn.softmax(matmul(normed_moe, weight_router), axis=-1)
    flat_routes = routes.reshape(pairs)
    choose = (flat_routes[:, None] == jnp.arange(experts, dtype=jnp.int32)[None, :]).astype(
        jnp.int32
    )
    rank = jnp.sum((jnp.cumsum(choose, axis=0) - choose) * choose, axis=1)
    slots = flat_routes * capacity + rank
    pair_source = (
        jnp.full((experts * capacity,), pairs, jnp.int32)
        .at[slots]
        .set(jnp.arange(pairs, dtype=jnp.int32))
    )
    token_source = jnp.where(pair_source < pairs, pair_source // TOP, local_rows)
    zero_row = jnp.zeros((1, width), jnp.bfloat16)
    outgoing = jnp.concatenate([normed_moe, zero_row], 0)[token_source].reshape(
        experts, capacity, width
    )
    choose_float = choose.reshape(local_rows, TOP, experts).astype(jnp.float32)
    gate_value = jnp.sum(choose_float * router_probs[:, None, :], axis=2)
    gate_weight = w_gate[0]
    up_weight = w_up[0]
    down_weight = w_down[0]
    piece = lax.all_to_all(outgoing, "ep", split_axis=0, concat_axis=0, tiled=True)
    flat = piece.reshape(-1, width)
    gate_pre = matmul(flat, gate_weight)
    up_pre = matmul(flat, up_weight)
    middle = (jax.nn.silu(gate_pre) * up_pre).astype(jnp.bfloat16)
    expert_out = matmul(middle, down_weight).astype(jnp.bfloat16)
    lead = piece.shape[:2]
    returned = expert_out.reshape(piece.shape)
    gate_kept = gate_pre.reshape(lead + (-1,))
    up_kept = up_pre.reshape(lead + (-1,))
    arrived = lax.all_to_all(returned, "ep", split_axis=0, concat_axis=0, tiled=True)
    expert_rows = arrived.reshape(experts * capacity, width)[slots].reshape(local_rows, TOP, width)
    result = residual + jnp.sum(gate_value[:, :, None] * expert_rows, axis=1)
    output = result.astype(jnp.bfloat16)
    valid = valid_mask.reshape(local_rows).astype(jnp.float32)
    error = result - teacher.astype(jnp.float32)
    squares = jnp.sum(valid * jnp.sum(error * error, axis=1))
    total_squares, count = lax.psum((squares, jnp.sum(valid)), ("rep", "ep"))
    loss = total_squares / (2.0 * count * width)
    result_grad = total_tokens / count * valid[:, None] * error
    gate_value_grad = jnp.sum(result_grad[:, None, :] * expert_rows, axis=2)
    pair_grad = (
        (gate_value[:, :, None] * result_grad[:, None, :])
        .astype(jnp.bfloat16)
        .reshape(pairs, width)
    )
    grad_outgoing = jnp.concatenate([pair_grad, zero_row], 0)[pair_source].reshape(
        experts, capacity, width
    )
    grad_in = lax.all_to_all(grad_outgoing, "ep", split_axis=0, concat_axis=0, tiled=True)
    rows_in = piece.reshape(-1, width)
    gate_pre = gate_kept.reshape(rows_in.shape[0], -1)
    up_pre = up_kept.reshape(rows_in.shape[0], -1)
    flat_grad = grad_in.reshape(-1, width)
    sigma = jax.nn.sigmoid(gate_pre)
    active = gate_pre * sigma
    middle = (active * up_pre).astype(jnp.bfloat16)
    down_local = matmul(middle.T, flat_grad)
    middle_grad = matmul(flat_grad, down_weight.T)
    gate_pre_grad = (middle_grad * up_pre * sigma * (1.0 + gate_pre * (1.0 - sigma))).astype(
        jnp.bfloat16
    )
    up_pre_grad = (middle_grad * active).astype(jnp.bfloat16)
    gate_local = matmul(rows_in.T, gate_pre_grad)
    up_local = matmul(rows_in.T, up_pre_grad)
    input_grad = (matmul(gate_pre_grad, gate_weight.T) + matmul(up_pre_grad, up_weight.T)).astype(
        jnp.bfloat16
    )
    back_rows = lax.all_to_all(
        input_grad.reshape(experts, capacity, width), "ep", split_axis=0, concat_axis=0, tiled=True
    )
    pair_back = back_rows.reshape(experts * capacity, width)[slots].reshape(local_rows, TOP, width)
    everything = (
        lax.all_gather(attn_gain, ("rep", "ep"), axis=0, tiled=True),
        lax.all_gather(q_gain, ("rep", "ep"), axis=0, tiled=True),
        lax.all_gather(k_gain, ("rep", "ep"), axis=0, tiled=True),
        lax.all_gather(moe_gain, ("rep", "ep"), axis=0, tiled=True),
        lax.all_gather(w_query, ("rep", "ep"), axis=0, tiled=True),
        lax.all_gather(w_key, ("rep", "ep"), axis=0, tiled=True),
        lax.all_gather(w_value, ("rep", "ep"), axis=0, tiled=True),
        lax.all_gather(w_out, ("rep", "ep"), axis=0, tiled=True),
        lax.all_gather(w_router, ("rep", "ep"), axis=0, tiled=True),
    )
    gains, weight_query, weight_key, weight_value, weight_out, weight_router = unpack(everything)
    gain_attn, gain_query, gain_key, gain_moe = gains
    prob_grad = jnp.sum(choose_float * gate_value_grad[:, :, None], axis=1)
    logit_grad = router_probs * (
        prob_grad - jnp.sum(prob_grad * router_probs, axis=-1, keepdims=True)
    )
    router_local = jnp.dot(
        normed_moe.T, logit_grad, precision=highest, preferred_element_type=jnp.float32
    )
    normed_moe_grad = jnp.sum(pair_back.astype(jnp.float32), axis=1) + jnp.dot(
        logit_grad, weight_router.T, precision=highest, preferred_element_type=jnp.float32
    )
    residual_part, moe_gain_local = norm_back(residual, scale_moe, gain_moe, normed_moe_grad)
    residual_grad = result_grad + residual_part
    branch_grad = residual_grad.astype(jnp.bfloat16)
    out_local = matmul(mixed_rows.T, branch_grad)
    mixed_grad = (
        matmul(branch_grad, weight_out.T).astype(jnp.bfloat16).reshape(local_rows, HEADS, HEAD_DIM)
    )

    def attend_backward(item):
        query_group, key_group, value_group, grad_group, peak, total = item
        scores = scores_of(query_group, key_group)
        probs = jnp.exp(scores - peak) / total
        weights = probs.astype(jnp.bfloat16)
        value_part = jnp.einsum(
            "hqk,qhd->khd", weights, grad_group, preferred_element_type=jnp.float32
        )
        probs_grad = jnp.einsum(
            "qhd,khd->hqk", grad_group, value_group, preferred_element_type=jnp.float32
        )
        inner = jnp.sum(probs * probs_grad, axis=-1, keepdims=True)
        score_grad = (probs * (probs_grad - inner)).astype(jnp.bfloat16)
        query_part = (
            jnp.einsum("hqk,khd->qhd", score_grad, key_group, preferred_element_type=jnp.float32)
            * score_scale
        )
        key_part = (
            jnp.einsum("hqk,qhd->khd", score_grad, query_group, preferred_element_type=jnp.float32)
            * score_scale
        )
        return (query_part, key_part, value_part)

    query_parts, key_parts_grad, value_parts_grad = lax.map(
        attend_backward,
        (query_groups, key_groups, value_groups, by_group(mixed_grad), peaks, totals),
    )
    query_row_grad = from_group(query_parts)
    key_all_grad = from_group(key_parts_grad)
    value_all_grad = from_group(value_parts_grad)
    own_keys = key_all_grad[reach * local_rows :]
    own_values = value_all_grad[reach * local_rows :]
    for back in range(1, reach + 1):
        start = (reach - back) * local_rows
        moved = from_behind(
            (key_all_grad[start : start + local_rows], value_all_grad[start : start + local_rows]),
            "ep",
            -back,
        )
        own_keys = own_keys + moved[0]
        own_values = own_values + moved[1]
    query_turned = rotate_back(
        rounded(query_row_grad).reshape(local_rows, HEADS, HEAD_DIM), cosine, sine
    ).reshape(local_rows, width)
    key_turned = rotate_back(
        rounded(own_keys).reshape(local_rows, HEADS, HEAD_DIM), cosine, sine
    ).reshape(local_rows, width)
    query_lin_grad, q_gain_local = norm_back(query_lin, scale_query, gain_query, query_turned)
    key_lin_grad, k_gain_local = norm_back(key_lin, scale_key, gain_key, key_turned)
    query_lin_grad = query_lin_grad.astype(jnp.bfloat16)
    key_lin_grad = key_lin_grad.astype(jnp.bfloat16)
    value_row_grad = own_values.astype(jnp.bfloat16)
    query_local = matmul(normed.T, query_lin_grad)
    key_local = matmul(normed.T, key_lin_grad)
    value_local = matmul(normed.T, value_row_grad)
    normed_grad = (
        matmul(query_lin_grad, weight_query.T)
        + matmul(key_lin_grad, weight_key.T)
        + matmul(value_row_grad, weight_value.T)
    )
    inputs_part, attn_gain_local = norm_back(inputs, scale_attn, gain_attn, normed_grad)
    tokens_grad = residual_grad + inputs_part
    summed = (
        lax.psum_scatter(attn_gain_local, ("rep", "ep"), scatter_dimension=0, tiled=True),
        lax.psum_scatter(q_gain_local, ("rep", "ep"), scatter_dimension=0, tiled=True),
        lax.psum_scatter(k_gain_local, ("rep", "ep"), scatter_dimension=0, tiled=True),
        lax.psum_scatter(moe_gain_local, ("rep", "ep"), scatter_dimension=0, tiled=True),
        lax.psum_scatter(query_local, ("rep", "ep"), scatter_dimension=0, tiled=True),
        lax.psum_scatter(key_local, ("rep", "ep"), scatter_dimension=0, tiled=True),
        lax.psum_scatter(value_local, ("rep", "ep"), scatter_dimension=0, tiled=True),
        lax.psum_scatter(out_local, ("rep", "ep"), scatter_dimension=0, tiled=True),
        lax.psum_scatter(router_local, ("rep", "ep"), scatter_dimension=0, tiled=True),
    )
    expert_summed = (
        lax.psum_scatter(gate_local[None], "rep", scatter_dimension=1, tiled=True),
        lax.psum_scatter(up_local[None], "rep", scatter_dimension=1, tiled=True),
        lax.psum_scatter(down_local[None], "rep", scatter_dimension=1, tiled=True),
    )
    return (
        output,
        loss,
        tokens_grad,
        summed[0],
        summed[1],
        summed[2],
        summed[3],
        summed[4],
        summed[5],
        summed[6],
        summed[7],
        summed[8],
        expert_summed[0],
        expert_summed[1],
        expert_summed[2],
    )


def across(value, bit):
    count = lax.axis_size("rep")
    return lax.ppermute(value, "rep", [(place, place ^ bit) for place in range(count)])


def along(value, steps):
    count = lax.axis_size("ep")
    return lax.ppermute(value, "ep", [(place, (place + steps) % count) for place in range(count)])


def mirrored(value, moves):
    reps, count = lax.axis_size("rep"), lax.axis_size("ep")
    pairs = []
    for rep in range(reps):
        for source, target in moves:
            if rep % 2:
                source, target = count - 1 - source, count - 1 - target
            pairs.append((rep * count + source, rep * count + target))
    return lax.ppermute(value, ("rep", "ep"), pairs)


def pick(value, index, axis):
    return lax.dynamic_index_in_dim(value, index, axis, keepdims=False)


def in_order(own, other, bit, axis):
    return jnp.where(bit == 1, jnp.stack([other, own], axis), jnp.stack([own, other], axis))


def gather_pair(left, right, place):
    y_bit, x_bit, core, shard = place
    experts = lax.axis_size("ep")
    both = jnp.stack([left, right])
    parts = jnp.zeros((experts,) + both.shape, both.dtype)
    parts = lax.dynamic_update_index_in_dim(parts, both, shard, 0)
    for steps in range(1, experts):
        parts = lax.dynamic_update_index_in_dim(
            parts, along(both, steps), lax.rem(shard - steps + experts, experts), 0
        )
    a, b = parts[:, 0], parts[:, 1]
    a_x, b_y = across(a, 2), across(b, 4)
    a, b = in_order(a, a_x, x_bit, 0), in_order(b, b_y, y_bit, 0)
    a_y, b_x = across(a, 4), across(b, 2)
    a, b = in_order(a, a_y, y_bit, 0), in_order(b, b_x, x_bit, 1)
    a_c, b_c = across(a, 1), across(b, 1)
    a, b = in_order(a, a_c, core, 2), in_order(b, b_c, core, 2)
    width = left.shape[1]
    return a.reshape(-1, width), b.reshape(-1, width)


def half_step(value, bit, axis, link):
    sent = across(pick(value, 1 - bit, axis), link)
    kept = pick(value, bit, axis)
    return (kept.astype(jnp.float32) + sent.astype(jnp.float32)).astype(jnp.bfloat16)


def plane_sum(left, right, place):
    y_bit, x_bit, core, shard = place
    a = half_step(left, x_bit, 1, 2)
    b = half_step(right, y_bit, 0, 4)
    return half_step(a, y_bit, 0, 4), half_step(b, x_bit, 0, 2)


def scatter_pair(left, right, place):
    y_bit, x_bit, core, shard = place
    experts = lax.axis_size("ep")
    rows, width = left.shape
    shape = (2, 2, 2, rows // 8, width)
    a = half_step(left.reshape(shape), core, 2, 1)
    b = half_step(right.reshape(shape), core, 2, 1)
    a, b = plane_sum(a, b, place)
    both = jnp.stack([a, b]).reshape(2, experts, rows // (8 * experts), width)
    both = lax.all_to_all(both, "ep", split_axis=1, concat_axis=1, tiled=True)
    both = jnp.sum(both.astype(jnp.float32), axis=1)
    return both[0], both[1]


def gather_experts(quarter, place):
    y_bit, x_bit, core, shard = place
    m = jnp.where(core == 0, shard, lax.axis_size("ep") - 1 - shard)
    one = mirrored(quarter, [(0, 1), (1, 2)])
    two = mirrored(jnp.where(m == 2, one, quarter), [(1, 0), (2, 3)])
    three = mirrored(one, [(1, 2)])
    four = mirrored(three, [(2, 3)])
    a = jnp.where(m == 0, quarter, jnp.where(m == 1, one, jnp.where(m == 2, three, four)))
    b = jnp.where(m == 1, quarter, jnp.where(m == 2, one, two))
    a_x, b_y = across(a, 2), across(b, 4)
    a, b = in_order(a, a_x, x_bit, 0), in_order(b, b_y, y_bit, 0)
    a_y, b_x = across(a, 4), across(b, 2)
    return in_order(a, a_y, y_bit, 0), in_order(b, b_x, x_bit, 1)


def scatter_experts(left, right, place):
    y_bit, x_bit, core, shard = place
    m = jnp.where(core == 0, shard, lax.axis_size("ep") - 1 - shard)
    a, b = plane_sum(left, right, place)
    both = jnp.stack([a, b])
    up = mirrored(b, [(0, 1)])
    got = mirrored(both, [(3, 2)])
    both = (both.astype(jnp.float32) + got.astype(jnp.float32)).astype(jnp.bfloat16)
    got = mirrored(both, [(2, 1)])
    both = both.astype(jnp.float32) + got.astype(jnp.float32)
    a, b = both[0], both[1]
    got = mirrored(a.astype(jnp.bfloat16), [(1, 0)])
    mine = jnp.where(m == 0, a + got.astype(jnp.float32), b + up.astype(jnp.float32))
    return mine, m


def body(
    tokens,
    teacher,
    segment_ids,
    valid_mask,
    routes,
    attn_gain,
    q_gain,
    k_gain,
    moe_gain,
    w_query,
    w_key,
    w_value,
    w_out,
    w_router,
    w_gate,
    w_up,
    w_down,
):
    bf16, f32 = jnp.bfloat16, jnp.float32
    local_rows, width = tokens.shape
    experts = lax.axis_size("ep")
    reps = lax.axis_size("rep")
    reach = min(-(-WINDOW // local_rows), experts - 1)
    group = min(HEADS, 4)
    score_scale = HEAD_DIM ** (-0.5)
    shard = lax.axis_index("ep")
    rep = lax.axis_index("rep")
    place = (rep // 4, rep // 2 % 2, rep % 2, shard)
    core = rep % 2
    total_tokens = local_rows * reps * experts

    valid = valid_mask.reshape(local_rows).astype(f32)
    own_count = jnp.sum(valid_mask)
    counts = jnp.stack([own_count // 16, own_count % 16]).astype(bf16)
    small = jnp.concatenate(
        [
            jnp.stack([attn_gain, q_gain, k_gain, moe_gain], 1),
            w_router,
            jnp.broadcast_to(counts[None], (attn_gain.shape[0], 2)),
        ],
        1,
    )
    small = lax.all_gather(small, ("rep", "ep"), axis=0, tiled=True)
    gain_attn, gain_query, gain_key, gain_moe = [small[:, i].astype(f32) for i in range(4)]
    weight_router = small[:, 4 : 4 + experts]
    counts = small[:: attn_gain.shape[0], 4 + experts :].astype(f32)
    count = jnp.sum(counts[:, 0]) * 16.0 + jnp.sum(counts[:, 1])

    weight_key, weight_value = gather_pair(w_key, w_value, place)
    weight_query, weight_out = gather_pair(w_query, w_out, place)

    moved, moved_segments = tokens, segment_ids.reshape(local_rows)
    token_parts, segment_parts = [tokens], [moved_segments]
    for back in range(reach):
        moved = from_behind(moved, "ep", 1)
        moved_segments = from_behind(moved_segments, "ep", 1)
        token_parts.insert(0, moved)
        segment_parts.insert(0, moved_segments)
    behind = reach * local_rows
    inputs_all = jnp.concatenate(token_parts, 0).astype(f32)
    key_segments = jnp.concatenate(segment_parts, 0)
    inputs = tokens.astype(f32)
    segments = segment_ids.reshape(local_rows)

    quarter_rows = w_gate.shape[1] // 4
    quarter_down = w_down.shape[1] // 4
    quarter = rep // 2
    quarter_gate = lax.dynamic_slice_in_dim(w_gate[0], quarter * quarter_rows, quarter_rows, 0)
    quarter_up = lax.dynamic_slice_in_dim(w_up[0], quarter * quarter_rows, quarter_rows, 0)
    quarter_down_w = lax.dynamic_slice_in_dim(w_down[0], quarter * quarter_down, quarter_down, 0)
    own_quarter = jnp.concatenate(
        [jnp.concatenate([quarter_gate, quarter_up], 1), quarter_down_w], 0
    )

    scale_all = rms_scale(inputs_all)
    normed_all = (inputs_all * scale_all * gain_attn).astype(bf16)
    scale_attn = scale_all[behind:]
    normed = normed_all[behind:]
    key_lin = matmul(normed_all, weight_key)
    value_all = matmul(normed_all, weight_value).astype(bf16)
    query_lin = matmul(normed, weight_query)
    scale_query = rms_scale(query_lin)
    scale_key = rms_scale(key_lin)
    all_rows = local_rows + behind
    key_positions = (shard - reach) * local_rows + jnp.arange(all_rows, dtype=jnp.int32)
    positions = shard * local_rows + jnp.arange(local_rows, dtype=jnp.int32)
    cosine_all, sine_all = rotary_tables(key_positions, HEAD_DIM)
    cosine, sine = cosine_all[behind:], sine_all[behind:]
    query_rows = rotate(
        (query_lin * scale_query * gain_query).reshape(local_rows, HEADS, HEAD_DIM), cosine, sine
    ).astype(bf16)
    all_keys = rotate(
        (key_lin * scale_key * gain_key).reshape(all_rows, HEADS, HEAD_DIM), cosine_all, sine_all
    ).astype(bf16)
    all_values = value_all.reshape(all_rows, HEADS, HEAD_DIM)
    distance = positions[:, None] - key_positions[None, :]
    allowed = (
        (distance >= 0)
        & (distance < WINDOW)
        & (key_positions[None, :] >= 0)
        & (segments[:, None] == key_segments[None, :])
    )

    def by_group(value):
        return jnp.moveaxis(value.reshape(value.shape[0], HEADS // group, group, HEAD_DIM), 1, 0)

    def from_group(value):
        return jnp.moveaxis(value, 0, 1).reshape(value.shape[1], HEADS * HEAD_DIM)

    def scores_of(query_group, key_group):
        raw = (
            jnp.einsum("qhd,khd->hqk", query_group, key_group, preferred_element_type=jnp.float32)
            * score_scale
        )
        return jnp.where(allowed[None], raw, -1e30)

    def attend_forward(item):
        query_group, key_group, value_group = item
        scores = scores_of(query_group, key_group)
        peak = jnp.max(scores, axis=-1, keepdims=True)
        shifted = jnp.exp(scores - peak)
        total = jnp.sum(shifted, axis=-1, keepdims=True)
        weights = (shifted / total).astype(jnp.bfloat16)
        mixed = jnp.einsum("hqk,khd->qhd", weights, value_group, preferred_element_type=jnp.float32)
        return (mixed, peak, total)

    query_groups = by_group(query_rows)
    key_groups = by_group(all_keys)
    value_groups = by_group(all_values)
    mixed, peaks, totals = lax.map(attend_forward, (query_groups, key_groups, value_groups))
    mixed_rows = from_group(mixed).astype(bf16)
    residual = inputs + matmul(mixed_rows, weight_out)
    scale_moe = rms_scale(residual)
    normed_moe = (residual * scale_moe * gain_moe).astype(bf16)
    partner_moe = across(normed_moe, 1)
    router_probs = jax.nn.softmax(matmul(normed_moe, weight_router), axis=-1)
    chosen = jnp.sum(
        (routes[:, :, None] == jnp.arange(experts, dtype=jnp.int32)).astype(f32), axis=1
    )
    gates = router_probs * chosen
    ends = ((0, experts - 1), (1, experts - 2))

    def slot_of(value, slot, of_core):
        low, high = ends[slot]
        return jnp.where(of_core == 0, value[:, low], value[:, high])

    gates_both = jnp.concatenate([gates, across(gates, 1)], 0)
    moe_both = jnp.concatenate([normed_moe, partner_moe], 0)

    experts_a, experts_b = gather_experts(own_quarter, place)
    slots = []
    mixture = 0.0
    for slot, pieces in enumerate((experts_a, experts_b)):
        weight_gu = pieces[:, :, :quarter_rows].reshape(4 * quarter_rows, width)
        weight_down = pieces[:, :, quarter_rows:].reshape(4 * quarter_down, width)
        hidden = width // 2
        pre = matmul(moe_both, weight_gu)
        gate_pre, up_pre = pre[:, :hidden], pre[:, hidden:]
        middle = (jax.nn.silu(gate_pre) * up_pre).astype(bf16)
        expert_out = matmul(middle, weight_down).astype(bf16)
        gate = slot_of(gates_both, slot, core)
        mixture = mixture + gate[:, None] * expert_out
        slots.append((weight_gu, weight_down, gate_pre, up_pre, middle, expert_out, gate))
    result = residual + (mixture[:local_rows] + across(mixture[local_rows:], 1))
    output = result.astype(bf16)
    error = result - teacher.astype(f32)
    squares = jnp.sum(valid * jnp.sum(error * error, axis=1))
    result_grad = total_tokens / count * valid[:, None] * error
    result_grad_both = jnp.concatenate([result_grad, across(result_grad, 1)], 0)

    input_grad = 0.0
    gate_grads, expert_grads = [], []
    for weight_gu, weight_down, gate_pre, up_pre, middle, expert_out, gate in slots:
        gate_grads.append(jnp.sum(result_grad_both * expert_out, axis=1))
        pair_grad = (gate[:, None] * result_grad_both).astype(bf16)
        down_local = matmul(middle.T, pair_grad).astype(bf16)
        middle_grad = matmul(pair_grad, weight_down.T)
        sigma = jax.nn.sigmoid(gate_pre)
        active = gate_pre * sigma
        gate_pre_grad = (middle_grad * up_pre * sigma * (1.0 + gate_pre * (1.0 - sigma))).astype(
            bf16
        )
        up_pre_grad = (middle_grad * active).astype(bf16)
        pre_grad = jnp.concatenate([gate_pre_grad, up_pre_grad], 1)
        gu_local = matmul(moe_both.T, pre_grad).astype(bf16)
        input_grad = input_grad + matmul(pre_grad, weight_gu.T).astype(bf16).astype(f32)
        expert_grads.append(
            jnp.concatenate(
                [
                    gu_local.reshape(2, 2, quarter_rows, width),
                    down_local.reshape(2, 2, quarter_down, width),
                ],
                2,
            )
        )
    expert_mine, m = scatter_experts(expert_grads[0], expert_grads[1], place)
    half_rows, half_down = quarter_rows // 2, quarter_down // 2
    gu_halves = expert_mine[:quarter_rows].reshape(2, half_rows, width)
    down_halves = expert_mine[quarter_rows:].reshape(2, half_down, width)
    halves = jnp.concatenate([gu_halves, down_halves], 1)
    from_holder = across(pick(halves, 1 - core, 0), 1)
    expert_half = jnp.where(m < 2, pick(halves, core, 0), from_holder)
    gate_out = expert_half[None, :half_rows, : width // 2]
    up_out = expert_half[None, :half_rows, width // 2 :]
    down_out = expert_half[None, half_rows:]

    input_grad = input_grad[:local_rows] + across(input_grad[local_rows:], 1)
    slot_grads = jnp.stack(gate_grads, 1)
    own_slots, partner_slots = slot_grads[:local_rows], across(slot_grads[local_rows:], 1)
    from_low = jnp.where(core == 0, own_slots, partner_slots)
    from_high = jnp.where(core == 0, partner_slots, own_slots)
    prob_grad = chosen * jnp.concatenate([from_low, from_high[:, ::-1]], 1)
    logit_grad = router_probs * (
        prob_grad - jnp.sum(prob_grad * router_probs, axis=-1, keepdims=True)
    )
    router_local = jnp.dot(
        normed_moe.T, logit_grad, precision=highest, preferred_element_type=f32
    )
    normed_moe_grad = input_grad + jnp.dot(
        logit_grad, weight_router.T, precision=highest, preferred_element_type=f32
    )
    residual_part, moe_gain_local = norm_back(residual, scale_moe, gain_moe, normed_moe_grad)
    residual_grad = result_grad + residual_part
    branch_grad = residual_grad.astype(bf16)
    half = width // 2
    out_a = matmul(mixed_rows.T, branch_grad[:, :half]).astype(bf16)
    out_b = matmul(mixed_rows.T, branch_grad[:, half:]).astype(bf16)
    out_a, out_b = scatter_pair(out_a, out_b, place)
    out_out = jnp.concatenate([out_a, out_b], 1)
    mixed_grad = (
        matmul(branch_grad, weight_out.T).astype(bf16).reshape(local_rows, HEADS, HEAD_DIM)
    )

    def attend_backward(item):
        query_group, key_group, value_group, grad_group, peak, total = item
        scores = scores_of(query_group, key_group)
        probs = jnp.exp(scores - peak) / total
        weights = probs.astype(jnp.bfloat16)
        value_part = jnp.einsum(
            "hqk,qhd->khd", weights, grad_group, preferred_element_type=jnp.float32
        )
        probs_grad = jnp.einsum(
            "qhd,khd->hqk", grad_group, value_group, preferred_element_type=jnp.float32
        )
        inner = jnp.sum(probs * probs_grad, axis=-1, keepdims=True)
        score_grad = (probs * (probs_grad - inner)).astype(jnp.bfloat16)
        query_part = (
            jnp.einsum("hqk,khd->qhd", score_grad, key_group, preferred_element_type=jnp.float32)
            * score_scale
        )
        key_part = (
            jnp.einsum("hqk,qhd->khd", score_grad, query_group, preferred_element_type=jnp.float32)
            * score_scale
        )
        return (query_part.astype(bf16), key_part.astype(bf16), value_part.astype(bf16))

    query_parts, key_parts_grad, value_parts_grad = lax.map(
        attend_backward,
        (query_groups, key_groups, value_groups, by_group(mixed_grad), peaks, totals),
    )
    query_turned = rotate_back(
        from_group(query_parts).astype(f32).reshape(local_rows, HEADS, HEAD_DIM), cosine, sine
    ).reshape(local_rows, width)
    key_turned = rotate_back(
        from_group(key_parts_grad).astype(f32).reshape(all_rows, HEADS, HEAD_DIM),
        cosine_all,
        sine_all,
    ).reshape(all_rows, width)
    value_row_grad = from_group(value_parts_grad)
    query_lin_grad, q_gain_local = norm_back(query_lin, scale_query, gain_query, query_turned)
    key_lin_grad, k_gain_local = norm_back(key_lin, scale_key, gain_key, key_turned)
    query_lin_grad = query_lin_grad.astype(bf16)
    key_lin_grad = key_lin_grad.astype(bf16)
    value_a = matmul(normed_all.T, value_row_grad[:, :half]).astype(bf16)
    value_b = matmul(normed_all.T, value_row_grad[:, half:]).astype(bf16)
    value_a, value_b = scatter_pair(value_a, value_b, place)
    value_out = jnp.concatenate([value_a, value_b], 1)
    query_local = matmul(normed.T, query_lin_grad).astype(bf16)
    key_local = matmul(normed_all.T, key_lin_grad).astype(bf16)
    query_out, key_out = scatter_pair(query_local, key_local, place)
    normed_grad = matmul(key_lin_grad, weight_key.T) + matmul(value_row_grad, weight_value.T)
    normed_grad_own = normed_grad[behind:] + matmul(query_lin_grad, weight_query.T)
    attn_gain_local = jnp.sum(normed_grad * inputs_all * scale_all, axis=0) + jnp.sum(
        (normed_grad_own - normed_grad[behind:]) * inputs * scale_attn, axis=0
    )
    carried = 0.0
    for back in range(reach):
        carried = carried + normed_grad[back * local_rows : (back + 1) * local_rows]
        carried = from_behind(carried.astype(bf16), "ep", -1).astype(f32)
    normed_grad_own = normed_grad_own + carried
    inputs_part, _ = norm_back(inputs, scale_attn, gain_attn, normed_grad_own)
    tokens_grad = residual_grad + inputs_part

    packed = jnp.concatenate(
        [
            jnp.broadcast_to(squares, (1, width)),
            attn_gain_local[None],
            q_gain_local[None],
            k_gain_local[None],
            moe_gain_local[None],
            router_local.T,
        ],
        0,
    )
    packed = lax.psum(packed, ("rep", "ep"))
    loss = packed[0, 0] / (2.0 * count * width)
    own_rows = attn_gain.shape[0]
    mine = lax.dynamic_slice_in_dim(packed, (rep * experts + shard) * own_rows, own_rows, 1)
    return (
        output,
        loss,
        tokens_grad,
        mine[1],
        mine[2],
        mine[3],
        mine[4],
        query_out,
        key_out,
        value_out,
        out_out,
        mine[5:].T,
        gate_out,
        up_out,
        down_out,
    )


def solution(mesh):
    placed = (
        P(("rep", "ep"), None),
        P(("rep", "ep"), None),
        P("rep", "ep"),
        P("rep", "ep"),
        P(("rep", "ep"), None),
        P(("rep", "ep")),
        P(("rep", "ep")),
        P(("rep", "ep")),
        P(("rep", "ep")),
        P(("rep", "ep"), None),
        P(("rep", "ep"), None),
        P(("rep", "ep"), None),
        P(("rep", "ep"), None),
        P(("rep", "ep"), None),
        P("ep", None, None),
        P("ep", None, None),
        P("ep", None, None),
    )
    chips = mesh.shape["rep"] == 8 and mesh.shape["ep"] == 4
    return jax.shard_map(
        body if chips else body_plain,
        mesh=mesh,
        in_specs=placed,
        out_specs=(
            P(("rep", "ep"), None),
            P(),
            P(("rep", "ep"), None),
            P(("rep", "ep")),
            P(("rep", "ep")),
            P(("rep", "ep")),
            P(("rep", "ep")),
            P(("rep", "ep"), None),
            P(("rep", "ep"), None),
            P(("rep", "ep"), None),
            P(("rep", "ep"), None),
            P(("rep", "ep"), None),
            P("ep", "rep", None),
            P("ep", "rep", None),
            P("ep", "rep", None),
        ),
        check_vma=False,
    )
```

```python
import functools

import jax
import jax.numpy as jnp
from jax import lax
from jax.experimental import pallas as pl
from jax.experimental.pallas import tpu as pltpu
from jax.sharding import PartitionSpec as P

HEADS = 16
HEAD_DIM = 128
WINDOW = 1024
TOP = 2
VMEM_LIMIT = 56 * 1024 * 1024


norm_eps = 1e-05
highest = lax.Precision.HIGHEST


def from_behind(value, axis, steps):
    count = lax.axis_size(axis)
    leading, last = (max(0, -steps), min(count, count - steps))
    return lax.ppermute(value, axis, [(source, source + steps) for source in range(leading, last)])


def matmul(left, right):
    return jnp.dot(left, right, preferred_element_type=jnp.float32)


def rms_scale(value):
    return lax.rsqrt(jnp.mean(value * value, axis=-1, keepdims=True) + norm_eps)


def norm_back(value, scale, gain, grad):
    weighted = grad * gain
    inner = jnp.mean(weighted * value, axis=-1, keepdims=True)
    return (
        scale * weighted - value * (scale * scale * scale) * inner,
        jnp.sum(grad * value * scale, axis=0),
    )


def rounded(value):
    return lax.optimization_barrier(value.astype(jnp.bfloat16)).astype(jnp.float32)


def rotary_tables(positions, head_size):
    half = head_size // 2
    frequency = 10000.0 ** (-jnp.arange(half, dtype=jnp.float32) * 2.0 / head_size)
    angles = positions[:, None].astype(jnp.float32) * frequency[None, :]
    cosine = jnp.cos(angles)
    sine = jnp.sin(angles)
    return (
        jnp.concatenate([cosine, cosine], -1)[:, None, :],
        jnp.concatenate([sine, sine], -1)[:, None, :],
    )


def rotate(value, cosine, sine):
    half = value.shape[-1] // 2
    turned = jnp.concatenate([-value[..., half:], value[..., :half]], -1)
    return value * cosine + turned * sine


def rotate_back(grad, cosine, sine):
    half = grad.shape[-1] // 2
    scaled = grad * sine
    turned = jnp.concatenate([scaled[..., half:], -scaled[..., :half]], -1)
    return grad * cosine + turned


def unpack(everything):
    gains = [everything[index].astype(jnp.float32) for index in range(4)]
    return (gains, everything[4], everything[5], everything[6], everything[7], everything[8])


def body_plain(
    tokens,
    teacher,
    segment_ids,
    valid_mask,
    routes,
    attn_gain,
    q_gain,
    k_gain,
    moe_gain,
    w_query,
    w_key,
    w_value,
    w_out,
    w_router,
    w_gate,
    w_up,
    w_down,
):
    local_rows, width = tokens.shape
    experts = lax.axis_size("ep")
    pairs = local_rows * TOP
    capacity = 5 * pairs // (4 * experts)
    reach = min(-(-WINDOW // local_rows), experts - 1)
    group = min(HEADS, 4)
    score_scale = HEAD_DIM ** (-0.5)
    shard = lax.axis_index("ep")
    total_tokens = local_rows * lax.axis_size("rep") * experts
    everything = (
        lax.all_gather(attn_gain, ("rep", "ep"), axis=0, tiled=True),
        lax.all_gather(q_gain, ("rep", "ep"), axis=0, tiled=True),
        lax.all_gather(k_gain, ("rep", "ep"), axis=0, tiled=True),
        lax.all_gather(moe_gain, ("rep", "ep"), axis=0, tiled=True),
        lax.all_gather(w_query, ("rep", "ep"), axis=0, tiled=True),
        lax.all_gather(w_key, ("rep", "ep"), axis=0, tiled=True),
        lax.all_gather(w_value, ("rep", "ep"), axis=0, tiled=True),
        lax.all_gather(w_out, ("rep", "ep"), axis=0, tiled=True),
        lax.all_gather(w_router, ("rep", "ep"), axis=0, tiled=True),
    )
    gains, weight_query, weight_key, weight_value, weight_out, weight_router = unpack(everything)
    gain_attn, gain_query, gain_key, gain_moe = gains
    inputs = tokens.astype(jnp.float32)
    scale_attn = rms_scale(inputs)
    normed = (inputs * scale_attn * gain_attn).astype(jnp.bfloat16)
    query_lin = matmul(normed, weight_query)
    key_lin = matmul(normed, weight_key)
    value_rows = (
        matmul(normed, weight_value).astype(jnp.bfloat16).reshape(local_rows, HEADS, HEAD_DIM)
    )
    scale_query = rms_scale(query_lin)
    scale_key = rms_scale(key_lin)
    positions = shard * local_rows + jnp.arange(local_rows, dtype=jnp.int32)
    cosine, sine = rotary_tables(positions, HEAD_DIM)
    query_rows = rotate(
        (query_lin * scale_query * gain_query).reshape(local_rows, HEADS, HEAD_DIM), cosine, sine
    ).astype(jnp.bfloat16)
    key_rows = rotate(
        (key_lin * scale_key * gain_key).reshape(local_rows, HEADS, HEAD_DIM), cosine, sine
    ).astype(jnp.bfloat16)
    segments = segment_ids.reshape(local_rows)
    key_parts, value_parts, segment_parts = ([], [], [])
    for back in range(reach, 0, -1):
        moved = from_behind((key_rows, value_rows, segments.astype(jnp.bfloat16)), "ep", back)
        key_parts.append(moved[0])
        value_parts.append(moved[1])
        segment_parts.append(moved[2].astype(jnp.int32))
    all_keys = jnp.concatenate(key_parts + [key_rows], 0)
    all_values = jnp.concatenate(value_parts + [value_rows], 0)
    key_segments = jnp.concatenate(segment_parts + [segments], 0)
    key_positions = (shard - reach) * local_rows + jnp.arange(
        (reach + 1) * local_rows, dtype=jnp.int32
    )
    distance = positions[:, None] - key_positions[None, :]
    allowed = (
        (distance >= 0)
        & (distance < WINDOW)
        & (key_positions[None, :] >= 0)
        & (segments[:, None] == key_segments[None, :])
    )

    def by_group(value):
        return jnp.moveaxis(value.reshape(value.shape[0], HEADS // group, group, HEAD_DIM), 1, 0)

    def from_group(value):
        return jnp.moveaxis(value, 0, 1).reshape(value.shape[1], HEADS * HEAD_DIM)

    def scores_of(query_group, key_group):
        raw = (
            jnp.einsum("qhd,khd->hqk", query_group, key_group, preferred_element_type=jnp.float32)
            * score_scale
        )
        return jnp.where(allowed[None], raw, -1e30)

    def attend_forward(item):
        query_group, key_group, value_group = item
        scores = scores_of(query_group, key_group)
        peak = jnp.max(scores, axis=-1, keepdims=True)
        shifted = jnp.exp(scores - peak)
        total = jnp.sum(shifted, axis=-1, keepdims=True)
        weights = (shifted / total).astype(jnp.bfloat16)
        mixed = jnp.einsum("hqk,khd->qhd", weights, value_group, preferred_element_type=jnp.float32)
        return (mixed, peak, total)

    query_groups = by_group(query_rows)
    key_groups = by_group(all_keys)
    value_groups = by_group(all_values)
    mixed, peaks, totals = lax.map(attend_forward, (query_groups, key_groups, value_groups))
    mixed_rows = from_group(mixed).astype(jnp.bfloat16)
    residual = inputs + matmul(mixed_rows, weight_out)
    scale_moe = rms_scale(residual)
    normed_moe = (residual * scale_moe * gain_moe).astype(jnp.bfloat16)
    router_probs = jax.nn.softmax(matmul(normed_moe, weight_router), axis=-1)
    flat_routes = routes.reshape(pairs)
    choose = (flat_routes[:, None] == jnp.arange(experts, dtype=jnp.int32)[None, :]).astype(
        jnp.int32
    )
    rank = jnp.sum((jnp.cumsum(choose, axis=0) - choose) * choose, axis=1)
    slots = flat_routes * capacity + rank
    pair_source = (
        jnp.full((experts * capacity,), pairs, jnp.int32)
        .at[slots]
        .set(jnp.arange(pairs, dtype=jnp.int32))
    )
    token_source = jnp.where(pair_source < pairs, pair_source // TOP, local_rows)
    zero_row = jnp.zeros((1, width), jnp.bfloat16)
    outgoing = jnp.concatenate([normed_moe, zero_row], 0)[token_source].reshape(
        experts, capacity, width
    )
    choose_float = choose.reshape(local_rows, TOP, experts).astype(jnp.float32)
    gate_value = jnp.sum(choose_float * router_probs[:, None, :], axis=2)
    gate_weight = w_gate[0]
    up_weight = w_up[0]
    down_weight = w_down[0]
    piece = lax.all_to_all(outgoing, "ep", split_axis=0, concat_axis=0, tiled=True)
    flat = piece.reshape(-1, width)
    gate_pre = matmul(flat, gate_weight)
    up_pre = matmul(flat, up_weight)
    middle = (jax.nn.silu(gate_pre) * up_pre).astype(jnp.bfloat16)
    expert_out = matmul(middle, down_weight).astype(jnp.bfloat16)
    lead = piece.shape[:2]
    returned = expert_out.reshape(piece.shape)
    gate_kept = gate_pre.reshape(lead + (-1,))
    up_kept = up_pre.reshape(lead + (-1,))
    arrived = lax.all_to_all(returned, "ep", split_axis=0, concat_axis=0, tiled=True)
    expert_rows = arrived.reshape(experts * capacity, width)[slots].reshape(local_rows, TOP, width)
    result = residual + jnp.sum(gate_value[:, :, None] * expert_rows, axis=1)
    output = result.astype(jnp.bfloat16)
    valid = valid_mask.reshape(local_rows).astype(jnp.float32)
    error = result - teacher.astype(jnp.float32)
    squares = jnp.sum(valid * jnp.sum(error * error, axis=1))
    total_squares, count = lax.psum((squares, jnp.sum(valid)), ("rep", "ep"))
    loss = total_squares / (2.0 * count * width)
    result_grad = total_tokens / count * valid[:, None] * error
    gate_value_grad = jnp.sum(result_grad[:, None, :] * expert_rows, axis=2)
    pair_grad = (
        (gate_value[:, :, None] * result_grad[:, None, :])
        .astype(jnp.bfloat16)
        .reshape(pairs, width)
    )
    grad_outgoing = jnp.concatenate([pair_grad, zero_row], 0)[pair_source].reshape(
        experts, capacity, width
    )
    grad_in = lax.all_to_all(grad_outgoing, "ep", split_axis=0, concat_axis=0, tiled=True)
    rows_in = piece.reshape(-1, width)
    gate_pre = gate_kept.reshape(rows_in.shape[0], -1)
    up_pre = up_kept.reshape(rows_in.shape[0], -1)
    flat_grad = grad_in.reshape(-1, width)
    sigma = jax.nn.sigmoid(gate_pre)
    active = gate_pre * sigma
    middle = (active * up_pre).astype(jnp.bfloat16)
    down_local = matmul(middle.T, flat_grad)
    middle_grad = matmul(flat_grad, down_weight.T)
    gate_pre_grad = (middle_grad * up_pre * sigma * (1.0 + gate_pre * (1.0 - sigma))).astype(
        jnp.bfloat16
    )
    up_pre_grad = (middle_grad * active).astype(jnp.bfloat16)
    gate_local = matmul(rows_in.T, gate_pre_grad)
    up_local = matmul(rows_in.T, up_pre_grad)
    input_grad = (matmul(gate_pre_grad, gate_weight.T) + matmul(up_pre_grad, up_weight.T)).astype(
        jnp.bfloat16
    )
    back_rows = lax.all_to_all(
        input_grad.reshape(experts, capacity, width), "ep", split_axis=0, concat_axis=0, tiled=True
    )
    pair_back = back_rows.reshape(experts * capacity, width)[slots].reshape(local_rows, TOP, width)
    everything = (
        lax.all_gather(attn_gain, ("rep", "ep"), axis=0, tiled=True),
        lax.all_gather(q_gain, ("rep", "ep"), axis=0, tiled=True),
        lax.all_gather(k_gain, ("rep", "ep"), axis=0, tiled=True),
        lax.all_gather(moe_gain, ("rep", "ep"), axis=0, tiled=True),
        lax.all_gather(w_query, ("rep", "ep"), axis=0, tiled=True),
        lax.all_gather(w_key, ("rep", "ep"), axis=0, tiled=True),
        lax.all_gather(w_value, ("rep", "ep"), axis=0, tiled=True),
        lax.all_gather(w_out, ("rep", "ep"), axis=0, tiled=True),
        lax.all_gather(w_router, ("rep", "ep"), axis=0, tiled=True),
    )
    gains, weight_query, weight_key, weight_value, weight_out, weight_router = unpack(everything)
    gain_attn, gain_query, gain_key, gain_moe = gains
    prob_grad = jnp.sum(choose_float * gate_value_grad[:, :, None], axis=1)
    logit_grad = router_probs * (
        prob_grad - jnp.sum(prob_grad * router_probs, axis=-1, keepdims=True)
    )
    router_local = jnp.dot(
        normed_moe.T, logit_grad, precision=highest, preferred_element_type=jnp.float32
    )
    normed_moe_grad = jnp.sum(pair_back.astype(jnp.float32), axis=1) + jnp.dot(
        logit_grad, weight_router.T, precision=highest, preferred_element_type=jnp.float32
    )
    residual_part, moe_gain_local = norm_back(residual, scale_moe, gain_moe, normed_moe_grad)
    residual_grad = result_grad + residual_part
    branch_grad = residual_grad.astype(jnp.bfloat16)
    out_local = matmul(mixed_rows.T, branch_grad)
    mixed_grad = (
        matmul(branch_grad, weight_out.T).astype(jnp.bfloat16).reshape(local_rows, HEADS, HEAD_DIM)
    )

    def attend_backward(item):
        query_group, key_group, value_group, grad_group, peak, total = item
        scores = scores_of(query_group, key_group)
        probs = jnp.exp(scores - peak) / total
        weights = probs.astype(jnp.bfloat16)
        value_part = jnp.einsum(
            "hqk,qhd->khd", weights, grad_group, preferred_element_type=jnp.float32
        )
        probs_grad = jnp.einsum(
            "qhd,khd->hqk", grad_group, value_group, preferred_element_type=jnp.float32
        )
        inner = jnp.sum(probs * probs_grad, axis=-1, keepdims=True)
        score_grad = (probs * (probs_grad - inner)).astype(jnp.bfloat16)
        query_part = (
            jnp.einsum("hqk,khd->qhd", score_grad, key_group, preferred_element_type=jnp.float32)
            * score_scale
        )
        key_part = (
            jnp.einsum("hqk,qhd->khd", score_grad, query_group, preferred_element_type=jnp.float32)
            * score_scale
        )
        return (query_part, key_part, value_part)

    query_parts, key_parts_grad, value_parts_grad = lax.map(
        attend_backward,
        (query_groups, key_groups, value_groups, by_group(mixed_grad), peaks, totals),
    )
    query_row_grad = from_group(query_parts)
    key_all_grad = from_group(key_parts_grad)
    value_all_grad = from_group(value_parts_grad)
    own_keys = key_all_grad[reach * local_rows :]
    own_values = value_all_grad[reach * local_rows :]
    for back in range(1, reach + 1):
        start = (reach - back) * local_rows
        moved = from_behind(
            (key_all_grad[start : start + local_rows], value_all_grad[start : start + local_rows]),
            "ep",
            -back,
        )
        own_keys = own_keys + moved[0]
        own_values = own_values + moved[1]
    query_turned = rotate_back(
        rounded(query_row_grad).reshape(local_rows, HEADS, HEAD_DIM), cosine, sine
    ).reshape(local_rows, width)
    key_turned = rotate_back(
        rounded(own_keys).reshape(local_rows, HEADS, HEAD_DIM), cosine, sine
    ).reshape(local_rows, width)
    query_lin_grad, q_gain_local = norm_back(query_lin, scale_query, gain_query, query_turned)
    key_lin_grad, k_gain_local = norm_back(key_lin, scale_key, gain_key, key_turned)
    query_lin_grad = query_lin_grad.astype(jnp.bfloat16)
    key_lin_grad = key_lin_grad.astype(jnp.bfloat16)
    value_row_grad = own_values.astype(jnp.bfloat16)
    query_local = matmul(normed.T, query_lin_grad)
    key_local = matmul(normed.T, key_lin_grad)
    value_local = matmul(normed.T, value_row_grad)
    normed_grad = (
        matmul(query_lin_grad, weight_query.T)
        + matmul(key_lin_grad, weight_key.T)
        + matmul(value_row_grad, weight_value.T)
    )
    inputs_part, attn_gain_local = norm_back(inputs, scale_attn, gain_attn, normed_grad)
    tokens_grad = residual_grad + inputs_part
    summed = (
        lax.psum_scatter(attn_gain_local, ("rep", "ep"), scatter_dimension=0, tiled=True),
        lax.psum_scatter(q_gain_local, ("rep", "ep"), scatter_dimension=0, tiled=True),
        lax.psum_scatter(k_gain_local, ("rep", "ep"), scatter_dimension=0, tiled=True),
        lax.psum_scatter(moe_gain_local, ("rep", "ep"), scatter_dimension=0, tiled=True),
        lax.psum_scatter(query_local, ("rep", "ep"), scatter_dimension=0, tiled=True),
        lax.psum_scatter(key_local, ("rep", "ep"), scatter_dimension=0, tiled=True),
        lax.psum_scatter(value_local, ("rep", "ep"), scatter_dimension=0, tiled=True),
        lax.psum_scatter(out_local, ("rep", "ep"), scatter_dimension=0, tiled=True),
        lax.psum_scatter(router_local, ("rep", "ep"), scatter_dimension=0, tiled=True),
    )
    expert_summed = (
        lax.psum_scatter(gate_local[None], "rep", scatter_dimension=1, tiled=True),
        lax.psum_scatter(up_local[None], "rep", scatter_dimension=1, tiled=True),
        lax.psum_scatter(down_local[None], "rep", scatter_dimension=1, tiled=True),
    )
    return (
        output,
        loss,
        tokens_grad,
        summed[0],
        summed[1],
        summed[2],
        summed[3],
        summed[4],
        summed[5],
        summed[6],
        summed[7],
        summed[8],
        expert_summed[0],
        expert_summed[1],
        expert_summed[2],
    )


def dot_t(left, right):
    return lax.dot_general(left, right, (((1,), (1,)), ((), ())), preferred_element_type=jnp.float32)


def t_dot(left, right):
    return lax.dot_general(left, right, (((0,), (0,)), ((), ())), preferred_element_type=jnp.float32)


def kernel_call(kernel, **options):
    return pl.pallas_call(
        kernel,
        compiler_params=pltpu.CompilerParams(vmem_limit_bytes=VMEM_LIMIT),
        **options,
    )


def turn(value, cosine, sine):
    return value * cosine + pltpu.roll(value, HEAD_DIM // 2, 1) * sine


def code_of(place, blocks):
    return place % (blocks // 2) * 2 + place // (blocks // 2)


def place_of(code, blocks):
    return code % 2 * (blocks // 2) + code // 2


def norm_kernel(rank, x_ref, gain_ref, o_ref, scale_ref, *, blocks):
    value = x_ref[...].astype(jnp.float32)
    scale = lax.rsqrt(jnp.mean(value * value, axis=1, keepdims=True) + norm_eps)
    scale_ref[...] = scale
    block = x_ref.shape[1] // blocks
    for place in range(blocks):
        start = pl.multiple_of((rank[0] ^ code_of(place, blocks)) * block, block)
        piece = x_ref[:, pl.ds(start, block)].astype(jnp.float32)
        piece = piece * scale * gain_ref[:, pl.ds(start, block)]
        at = place % (blocks // 2) * block
        o_ref[place // (blocks // 2), :, at : at + block] = piece.astype(jnp.bfloat16)


def norm_rows(rank, value, gain, blocks):
    rows, width = value.shape
    tile = 256
    return kernel_call(
        functools.partial(norm_kernel, blocks=blocks),
        grid_spec=pltpu.PrefetchScalarGridSpec(
            num_scalar_prefetch=1,
            grid=(rows // tile,),
            in_specs=[
                pl.BlockSpec((tile, width), lambda i, rank: (i, 0)),
                pl.BlockSpec((1, width), lambda i, rank: (0, 0)),
            ],
            out_specs=[
                pl.BlockSpec((2, tile, width // 2), lambda i, rank: (0, i, 0)),
                pl.BlockSpec((tile, 1), lambda i, rank: (i, 0)),
            ],
        ),
        out_shape=[
            jax.ShapeDtypeStruct((2, rows, width // 2), jnp.bfloat16),
            jax.ShapeDtypeStruct((rows, 1), jnp.float32),
        ],
        cost_estimate=pl.CostEstimate(
            flops=8 * rows * width, bytes_accessed=4 * rows * width, transcendentals=0
        ),
    )(rank, value, gain[None])


def project_kernel(low_ref, high_ref, a_ref, b_ref, o_ref, s_ref):
    total = matmul(low_ref[0], a_ref[...]) + matmul(high_ref[0], b_ref[...])
    o_ref[...] = total.astype(o_ref.dtype)
    s_ref[...] = jnp.sum(total * total, axis=1, keepdims=True)


def project(halves, a, b, dtype, start=0):
    _, rows, depth = halves.shape
    rows = rows - start
    width = a.shape[1]
    tile = 256
    first = start // tile
    weight = pl.BlockSpec((depth, width), lambda i: (0, 0))
    return kernel_call(
        project_kernel,
        grid=(rows // tile,),
        in_specs=[
            pl.BlockSpec((1, tile, depth), lambda i: (0, i + first, 0)),
            pl.BlockSpec((1, tile, depth), lambda i: (1, i + first, 0)),
            weight,
            weight,
        ],
        out_specs=[
            pl.BlockSpec((tile, width), lambda i: (i, 0)),
            pl.BlockSpec((tile, 1), lambda i: (i, 0)),
        ],
        out_shape=[
            jax.ShapeDtypeStruct((rows, width), dtype),
            jax.ShapeDtypeStruct((rows, 1), jnp.float32),
        ],
        cost_estimate=pl.CostEstimate(
            flops=4 * rows * depth * width, bytes_accessed=8 * depth * width, transcendentals=0
        ),
    )(halves, halves, a, b)


def project_back_kernel(k_ref, v_ref, q_ref, ka, kb, va, vb, qa, qb, o_ref, *, own):
    i, j = pl.program_id(0), pl.program_id(1)
    half = pl.num_programs(1) // 2

    def part(key, value, query):
        total = dot_t(k_ref[...], key[...]) + dot_t(v_ref[...], value[...])
        o_ref[0] = total

        @pl.when(i >= own)
        def _():
            o_ref[0] += dot_t(q_ref[...], query[...])

    @pl.when(j < half)
    def _():
        part(ka, va, qa)

    @pl.when(j >= half)
    def _():
        part(kb, vb, qb)


def project_back(key, value, query, key_w, value_w, query_w):
    rows, width = key.shape
    depth = key_w[0].shape[0]
    tile, step = 512, 512
    half = depth // step
    own = (rows - query.shape[0]) // tile
    x_spec = pl.BlockSpec((tile, width), lambda i, j: (i, 0))
    low = pl.BlockSpec((step, width), lambda i, j: (jnp.minimum(j, half - 1), 0))
    high = pl.BlockSpec((step, width), lambda i, j: (jnp.maximum(j - half, 0), 0))
    return kernel_call(
        functools.partial(project_back_kernel, own=own),
        grid=(rows // tile, 2 * half),
        in_specs=[
            x_spec,
            x_spec,
            pl.BlockSpec((tile, width), lambda i, j: (jnp.maximum(i - own, 0), 0)),
        ]
        + [low, high] * 3,
        out_specs=pl.BlockSpec((1, tile, step), lambda i, j: (j // half, i, j % half)),
        out_shape=jax.ShapeDtypeStruct((2, rows, depth), jnp.float32),
        cost_estimate=pl.CostEstimate(
            flops=9 * rows * depth * width, bytes_accessed=32 * depth * width, transcendentals=0
        ),
    )(key, value, query, *key_w, *value_w, *query_w)


def tokens_back_kernel(
    rank, g_ref, c_ref, x_ref, res_ref, scale_ref, gain_ref, o_ref, gain_grad_ref, *, blocks
):
    scale = scale_ref[...]
    block = x_ref.shape[1] // blocks
    half = blocks // 2

    @pl.when(pl.program_id(0) == 0)
    def _():
        gain_grad_ref[...] = jnp.zeros_like(gain_grad_ref)

    def pieces(place):
        start = pl.multiple_of((rank[0] ^ code_of(place, blocks)) * block, block)
        at = slice(place % half * block, place % half * block + block)
        grad = g_ref[place // half, :, at] + c_ref[place // half, :, at].astype(jnp.float32)
        columns = pl.ds(start, block)
        return columns, grad, x_ref[:, columns].astype(jnp.float32), gain_ref[:, columns]

    inner = jnp.zeros_like(scale)
    for place in range(blocks):
        columns, grad, value, gain = pieces(place)
        product = grad * value
        inner += jnp.sum(product * gain, axis=1, keepdims=True)
        gain_grad_ref[:, columns] += jnp.sum(product * scale, axis=0, keepdims=True)
    inner = inner * (1.0 / x_ref.shape[1]) * (scale * scale * scale)
    for place in range(blocks):
        columns, grad, value, gain = pieces(place)
        o_ref[:, columns] = res_ref[:, columns] + (scale * (grad * gain) - value * inner)


def tokens_back(rank, grad, carried, tokens, residual_grad, scale, gain, blocks):
    rows, width = tokens.shape
    tile = 128
    first = (grad.shape[1] - rows) // tile
    wide = pl.BlockSpec((tile, width), lambda i, rank: (i, 0))
    one = pl.BlockSpec((1, width), lambda i, rank: (0, 0))
    return kernel_call(
        functools.partial(tokens_back_kernel, blocks=blocks),
        grid_spec=pltpu.PrefetchScalarGridSpec(
            num_scalar_prefetch=1,
            grid=(rows // tile,),
            in_specs=[
                pl.BlockSpec((2, tile, width // 2), lambda i, rank: (0, i + first, 0)),
                pl.BlockSpec((2, tile, width // 2), lambda i, rank: (0, i, 0)),
                wide,
                wide,
                pl.BlockSpec((tile, 1), lambda i, rank: (i + first, 0)),
                one,
            ],
            out_specs=[wide, one],
        ),
        out_shape=[
            jax.ShapeDtypeStruct((rows, width), jnp.float32),
            jax.ShapeDtypeStruct((1, width), jnp.float32),
        ],
        cost_estimate=pl.CostEstimate(
            flops=10 * rows * width, bytes_accessed=16 * rows * width, transcendentals=0
        ),
    )(rank, grad, carried, tokens, residual_grad, scale, gain[None])


def head_rows(lin, scale, gain, cosine, sine):
    return turn(lin * scale * gain, cosine, sine).astype(jnp.bfloat16)


def moved_head(head, rank):
    place = place_of((head // 2) ^ rank[0], HEADS // 2) * 2 + head % 2
    return place // (HEADS // 2), 0, place % (HEADS // 2)


def attention_specs(rows, all_rows, bias):
    head = lambda h, rank: (0, h)
    fixed = lambda h, rank: (0, 0)
    return [
        pl.BlockSpec((rows, HEAD_DIM), head),
        pl.BlockSpec((all_rows, HEAD_DIM), head),
        pl.BlockSpec((all_rows, HEAD_DIM), head),
        pl.BlockSpec((rows, 1), fixed),
        pl.BlockSpec((all_rows, 1), fixed),
        pl.BlockSpec((1, HEAD_DIM), head),
        pl.BlockSpec((1, HEAD_DIM), head),
        pl.BlockSpec((all_rows, HEAD_DIM), fixed),
        pl.BlockSpec((all_rows, HEAD_DIM), fixed),
        pl.BlockSpec(bias.shape, lambda h, rank: (0, 0, 0)),
    ]


def attend_kernel(
    rank,
    q_ref,
    k_ref,
    v_ref,
    sq_ref,
    sk_ref,
    gq_ref,
    gk_ref,
    cos_ref,
    sin_ref,
    bias_ref,
    o_ref,
    lse_ref,
    *,
    behind,
    tile,
    span,
):
    rows = q_ref.shape[0]
    cosine, sine = cos_ref[...], sin_ref[...]
    keys = head_rows(k_ref[...], sk_ref[...], gk_ref[...], cosine, sine)
    queries = head_rows(q_ref[...], sq_ref[...], gq_ref[...], cosine[behind:], sine[behind:])
    for t in range(rows // tile):
        at = slice(t * tile, (t + 1) * tile)
        seen = slice(t * tile, t * tile + span)
        scores = dot_t(keys[seen], queries[at])
        scores = scores * HEAD_DIM ** (-0.5) + bias_ref[t].astype(jnp.float32)
        peak = jnp.max(scores, axis=0, keepdims=True)
        shifted = jnp.exp(scores - peak)
        total = jnp.sum(shifted, axis=0, keepdims=True)
        weights = (shifted * (1.0 / total)).astype(jnp.bfloat16)
        o_ref[0, at, :] = t_dot(weights, v_ref[seen, :]).astype(jnp.bfloat16)
        lse_ref[0, :, at] = peak + jnp.log(total)


def attend(rank, operands, bias):
    rows, width = operands[0].shape
    all_rows = operands[1].shape[0]
    tiles, span, tile = bias.shape
    return kernel_call(
        functools.partial(attend_kernel, behind=all_rows - rows, tile=tile, span=span),
        grid_spec=pltpu.PrefetchScalarGridSpec(
            num_scalar_prefetch=1,
            grid=(HEADS,),
            in_specs=attention_specs(rows, all_rows, bias),
            out_specs=[
                pl.BlockSpec((1, rows, HEAD_DIM), moved_head),
                pl.BlockSpec((1, 1, rows), lambda h, rank: (h, 0, 0)),
            ],
        ),
        out_shape=[
            jax.ShapeDtypeStruct((2, rows, width // 2), jnp.bfloat16),
            jax.ShapeDtypeStruct((HEADS, 1, rows), jnp.float32),
        ],
        cost_estimate=pl.CostEstimate(
            flops=4 * rows * span * width,
            bytes_accessed=8 * all_rows * width,
            transcendentals=rows * span * HEADS,
        ),
    )(rank, *operands, bias)


def attend_back_kernel(
    rank,
    q_ref,
    k_ref,
    v_ref,
    sq_ref,
    sk_ref,
    gq_ref,
    gk_ref,
    cos_ref,
    sin_ref,
    bias_ref,
    g_ref,
    lse_ref,
    dq_ref,
    dk_ref,
    dv_ref,
    key_total,
    value_total,
    *,
    behind,
    tile,
    span,
):
    rows = q_ref.shape[0]
    score_scale = HEAD_DIM ** (-0.5)
    cosine, sine = cos_ref[...], sin_ref[...]
    keys = head_rows(k_ref[...], sk_ref[...], gk_ref[...], cosine, sine)
    queries = head_rows(q_ref[...], sq_ref[...], gq_ref[...], cosine[behind:], sine[behind:])
    key_total[...] = jnp.zeros_like(key_total)
    value_total[...] = jnp.zeros_like(value_total)
    for t in range(rows // tile):
        at = slice(t * tile, (t + 1) * tile)
        seen = slice(t * tile, t * tile + span)
        scores = dot_t(keys[seen], queries[at])
        scores = scores * score_scale + bias_ref[t].astype(jnp.float32)
        probs = jnp.exp(scores - lse_ref[0, :, at])
        grad = g_ref[0, at, :]
        value_total[seen, :] += matmul(probs.astype(jnp.bfloat16), grad)
        probs_grad = dot_t(v_ref[seen, :], grad)
        inner = jnp.sum(probs * probs_grad, axis=0, keepdims=True)
        score_grad = (probs * (probs_grad - inner)).astype(jnp.bfloat16)
        dq_ref[at, :] = (t_dot(score_grad, keys[seen]) * score_scale).astype(jnp.bfloat16)
        key_total[seen, :] += matmul(score_grad, queries[at])
    dk_ref[...] = (key_total[...] * score_scale).astype(jnp.bfloat16)
    dv_ref[...] = value_total[...].astype(jnp.bfloat16)


def attend_back(rank, operands, bias, grad, lse):
    rows, width = operands[0].shape
    all_rows = operands[1].shape[0]
    tiles, span, tile = bias.shape
    head = lambda h, rank: (0, h)
    return kernel_call(
        functools.partial(attend_back_kernel, behind=all_rows - rows, tile=tile, span=span),
        grid_spec=pltpu.PrefetchScalarGridSpec(
            num_scalar_prefetch=1,
            grid=(HEADS,),
            in_specs=attention_specs(rows, all_rows, bias)
            + [
                pl.BlockSpec((1, rows, HEAD_DIM), moved_head),
                pl.BlockSpec((1, 1, rows), lambda h, rank: (h, 0, 0)),
            ],
            out_specs=[
                pl.BlockSpec((rows, HEAD_DIM), head),
                pl.BlockSpec((all_rows, HEAD_DIM), head),
                pl.BlockSpec((all_rows, HEAD_DIM), head),
            ],
            scratch_shapes=[
                pltpu.VMEM((all_rows, HEAD_DIM), jnp.float32),
                pltpu.VMEM((all_rows, HEAD_DIM), jnp.float32),
            ],
        ),
        out_shape=[
            jax.ShapeDtypeStruct((rows, width), jnp.bfloat16),
            jax.ShapeDtypeStruct((all_rows, width), jnp.bfloat16),
            jax.ShapeDtypeStruct((all_rows, width), jnp.bfloat16),
        ],
        cost_estimate=pl.CostEstimate(
            flops=10 * rows * span * width,
            bytes_accessed=12 * all_rows * width,
            transcendentals=rows * span * HEADS,
        ),
    )(rank, *operands, bias, grad, lse)


def lin_back_kernel(g_ref, lin_ref, scale_ref, gain_ref, cos_ref, sin_ref, o_ref, gain_grad_ref):
    scale = scale_ref[...]
    cosine, sine = cos_ref[...], -sin_ref[...]
    inner = jnp.zeros_like(scale)

    @pl.when(pl.program_id(0) == 0)
    def _():
        gain_grad_ref[...] = jnp.zeros_like(gain_grad_ref)

    turned = []
    for h in range(HEADS):
        at = slice(h * HEAD_DIM, (h + 1) * HEAD_DIM)
        grad = turn(g_ref[:, at].astype(jnp.float32), cosine, sine)
        lin = lin_ref[:, at]
        product = grad * lin
        gain_grad_ref[:, at] += jnp.sum(product * scale, axis=0, keepdims=True)
        inner += jnp.sum(product * gain_ref[:, at], axis=1, keepdims=True)
    inner = inner * (1.0 / (HEADS * HEAD_DIM)) * (scale * scale * scale)
    for h in range(HEADS):
        at = slice(h * HEAD_DIM, (h + 1) * HEAD_DIM)
        grad = turn(g_ref[:, at].astype(jnp.float32), cosine, sine)
        value = scale * (grad * gain_ref[:, at]) - lin_ref[:, at] * inner
        o_ref[:, at] = value.astype(jnp.bfloat16)


def lin_back(grad, lin, scale, gain, cosine, sine):
    rows, width = lin.shape
    tile = 256
    wide = pl.BlockSpec((tile, width), lambda i: (i, 0))
    one = pl.BlockSpec((1, width), lambda i: (0, 0))
    table = pl.BlockSpec((tile, HEAD_DIM), lambda i: (i, 0))
    return kernel_call(
        lin_back_kernel,
        grid=(rows // tile,),
        in_specs=[wide, wide, pl.BlockSpec((tile, 1), lambda i: (i, 0)), one, table, table],
        out_specs=[wide, one],
        out_shape=[
            jax.ShapeDtypeStruct((rows, width), jnp.bfloat16),
            jax.ShapeDtypeStruct((1, width), jnp.float32),
        ],
        cost_estimate=pl.CostEstimate(
            flops=10 * rows * width, bytes_accessed=8 * rows * width, transcendentals=0
        ),
    )(grad, lin, scale, gain, cosine, sine)


def across(value, bit):
    count = lax.axis_size("rep")
    return lax.ppermute(value, "rep", [(place, place ^ bit) for place in range(count)])


def along(value, steps):
    count = lax.axis_size("ep")
    return lax.ppermute(value, "ep", [(place, (place + steps) % count) for place in range(count)])


def mirrored(value, moves):
    reps, count = lax.axis_size("rep"), lax.axis_size("ep")
    pairs = []
    for rep in range(reps):
        for source, target in moves:
            if rep % 2:
                source, target = count - 1 - source, count - 1 - target
            pairs.append((rep * count + source, rep * count + target))
    return lax.ppermute(value, ("rep", "ep"), pairs)


def pick(value, index, axis):
    return lax.dynamic_index_in_dim(value, index, axis, keepdims=False)


def in_order(own, other, bit, axis):
    return jnp.where(bit == 1, jnp.stack([other, own], axis), jnp.stack([own, other], axis))


def over_ep(value, place):
    shard = place[3]
    experts = lax.axis_size("ep")
    parts = jnp.zeros((experts,) + value.shape, value.dtype)
    parts = lax.dynamic_update_index_in_dim(parts, value, shard, 0)
    for steps in range(1, experts):
        parts = lax.dynamic_update_index_in_dim(
            parts, along(value, steps), lax.rem(shard - steps + experts, experts), 0
        )
    return parts


def gather_small(value, place):
    y_bit, x_bit, core, shard = place
    value = over_ep(value, place)
    value = in_order(value, across(value, 1), core, 0)
    value = in_order(value, across(value, 2), x_bit, 0)
    return in_order(value, across(value, 4), y_bit, 0)


def sum_small(value, place):
    value = value + across(value, 1)
    value = value + across(value, 2)
    value = value + across(value, 4)
    return jnp.sum(over_ep(value, place), axis=0)


def gather_pair(left, right, place):
    width = left.shape[1]
    parts = over_ep(jnp.stack([left, right]), place)
    a, b = parts[:, 0].reshape(-1, width), parts[:, 1].reshape(-1, width)
    a_x, b_y = across(a, 2), across(b, 4)
    a = jnp.concatenate([a, a_x], 0)
    b_both = jnp.stack([b, b_y])
    a_y, b_x = across(a, 4), across(b_both, 2)
    a = jnp.concatenate([a, a_y], 0)
    b = jnp.concatenate([b, b_x[0], b_y, b_x[1]], 0)
    return (a, across(a, 1)), (b, across(b, 1))


def half_step(value, bit, axis, link):
    sent = across(pick(value, 1 - bit, axis), link)
    kept = pick(value, bit, axis)
    return (kept.astype(jnp.float32) + sent.astype(jnp.float32)).astype(jnp.bfloat16)


def plane_sum(left, right, place):
    y_bit, x_bit, core, shard = place
    a = half_step(left, x_bit, 1, 2)
    b = half_step(right, y_bit, 0, 4)
    return half_step(a, y_bit, 0, 4), half_step(b, x_bit, 0, 2)


def chip_sum(halves, grad):
    sent = across(t_dot(halves[1], grad).astype(jnp.bfloat16), 1)
    kept = t_dot(halves[0], grad) + sent.astype(jnp.float32)
    return kept.astype(jnp.bfloat16).reshape(2, 2, -1, grad.shape[1])


def add(left, right):
    return (left.astype(jnp.float32) + right.astype(jnp.float32)).astype(jnp.bfloat16)


def scatter_pair(a, b, place):
    shard = place[3]
    experts = lax.axis_size("ep")
    a_x, b_y = across(a[:, 1], 2), across(b[1], 4)
    a, b = add(a[:, 0], a_x), add(b[0], b_y)
    a_y, b_x = across(a[1], 4), across(b[1], 2)
    a, b = add(a[0], a_y), add(b[0], b_x)
    both = jnp.stack([a, b])
    both = both.reshape(2, experts, both.shape[1] // experts, both.shape[2])
    total = pick(both, shard, 1).astype(jnp.float32)
    for steps in range(1, experts):
        total = total + along(pick(both, lax.rem(shard + steps, experts), 1), steps)
    return total[0], total[1]


def gather_experts(quarter, place):
    y_bit, x_bit, core, shard = place
    m = jnp.where(core == 0, shard, lax.axis_size("ep") - 1 - shard)
    one = mirrored(quarter, [(0, 1), (1, 2)])
    two = mirrored(jnp.where(m == 2, one, quarter), [(1, 0), (2, 3)])
    three = mirrored(one, [(1, 2)])
    four = mirrored(three, [(2, 3)])
    a = jnp.where(m == 0, quarter, jnp.where(m == 1, one, jnp.where(m == 2, three, four)))
    b = jnp.where(m == 1, quarter, jnp.where(m == 2, one, two))
    a_x, b_y = across(a, 2), across(b, 4)
    a, b = in_order(a, a_x, x_bit, 0), in_order(b, b_y, y_bit, 0)
    a_y, b_x = across(a, 4), across(b, 2)
    return in_order(a, a_y, y_bit, 0), in_order(b, b_x, x_bit, 1)


def scatter_experts(left, right, place):
    y_bit, x_bit, core, shard = place
    m = jnp.where(core == 0, shard, lax.axis_size("ep") - 1 - shard)
    a, b = plane_sum(left, right, place)
    both = jnp.stack([a, b])
    up = mirrored(b, [(0, 1)])
    got = mirrored(both, [(3, 2)])
    both = (both.astype(jnp.float32) + got.astype(jnp.float32)).astype(jnp.bfloat16)
    got = mirrored(both, [(2, 1)])
    both = both.astype(jnp.float32) + got.astype(jnp.float32)
    a, b = both[0], both[1]
    got = mirrored(a.astype(jnp.bfloat16), [(1, 0)])
    mine = jnp.where(m == 0, a + got.astype(jnp.float32), b + up.astype(jnp.float32))
    return mine, m


def body(
    tokens,
    teacher,
    segment_ids,
    valid_mask,
    routes,
    attn_gain,
    q_gain,
    k_gain,
    moe_gain,
    w_query,
    w_key,
    w_value,
    w_out,
    w_router,
    w_gate,
    w_up,
    w_down,
):
    bf16, f32 = jnp.bfloat16, jnp.float32
    local_rows, width = tokens.shape
    experts = lax.axis_size("ep")
    reps = lax.axis_size("rep")
    reach = min(-(-WINDOW // local_rows), experts - 1)
    shard = lax.axis_index("ep")
    rep = lax.axis_index("rep")
    place = (rep // 4, rep // 2 % 2, rep % 2, shard)
    core = rep % 2
    total_tokens = local_rows * reps * experts

    valid = valid_mask.reshape(local_rows).astype(f32)
    own_count = jnp.sum(valid_mask)
    counts = jnp.stack([own_count // 16, own_count % 16]).astype(bf16)
    small = jnp.concatenate(
        [
            jnp.stack([attn_gain, q_gain, k_gain, moe_gain], 1),
            w_router,
            jnp.broadcast_to(counts[None], (attn_gain.shape[0], 2)),
        ],
        1,
    )
    small = gather_small(small.T, place)
    small = jnp.moveaxis(small, 4, 0).reshape(small.shape[4], -1)
    gain_attn, gain_query, gain_key, gain_moe = [small[i].astype(f32) for i in range(4)]
    weight_router = small[4 : 4 + experts].T
    counts = small[4 + experts :, :: attn_gain.shape[0]].astype(f32)
    count = jnp.sum(counts[0]) * 16.0 + jnp.sum(counts[1])

    key_w, value_w = gather_pair(w_key, w_value, place)
    query_w, out_w = gather_pair(w_query, w_out, place)
    rank = rep.astype(jnp.int32)[None]
    blocks = reps

    moved, moved_segments = tokens, segment_ids.reshape(local_rows)
    token_parts, segment_parts = [tokens], [moved_segments]
    for back in range(reach):
        moved = from_behind(moved, "ep", 1)
        moved_segments = from_behind(moved_segments, "ep", 1)
        token_parts.insert(0, moved)
        segment_parts.insert(0, moved_segments)
    behind = reach * local_rows
    tokens_all = jnp.concatenate(token_parts, 0)
    key_segments = jnp.concatenate(segment_parts, 0)
    inputs = tokens.astype(f32)

    quarter_rows = w_gate.shape[1] // 4
    quarter_down = w_down.shape[1] // 4
    quarter = rep // 2
    quarter_gate = lax.dynamic_slice_in_dim(w_gate[0], quarter * quarter_rows, quarter_rows, 0)
    quarter_up = lax.dynamic_slice_in_dim(w_up[0], quarter * quarter_rows, quarter_rows, 0)
    quarter_down_w = lax.dynamic_slice_in_dim(w_down[0], quarter * quarter_down, quarter_down, 0)
    own_quarter = jnp.concatenate(
        [jnp.concatenate([quarter_gate, quarter_up], 1), quarter_down_w], 0
    )

    all_rows = local_rows + behind
    normed, scale_all = norm_rows(rank, tokens_all, gain_attn, blocks)
    key_lin, key_squares = project(normed, *key_w, f32)
    value_all, _ = project(normed, *value_w, bf16)
    query_lin, query_squares = project(normed, *query_w, f32, behind)
    scale_key = lax.rsqrt(key_squares / width + norm_eps)
    scale_query = lax.rsqrt(query_squares / width + norm_eps)
    key_positions = (shard - reach) * local_rows + jnp.arange(all_rows, dtype=jnp.int32)
    half_head = HEAD_DIM // 2
    frequency = 10000.0 ** (-jnp.arange(half_head, dtype=f32) * 2.0 / HEAD_DIM)
    angles = key_positions[:, None].astype(f32) * frequency[None, :]
    cosine, sine = jnp.cos(angles), jnp.sin(angles)
    cosine, sine = jnp.concatenate([cosine, cosine], 1), jnp.concatenate([-sine, sine], 1)

    def mask_of(tile):
        span = behind + tile
        parts = []
        for start in range(0, local_rows, tile):
            keys = slice(start, start + span)
            queries = slice(behind + start, behind + start + tile)
            distance = key_positions[None, queries] - key_positions[keys, None]
            allowed = (
                (distance >= 0)
                & (distance < WINDOW)
                & (key_positions[keys, None] >= 0)
                & (key_segments[None, queries] == key_segments[keys, None])
            )
            parts.append(jnp.where(allowed, 0.0, -1e30).astype(f32))
        return jnp.stack(parts)

    operands = (
        query_lin,
        key_lin,
        value_all,
        scale_query,
        scale_key,
        gain_query[None],
        gain_key[None],
        cosine,
        sine,
    )
    mixed, lse = attend(rank, operands, mask_of(local_rows // 4))
    branch, _ = project(mixed, *out_w, f32)
    residual = inputs + branch
    scale_moe = rms_scale(residual)
    normed_moe = (residual * scale_moe * gain_moe).astype(bf16)
    partner_moe = across(normed_moe, 1)
    router_probs = jax.nn.softmax(matmul(normed_moe, weight_router), axis=-1)
    chosen = jnp.sum(
        (routes[:, :, None] == jnp.arange(experts, dtype=jnp.int32)).astype(f32), axis=1
    )
    gates = router_probs * chosen
    ends = ((0, experts - 1), (1, experts - 2))

    def slot_of(value, slot, of_core):
        low, high = ends[slot]
        return jnp.where(of_core == 0, value[:, low], value[:, high])

    gates_both = jnp.concatenate([gates, across(gates, 1)], 0)
    moe_both = jnp.concatenate([normed_moe, partner_moe], 0)

    experts_a, experts_b = gather_experts(own_quarter, place)
    slots = []
    mixture = 0.0
    for slot, pieces in enumerate((experts_a, experts_b)):
        weight_gu = pieces[:, :, :quarter_rows].reshape(4 * quarter_rows, width)
        weight_down = pieces[:, :, quarter_rows:].reshape(4 * quarter_down, width)
        hidden = width // 2
        pre = matmul(moe_both, weight_gu)
        gate_pre, up_pre = pre[:, :hidden], pre[:, hidden:]
        middle = (jax.nn.silu(gate_pre) * up_pre).astype(bf16)
        expert_out = matmul(middle, weight_down).astype(bf16)
        gate = slot_of(gates_both, slot, core)
        mixture = mixture + gate[:, None] * expert_out
        slots.append((weight_gu, weight_down, gate_pre, up_pre, middle, expert_out, gate))
    result = residual + (mixture[:local_rows] + across(mixture[local_rows:], 1))
    output = result.astype(bf16)
    error = result - teacher.astype(f32)
    squares = jnp.sum(valid * jnp.sum(error * error, axis=1))
    result_grad = total_tokens / count * valid[:, None] * error
    result_grad_both = jnp.concatenate([result_grad, across(result_grad, 1)], 0)

    input_grad = 0.0
    gate_grads, expert_grads = [], []
    for weight_gu, weight_down, gate_pre, up_pre, middle, expert_out, gate in slots:
        gate_grads.append(jnp.sum(result_grad_both * expert_out, axis=1))
        pair_grad = (gate[:, None] * result_grad_both).astype(bf16)
        down_local = matmul(middle.T, pair_grad).astype(bf16)
        middle_grad = matmul(pair_grad, weight_down.T)
        sigma = jax.nn.sigmoid(gate_pre)
        active = gate_pre * sigma
        gate_pre_grad = (middle_grad * up_pre * sigma * (1.0 + gate_pre * (1.0 - sigma))).astype(
            bf16
        )
        up_pre_grad = (middle_grad * active).astype(bf16)
        pre_grad = jnp.concatenate([gate_pre_grad, up_pre_grad], 1)
        gu_local = matmul(moe_both.T, pre_grad).astype(bf16)
        input_grad = input_grad + matmul(pre_grad, weight_gu.T).astype(bf16).astype(f32)
        expert_grads.append(
            jnp.concatenate(
                [
                    gu_local.reshape(2, 2, quarter_rows, width),
                    down_local.reshape(2, 2, quarter_down, width),
                ],
                2,
            )
        )
    expert_mine, m = scatter_experts(expert_grads[0], expert_grads[1], place)
    half_rows, half_down = quarter_rows // 2, quarter_down // 2
    gu_halves = expert_mine[:quarter_rows].reshape(2, half_rows, width)
    down_halves = expert_mine[quarter_rows:].reshape(2, half_down, width)
    halves = jnp.concatenate([gu_halves, down_halves], 1)
    from_holder = across(pick(halves, 1 - core, 0), 1)
    expert_half = jnp.where(m < 2, pick(halves, core, 0), from_holder)
    gate_out = expert_half[None, :half_rows, : width // 2]
    up_out = expert_half[None, :half_rows, width // 2 :]
    down_out = expert_half[None, half_rows:]

    input_grad = input_grad[:local_rows] + across(input_grad[local_rows:], 1)
    slot_grads = jnp.stack(gate_grads, 1)
    own_slots, partner_slots = slot_grads[:local_rows], across(slot_grads[local_rows:], 1)
    from_low = jnp.where(core == 0, own_slots, partner_slots)
    from_high = jnp.where(core == 0, partner_slots, own_slots)
    prob_grad = chosen * jnp.concatenate([from_low, from_high[:, ::-1]], 1)
    logit_grad = router_probs * (
        prob_grad - jnp.sum(prob_grad * router_probs, axis=-1, keepdims=True)
    )
    router_local = jnp.dot(
        normed_moe.T, logit_grad, precision=highest, preferred_element_type=f32
    )
    normed_moe_grad = input_grad + jnp.dot(
        logit_grad, weight_router.T, precision=highest, preferred_element_type=f32
    )
    residual_part, moe_gain_local = norm_back(residual, scale_moe, gain_moe, normed_moe_grad)
    residual_grad = result_grad + residual_part
    branch_grad = residual_grad.astype(bf16)
    half = width // 2
    out_a, out_b = scatter_pair(
        chip_sum(mixed, branch_grad[:, :half]), chip_sum(mixed, branch_grad[:, half:]), place
    )
    out_out = jnp.concatenate([out_a, out_b], 1)
    mixed_grad = jnp.stack([dot_t(branch_grad, weight).astype(bf16) for weight in out_w])
    query_row_grad, key_row_grad, value_row_grad = attend_back(
        rank, operands, mask_of(local_rows // 2), mixed_grad, lse
    )
    value_a, value_b = scatter_pair(
        chip_sum(normed, value_row_grad[:, :half]),
        chip_sum(normed, value_row_grad[:, half:]),
        place,
    )
    value_out = jnp.concatenate([value_a, value_b], 1)
    query_lin_grad, q_gain_local = lin_back(
        query_row_grad,
        query_lin,
        scale_query,
        gain_query[None],
        cosine[behind:],
        sine[behind:],
    )
    key_lin_grad, k_gain_local = lin_back(
        key_row_grad, key_lin, scale_key, gain_key[None], cosine, sine
    )
    query_out, key_out = scatter_pair(
        chip_sum(normed[:, behind:], query_lin_grad), chip_sum(normed, key_lin_grad), place
    )
    normed_grad = project_back(
        key_lin_grad, value_row_grad, query_lin_grad, key_w, value_w, query_w
    )
    carried = jnp.zeros((2, local_rows, width // 2), f32)
    for back in range(reach):
        carried = carried + normed_grad[:, back * local_rows : (back + 1) * local_rows]
        carried = from_behind(carried.astype(bf16), "ep", -1).astype(f32)
    tokens_grad, attn_gain_local = tokens_back(
        rank,
        normed_grad,
        carried.astype(bf16),
        tokens,
        residual_grad,
        scale_all,
        gain_attn,
        blocks,
    )

    packed = jnp.concatenate(
        [
            jnp.broadcast_to(squares, (1, width)),
            attn_gain_local,
            q_gain_local,
            k_gain_local,
            moe_gain_local[None],
            router_local.T,
        ],
        0,
    )
    packed = sum_small(packed, place)
    loss = packed[0, 0] / (2.0 * count * width)
    own_rows = attn_gain.shape[0]
    mine = lax.dynamic_slice_in_dim(packed, (rep * experts + shard) * own_rows, own_rows, 1)
    return (
        output,
        loss,
        tokens_grad,
        mine[1],
        mine[2],
        mine[3],
        mine[4],
        query_out,
        key_out,
        value_out,
        out_out,
        mine[5:].T,
        gate_out,
        up_out,
        down_out,
    )


def solution(mesh):
    placed = (
        P(("rep", "ep"), None),
        P(("rep", "ep"), None),
        P("rep", "ep"),
        P("rep", "ep"),
        P(("rep", "ep"), None),
        P(("rep", "ep")),
        P(("rep", "ep")),
        P(("rep", "ep")),
        P(("rep", "ep")),
        P(("rep", "ep"), None),
        P(("rep", "ep"), None),
        P(("rep", "ep"), None),
        P(("rep", "ep"), None),
        P(("rep", "ep"), None),
        P("ep", None, None),
        P("ep", None, None),
        P("ep", None, None),
    )
    chips = mesh.shape["rep"] == 8 and mesh.shape["ep"] == 4
    return jax.shard_map(
        body if chips else body_plain,
        mesh=mesh,
        in_specs=placed,
        out_specs=(
            P(("rep", "ep"), None),
            P(),
            P(("rep", "ep"), None),
            P(("rep", "ep")),
            P(("rep", "ep")),
            P(("rep", "ep")),
            P(("rep", "ep")),
            P(("rep", "ep"), None),
            P(("rep", "ep"), None),
            P(("rep", "ep"), None),
            P(("rep", "ep"), None),
            P(("rep", "ep"), None),
            P("ep", "rep", None),
            P("ep", "rep", None),
            P("ep", "rep", None),
        ),
        check_vma=False,
    )
```

```python
import functools

import jax
import jax.numpy as jnp
from jax import lax
from jax.experimental import pallas as pl
from jax.experimental.pallas import tpu as pltpu
from jax.sharding import PartitionSpec as P

HEADS = 16
HEAD_DIM = 128
WINDOW = 1024
TOP = 2
VMEM_LIMIT = 56 * 1024 * 1024


norm_eps = 1e-05
highest = lax.Precision.HIGHEST


def from_behind(value, axis, steps):
    count = lax.axis_size(axis)
    leading, last = (max(0, -steps), min(count, count - steps))
    return lax.ppermute(value, axis, [(source, source + steps) for source in range(leading, last)])


def matmul(left, right):
    return jnp.dot(left, right, preferred_element_type=jnp.float32)


def rms_scale(value):
    return lax.rsqrt(jnp.mean(value * value, axis=-1, keepdims=True) + norm_eps)


def norm_back(value, scale, gain, grad):
    weighted = grad * gain
    inner = jnp.mean(weighted * value, axis=-1, keepdims=True)
    return (
        scale * weighted - value * (scale * scale * scale) * inner,
        jnp.sum(grad * value * scale, axis=0),
    )


def rounded(value):
    return lax.optimization_barrier(value.astype(jnp.bfloat16)).astype(jnp.float32)


def rotary_tables(positions, head_size):
    half = head_size // 2
    frequency = 10000.0 ** (-jnp.arange(half, dtype=jnp.float32) * 2.0 / head_size)
    angles = positions[:, None].astype(jnp.float32) * frequency[None, :]
    cosine = jnp.cos(angles)
    sine = jnp.sin(angles)
    return (
        jnp.concatenate([cosine, cosine], -1)[:, None, :],
        jnp.concatenate([sine, sine], -1)[:, None, :],
    )


def rotate(value, cosine, sine):
    half = value.shape[-1] // 2
    turned = jnp.concatenate([-value[..., half:], value[..., :half]], -1)
    return value * cosine + turned * sine


def rotate_back(grad, cosine, sine):
    half = grad.shape[-1] // 2
    scaled = grad * sine
    turned = jnp.concatenate([scaled[..., half:], -scaled[..., :half]], -1)
    return grad * cosine + turned


def unpack(everything):
    gains = [everything[index].astype(jnp.float32) for index in range(4)]
    return (gains, everything[4], everything[5], everything[6], everything[7], everything[8])


def body_plain(
    tokens,
    teacher,
    segment_ids,
    valid_mask,
    routes,
    attn_gain,
    q_gain,
    k_gain,
    moe_gain,
    w_query,
    w_key,
    w_value,
    w_out,
    w_router,
    w_gate,
    w_up,
    w_down,
):
    local_rows, width = tokens.shape
    experts = lax.axis_size("ep")
    pairs = local_rows * TOP
    capacity = 5 * pairs // (4 * experts)
    reach = min(-(-WINDOW // local_rows), experts - 1)
    group = min(HEADS, 4)
    score_scale = HEAD_DIM ** (-0.5)
    shard = lax.axis_index("ep")
    total_tokens = local_rows * lax.axis_size("rep") * experts
    everything = (
        lax.all_gather(attn_gain, ("rep", "ep"), axis=0, tiled=True),
        lax.all_gather(q_gain, ("rep", "ep"), axis=0, tiled=True),
        lax.all_gather(k_gain, ("rep", "ep"), axis=0, tiled=True),
        lax.all_gather(moe_gain, ("rep", "ep"), axis=0, tiled=True),
        lax.all_gather(w_query, ("rep", "ep"), axis=0, tiled=True),
        lax.all_gather(w_key, ("rep", "ep"), axis=0, tiled=True),
        lax.all_gather(w_value, ("rep", "ep"), axis=0, tiled=True),
        lax.all_gather(w_out, ("rep", "ep"), axis=0, tiled=True),
        lax.all_gather(w_router, ("rep", "ep"), axis=0, tiled=True),
    )
    gains, weight_query, weight_key, weight_value, weight_out, weight_router = unpack(everything)
    gain_attn, gain_query, gain_key, gain_moe = gains
    inputs = tokens.astype(jnp.float32)
    scale_attn = rms_scale(inputs)
    normed = (inputs * scale_attn * gain_attn).astype(jnp.bfloat16)
    query_lin = matmul(normed, weight_query)
    key_lin = matmul(normed, weight_key)
    value_rows = (
        matmul(normed, weight_value).astype(jnp.bfloat16).reshape(local_rows, HEADS, HEAD_DIM)
    )
    scale_query = rms_scale(query_lin)
    scale_key = rms_scale(key_lin)
    positions = shard * local_rows + jnp.arange(local_rows, dtype=jnp.int32)
    cosine, sine = rotary_tables(positions, HEAD_DIM)
    query_rows = rotate(
        (query_lin * scale_query * gain_query).reshape(local_rows, HEADS, HEAD_DIM), cosine, sine
    ).astype(jnp.bfloat16)
    key_rows = rotate(
        (key_lin * scale_key * gain_key).reshape(local_rows, HEADS, HEAD_DIM), cosine, sine
    ).astype(jnp.bfloat16)
    segments = segment_ids.reshape(local_rows)
    key_parts, value_parts, segment_parts = ([], [], [])
    for back in range(reach, 0, -1):
        moved = from_behind((key_rows, value_rows, segments.astype(jnp.bfloat16)), "ep", back)
        key_parts.append(moved[0])
        value_parts.append(moved[1])
        segment_parts.append(moved[2].astype(jnp.int32))
    all_keys = jnp.concatenate(key_parts + [key_rows], 0)
    all_values = jnp.concatenate(value_parts + [value_rows], 0)
    key_segments = jnp.concatenate(segment_parts + [segments], 0)
    key_positions = (shard - reach) * local_rows + jnp.arange(
        (reach + 1) * local_rows, dtype=jnp.int32
    )
    distance = positions[:, None] - key_positions[None, :]
    allowed = (
        (distance >= 0)
        & (distance < WINDOW)
        & (key_positions[None, :] >= 0)
        & (segments[:, None] == key_segments[None, :])
    )

    def by_group(value):
        return jnp.moveaxis(value.reshape(value.shape[0], HEADS // group, group, HEAD_DIM), 1, 0)

    def from_group(value):
        return jnp.moveaxis(value, 0, 1).reshape(value.shape[1], HEADS * HEAD_DIM)

    def scores_of(query_group, key_group):
        raw = (
            jnp.einsum("qhd,khd->hqk", query_group, key_group, preferred_element_type=jnp.float32)
            * score_scale
        )
        return jnp.where(allowed[None], raw, -1e30)

    def attend_forward(item):
        query_group, key_group, value_group = item
        scores = scores_of(query_group, key_group)
        peak = jnp.max(scores, axis=-1, keepdims=True)
        shifted = jnp.exp(scores - peak)
        total = jnp.sum(shifted, axis=-1, keepdims=True)
        weights = (shifted / total).astype(jnp.bfloat16)
        mixed = jnp.einsum("hqk,khd->qhd", weights, value_group, preferred_element_type=jnp.float32)
        return (mixed, peak, total)

    query_groups = by_group(query_rows)
    key_groups = by_group(all_keys)
    value_groups = by_group(all_values)
    mixed, peaks, totals = lax.map(attend_forward, (query_groups, key_groups, value_groups))
    mixed_rows = from_group(mixed).astype(jnp.bfloat16)
    residual = inputs + matmul(mixed_rows, weight_out)
    scale_moe = rms_scale(residual)
    normed_moe = (residual * scale_moe * gain_moe).astype(jnp.bfloat16)
    router_probs = jax.nn.softmax(matmul(normed_moe, weight_router), axis=-1)
    flat_routes = routes.reshape(pairs)
    choose = (flat_routes[:, None] == jnp.arange(experts, dtype=jnp.int32)[None, :]).astype(
        jnp.int32
    )
    rank = jnp.sum((jnp.cumsum(choose, axis=0) - choose) * choose, axis=1)
    slots = flat_routes * capacity + rank
    pair_source = (
        jnp.full((experts * capacity,), pairs, jnp.int32)
        .at[slots]
        .set(jnp.arange(pairs, dtype=jnp.int32))
    )
    token_source = jnp.where(pair_source < pairs, pair_source // TOP, local_rows)
    zero_row = jnp.zeros((1, width), jnp.bfloat16)
    outgoing = jnp.concatenate([normed_moe, zero_row], 0)[token_source].reshape(
        experts, capacity, width
    )
    choose_float = choose.reshape(local_rows, TOP, experts).astype(jnp.float32)
    gate_value = jnp.sum(choose_float * router_probs[:, None, :], axis=2)
    gate_weight = w_gate[0]
    up_weight = w_up[0]
    down_weight = w_down[0]
    piece = lax.all_to_all(outgoing, "ep", split_axis=0, concat_axis=0, tiled=True)
    flat = piece.reshape(-1, width)
    gate_pre = matmul(flat, gate_weight)
    up_pre = matmul(flat, up_weight)
    middle = (jax.nn.silu(gate_pre) * up_pre).astype(jnp.bfloat16)
    expert_out = matmul(middle, down_weight).astype(jnp.bfloat16)
    lead = piece.shape[:2]
    returned = expert_out.reshape(piece.shape)
    gate_kept = gate_pre.reshape(lead + (-1,))
    up_kept = up_pre.reshape(lead + (-1,))
    arrived = lax.all_to_all(returned, "ep", split_axis=0, concat_axis=0, tiled=True)
    expert_rows = arrived.reshape(experts * capacity, width)[slots].reshape(local_rows, TOP, width)
    result = residual + jnp.sum(gate_value[:, :, None] * expert_rows, axis=1)
    output = result.astype(jnp.bfloat16)
    valid = valid_mask.reshape(local_rows).astype(jnp.float32)
    error = result - teacher.astype(jnp.float32)
    squares = jnp.sum(valid * jnp.sum(error * error, axis=1))
    total_squares, count = lax.psum((squares, jnp.sum(valid)), ("rep", "ep"))
    loss = total_squares / (2.0 * count * width)
    result_grad = total_tokens / count * valid[:, None] * error
    gate_value_grad = jnp.sum(result_grad[:, None, :] * expert_rows, axis=2)
    pair_grad = (
        (gate_value[:, :, None] * result_grad[:, None, :])
        .astype(jnp.bfloat16)
        .reshape(pairs, width)
    )
    grad_outgoing = jnp.concatenate([pair_grad, zero_row], 0)[pair_source].reshape(
        experts, capacity, width
    )
    grad_in = lax.all_to_all(grad_outgoing, "ep", split_axis=0, concat_axis=0, tiled=True)
    rows_in = piece.reshape(-1, width)
    gate_pre = gate_kept.reshape(rows_in.shape[0], -1)
    up_pre = up_kept.reshape(rows_in.shape[0], -1)
    flat_grad = grad_in.reshape(-1, width)
    sigma = jax.nn.sigmoid(gate_pre)
    active = gate_pre * sigma
    middle = (active * up_pre).astype(jnp.bfloat16)
    down_local = matmul(middle.T, flat_grad)
    middle_grad = matmul(flat_grad, down_weight.T)
    gate_pre_grad = (middle_grad * up_pre * sigma * (1.0 + gate_pre * (1.0 - sigma))).astype(
        jnp.bfloat16
    )
    up_pre_grad = (middle_grad * active).astype(jnp.bfloat16)
    gate_local = matmul(rows_in.T, gate_pre_grad)
    up_local = matmul(rows_in.T, up_pre_grad)
    input_grad = (matmul(gate_pre_grad, gate_weight.T) + matmul(up_pre_grad, up_weight.T)).astype(
        jnp.bfloat16
    )
    back_rows = lax.all_to_all(
        input_grad.reshape(experts, capacity, width), "ep", split_axis=0, concat_axis=0, tiled=True
    )
    pair_back = back_rows.reshape(experts * capacity, width)[slots].reshape(local_rows, TOP, width)
    everything = (
        lax.all_gather(attn_gain, ("rep", "ep"), axis=0, tiled=True),
        lax.all_gather(q_gain, ("rep", "ep"), axis=0, tiled=True),
        lax.all_gather(k_gain, ("rep", "ep"), axis=0, tiled=True),
        lax.all_gather(moe_gain, ("rep", "ep"), axis=0, tiled=True),
        lax.all_gather(w_query, ("rep", "ep"), axis=0, tiled=True),
        lax.all_gather(w_key, ("rep", "ep"), axis=0, tiled=True),
        lax.all_gather(w_value, ("rep", "ep"), axis=0, tiled=True),
        lax.all_gather(w_out, ("rep", "ep"), axis=0, tiled=True),
        lax.all_gather(w_router, ("rep", "ep"), axis=0, tiled=True),
    )
    gains, weight_query, weight_key, weight_value, weight_out, weight_router = unpack(everything)
    gain_attn, gain_query, gain_key, gain_moe = gains
    prob_grad = jnp.sum(choose_float * gate_value_grad[:, :, None], axis=1)
    logit_grad = router_probs * (
        prob_grad - jnp.sum(prob_grad * router_probs, axis=-1, keepdims=True)
    )
    router_local = jnp.dot(
        normed_moe.T, logit_grad, precision=highest, preferred_element_type=jnp.float32
    )
    normed_moe_grad = jnp.sum(pair_back.astype(jnp.float32), axis=1) + jnp.dot(
        logit_grad, weight_router.T, precision=highest, preferred_element_type=jnp.float32
    )
    residual_part, moe_gain_local = norm_back(residual, scale_moe, gain_moe, normed_moe_grad)
    residual_grad = result_grad + residual_part
    branch_grad = residual_grad.astype(jnp.bfloat16)
    out_local = matmul(mixed_rows.T, branch_grad)
    mixed_grad = (
        matmul(branch_grad, weight_out.T).astype(jnp.bfloat16).reshape(local_rows, HEADS, HEAD_DIM)
    )

    def attend_backward(item):
        query_group, key_group, value_group, grad_group, peak, total = item
        scores = scores_of(query_group, key_group)
        probs = jnp.exp(scores - peak) / total
        weights = probs.astype(jnp.bfloat16)
        value_part = jnp.einsum(
            "hqk,qhd->khd", weights, grad_group, preferred_element_type=jnp.float32
        )
        probs_grad = jnp.einsum(
            "qhd,khd->hqk", grad_group, value_group, preferred_element_type=jnp.float32
        )
        inner = jnp.sum(probs * probs_grad, axis=-1, keepdims=True)
        score_grad = (probs * (probs_grad - inner)).astype(jnp.bfloat16)
        query_part = (
            jnp.einsum("hqk,khd->qhd", score_grad, key_group, preferred_element_type=jnp.float32)
            * score_scale
        )
        key_part = (
            jnp.einsum("hqk,qhd->khd", score_grad, query_group, preferred_element_type=jnp.float32)
            * score_scale
        )
        return (query_part, key_part, value_part)

    query_parts, key_parts_grad, value_parts_grad = lax.map(
        attend_backward,
        (query_groups, key_groups, value_groups, by_group(mixed_grad), peaks, totals),
    )
    query_row_grad = from_group(query_parts)
    key_all_grad = from_group(key_parts_grad)
    value_all_grad = from_group(value_parts_grad)
    own_keys = key_all_grad[reach * local_rows :]
    own_values = value_all_grad[reach * local_rows :]
    for back in range(1, reach + 1):
        start = (reach - back) * local_rows
        moved = from_behind(
            (key_all_grad[start : start + local_rows], value_all_grad[start : start + local_rows]),
            "ep",
            -back,
        )
        own_keys = own_keys + moved[0]
        own_values = own_values + moved[1]
    query_turned = rotate_back(
        rounded(query_row_grad).reshape(local_rows, HEADS, HEAD_DIM), cosine, sine
    ).reshape(local_rows, width)
    key_turned = rotate_back(
        rounded(own_keys).reshape(local_rows, HEADS, HEAD_DIM), cosine, sine
    ).reshape(local_rows, width)
    query_lin_grad, q_gain_local = norm_back(query_lin, scale_query, gain_query, query_turned)
    key_lin_grad, k_gain_local = norm_back(key_lin, scale_key, gain_key, key_turned)
    query_lin_grad = query_lin_grad.astype(jnp.bfloat16)
    key_lin_grad = key_lin_grad.astype(jnp.bfloat16)
    value_row_grad = own_values.astype(jnp.bfloat16)
    query_local = matmul(normed.T, query_lin_grad)
    key_local = matmul(normed.T, key_lin_grad)
    value_local = matmul(normed.T, value_row_grad)
    normed_grad = (
        matmul(query_lin_grad, weight_query.T)
        + matmul(key_lin_grad, weight_key.T)
        + matmul(value_row_grad, weight_value.T)
    )
    inputs_part, attn_gain_local = norm_back(inputs, scale_attn, gain_attn, normed_grad)
    tokens_grad = residual_grad + inputs_part
    summed = (
        lax.psum_scatter(attn_gain_local, ("rep", "ep"), scatter_dimension=0, tiled=True),
        lax.psum_scatter(q_gain_local, ("rep", "ep"), scatter_dimension=0, tiled=True),
        lax.psum_scatter(k_gain_local, ("rep", "ep"), scatter_dimension=0, tiled=True),
        lax.psum_scatter(moe_gain_local, ("rep", "ep"), scatter_dimension=0, tiled=True),
        lax.psum_scatter(query_local, ("rep", "ep"), scatter_dimension=0, tiled=True),
        lax.psum_scatter(key_local, ("rep", "ep"), scatter_dimension=0, tiled=True),
        lax.psum_scatter(value_local, ("rep", "ep"), scatter_dimension=0, tiled=True),
        lax.psum_scatter(out_local, ("rep", "ep"), scatter_dimension=0, tiled=True),
        lax.psum_scatter(router_local, ("rep", "ep"), scatter_dimension=0, tiled=True),
    )
    expert_summed = (
        lax.psum_scatter(gate_local[None], "rep", scatter_dimension=1, tiled=True),
        lax.psum_scatter(up_local[None], "rep", scatter_dimension=1, tiled=True),
        lax.psum_scatter(down_local[None], "rep", scatter_dimension=1, tiled=True),
    )
    return (
        output,
        loss,
        tokens_grad,
        summed[0],
        summed[1],
        summed[2],
        summed[3],
        summed[4],
        summed[5],
        summed[6],
        summed[7],
        summed[8],
        expert_summed[0],
        expert_summed[1],
        expert_summed[2],
    )


def dot_t(left, right):
    return lax.dot_general(left, right, (((1,), (1,)), ((), ())), preferred_element_type=jnp.float32)


def t_dot(left, right):
    return lax.dot_general(left, right, (((0,), (0,)), ((), ())), preferred_element_type=jnp.float32)


def kernel_call(kernel, **options):
    return pl.pallas_call(
        kernel,
        compiler_params=pltpu.CompilerParams(vmem_limit_bytes=VMEM_LIMIT),
        **options,
    )


def turn(value, cosine, sine):
    return value * cosine + pltpu.roll(value, HEAD_DIM // 2, 1) * sine


def code_of(place, blocks):
    return place % (blocks // 2) * 2 + place // (blocks // 2)


def place_of(code, blocks):
    return code % 2 * (blocks // 2) + code // 2


def norm_kernel(rank, x_ref, gain_ref, o_ref, scale_ref, *, codes):
    value = x_ref[...].astype(jnp.float32)
    scale = lax.rsqrt(jnp.mean(value * value, axis=1, keepdims=True) + norm_eps)
    scale_ref[...] = scale
    half = len(codes) // 2
    block = x_ref.shape[1] // len(codes)
    for place, code in enumerate(codes):
        start = pl.multiple_of((rank[0] ^ code) * block, block)
        piece = x_ref[:, pl.ds(start, block)].astype(jnp.float32)
        piece = piece * scale * gain_ref[:, pl.ds(start, block)]
        at = place % half * block
        o_ref[place // half, :, at : at + block] = piece.astype(jnp.bfloat16)


def norm_rows(rank, value, gain, codes):
    rows, width = value.shape
    tile = 256
    return kernel_call(
        functools.partial(norm_kernel, codes=codes),
        grid_spec=pltpu.PrefetchScalarGridSpec(
            num_scalar_prefetch=1,
            grid=(rows // tile,),
            in_specs=[
                pl.BlockSpec((tile, width), lambda i, rank: (i, 0)),
                pl.BlockSpec((1, width), lambda i, rank: (0, 0)),
            ],
            out_specs=[
                pl.BlockSpec((2, tile, width // 2), lambda i, rank: (0, i, 0)),
                pl.BlockSpec((tile, 1), lambda i, rank: (i, 0)),
            ],
        ),
        out_shape=[
            jax.ShapeDtypeStruct((2, rows, width // 2), jnp.bfloat16),
            jax.ShapeDtypeStruct((rows, 1), jnp.float32),
        ],
        cost_estimate=pl.CostEstimate(
            flops=8 * rows * width, bytes_accessed=4 * rows * width, transcendentals=0
        ),
    )(rank, value, gain[None])


def project_kernel(low_ref, high_ref, a_ref, b_ref, o_ref, s_ref):
    total = matmul(low_ref[0], a_ref[...]) + matmul(high_ref[0], b_ref[...])
    o_ref[...] = total.astype(o_ref.dtype)
    s_ref[...] = jnp.sum(total * total, axis=1, keepdims=True)


def project(halves, a, b, dtype, start=0):
    _, rows, depth = halves.shape
    rows = rows - start
    width = a.shape[1]
    tile = 256
    first = start // tile
    weight = pl.BlockSpec((depth, width), lambda i: (0, 0))
    return kernel_call(
        project_kernel,
        grid=(rows // tile,),
        in_specs=[
            pl.BlockSpec((1, tile, depth), lambda i: (0, i + first, 0)),
            pl.BlockSpec((1, tile, depth), lambda i: (1, i + first, 0)),
            weight,
            weight,
        ],
        out_specs=[
            pl.BlockSpec((tile, width), lambda i: (i, 0)),
            pl.BlockSpec((tile, 1), lambda i: (i, 0)),
        ],
        out_shape=[
            jax.ShapeDtypeStruct((rows, width), dtype),
            jax.ShapeDtypeStruct((rows, 1), jnp.float32),
        ],
        cost_estimate=pl.CostEstimate(
            flops=4 * rows * depth * width, bytes_accessed=8 * depth * width, transcendentals=0
        ),
    )(halves, halves, a, b)


def project_back_kernel(k_ref, v_ref, w_ref, q_ref, ka, kb, va, vb, qa, qb, o_ref, *, own):
    i, j = pl.program_id(0), pl.program_id(1)
    half = pl.num_programs(1) // 2

    def part(key, value, query):
        half_width = v_ref.shape[1]
        total = dot_t(k_ref[...], key[...]) + dot_t(v_ref[...], value[:, :half_width])
        o_ref[0] = total + dot_t(w_ref[...], value[:, half_width:])

        @pl.when(i >= own)
        def _():
            o_ref[0] += dot_t(q_ref[...], query[...])

    @pl.when(j < half)
    def _():
        part(ka, va, qa)

    @pl.when(j >= half)
    def _():
        part(kb, vb, qb)


def project_back(key, value, value_high, query, key_w, value_w, query_w):
    rows, width = key.shape
    depth = key_w[0].shape[0]
    tile, step = 512, 512
    half = depth // step
    own = (rows - query.shape[0]) // tile
    x_spec = pl.BlockSpec((tile, width), lambda i, j: (i, 0))
    half_spec = pl.BlockSpec((tile, width // 2), lambda i, j: (i, 0))
    low = pl.BlockSpec((step, width), lambda i, j: (jnp.minimum(j, half - 1), 0))
    high = pl.BlockSpec((step, width), lambda i, j: (jnp.maximum(j - half, 0), 0))
    return kernel_call(
        functools.partial(project_back_kernel, own=own),
        grid=(rows // tile, 2 * half),
        in_specs=[
            x_spec,
            half_spec,
            half_spec,
            pl.BlockSpec((tile, width), lambda i, j: (jnp.maximum(i - own, 0), 0)),
        ]
        + [low, high] * 3,
        out_specs=pl.BlockSpec((1, tile, step), lambda i, j: (j // half, i, j % half)),
        out_shape=jax.ShapeDtypeStruct((2, rows, depth), jnp.float32),
        cost_estimate=pl.CostEstimate(
            flops=9 * rows * depth * width, bytes_accessed=32 * depth * width, transcendentals=0
        ),
    )(key, value, value_high, query, *key_w, *value_w, *query_w)


def tokens_back_kernel(
    rank, g_ref, c_ref, x_ref, res_ref, scale_ref, gain_ref, o_ref, gain_grad_ref, *, blocks
):
    scale = scale_ref[...]
    block = x_ref.shape[1] // blocks
    half = blocks // 2

    @pl.when(pl.program_id(0) == 0)
    def _():
        gain_grad_ref[...] = jnp.zeros_like(gain_grad_ref)

    def pieces(place):
        start = pl.multiple_of((rank[0] ^ code_of(place, blocks)) * block, block)
        at = slice(place % half * block, place % half * block + block)
        grad = g_ref[place // half, :, at] + c_ref[place // half, :, at].astype(jnp.float32)
        columns = pl.ds(start, block)
        return columns, grad, x_ref[:, columns].astype(jnp.float32), gain_ref[:, columns]

    inner = jnp.zeros_like(scale)
    for place in range(blocks):
        columns, grad, value, gain = pieces(place)
        product = grad * value
        inner += jnp.sum(product * gain, axis=1, keepdims=True)
        gain_grad_ref[:, columns] += jnp.sum(product * scale, axis=0, keepdims=True)
    inner = inner * (1.0 / x_ref.shape[1]) * (scale * scale * scale)
    for place in range(blocks):
        columns, grad, value, gain = pieces(place)
        o_ref[:, columns] = res_ref[:, columns] + (scale * (grad * gain) - value * inner)


def tokens_back(rank, grad, carried, tokens, residual_grad, scale, gain, blocks):
    rows, width = tokens.shape
    tile = 128
    first = (grad.shape[1] - rows) // tile
    wide = pl.BlockSpec((tile, width), lambda i, rank: (i, 0))
    one = pl.BlockSpec((1, width), lambda i, rank: (0, 0))
    return kernel_call(
        functools.partial(tokens_back_kernel, blocks=blocks),
        grid_spec=pltpu.PrefetchScalarGridSpec(
            num_scalar_prefetch=1,
            grid=(rows // tile,),
            in_specs=[
                pl.BlockSpec((2, tile, width // 2), lambda i, rank: (0, i + first, 0)),
                pl.BlockSpec((2, tile, width // 2), lambda i, rank: (0, i, 0)),
                wide,
                wide,
                pl.BlockSpec((tile, 1), lambda i, rank: (i + first, 0)),
                one,
            ],
            out_specs=[wide, one],
        ),
        out_shape=[
            jax.ShapeDtypeStruct((rows, width), jnp.float32),
            jax.ShapeDtypeStruct((1, width), jnp.float32),
        ],
        cost_estimate=pl.CostEstimate(
            flops=10 * rows * width, bytes_accessed=16 * rows * width, transcendentals=0
        ),
    )(rank, grad, carried, tokens, residual_grad, scale, gain[None])


def head_rows(lin, scale, gain, cosine, sine):
    return turn(lin * scale * gain, cosine, sine).astype(jnp.bfloat16)


def moved_head(head, rank):
    place = place_of((head // 2) ^ rank[0], HEADS // 2) * 2 + head % 2
    return place // (HEADS // 2), 0, place % (HEADS // 2)


def attention_specs(rows, all_rows, bias, first=0):
    head = lambda h, rank: (0, h + first)
    fixed = lambda h, rank: (0, 0)
    return [
        pl.BlockSpec((rows, HEAD_DIM), head),
        pl.BlockSpec((all_rows, HEAD_DIM), head),
        pl.BlockSpec((all_rows, HEAD_DIM), head),
        pl.BlockSpec((rows, 1), fixed),
        pl.BlockSpec((all_rows, 1), fixed),
        pl.BlockSpec((1, HEAD_DIM), head),
        pl.BlockSpec((1, HEAD_DIM), head),
        pl.BlockSpec((all_rows, HEAD_DIM), fixed),
        pl.BlockSpec((all_rows, HEAD_DIM), fixed),
        pl.BlockSpec(bias.shape, lambda h, rank: (0, 0, 0)),
    ]


def attend_kernel(
    rank,
    q_ref,
    k_ref,
    v_ref,
    sq_ref,
    sk_ref,
    gq_ref,
    gk_ref,
    cos_ref,
    sin_ref,
    bias_ref,
    o_ref,
    lse_ref,
    *,
    behind,
    tile,
    span,
):
    rows = q_ref.shape[0]
    cosine, sine = cos_ref[...], sin_ref[...]
    keys = head_rows(k_ref[...], sk_ref[...], gk_ref[...], cosine, sine)
    queries = head_rows(q_ref[...], sq_ref[...], gq_ref[...], cosine[behind:], sine[behind:])
    for t in range(rows // tile):
        at = slice(t * tile, (t + 1) * tile)
        seen = slice(t * tile, t * tile + span)
        scores = dot_t(keys[seen], queries[at])
        scores = scores * HEAD_DIM ** (-0.5) + bias_ref[t].astype(jnp.float32)
        peak = jnp.max(scores, axis=0, keepdims=True)
        shifted = jnp.exp(scores - peak)
        total = jnp.sum(shifted, axis=0, keepdims=True)
        weights = (shifted * (1.0 / total)).astype(jnp.bfloat16)
        o_ref[0, at, :] = t_dot(weights, v_ref[seen, :]).astype(jnp.bfloat16)
        lse_ref[0, :, at] = peak + jnp.log(total)


def attend(rank, operands, bias):
    rows, width = operands[0].shape
    all_rows = operands[1].shape[0]
    tiles, span, tile = bias.shape
    return kernel_call(
        functools.partial(attend_kernel, behind=all_rows - rows, tile=tile, span=span),
        grid_spec=pltpu.PrefetchScalarGridSpec(
            num_scalar_prefetch=1,
            grid=(HEADS,),
            in_specs=attention_specs(rows, all_rows, bias),
            out_specs=[
                pl.BlockSpec((1, rows, HEAD_DIM), moved_head),
                pl.BlockSpec((1, 1, rows), lambda h, rank: (h, 0, 0)),
            ],
        ),
        out_shape=[
            jax.ShapeDtypeStruct((2, rows, width // 2), jnp.bfloat16),
            jax.ShapeDtypeStruct((HEADS, 1, rows), jnp.float32),
        ],
        cost_estimate=pl.CostEstimate(
            flops=4 * rows * span * width,
            bytes_accessed=8 * all_rows * width,
            transcendentals=rows * span * HEADS,
        ),
    )(rank, *operands, bias)


def attend_back_kernel(
    rank,
    q_ref,
    k_ref,
    v_ref,
    sq_ref,
    sk_ref,
    gq_ref,
    gk_ref,
    cos_ref,
    sin_ref,
    bias_ref,
    g_ref,
    lse_ref,
    dq_ref,
    dk_ref,
    dv_ref,
    key_total,
    value_total,
    *,
    behind,
    tile,
    span,
):
    rows = q_ref.shape[0]
    score_scale = HEAD_DIM ** (-0.5)
    cosine, sine = cos_ref[...], sin_ref[...]
    keys = head_rows(k_ref[...], sk_ref[...], gk_ref[...], cosine, sine)
    queries = head_rows(q_ref[...], sq_ref[...], gq_ref[...], cosine[behind:], sine[behind:])
    key_total[...] = jnp.zeros_like(key_total)
    value_total[...] = jnp.zeros_like(value_total)
    for t in range(rows // tile):
        at = slice(t * tile, (t + 1) * tile)
        seen = slice(t * tile, t * tile + span)
        scores = dot_t(keys[seen], queries[at])
        scores = scores * score_scale + bias_ref[t].astype(jnp.float32)
        probs = jnp.exp(scores - lse_ref[0, :, at])
        grad = g_ref[0, at, :]
        value_total[seen, :] += matmul(probs.astype(jnp.bfloat16), grad)
        probs_grad = dot_t(v_ref[seen, :], grad)
        inner = jnp.sum(probs * probs_grad, axis=0, keepdims=True)
        score_grad = (probs * (probs_grad - inner)).astype(jnp.bfloat16)
        dq_ref[at, :] = (t_dot(score_grad, keys[seen]) * score_scale).astype(jnp.bfloat16)
        key_total[seen, :] += matmul(score_grad, queries[at])
    dk_ref[...] = (key_total[...] * score_scale).astype(jnp.bfloat16)
    dv_ref[...] = value_total[...].astype(jnp.bfloat16)


def attend_back(rank, operands, bias, grad, lse, first):
    rows, width = operands[0].shape
    width = width // 2
    all_rows = operands[1].shape[0]
    tiles, span, tile = bias.shape
    head = lambda h, rank: (0, h)
    return kernel_call(
        functools.partial(attend_back_kernel, behind=all_rows - rows, tile=tile, span=span),
        grid_spec=pltpu.PrefetchScalarGridSpec(
            num_scalar_prefetch=1,
            grid=(HEADS // 2,),
            in_specs=attention_specs(rows, all_rows, bias, first)
            + [
                pl.BlockSpec((1, rows, HEAD_DIM), lambda h, rank: moved_head(h + first, rank)),
                pl.BlockSpec((1, 1, rows), lambda h, rank: (h + first, 0, 0)),
            ],
            out_specs=[
                pl.BlockSpec((rows, HEAD_DIM), head),
                pl.BlockSpec((all_rows, HEAD_DIM), head),
                pl.BlockSpec((all_rows, HEAD_DIM), head),
            ],
            scratch_shapes=[
                pltpu.VMEM((all_rows, HEAD_DIM), jnp.float32),
                pltpu.VMEM((all_rows, HEAD_DIM), jnp.float32),
            ],
        ),
        out_shape=[
            jax.ShapeDtypeStruct((rows, width), jnp.bfloat16),
            jax.ShapeDtypeStruct((all_rows, width), jnp.bfloat16),
            jax.ShapeDtypeStruct((all_rows, width), jnp.bfloat16),
        ],
        cost_estimate=pl.CostEstimate(
            flops=10 * rows * span * width,
            bytes_accessed=12 * all_rows * width,
            transcendentals=rows * span * HEADS // 2,
        ),
    )(rank, *operands, bias, grad, lse)


def lin_back_kernel(low_ref, high_ref, lin_ref, scale_ref, gain_ref, cos_ref, sin_ref, o_ref, gain_grad_ref):
    scale = scale_ref[...]
    cosine, sine = cos_ref[...], -sin_ref[...]
    inner = jnp.zeros_like(scale)

    @pl.when(pl.program_id(0) == 0)
    def _():
        gain_grad_ref[...] = jnp.zeros_like(gain_grad_ref)

    def grad_of(h):
        ref = low_ref if h < HEADS // 2 else high_ref
        return ref[:, h % (HEADS // 2) * HEAD_DIM : (h % (HEADS // 2) + 1) * HEAD_DIM]

    for h in range(HEADS):
        at = slice(h * HEAD_DIM, (h + 1) * HEAD_DIM)
        grad = turn(grad_of(h).astype(jnp.float32), cosine, sine)
        lin = lin_ref[:, at]
        product = grad * lin
        gain_grad_ref[:, at] += jnp.sum(product * scale, axis=0, keepdims=True)
        inner += jnp.sum(product * gain_ref[:, at], axis=1, keepdims=True)
    inner = inner * (1.0 / (HEADS * HEAD_DIM)) * (scale * scale * scale)
    for h in range(HEADS):
        at = slice(h * HEAD_DIM, (h + 1) * HEAD_DIM)
        grad = turn(grad_of(h).astype(jnp.float32), cosine, sine)
        value = scale * (grad * gain_ref[:, at]) - lin_ref[:, at] * inner
        o_ref[:, at] = value.astype(jnp.bfloat16)


def lin_back(low, high, lin, scale, gain, cosine, sine):
    rows, width = lin.shape
    tile = 256
    wide = pl.BlockSpec((tile, width), lambda i: (i, 0))
    one = pl.BlockSpec((1, width), lambda i: (0, 0))
    half = pl.BlockSpec((tile, width // 2), lambda i: (i, 0))
    table = pl.BlockSpec((tile, HEAD_DIM), lambda i: (i, 0))
    return kernel_call(
        lin_back_kernel,
        grid=(rows // tile,),
        in_specs=[half, half, wide, pl.BlockSpec((tile, 1), lambda i: (i, 0)), one, table, table],
        out_specs=[wide, one],
        out_shape=[
            jax.ShapeDtypeStruct((rows, width), jnp.bfloat16),
            jax.ShapeDtypeStruct((1, width), jnp.float32),
        ],
        cost_estimate=pl.CostEstimate(
            flops=10 * rows * width, bytes_accessed=8 * rows * width, transcendentals=0
        ),
    )(low, high, lin, scale, gain, cosine, sine)


def dynamic_block(index, block):
    return pl.ds(pl.multiple_of(index * block, block), block)


def experts_up_kernel(rank, x_ref, z_ref, ga, gb, ua, ub, g_ref, u_ref, my_ref, mx_ref, middle_ref):
    gate = matmul(x_ref[0], ga[...]) + matmul(x_ref[1], gb[...])
    up = matmul(z_ref[0], ua[...]) + matmul(z_ref[1], ub[...])
    g_ref[...] = gate
    u_ref[...] = up
    middle_ref[...] = (gate * jax.nn.sigmoid(gate) * up).astype(jnp.bfloat16)
    block = gate.shape[1] // 4
    for j in range(4):
        piece = middle_ref[:, dynamic_block(rank[0] ^ j, block)]
        dy, dx = j // 2, j % 2
        my_ref[dy, :, dx * block : (dx + 1) * block] = piece
        mx_ref[dx, :, dy * block : (dy + 1) * block] = piece


def experts_up(rank, by_y, by_x, weights):
    _, rows, depth = by_y.shape
    hidden = weights[0].shape[1]
    tile = 256
    x_spec = pl.BlockSpec((2, tile, depth), lambda i, rank: (0, i, 0))
    w_spec = pl.BlockSpec((depth, hidden), lambda i, rank: (0, 0))
    wide = pl.BlockSpec((tile, hidden), lambda i, rank: (i, 0))
    half = pl.BlockSpec((2, tile, hidden // 2), lambda i, rank: (0, i, 0))
    return kernel_call(
        experts_up_kernel,
        grid_spec=pltpu.PrefetchScalarGridSpec(
            num_scalar_prefetch=1,
            grid=(rows // tile,),
            in_specs=[x_spec, x_spec] + [w_spec] * 4,
            out_specs=[wide, wide, half, half],
            scratch_shapes=[pltpu.VMEM((tile, hidden), jnp.bfloat16)],
        ),
        out_shape=[jax.ShapeDtypeStruct((rows, hidden), jnp.float32)] * 2
        + [jax.ShapeDtypeStruct((2, rows, hidden // 2), jnp.bfloat16)] * 2,
        cost_estimate=pl.CostEstimate(
            flops=8 * rows * depth * hidden, bytes_accessed=30 * rows * hidden, transcendentals=0
        ),
    )(rank, by_y, by_x, *weights)


def experts_down_kernel(*refs):
    gates, slots, outs = refs[:2], (refs[2:8], refs[8:14]), refs[14:]
    half = outs[0].shape[1] // 2
    for side in range(2):
        at = slice(side * half, (side + 1) * half)
        mixture = 0.0
        for slot, (my, mx, la, lb, ra, rb) in enumerate(slots):
            if side == 0:
                out = matmul(my[0], la[...]) + matmul(my[1], lb[...])
            else:
                out = matmul(mx[0], ra[...]) + matmul(mx[1], rb[...])
            out = out.astype(jnp.bfloat16)
            outs[slot][:, at] = out
            mixture += gates[slot][...] * out.astype(jnp.float32)
        outs[2][:, at] = mixture


def experts_down(gates, slots):
    _, rows, depth = slots[0][0].shape
    half = slots[0][2].shape[1]
    tile = 256
    x_spec = pl.BlockSpec((2, tile, depth), lambda i: (0, i, 0))
    w_spec = pl.BlockSpec((depth, half), lambda i: (0, 0))
    wide = pl.BlockSpec((tile, 2 * half), lambda i: (i, 0))
    column = pl.BlockSpec((tile, 1), lambda i: (i, 0))
    return kernel_call(
        experts_down_kernel,
        grid=(rows // tile,),
        in_specs=[column] * 2 + ([x_spec] * 2 + [w_spec] * 4) * 2,
        out_specs=[wide] * 3,
        out_shape=[
            jax.ShapeDtypeStruct((rows, 2 * half), jnp.bfloat16),
            jax.ShapeDtypeStruct((rows, 2 * half), jnp.bfloat16),
            jax.ShapeDtypeStruct((rows, 2 * half), jnp.float32),
        ],
        cost_estimate=pl.CostEstimate(
            flops=16 * rows * depth * half, bytes_accessed=24 * rows * half, transcendentals=0
        ),
    )(*gates, *slots[0], *slots[1])


def experts_back_kernel(
    rank, r_ref, out_ref, gate_ref, g_ref, u_ref, la, lb, ra, rb, p_ref, dg_ref, du_ref, gg_ref
):
    grad = r_ref[...]
    gg_ref[...] = jnp.sum(grad * out_ref[...].astype(jnp.float32), axis=1, keepdims=True)
    p_ref[...] = (gate_ref[...] * grad).astype(jnp.bfloat16)
    half = grad.shape[1] // 2
    left, right = p_ref[:, :half], p_ref[:, half:]
    block = la.shape[0] // 2
    first, second = slice(0, block), slice(block, 2 * block)
    for j in range(4):
        dy, dx = j // 2, j % 2
        left_w = (la, lb)[dy][(first, second)[dx], :]
        right_w = (ra, rb)[dx][(first, second)[dy], :]
        middle_grad = dot_t(left, left_w) + dot_t(right, right_w)
        at = dynamic_block(rank[0] ^ j, block)
        gate_pre, up_pre = g_ref[:, at], u_ref[:, at]
        sigma = jax.nn.sigmoid(gate_pre)
        change = middle_grad * up_pre * sigma * (1.0 + gate_pre * (1.0 - sigma))
        dg_ref[:, at] = change.astype(jnp.bfloat16)
        du_ref[:, at] = (middle_grad * (gate_pre * sigma)).astype(jnp.bfloat16)


def experts_back(rank, result_grad, out, gate, gate_pre, up_pre, weights):
    rows, width = result_grad.shape
    hidden = gate_pre.shape[1]
    tile = 256
    wide = pl.BlockSpec((tile, width), lambda i, rank: (i, 0))
    narrow = pl.BlockSpec((tile, hidden), lambda i, rank: (i, 0))
    column = pl.BlockSpec((tile, 1), lambda i, rank: (i, 0))
    w_spec = pl.BlockSpec(weights[0].shape, lambda i, rank: (0, 0))
    return kernel_call(
        experts_back_kernel,
        grid_spec=pltpu.PrefetchScalarGridSpec(
            num_scalar_prefetch=1,
            grid=(rows // tile,),
            in_specs=[wide, wide, column, narrow, narrow] + [w_spec] * 4,
            out_specs=[wide, narrow, narrow, column],
        ),
        out_shape=[
            jax.ShapeDtypeStruct((rows, width), jnp.bfloat16),
            jax.ShapeDtypeStruct((rows, hidden), jnp.bfloat16),
            jax.ShapeDtypeStruct((rows, hidden), jnp.bfloat16),
            jax.ShapeDtypeStruct((rows, 1), jnp.float32),
        ],
        cost_estimate=pl.CostEstimate(
            flops=2 * rows * width * hidden, bytes_accessed=26 * rows * hidden, transcendentals=0
        ),
    )(rank, result_grad, out, gate, gate_pre, up_pre, *weights)


def experts_input_kernel(*refs):
    o_ref = refs[-1]
    depth = o_ref.shape[2]
    first, second = slice(0, depth), slice(depth, 2 * depth)
    for j in range(4):
        dy, dx = j // 2, j % 2
        total = 0.0
        for dg, du, ga, gb, ua, ub in (refs[:6], refs[6:12]):
            gate_w = (ga, gb)[dy][(first, second)[dx], :]
            up_w = (ua, ub)[dx][(first, second)[dy], :]
            part = dot_t(dg[...], gate_w) + dot_t(du[...], up_w)
            total += part.astype(jnp.bfloat16).astype(jnp.float32)
        o_ref[j] = total


def experts_input(slots):
    rows, hidden = slots[0][0].shape
    depth = slots[0][2].shape[0] // 2
    tile = 256
    narrow = pl.BlockSpec((tile, hidden), lambda i: (i, 0))
    w_spec = pl.BlockSpec((2 * depth, hidden), lambda i: (0, 0))
    return kernel_call(
        experts_input_kernel,
        grid=(rows // tile,),
        in_specs=([narrow] * 2 + [w_spec] * 4) * 2,
        out_specs=pl.BlockSpec((4, tile, depth), lambda i: (0, i, 0)),
        out_shape=jax.ShapeDtypeStruct((4, rows, depth), jnp.float32),
        cost_estimate=pl.CostEstimate(
            flops=32 * rows * depth * hidden, bytes_accessed=48 * rows * depth, transcendentals=0
        ),
    )(*slots[0], *slots[1])


def residual_back_kernel(
    rank, a_ref, b_ref, lg_ref, wr_ref, x_ref, r_ref, scale_ref, gain_ref, o_ref, c_ref, gg_ref
):
    scale = scale_ref[...]
    block = a_ref.shape[2]

    @pl.when(pl.program_id(0) == 0)
    def _():
        gg_ref[...] = jnp.zeros_like(gg_ref)

    inner = jnp.zeros_like(scale)
    for j in range(4):
        at = dynamic_block(rank[0] ^ j, block)
        grad = a_ref[j] + b_ref[j]
        for e in range(wr_ref.shape[0]):
            grad += lg_ref[:, e : e + 1] * wr_ref[e : e + 1, at]
        o_ref[:, at] = grad
        product = grad * x_ref[:, at]
        inner += jnp.sum(product * gain_ref[:, at], axis=1, keepdims=True)
        gg_ref[:, at] += jnp.sum(product * scale, axis=0, keepdims=True)
    inner = inner * (1.0 / x_ref.shape[1]) * (scale * scale * scale)
    for j in range(4):
        at = slice(j * block, (j + 1) * block)
        value = scale * (o_ref[:, at] * gain_ref[:, at]) - x_ref[:, at] * inner
        value = r_ref[:, at] + value
        o_ref[:, at] = value
        c_ref[:, at] = value.astype(jnp.bfloat16)


def residual_back(rank, own, other, logit_grad, router, residual, result_grad, scale, gain):
    rows, width = residual.shape
    tile = 128
    wide = pl.BlockSpec((tile, width), lambda i, rank: (i, 0))
    piece = pl.BlockSpec((4, tile, width // 4), lambda i, rank: (0, i, 0))
    one = pl.BlockSpec((1, width), lambda i, rank: (0, 0))
    experts = logit_grad.shape[1]
    return kernel_call(
        residual_back_kernel,
        grid_spec=pltpu.PrefetchScalarGridSpec(
            num_scalar_prefetch=1,
            grid=(rows // tile,),
            in_specs=[
                piece,
                piece,
                pl.BlockSpec((tile, experts), lambda i, rank: (i, 0)),
                pl.BlockSpec((experts, width), lambda i, rank: (0, 0)),
                wide,
                wide,
                pl.BlockSpec((tile, 1), lambda i, rank: (i, 0)),
                one,
            ],
            out_specs=[wide, wide, one],
        ),
        out_shape=[
            jax.ShapeDtypeStruct((rows, width), jnp.float32),
            jax.ShapeDtypeStruct((rows, width), jnp.bfloat16),
            jax.ShapeDtypeStruct((1, width), jnp.float32),
        ],
        cost_estimate=pl.CostEstimate(
            flops=20 * rows * width, bytes_accessed=22 * rows * width, transcendentals=0
        ),
    )(rank, own, other, logit_grad, router, residual, result_grad, scale, gain[None])


def across(value, bit):
    count = lax.axis_size("rep")
    return lax.ppermute(value, "rep", [(place, place ^ bit) for place in range(count)])


def along(value, steps):
    count = lax.axis_size("ep")
    return lax.ppermute(value, "ep", [(place, (place + steps) % count) for place in range(count)])


def mirrored(value, moves):
    reps, count = lax.axis_size("rep"), lax.axis_size("ep")
    pairs = []
    for rep in range(reps):
        for source, target in moves:
            if rep % 2:
                source, target = count - 1 - source, count - 1 - target
            pairs.append((rep * count + source, rep * count + target))
    return lax.ppermute(value, ("rep", "ep"), pairs)


def pick(value, index, axis):
    return lax.dynamic_index_in_dim(value, index, axis, keepdims=False)


def in_order(own, other, bit, axis):
    return jnp.where(bit == 1, jnp.stack([other, own], axis), jnp.stack([own, other], axis))


def over_ep(value, place):
    shard = place[3]
    experts = lax.axis_size("ep")
    parts = jnp.zeros((experts,) + value.shape, value.dtype)
    parts = lax.dynamic_update_index_in_dim(parts, value, shard, 0)
    for steps in range(1, experts):
        parts = lax.dynamic_update_index_in_dim(
            parts, along(value, steps), lax.rem(shard - steps + experts, experts), 0
        )
    return parts


def sum_small(value, place):
    value = value + across(value, 1)
    value = value + across(value, 2)
    value = value + across(value, 4)
    return jnp.sum(over_ep(value, place), axis=0)


def hold(*values):
    return lax.optimization_barrier(values)


def both_ways(value):
    return across(value[0], 2), across(value[1], 4)


def other_ways(first, second):
    return across(first, 4), across(second, 2)


def chip_sum(halves, grad):
    sent = across(t_dot(halves[1], grad).astype(jnp.bfloat16), 1)
    kept = t_dot(halves[0], grad) + sent.astype(jnp.float32)
    return kept.astype(jnp.bfloat16).reshape(2, 2, -1, grad.shape[1])


def add(left, right):
    return (left.astype(jnp.float32) + right.astype(jnp.float32)).astype(jnp.bfloat16)


def over_ep_sum(both, place):
    shard = place[3]
    experts = lax.axis_size("ep")
    both = both.reshape(2, experts, both.shape[1] // experts, both.shape[2])
    total = pick(both, shard, 1).astype(jnp.float32)
    for steps in range(1, experts):
        total = total + along(pick(both, lax.rem(shard + steps, experts), 1), steps)
    return total


def part_sum(left, grad):
    return t_dot(left, grad).astype(jnp.bfloat16)


def kept_sum(left, grad, got):
    total = t_dot(left, grad) + got.astype(jnp.float32)
    return total.astype(jnp.bfloat16).reshape(2, -1, grad.shape[1])


def body(
    tokens,
    teacher,
    segment_ids,
    valid_mask,
    routes,
    attn_gain,
    q_gain,
    k_gain,
    moe_gain,
    w_query,
    w_key,
    w_value,
    w_out,
    w_router,
    w_gate,
    w_up,
    w_down,
):
    bf16, f32 = jnp.bfloat16, jnp.float32
    local_rows, width = tokens.shape
    experts = lax.axis_size("ep")
    reps = lax.axis_size("rep")
    reach = min(-(-WINDOW // local_rows), experts - 1)
    shard = lax.axis_index("ep")
    rep = lax.axis_index("rep")
    place = (rep // 4, rep // 2 % 2, rep % 2, shard)
    core = rep % 2
    total_tokens = local_rows * reps * experts

    valid = valid_mask.reshape(local_rows).astype(f32)
    own_count = jnp.sum(valid_mask)
    counts = jnp.stack([own_count // 16, own_count % 16]).astype(bf16)
    small = jnp.concatenate(
        [
            jnp.stack([attn_gain, q_gain, k_gain, moe_gain], 1),
            w_router,
            jnp.broadcast_to(counts[None], (attn_gain.shape[0], 2)),
        ],
        1,
    )
    small = small.T
    rank = rep.astype(jnp.int32)[None]
    quarter = rep // 2
    quarter_rank = quarter.astype(jnp.int32)[None]
    order = tuple(code_of(j, reps) for j in range(reps))
    half = width // 2
    behind = reach * local_rows
    all_rows = local_rows + behind
    m = jnp.where(core == 0, shard, experts - 1 - shard)
    quarter_rows = w_gate.shape[1] // 4
    quarter_down = w_down.shape[1] // 4
    own_gu = jnp.stack(
        [
            lax.dynamic_slice_in_dim(w[0], quarter * quarter_rows, quarter_rows, 0)
            for w in (w_gate, w_up)
        ]
    )
    own_d = lax.dynamic_slice_in_dim(w_down[0], quarter * quarter_down, quarter_down, 0)
    own_d = jnp.stack([own_d[:, :half], own_d[:, half:]])
    segments = segment_ids.reshape(local_rows)

    small = over_ep(small, place)
    kv = over_ep(jnp.stack([w_key, w_value]), place)
    gu_1 = mirrored(own_gu, [(0, 1), (1, 2)])
    segment_parts = [segments]
    for back in range(reach):
        segment_parts.insert(0, from_behind(segment_parts[0], "ep", 1))
    qo = jnp.stack([w_query, w_out])
    small, kv, gu_1, qo, tokens_1, own_gu = hold(small, kv, gu_1, qo, tokens, own_gu)

    qo = over_ep(qo, place)
    k_w, v_w = kv[:, 0].reshape(-1, width), kv[:, 1].reshape(-1, width)
    k_x, v_y = both_ways((k_w, v_w))
    small = in_order(small, across(small, 1), core, 0)
    small = in_order(small, across(small, 2), place[1], 0)
    small = in_order(small, across(small, 4), place[0], 0)
    qo, k_w, k_x, v_w, v_y, tokens_1, gu_1, own_gu, own_d = hold(
        qo, k_w, k_x, v_w, v_y, tokens_1, gu_1, own_gu, own_d
    )

    k_w = jnp.concatenate([k_w, k_x], 0)
    k_y, v_x = other_ways(k_w, jnp.stack([v_w, v_y]))
    k_w = jnp.concatenate([k_w, k_y], 0)
    v_w = jnp.concatenate([v_w, v_x[0], v_y, v_x[1]], 0)
    token_parts = [from_behind(tokens_1, "ep", 1), tokens]
    gu_2 = mirrored(jnp.where(m == 2, gu_1, own_gu), [(1, 0), (2, 3)])
    qo, k_w, v_w, token_1, gu_1, gu_2, own_d = hold(
        qo, k_w, v_w, token_parts[0], gu_1, gu_2, own_d
    )

    token_parts[0] = token_1
    for back in range(reach - 1):
        token_parts.insert(0, from_behind(token_parts[0], "ep", 1))
    key_w, value_w = (k_w, across(k_w, 1)), (v_w, across(v_w, 1))
    q_w, o_w = qo[:, 0].reshape(-1, width), qo[:, 1].reshape(-1, width)
    q_x, o_y = both_ways((q_w, o_w))
    gu_b = jnp.where(m == 1, own_gu, jnp.where(m == 2, gu_1, gu_2))
    b_x, b_y = both_ways(gu_b)
    gu_3 = mirrored(gu_1, [(1, 2)])
    d_1 = mirrored(own_d, [(0, 1), (1, 2)])
    token_0, key_w, value_w, q_w, q_x, o_w, o_y, gu_b, b_x, b_y, gu_3, d_1, own_d = hold(
        token_parts[0], key_w, value_w, q_w, q_x, o_w, o_y, gu_b, b_x, b_y, gu_3, d_1, own_d
    )
    token_parts[0] = token_0

    q_w = jnp.concatenate([q_w, q_x], 0)
    q_y, o_x = other_ways(q_w, jnp.stack([o_w, o_y]))
    q_w = jnp.concatenate([q_w, q_y], 0)
    o_w = jnp.concatenate([o_w, o_x[0], o_y, o_x[1]], 0)
    gate_b, up_b = jnp.stack([gu_b[0], b_x]), jnp.stack([gu_b[1], b_y])
    gate_b2, up_b2 = other_ways(gate_b, up_b)
    gu_4 = mirrored(gu_3, [(2, 3)])
    d_2 = mirrored(jnp.where(m == 2, d_1, own_d), [(1, 0), (2, 3)])
    small = jnp.moveaxis(small, 4, 0).reshape(small.shape[4], -1)
    gain_attn, gain_query, gain_key, gain_moe = [small[i].astype(f32) for i in range(4)]
    weight_router = small[4 : 4 + experts].T
    counts = small[4 + experts :, :: attn_gain.shape[0]].astype(f32)
    count = jnp.sum(counts[0]) * 16.0 + jnp.sum(counts[1])

    tokens_all = jnp.concatenate(token_parts, 0)
    key_segments = jnp.concatenate(segment_parts, 0)
    normed, scale_all = norm_rows(rank, tokens_all, gain_attn, order)
    key_lin, key_squares = project(normed, *key_w, f32)
    value_all, _ = project(normed, *value_w, bf16)
    q_w, o_w, gate_b2, up_b2, gu_4, d_2, normed, key_lin, value_all = hold(
        q_w, o_w, gate_b2, up_b2, gu_4, d_2, normed, key_lin, value_all
    )

    query_w, out_w = (q_w, across(q_w, 1)), (o_w, across(o_w, 1))
    gu_a = jnp.where(
        m == 0, own_gu, jnp.where(m == 1, gu_1, jnp.where(m == 2, gu_3, gu_4))
    )
    a_x, a_y = both_ways(gu_a)
    d_3 = mirrored(d_1, [(1, 2)])
    query_lin, query_squares = project(normed, *query_w, f32, behind)
    scale_key = lax.rsqrt(key_squares / width + norm_eps)
    scale_query = lax.rsqrt(query_squares / width + norm_eps)
    key_positions = (shard - reach) * local_rows + jnp.arange(all_rows, dtype=jnp.int32)
    half_head = HEAD_DIM // 2
    frequency = 10000.0 ** (-jnp.arange(half_head, dtype=f32) * 2.0 / HEAD_DIM)
    angles = key_positions[:, None].astype(f32) * frequency[None, :]
    cosine, sine = jnp.cos(angles), jnp.sin(angles)
    cosine, sine = jnp.concatenate([cosine, cosine], 1), jnp.concatenate([-sine, sine], 1)

    def mask_of(tile):
        span = behind + tile
        parts = []
        for start in range(0, local_rows, tile):
            keys = slice(start, start + span)
            queries = slice(behind + start, behind + start + tile)
            distance = key_positions[None, queries] - key_positions[keys, None]
            allowed = (
                (distance >= 0)
                & (distance < WINDOW)
                & (key_positions[keys, None] >= 0)
                & (key_segments[None, queries] == key_segments[keys, None])
            )
            parts.append(jnp.where(allowed, 0.0, -1e30).astype(f32))
        return jnp.stack(parts)

    operands = (
        query_lin,
        key_lin,
        value_all,
        scale_query,
        scale_key,
        gain_query[None],
        gain_key[None],
        cosine,
        sine,
    )
    mixed, lse = attend(rank, operands, mask_of(local_rows // 4))
    mixed, lse, out_w, gu_a, a_x, a_y, d_3, d_1, d_2, own_d = hold(
        mixed, lse, out_w, gu_a, a_x, a_y, d_3, d_1, d_2, own_d
    )

    gate_a, up_a = jnp.stack([gu_a[0], a_x]), jnp.stack([gu_a[1], a_y])
    gate_a2, up_a2 = other_ways(gate_a, up_a)
    d_4 = mirrored(d_3, [(2, 3)])
    d_b = jnp.where(m == 1, own_d, jnp.where(m == 2, d_1, d_2))
    b_x, b_y = both_ways(d_b)
    branch, _ = project(mixed, *out_w, f32)
    residual = tokens.astype(f32) + branch
    moe, scale_moe = norm_rows(quarter_rank, residual, gain_moe, (0, 1, 2, 3))
    moe_y = jnp.concatenate([moe, across(moe, 1)], 1)
    piece = half // 2
    moe_x = jnp.stack(
        [
            jnp.concatenate([moe_y[0, :, i : i + piece], moe_y[1, :, i : i + piece]], 1)
            for i in (0, piece)
        ]
    )
    router_parts = weight_router.reshape(4, -1, experts)
    router_rel = jnp.concatenate([pick(router_parts, quarter ^ j, 0) for j in range(4)], 0)
    router_probs = jax.nn.softmax(
        matmul(moe[0], router_rel[:half]) + matmul(moe[1], router_rel[half:]), axis=-1
    )
    chosen = jnp.sum(
        (routes[:, :, None] == jnp.arange(experts, dtype=jnp.int32)).astype(f32), axis=1
    )
    gates = router_probs * chosen
    gates_both = jnp.concatenate([gates, across(gates, 1)], 0)
    gates_a = jnp.where(core == 0, gates_both[:, :1], gates_both[:, -1:])
    gates_b = jnp.where(core == 0, gates_both[:, 1:2], gates_both[:, -2:-1])
    gate_a2, up_a2, d_4, d_b, b_x, b_y, moe_y, moe_x = hold(
        gate_a2, up_a2, d_4, d_b, b_x, b_y, moe_y, moe_x
    )

    def flat(value):
        return value.reshape(-1, value.shape[-1])

    left_b, right_b = jnp.stack([d_b[0], b_x]), jnp.stack([d_b[1], b_y])
    left_b2, right_b2 = other_ways(left_b, right_b)
    d_a = jnp.where(m == 0, own_d, jnp.where(m == 1, d_1, jnp.where(m == 2, d_3, d_4)))
    a_x, a_y = both_ways(d_a)
    gu_weights_b = (flat(gate_b), flat(gate_b2), flat(up_b), flat(up_b2))
    gate_pre_b, up_pre_b, my_b, mx_b = experts_up(quarter_rank, moe_y, moe_x, gu_weights_b)
    left_b2, right_b2, d_a, a_x, a_y, my_b, mx_b, gate_a = hold(
        left_b2, right_b2, d_a, a_x, a_y, my_b, mx_b, gate_a
    )

    left_a, right_a = jnp.stack([d_a[0], a_x]), jnp.stack([d_a[1], a_y])
    left_a2, right_a2 = other_ways(left_a, right_a)
    gu_weights_a = (flat(gate_a), flat(gate_a2), flat(up_a), flat(up_a2))
    gate_pre_a, up_pre_a, my_a, mx_a = experts_up(quarter_rank, moe_y, moe_x, gu_weights_a)
    left_a2, right_a2, my_a, mx_a = hold(left_a2, right_a2, my_a, mx_a)
    d_weights_a = (flat(left_a), flat(left_a2), flat(right_a), flat(right_a2))
    d_weights_b = (flat(left_b), flat(left_b2), flat(right_b), flat(right_b2))
    expert_out_a, expert_out_b, mixture = experts_down(
        (gates_a, gates_b), ((my_a, mx_a) + d_weights_a, (my_b, mx_b) + d_weights_b)
    )
    result = residual + (mixture[:local_rows] + across(mixture[local_rows:], 1))
    output = result.astype(bf16)
    error = result - teacher.astype(f32)
    squares = jnp.sum(valid * jnp.sum(error * error, axis=1))
    result_grad = total_tokens / count * valid[:, None] * error
    result_grad_both = jnp.concatenate([result_grad, across(result_grad, 1)], 0)

    pair_b, dg_b, du_b, gate_grad_b = experts_back(
        quarter_rank, result_grad_both, expert_out_b, gates_b, gate_pre_b, up_pre_b, d_weights_b
    )
    pair_a, dg_a, du_a, gate_grad_a = experts_back(
        quarter_rank, result_grad_both, expert_out_a, gates_a, gate_pre_a, up_pre_a, d_weights_a
    )
    sent = [
        part_sum(mx[1], pair[:, :half])
        for mx, pair in ((mx_a, pair_a), (mx_b, pair_b))
    ] + [
        part_sum(my[1], pair[:, half:])
        for my, pair in ((my_a, pair_a), (my_b, pair_b))
    ]
    sent, dg_a, du_a, dg_b, du_b, gate_grad_a, pair_a, pair_b = hold(
        sent, dg_a, du_a, dg_b, du_b, gate_grad_a, pair_a, pair_b
    )

    got_d = [across(sent[0], 2), across(sent[1], 2), across(sent[2], 4), across(sent[3], 4)]
    sent_gu = [part_sum(moe_x[1], grad) for grad in (dg_a, dg_b)] + [
        part_sum(moe_y[1], grad) for grad in (du_a, du_b)
    ]
    input_grad = experts_input(((dg_a, du_a) + gu_weights_a, (dg_b, du_b) + gu_weights_b))
    input_other = across(input_grad[:, local_rows:], 1)
    slot_grads = jnp.concatenate([gate_grad_a, gate_grad_b], 1)
    own_slots, partner_slots = slot_grads[:local_rows], across(slot_grads[local_rows:], 1)
    from_low = jnp.where(core == 0, own_slots, partner_slots)
    from_high = jnp.where(core == 0, partner_slots, own_slots)
    prob_grad = chosen * jnp.concatenate([from_low, from_high[:, ::-1]], 1)
    logit_grad = router_probs * (
        prob_grad - jnp.sum(prob_grad * router_probs, axis=-1, keepdims=True)
    )
    got_d, sent_gu, input_grad, input_other, logit_grad = hold(
        got_d, sent_gu, input_grad, input_other, logit_grad
    )

    got_gu = [
        across(sent_gu[0], 2),
        across(sent_gu[1], 2),
        across(sent_gu[2], 4),
        across(sent_gu[3], 4),
    ]
    kept_d = [
        kept_sum(mx_a[0], pair_a[:, :half], got_d[0]),
        kept_sum(mx_b[0], pair_b[:, :half], got_d[1]),
        kept_sum(my_a[0], pair_a[:, half:], got_d[2]),
        kept_sum(my_b[0], pair_b[:, half:], got_d[3]),
    ]
    got_d = [
        across(kept_d[0][1], 4),
        across(kept_d[1][1], 4),
        across(kept_d[2][1], 2),
        across(kept_d[3][1], 2),
    ]
    router_local = jnp.concatenate(
        [
            jnp.dot(part.T.astype(f32), logit_grad, precision=highest, preferred_element_type=f32)
            for part in (moe[0], moe[1])
        ],
        0,
    )
    router_local = router_local.reshape(4, -1, experts)
    router_local = jnp.concatenate([pick(router_local, quarter ^ j, 0) for j in range(4)], 0)
    residual_grad, branch_grad, moe_gain_local = residual_back(
        quarter_rank,
        input_grad,
        input_other,
        logit_grad,
        weight_router.astype(f32).T,
        residual,
        result_grad,
        scale_moe,
        gain_moe,
    )
    out_a = chip_sum(mixed, branch_grad[:, :half])
    out_b = chip_sum(mixed, branch_grad[:, half:])
    mixed_grad = jnp.stack([dot_t(branch_grad, weight).astype(bf16) for weight in out_w])
    bias = mask_of(local_rows // 2)
    dq_0, dk_0, dv_0 = attend_back(rank, operands, bias, mixed_grad, lse, 0)
    got_gu, kept_d, got_d, out_a, out_b, mixed_grad, dq_0, dk_0, dv_0 = hold(
        got_gu, kept_d, got_d, out_a, out_b, mixed_grad, dq_0, dk_0, dv_0
    )

    def ends(kept, got):
        total = [add(k[0], g) for k, g in zip(kept, got)]
        return jnp.stack([jnp.stack([total[0], total[2]]), jnp.stack([total[1], total[3]])])

    def first_move(both):
        return mirrored(both, [(3, 2)]), mirrored(both[1], [(0, 1)])

    kept_gu = [
        kept_sum(moe_x[0], dg_a, got_gu[0]),
        kept_sum(moe_x[0], dg_b, got_gu[1]),
        kept_sum(moe_y[0], du_a, got_gu[2]),
        kept_sum(moe_y[0], du_b, got_gu[3]),
    ]
    got_gu = [
        across(kept_gu[0][1], 4),
        across(kept_gu[1][1], 4),
        across(kept_gu[2][1], 2),
        across(kept_gu[3][1], 2),
    ]
    out_x, out_y = across(out_a[:, 1], 2), across(out_b[1], 4)
    both_d = ends(kept_d, got_d)
    d_3, d_1 = first_move(both_d)
    dq_1, dk_1, dv_1 = attend_back(rank, operands, bias, mixed_grad, lse, HEADS // 2)
    query_lin_grad, q_gain_local = lin_back(
        dq_0, dq_1, query_lin, scale_query, gain_query[None], cosine[behind:], sine[behind:]
    )
    key_lin_grad, k_gain_local = lin_back(
        dk_0, dk_1, key_lin, scale_key, gain_key[None], cosine, sine
    )
    (
        kept_gu,
        got_gu,
        out_a,
        out_b,
        out_x,
        out_y,
        both_d,
        d_3,
        d_1,
        dv_0,
        dv_1,
        query_lin_grad,
        key_lin_grad,
    ) = hold(
        kept_gu,
        got_gu,
        out_a,
        out_b,
        out_x,
        out_y,
        both_d,
        d_3,
        d_1,
        dv_0,
        dv_1,
        query_lin_grad,
        key_lin_grad,
    )

    out_a, out_b = add(out_a[:, 0], out_x), add(out_b[0], out_y)
    out_x, out_y = across(out_b[1], 2), across(out_a[1], 4)
    both_d = add(both_d, d_3)
    d_2 = mirrored(both_d, [(2, 1)])
    both_gu = ends(kept_gu, got_gu)
    gu_3, gu_1 = first_move(both_gu)
    value_a, value_b = chip_sum(normed, dv_0), chip_sum(normed, dv_1)
    normed_grad = project_back(
        key_lin_grad, dv_0, dv_1, query_lin_grad, key_w, value_w, query_w
    )
    (
        out_a,
        out_b,
        out_x,
        out_y,
        both_d,
        d_2,
        both_gu,
        gu_3,
        gu_1,
        value_a,
        value_b,
        normed_grad,
        query_lin_grad,
        key_lin_grad,
    ) = hold(
        out_a,
        out_b,
        out_x,
        out_y,
        both_d,
        d_2,
        both_gu,
        gu_3,
        gu_1,
        value_a,
        value_b,
        normed_grad,
        query_lin_grad,
        key_lin_grad,
    )

    value_x, value_y = across(value_a[:, 1], 2), across(value_b[1], 4)
    query_sum = chip_sum(normed[:, behind:], query_lin_grad)
    key_sum = chip_sum(normed, key_lin_grad)
    carried = normed_grad[:, :local_rows].astype(bf16)
    carried = from_behind(carried, "ep", -1)
    d_a, d_b = both_d[0] + d_2[0].astype(f32), both_d[1] + d_2[1].astype(f32)
    d_0 = mirrored(d_a.astype(bf16), [(1, 0)])
    both_gu = add(both_gu, gu_3)
    gu_2 = mirrored(both_gu, [(2, 1)])
    out_total = over_ep_sum(jnp.stack([add(out_a[0], out_y), add(out_b[0], out_x)]), place)
    (
        value_a,
        value_b,
        value_x,
        value_y,
        query_sum,
        key_sum,
        carried,
        d_a,
        d_b,
        d_0,
        both_gu,
        gu_2,
        out_total,
    ) = hold(
        value_a,
        value_b,
        value_x,
        value_y,
        query_sum,
        key_sum,
        carried,
        d_a,
        d_b,
        d_0,
        both_gu,
        gu_2,
        out_total,
    )

    def own_half(mine):
        halves = mine.reshape(2, 2, -1, mine.shape[2])
        other = across(pick(halves, 1 - core, 1), 1)
        return jnp.where(m < 2, pick(halves, core, 1), other)

    query_x, key_y = across(query_sum[:, 1], 2), across(key_sum[1], 4)
    value_a, value_b = add(value_a[:, 0], value_x), add(value_b[0], value_y)
    value_x, value_y = across(value_b[1], 2), across(value_a[1], 4)
    for back in range(1, reach):
        here = normed_grad[:, back * local_rows : (back + 1) * local_rows] + carried.astype(f32)
        carried = from_behind(here.astype(bf16), "ep", -1)
    down_mine = jnp.where(m == 0, d_a + d_0.astype(f32), d_b + d_1.astype(f32))
    gu_a, gu_b = both_gu[0] + gu_2[0].astype(f32), both_gu[1] + gu_2[1].astype(f32)
    gu_0 = mirrored(gu_a.astype(bf16), [(1, 0)])
    (
        query_sum,
        key_sum,
        query_x,
        key_y,
        value_a,
        value_b,
        value_x,
        value_y,
        carried,
        gu_a,
        gu_b,
        gu_0,
        down_mine,
    ) = hold(
        query_sum,
        key_sum,
        query_x,
        key_y,
        value_a,
        value_b,
        value_x,
        value_y,
        carried,
        gu_a,
        gu_b,
        gu_0,
        down_mine,
    )

    query_sum, key_sum = add(query_sum[:, 0], query_x), add(key_sum[0], key_y)
    query_y, key_x = across(query_sum[1], 4), across(key_sum[1], 2)
    value_total = over_ep_sum(
        jnp.stack([add(value_a[0], value_y), add(value_b[0], value_x)]), place
    )
    gu_mine = jnp.where(m == 0, gu_a + gu_0.astype(f32), gu_b + gu_1.astype(f32))
    tokens_grad, attn_gain_local = tokens_back(
        rank,
        normed_grad,
        carried,
        tokens,
        residual_grad,
        scale_all,
        gain_attn,
        reps,
    )
    query_sum, key_sum, query_y, key_x, value_total, gu_mine, attn_gain_local = hold(
        query_sum, key_sum, query_y, key_x, value_total, gu_mine, attn_gain_local
    )

    qk_total = over_ep_sum(jnp.stack([add(query_sum[0], query_y), add(key_sum[0], key_x)]), place)
    gu_half, down_half = own_half(gu_mine), own_half(down_mine)
    down_out = jnp.concatenate([down_half[0], down_half[1]], 1)
    out_out = jnp.concatenate([out_total[0], out_total[1]], 1)
    value_out = jnp.concatenate([value_total[0], value_total[1]], 1)
    packed = jnp.concatenate(
        [
            jnp.broadcast_to(squares, (1, width)),
            attn_gain_local,
            q_gain_local,
            k_gain_local,
            moe_gain_local,
            router_local.T,
        ],
        0,
    )
    packed = sum_small(packed, place)
    loss = packed[0, 0] / (2.0 * count * width)
    own_rows = attn_gain.shape[0]
    mine = lax.dynamic_slice_in_dim(packed, (rep * experts + shard) * own_rows, own_rows, 1)
    return (
        output,
        loss,
        tokens_grad,
        mine[1],
        mine[2],
        mine[3],
        mine[4],
        qk_total[0],
        qk_total[1],
        value_out,
        out_out,
        mine[5:].T,
        gu_half[0][None],
        gu_half[1][None],
        down_out[None],
    )


def solution(mesh):
    placed = (
        P(("rep", "ep"), None),
        P(("rep", "ep"), None),
        P("rep", "ep"),
        P("rep", "ep"),
        P(("rep", "ep"), None),
        P(("rep", "ep")),
        P(("rep", "ep")),
        P(("rep", "ep")),
        P(("rep", "ep")),
        P(("rep", "ep"), None),
        P(("rep", "ep"), None),
        P(("rep", "ep"), None),
        P(("rep", "ep"), None),
        P(("rep", "ep"), None),
        P("ep", None, None),
        P("ep", None, None),
        P("ep", None, None),
    )
    chips = mesh.shape["rep"] == 8 and mesh.shape["ep"] == 4
    return jax.shard_map(
        body if chips else body_plain,
        mesh=mesh,
        in_specs=placed,
        out_specs=(
            P(("rep", "ep"), None),
            P(),
            P(("rep", "ep"), None),
            P(("rep", "ep")),
            P(("rep", "ep")),
            P(("rep", "ep")),
            P(("rep", "ep")),
            P(("rep", "ep"), None),
            P(("rep", "ep"), None),
            P(("rep", "ep"), None),
            P(("rep", "ep"), None),
            P(("rep", "ep"), None),
            P("ep", "rep", None),
            P("ep", "rep", None),
            P("ep", "rep", None),
        ),
        check_vma=False,
    )
```

```python
import functools

import jax
import jax.numpy as jnp
from jax import lax
from jax.experimental import pallas as pl
from jax.experimental.pallas import tpu as pltpu
from jax.sharding import PartitionSpec as P

HEADS = 16
HEAD_DIM = 128
WINDOW = 1024
TOP = 2
VMEM_LIMIT = 56 * 1024 * 1024


norm_eps = 1e-05
highest = lax.Precision.HIGHEST


def from_behind(value, axis, steps):
    count = lax.axis_size(axis)
    leading, last = (max(0, -steps), min(count, count - steps))
    return lax.ppermute(value, axis, [(source, source + steps) for source in range(leading, last)])


def matmul(left, right):
    return jnp.dot(left, right, preferred_element_type=jnp.float32)


def rms_scale(value):
    return lax.rsqrt(jnp.mean(value * value, axis=-1, keepdims=True) + norm_eps)


def norm_back(value, scale, gain, grad):
    weighted = grad * gain
    inner = jnp.mean(weighted * value, axis=-1, keepdims=True)
    return (
        scale * weighted - value * (scale * scale * scale) * inner,
        jnp.sum(grad * value * scale, axis=0),
    )


def rounded(value):
    return lax.optimization_barrier(value.astype(jnp.bfloat16)).astype(jnp.float32)


def rotary_tables(positions, head_size):
    half = head_size // 2
    frequency = 10000.0 ** (-jnp.arange(half, dtype=jnp.float32) * 2.0 / head_size)
    angles = positions[:, None].astype(jnp.float32) * frequency[None, :]
    cosine = jnp.cos(angles)
    sine = jnp.sin(angles)
    return (
        jnp.concatenate([cosine, cosine], -1)[:, None, :],
        jnp.concatenate([sine, sine], -1)[:, None, :],
    )


def rotate(value, cosine, sine):
    half = value.shape[-1] // 2
    turned = jnp.concatenate([-value[..., half:], value[..., :half]], -1)
    return value * cosine + turned * sine


def rotate_back(grad, cosine, sine):
    half = grad.shape[-1] // 2
    scaled = grad * sine
    turned = jnp.concatenate([scaled[..., half:], -scaled[..., :half]], -1)
    return grad * cosine + turned


def unpack(everything):
    gains = [everything[index].astype(jnp.float32) for index in range(4)]
    return (gains, everything[4], everything[5], everything[6], everything[7], everything[8])


def body_plain(
    tokens,
    teacher,
    segment_ids,
    valid_mask,
    routes,
    attn_gain,
    q_gain,
    k_gain,
    moe_gain,
    w_query,
    w_key,
    w_value,
    w_out,
    w_router,
    w_gate,
    w_up,
    w_down,
):
    local_rows, width = tokens.shape
    experts = lax.axis_size("ep")
    pairs = local_rows * TOP
    capacity = 5 * pairs // (4 * experts)
    reach = min(-(-WINDOW // local_rows), experts - 1)
    group = min(HEADS, 4)
    score_scale = HEAD_DIM ** (-0.5)
    shard = lax.axis_index("ep")
    total_tokens = local_rows * lax.axis_size("rep") * experts
    everything = (
        lax.all_gather(attn_gain, ("rep", "ep"), axis=0, tiled=True),
        lax.all_gather(q_gain, ("rep", "ep"), axis=0, tiled=True),
        lax.all_gather(k_gain, ("rep", "ep"), axis=0, tiled=True),
        lax.all_gather(moe_gain, ("rep", "ep"), axis=0, tiled=True),
        lax.all_gather(w_query, ("rep", "ep"), axis=0, tiled=True),
        lax.all_gather(w_key, ("rep", "ep"), axis=0, tiled=True),
        lax.all_gather(w_value, ("rep", "ep"), axis=0, tiled=True),
        lax.all_gather(w_out, ("rep", "ep"), axis=0, tiled=True),
        lax.all_gather(w_router, ("rep", "ep"), axis=0, tiled=True),
    )
    gains, weight_query, weight_key, weight_value, weight_out, weight_router = unpack(everything)
    gain_attn, gain_query, gain_key, gain_moe = gains
    inputs = tokens.astype(jnp.float32)
    scale_attn = rms_scale(inputs)
    normed = (inputs * scale_attn * gain_attn).astype(jnp.bfloat16)
    query_lin = matmul(normed, weight_query)
    key_lin = matmul(normed, weight_key)
    value_rows = (
        matmul(normed, weight_value).astype(jnp.bfloat16).reshape(local_rows, HEADS, HEAD_DIM)
    )
    scale_query = rms_scale(query_lin)
    scale_key = rms_scale(key_lin)
    positions = shard * local_rows + jnp.arange(local_rows, dtype=jnp.int32)
    cosine, sine = rotary_tables(positions, HEAD_DIM)
    query_rows = rotate(
        (query_lin * scale_query * gain_query).reshape(local_rows, HEADS, HEAD_DIM), cosine, sine
    ).astype(jnp.bfloat16)
    key_rows = rotate(
        (key_lin * scale_key * gain_key).reshape(local_rows, HEADS, HEAD_DIM), cosine, sine
    ).astype(jnp.bfloat16)
    segments = segment_ids.reshape(local_rows)
    key_parts, value_parts, segment_parts = ([], [], [])
    for back in range(reach, 0, -1):
        moved = from_behind((key_rows, value_rows, segments.astype(jnp.bfloat16)), "ep", back)
        key_parts.append(moved[0])
        value_parts.append(moved[1])
        segment_parts.append(moved[2].astype(jnp.int32))
    all_keys = jnp.concatenate(key_parts + [key_rows], 0)
    all_values = jnp.concatenate(value_parts + [value_rows], 0)
    key_segments = jnp.concatenate(segment_parts + [segments], 0)
    key_positions = (shard - reach) * local_rows + jnp.arange(
        (reach + 1) * local_rows, dtype=jnp.int32
    )
    distance = positions[:, None] - key_positions[None, :]
    allowed = (
        (distance >= 0)
        & (distance < WINDOW)
        & (key_positions[None, :] >= 0)
        & (segments[:, None] == key_segments[None, :])
    )

    def by_group(value):
        return jnp.moveaxis(value.reshape(value.shape[0], HEADS // group, group, HEAD_DIM), 1, 0)

    def from_group(value):
        return jnp.moveaxis(value, 0, 1).reshape(value.shape[1], HEADS * HEAD_DIM)

    def scores_of(query_group, key_group):
        raw = (
            jnp.einsum("qhd,khd->hqk", query_group, key_group, preferred_element_type=jnp.float32)
            * score_scale
        )
        return jnp.where(allowed[None], raw, -1e30)

    def attend_forward(item):
        query_group, key_group, value_group = item
        scores = scores_of(query_group, key_group)
        peak = jnp.max(scores, axis=-1, keepdims=True)
        shifted = jnp.exp(scores - peak)
        total = jnp.sum(shifted, axis=-1, keepdims=True)
        weights = (shifted / total).astype(jnp.bfloat16)
        mixed = jnp.einsum("hqk,khd->qhd", weights, value_group, preferred_element_type=jnp.float32)
        return (mixed, peak, total)

    query_groups = by_group(query_rows)
    key_groups = by_group(all_keys)
    value_groups = by_group(all_values)
    mixed, peaks, totals = lax.map(attend_forward, (query_groups, key_groups, value_groups))
    mixed_rows = from_group(mixed).astype(jnp.bfloat16)
    residual = inputs + matmul(mixed_rows, weight_out)
    scale_moe = rms_scale(residual)
    normed_moe = (residual * scale_moe * gain_moe).astype(jnp.bfloat16)
    router_probs = jax.nn.softmax(matmul(normed_moe, weight_router), axis=-1)
    flat_routes = routes.reshape(pairs)
    choose = (flat_routes[:, None] == jnp.arange(experts, dtype=jnp.int32)[None, :]).astype(
        jnp.int32
    )
    rank = jnp.sum((jnp.cumsum(choose, axis=0) - choose) * choose, axis=1)
    slots = flat_routes * capacity + rank
    pair_source = (
        jnp.full((experts * capacity,), pairs, jnp.int32)
        .at[slots]
        .set(jnp.arange(pairs, dtype=jnp.int32))
    )
    token_source = jnp.where(pair_source < pairs, pair_source // TOP, local_rows)
    zero_row = jnp.zeros((1, width), jnp.bfloat16)
    outgoing = jnp.concatenate([normed_moe, zero_row], 0)[token_source].reshape(
        experts, capacity, width
    )
    choose_float = choose.reshape(local_rows, TOP, experts).astype(jnp.float32)
    gate_value = jnp.sum(choose_float * router_probs[:, None, :], axis=2)
    gate_weight = w_gate[0]
    up_weight = w_up[0]
    down_weight = w_down[0]
    piece = lax.all_to_all(outgoing, "ep", split_axis=0, concat_axis=0, tiled=True)
    flat = piece.reshape(-1, width)
    gate_pre = matmul(flat, gate_weight)
    up_pre = matmul(flat, up_weight)
    middle = (jax.nn.silu(gate_pre) * up_pre).astype(jnp.bfloat16)
    expert_out = matmul(middle, down_weight).astype(jnp.bfloat16)
    lead = piece.shape[:2]
    returned = expert_out.reshape(piece.shape)
    gate_kept = gate_pre.reshape(lead + (-1,))
    up_kept = up_pre.reshape(lead + (-1,))
    arrived = lax.all_to_all(returned, "ep", split_axis=0, concat_axis=0, tiled=True)
    expert_rows = arrived.reshape(experts * capacity, width)[slots].reshape(local_rows, TOP, width)
    result = residual + jnp.sum(gate_value[:, :, None] * expert_rows, axis=1)
    output = result.astype(jnp.bfloat16)
    valid = valid_mask.reshape(local_rows).astype(jnp.float32)
    error = result - teacher.astype(jnp.float32)
    squares = jnp.sum(valid * jnp.sum(error * error, axis=1))
    total_squares, count = lax.psum((squares, jnp.sum(valid)), ("rep", "ep"))
    loss = total_squares / (2.0 * count * width)
    result_grad = total_tokens / count * valid[:, None] * error
    gate_value_grad = jnp.sum(result_grad[:, None, :] * expert_rows, axis=2)
    pair_grad = (
        (gate_value[:, :, None] * result_grad[:, None, :])
        .astype(jnp.bfloat16)
        .reshape(pairs, width)
    )
    grad_outgoing = jnp.concatenate([pair_grad, zero_row], 0)[pair_source].reshape(
        experts, capacity, width
    )
    grad_in = lax.all_to_all(grad_outgoing, "ep", split_axis=0, concat_axis=0, tiled=True)
    rows_in = piece.reshape(-1, width)
    gate_pre = gate_kept.reshape(rows_in.shape[0], -1)
    up_pre = up_kept.reshape(rows_in.shape[0], -1)
    flat_grad = grad_in.reshape(-1, width)
    sigma = jax.nn.sigmoid(gate_pre)
    active = gate_pre * sigma
    middle = (active * up_pre).astype(jnp.bfloat16)
    down_local = matmul(middle.T, flat_grad)
    middle_grad = matmul(flat_grad, down_weight.T)
    gate_pre_grad = (middle_grad * up_pre * sigma * (1.0 + gate_pre * (1.0 - sigma))).astype(
        jnp.bfloat16
    )
    up_pre_grad = (middle_grad * active).astype(jnp.bfloat16)
    gate_local = matmul(rows_in.T, gate_pre_grad)
    up_local = matmul(rows_in.T, up_pre_grad)
    input_grad = (matmul(gate_pre_grad, gate_weight.T) + matmul(up_pre_grad, up_weight.T)).astype(
        jnp.bfloat16
    )
    back_rows = lax.all_to_all(
        input_grad.reshape(experts, capacity, width), "ep", split_axis=0, concat_axis=0, tiled=True
    )
    pair_back = back_rows.reshape(experts * capacity, width)[slots].reshape(local_rows, TOP, width)
    everything = (
        lax.all_gather(attn_gain, ("rep", "ep"), axis=0, tiled=True),
        lax.all_gather(q_gain, ("rep", "ep"), axis=0, tiled=True),
        lax.all_gather(k_gain, ("rep", "ep"), axis=0, tiled=True),
        lax.all_gather(moe_gain, ("rep", "ep"), axis=0, tiled=True),
        lax.all_gather(w_query, ("rep", "ep"), axis=0, tiled=True),
        lax.all_gather(w_key, ("rep", "ep"), axis=0, tiled=True),
        lax.all_gather(w_value, ("rep", "ep"), axis=0, tiled=True),
        lax.all_gather(w_out, ("rep", "ep"), axis=0, tiled=True),
        lax.all_gather(w_router, ("rep", "ep"), axis=0, tiled=True),
    )
    gains, weight_query, weight_key, weight_value, weight_out, weight_router = unpack(everything)
    gain_attn, gain_query, gain_key, gain_moe = gains
    prob_grad = jnp.sum(choose_float * gate_value_grad[:, :, None], axis=1)
    logit_grad = router_probs * (
        prob_grad - jnp.sum(prob_grad * router_probs, axis=-1, keepdims=True)
    )
    router_local = jnp.dot(
        normed_moe.T, logit_grad, precision=highest, preferred_element_type=jnp.float32
    )
    normed_moe_grad = jnp.sum(pair_back.astype(jnp.float32), axis=1) + jnp.dot(
        logit_grad, weight_router.T, precision=highest, preferred_element_type=jnp.float32
    )
    residual_part, moe_gain_local = norm_back(residual, scale_moe, gain_moe, normed_moe_grad)
    residual_grad = result_grad + residual_part
    branch_grad = residual_grad.astype(jnp.bfloat16)
    out_local = matmul(mixed_rows.T, branch_grad)
    mixed_grad = (
        matmul(branch_grad, weight_out.T).astype(jnp.bfloat16).reshape(local_rows, HEADS, HEAD_DIM)
    )

    def attend_backward(item):
        query_group, key_group, value_group, grad_group, peak, total = item
        scores = scores_of(query_group, key_group)
        probs = jnp.exp(scores - peak) / total
        weights = probs.astype(jnp.bfloat16)
        value_part = jnp.einsum(
            "hqk,qhd->khd", weights, grad_group, preferred_element_type=jnp.float32
        )
        probs_grad = jnp.einsum(
            "qhd,khd->hqk", grad_group, value_group, preferred_element_type=jnp.float32
        )
        inner = jnp.sum(probs * probs_grad, axis=-1, keepdims=True)
        score_grad = (probs * (probs_grad - inner)).astype(jnp.bfloat16)
        query_part = (
            jnp.einsum("hqk,khd->qhd", score_grad, key_group, preferred_element_type=jnp.float32)
            * score_scale
        )
        key_part = (
            jnp.einsum("hqk,qhd->khd", score_grad, query_group, preferred_element_type=jnp.float32)
            * score_scale
        )
        return (query_part, key_part, value_part)

    query_parts, key_parts_grad, value_parts_grad = lax.map(
        attend_backward,
        (query_groups, key_groups, value_groups, by_group(mixed_grad), peaks, totals),
    )
    query_row_grad = from_group(query_parts)
    key_all_grad = from_group(key_parts_grad)
    value_all_grad = from_group(value_parts_grad)
    own_keys = key_all_grad[reach * local_rows :]
    own_values = value_all_grad[reach * local_rows :]
    for back in range(1, reach + 1):
        start = (reach - back) * local_rows
        moved = from_behind(
            (key_all_grad[start : start + local_rows], value_all_grad[start : start + local_rows]),
            "ep",
            -back,
        )
        own_keys = own_keys + moved[0]
        own_values = own_values + moved[1]
    query_turned = rotate_back(
        rounded(query_row_grad).reshape(local_rows, HEADS, HEAD_DIM), cosine, sine
    ).reshape(local_rows, width)
    key_turned = rotate_back(
        rounded(own_keys).reshape(local_rows, HEADS, HEAD_DIM), cosine, sine
    ).reshape(local_rows, width)
    query_lin_grad, q_gain_local = norm_back(query_lin, scale_query, gain_query, query_turned)
    key_lin_grad, k_gain_local = norm_back(key_lin, scale_key, gain_key, key_turned)
    query_lin_grad = query_lin_grad.astype(jnp.bfloat16)
    key_lin_grad = key_lin_grad.astype(jnp.bfloat16)
    value_row_grad = own_values.astype(jnp.bfloat16)
    query_local = matmul(normed.T, query_lin_grad)
    key_local = matmul(normed.T, key_lin_grad)
    value_local = matmul(normed.T, value_row_grad)
    normed_grad = (
        matmul(query_lin_grad, weight_query.T)
        + matmul(key_lin_grad, weight_key.T)
        + matmul(value_row_grad, weight_value.T)
    )
    inputs_part, attn_gain_local = norm_back(inputs, scale_attn, gain_attn, normed_grad)
    tokens_grad = residual_grad + inputs_part
    summed = (
        lax.psum_scatter(attn_gain_local, ("rep", "ep"), scatter_dimension=0, tiled=True),
        lax.psum_scatter(q_gain_local, ("rep", "ep"), scatter_dimension=0, tiled=True),
        lax.psum_scatter(k_gain_local, ("rep", "ep"), scatter_dimension=0, tiled=True),
        lax.psum_scatter(moe_gain_local, ("rep", "ep"), scatter_dimension=0, tiled=True),
        lax.psum_scatter(query_local, ("rep", "ep"), scatter_dimension=0, tiled=True),
        lax.psum_scatter(key_local, ("rep", "ep"), scatter_dimension=0, tiled=True),
        lax.psum_scatter(value_local, ("rep", "ep"), scatter_dimension=0, tiled=True),
        lax.psum_scatter(out_local, ("rep", "ep"), scatter_dimension=0, tiled=True),
        lax.psum_scatter(router_local, ("rep", "ep"), scatter_dimension=0, tiled=True),
    )
    expert_summed = (
        lax.psum_scatter(gate_local[None], "rep", scatter_dimension=1, tiled=True),
        lax.psum_scatter(up_local[None], "rep", scatter_dimension=1, tiled=True),
        lax.psum_scatter(down_local[None], "rep", scatter_dimension=1, tiled=True),
    )
    return (
        output,
        loss,
        tokens_grad,
        summed[0],
        summed[1],
        summed[2],
        summed[3],
        summed[4],
        summed[5],
        summed[6],
        summed[7],
        summed[8],
        expert_summed[0],
        expert_summed[1],
        expert_summed[2],
    )


def dot_t(left, right):
    return lax.dot_general(left, right, (((1,), (1,)), ((), ())), preferred_element_type=jnp.float32)


def t_dot(left, right):
    return lax.dot_general(left, right, (((0,), (0,)), ((), ())), preferred_element_type=jnp.float32)


def kernel_call(kernel, **options):
    return pl.pallas_call(
        kernel,
        compiler_params=pltpu.CompilerParams(vmem_limit_bytes=VMEM_LIMIT),
        **options,
    )


def turn(value, cosine, sine):
    return value * cosine + pltpu.roll(value, HEAD_DIM // 2, 1) * sine


def code_of(place, blocks):
    return place % (blocks // 2) * 2 + place // (blocks // 2)


def place_of(code, blocks):
    return code % 2 * (blocks // 2) + code // 2


def norm_kernel(rank, x_ref, gain_ref, o_ref, scale_ref, *, codes):
    value = x_ref[...].astype(jnp.float32)
    scale = lax.rsqrt(jnp.mean(value * value, axis=1, keepdims=True) + norm_eps)
    scale_ref[...] = scale
    half = len(codes) // 2
    block = x_ref.shape[1] // len(codes)
    for place, code in enumerate(codes):
        start = pl.multiple_of((rank[0] ^ code) * block, block)
        piece = x_ref[:, pl.ds(start, block)].astype(jnp.float32)
        piece = piece * scale * gain_ref[:, pl.ds(start, block)]
        at = place % half * block
        o_ref[place // half, :, at : at + block] = piece.astype(jnp.bfloat16)


def norm_rows(rank, value, gain, codes):
    rows, width = value.shape
    tile = 256
    return kernel_call(
        functools.partial(norm_kernel, codes=codes),
        grid_spec=pltpu.PrefetchScalarGridSpec(
            num_scalar_prefetch=1,
            grid=(rows // tile,),
            in_specs=[
                pl.BlockSpec((tile, width), lambda i, rank: (i, 0)),
                pl.BlockSpec((1, width), lambda i, rank: (0, 0)),
            ],
            out_specs=[
                pl.BlockSpec((2, tile, width // 2), lambda i, rank: (0, i, 0)),
                pl.BlockSpec((tile, 1), lambda i, rank: (i, 0)),
            ],
        ),
        out_shape=[
            jax.ShapeDtypeStruct((2, rows, width // 2), jnp.bfloat16),
            jax.ShapeDtypeStruct((rows, 1), jnp.float32),
        ],
    )(rank, value, gain[None])


def project_kernel(low_ref, high_ref, a_ref, b_ref, o_ref, s_ref):
    total = matmul(low_ref[0], a_ref[...]) + matmul(high_ref[0], b_ref[...])
    o_ref[...] = total.astype(o_ref.dtype)
    s_ref[...] = jnp.sum(total * total, axis=1, keepdims=True)


def project(halves, a, b, dtype, start=0):
    _, rows, depth = halves.shape
    rows = rows - start
    width = a.shape[1]
    tile = 256
    first = start // tile
    weight = pl.BlockSpec((depth, width), lambda i: (0, 0))
    return kernel_call(
        project_kernel,
        grid=(rows // tile,),
        in_specs=[
            pl.BlockSpec((1, tile, depth), lambda i: (0, i + first, 0)),
            pl.BlockSpec((1, tile, depth), lambda i: (1, i + first, 0)),
            weight,
            weight,
        ],
        out_specs=[
            pl.BlockSpec((tile, width), lambda i: (i, 0)),
            pl.BlockSpec((tile, 1), lambda i: (i, 0)),
        ],
        out_shape=[
            jax.ShapeDtypeStruct((rows, width), dtype),
            jax.ShapeDtypeStruct((rows, 1), jnp.float32),
        ],
    )(halves, halves, a, b)


def project_back_kernel(k_ref, v_ref, w_ref, q_ref, ka, kb, va, vb, qa, qb, o_ref, *, tile):
    j = pl.program_id(0)
    half = pl.num_programs(0) // 2
    half_width = v_ref.shape[1]
    own = k_ref.shape[0] - q_ref.shape[0]

    def part(key, value, query):
        for start in range(0, k_ref.shape[0], tile):
            at = slice(start, start + tile)
            total = dot_t(k_ref[at, :], key[...]) + dot_t(v_ref[at, :], value[:, :half_width])
            total += dot_t(w_ref[at, :], value[:, half_width:])
            if start >= own:
                total += dot_t(q_ref[start - own : start - own + tile, :], query[...])
            o_ref[0, at, :] = total

    @pl.when(j < half)
    def _():
        part(ka, va, qa)

    @pl.when(j >= half)
    def _():
        part(kb, vb, qb)


def project_back(key, value, value_high, query, key_w, value_w, query_w):
    rows, width = key.shape
    depth = value_w[0].shape[0]
    step = 256
    half = depth // step
    whole = lambda value: pl.BlockSpec(value.shape, lambda j: (0, 0), pipeline_mode=pl.Buffered(1))
    low = pl.BlockSpec((step, width), lambda j: (jnp.minimum(j, half - 1), 0))
    high = pl.BlockSpec((step, width), lambda j: (jnp.maximum(j - half, 0), 0))
    return kernel_call(
        functools.partial(project_back_kernel, tile=512),
        grid=(2 * half,),
        in_specs=[whole(key), whole(value), whole(value_high), whole(query)] + [low, high] * 3,
        out_specs=pl.BlockSpec((1, rows, step), lambda j: (j // half, 0, j % half)),
        out_shape=jax.ShapeDtypeStruct((2, rows, depth), jnp.float32),
    )(key, value, value_high, query, *key_w, *value_w, *query_w)


def tokens_back_kernel(
    rank, g_ref, c_ref, x_ref, res_ref, scale_ref, gain_ref, o_ref, *, blocks
):
    scale = scale_ref[...]
    block = x_ref.shape[1] // blocks
    half = blocks // 2

    def pieces(place):
        start = pl.multiple_of((rank[0] ^ code_of(place, blocks)) * block, block)
        at = slice(place % half * block, place % half * block + block)
        grad = g_ref[place // half, :, at] + c_ref[place // half, :, at].astype(jnp.float32)
        columns = pl.ds(start, block)
        return columns, grad, x_ref[:, columns].astype(jnp.float32), gain_ref[:, columns]

    inner = jnp.zeros_like(scale)
    for place in range(blocks):
        columns, grad, value, gain = pieces(place)
        inner += jnp.sum(grad * value * gain, axis=1, keepdims=True)
    inner = inner * (1.0 / x_ref.shape[1]) * (scale * scale * scale)
    for place in range(blocks):
        columns, grad, value, gain = pieces(place)
        o_ref[:, columns] = res_ref[:, columns] + (scale * (grad * gain) - value * inner)


def tokens_back(rank, grad, carried, tokens, residual_grad, scale, gain, blocks):
    rows, width = tokens.shape
    tile = 128
    first = (grad.shape[1] - rows) // tile
    wide = pl.BlockSpec((tile, width), lambda i, rank: (i, 0))
    one = pl.BlockSpec((1, width), lambda i, rank: (0, 0))
    return kernel_call(
        functools.partial(tokens_back_kernel, blocks=blocks),
        grid_spec=pltpu.PrefetchScalarGridSpec(
            num_scalar_prefetch=1,
            grid=(rows // tile,),
            in_specs=[
                pl.BlockSpec((2, tile, width // 2), lambda i, rank: (0, i + first, 0)),
                pl.BlockSpec((2, tile, width // 2), lambda i, rank: (0, i, 0)),
                wide,
                wide,
                pl.BlockSpec((tile, 1), lambda i, rank: (i + first, 0)),
                one,
            ],
            out_specs=wide,
        ),
        out_shape=jax.ShapeDtypeStruct((rows, width), jnp.float32),
    )(rank, grad, carried, tokens, residual_grad, scale, gain[None])


def head_rows(lin, scale, gain, cosine, sine):
    return turn(lin * scale * gain, cosine, sine).astype(jnp.bfloat16)


def moved_head(head, rank):
    place = place_of((head // 2) ^ rank[0], HEADS // 2) * 2 + head % 2
    return place // (HEADS // 2), 0, place % (HEADS // 2)


def attention_specs(rows, all_rows, bias, first=0):
    head = lambda h, rank: (0, h + first)
    fixed = lambda h, rank: (0, 0)
    return [
        pl.BlockSpec((rows, HEAD_DIM), head),
        pl.BlockSpec((all_rows, HEAD_DIM), head),
        pl.BlockSpec((all_rows, HEAD_DIM), head),
        pl.BlockSpec((rows, 1), fixed),
        pl.BlockSpec((all_rows, 1), fixed),
        pl.BlockSpec((1, HEAD_DIM), head),
        pl.BlockSpec((1, HEAD_DIM), head),
        pl.BlockSpec((all_rows, HEAD_DIM), fixed),
        pl.BlockSpec((all_rows, HEAD_DIM), fixed),
        pl.BlockSpec(bias.shape, lambda h, rank: (0, 0, 0)),
    ]


def attend_kernel(
    rank,
    q_ref,
    k_ref,
    v_ref,
    sq_ref,
    sk_ref,
    gq_ref,
    gk_ref,
    cos_ref,
    sin_ref,
    bias_ref,
    *refs,
    behind,
    tile,
    span,
):
    o_ref, lse_ref = refs[-2:]
    rows = q_ref.shape[0]
    cosine, sine = cos_ref[...], sin_ref[...]
    keys = head_rows(k_ref[...], sk_ref[...], gk_ref[...], cosine, sine)
    queries = head_rows(q_ref[...], sq_ref[...], gq_ref[...], cosine[behind:], sine[behind:])
    for t in range(rows // tile):
        at = slice(t * tile, (t + 1) * tile)
        seen = slice(t * tile, t * tile + span)
        scores = dot_t(keys[seen], queries[at])
        scores = scores * HEAD_DIM ** (-0.5) + bias_ref[t].astype(jnp.float32)
        peak = jnp.max(scores, axis=0, keepdims=True)
        shifted = jnp.exp(scores - peak)
        total = jnp.sum(shifted, axis=0, keepdims=True)
        weights = (shifted * (1.0 / total)).astype(jnp.bfloat16)
        o_ref[0, at, :] = t_dot(weights, v_ref[seen, :]).astype(jnp.bfloat16)
        lse_ref[0, :, at] = peak + jnp.log(total)


def attend(rank, operands, bias, first, into=()):
    rows, width = operands[0].shape
    all_rows = operands[1].shape[0]
    tiles, span, tile = bias.shape
    return kernel_call(
        functools.partial(attend_kernel, behind=all_rows - rows, tile=tile, span=span),
        grid_spec=pltpu.PrefetchScalarGridSpec(
            num_scalar_prefetch=1,
            grid=(HEADS // 2,),
            in_specs=attention_specs(rows, all_rows, bias, first)
            + [pl.BlockSpec(memory_space=pl.ANY)] * len(into),
            out_specs=[
                pl.BlockSpec((1, rows, HEAD_DIM), lambda h, rank: moved_head(h + first, rank)),
                pl.BlockSpec((1, 1, rows), lambda h, rank: (h, 0, 0)),
            ],
        ),
        input_output_aliases={2 + len(operands): 0} if into else {},
        out_shape=[
            jax.ShapeDtypeStruct((2, rows, width // 2), jnp.bfloat16),
            jax.ShapeDtypeStruct((HEADS // 2, 1, rows), jnp.float32),
        ],
    )(rank, *operands, bias, *into)


def attend_back_kernel(
    rank,
    q_ref,
    k_ref,
    v_ref,
    sq_ref,
    sk_ref,
    gq_ref,
    gk_ref,
    cos_ref,
    sin_ref,
    bias_ref,
    g_ref,
    lse_ref,
    dq_ref,
    dk_ref,
    dv_ref,
    key_total,
    value_total,
    *,
    behind,
    tile,
    span,
):
    rows = q_ref.shape[0]
    score_scale = HEAD_DIM ** (-0.5)
    cosine, sine = cos_ref[...], sin_ref[...]
    keys = head_rows(k_ref[...], sk_ref[...], gk_ref[...], cosine, sine)
    queries = head_rows(q_ref[...], sq_ref[...], gq_ref[...], cosine[behind:], sine[behind:])
    key_total[...] = jnp.zeros_like(key_total)
    value_total[...] = jnp.zeros_like(value_total)
    for t in range(rows // tile):
        at = slice(t * tile, (t + 1) * tile)
        seen = slice(t * tile, t * tile + span)
        scores = dot_t(keys[seen], queries[at])
        scores = scores * score_scale + bias_ref[t].astype(jnp.float32)
        probs = jnp.exp(scores - lse_ref[0, :, at])
        grad = g_ref[0, at, :]
        value_total[seen, :] += matmul(probs.astype(jnp.bfloat16), grad)
        probs_grad = dot_t(v_ref[seen, :], grad)
        inner = jnp.sum(probs * probs_grad, axis=0, keepdims=True)
        score_grad = (probs * (probs_grad - inner)).astype(jnp.bfloat16)
        dq_ref[at, :] = (t_dot(score_grad, keys[seen]) * score_scale).astype(jnp.bfloat16)
        key_total[seen, :] += matmul(score_grad, queries[at])
    dk_ref[...] = (key_total[...] * score_scale).astype(jnp.bfloat16)
    dv_ref[...] = value_total[...].astype(jnp.bfloat16)


def attend_back(rank, operands, bias, grad, lse, first):
    rows, width = operands[0].shape
    width = width // 2
    all_rows = operands[1].shape[0]
    tiles, span, tile = bias.shape
    head = lambda h, rank: (0, h)
    return kernel_call(
        functools.partial(attend_back_kernel, behind=all_rows - rows, tile=tile, span=span),
        grid_spec=pltpu.PrefetchScalarGridSpec(
            num_scalar_prefetch=1,
            grid=(HEADS // 2,),
            in_specs=attention_specs(rows, all_rows, bias, first)
            + [
                pl.BlockSpec((1, rows, HEAD_DIM), lambda h, rank: moved_head(h + first, rank)),
                pl.BlockSpec((1, 1, rows), lambda h, rank: (h, 0, 0)),
            ],
            out_specs=[
                pl.BlockSpec((rows, HEAD_DIM), head),
                pl.BlockSpec((all_rows, HEAD_DIM), head),
                pl.BlockSpec((all_rows, HEAD_DIM), head),
            ],
            scratch_shapes=[
                pltpu.VMEM((all_rows, HEAD_DIM), jnp.float32),
                pltpu.VMEM((all_rows, HEAD_DIM), jnp.float32),
            ],
        ),
        out_shape=[
            jax.ShapeDtypeStruct((rows, width), jnp.bfloat16),
            jax.ShapeDtypeStruct((all_rows, width), jnp.bfloat16),
            jax.ShapeDtypeStruct((all_rows, width), jnp.bfloat16),
        ],
    )(rank, *operands, bias, grad, lse)


def lin_back_kernel(
    low_ref, high_ref, lin_ref, scale_ref, gain_ref, cos_ref, sin_ref, o_ref, gain_grad_ref, kept
):
    rows = scale_ref.shape[0]
    scale = jnp.broadcast_to(scale_ref[...], (rows, HEAD_DIM))
    cosine, sine = cos_ref[...], -sin_ref[...]

    @pl.when(pl.program_id(0) == 0)
    def _():
        gain_grad_ref[...] = jnp.zeros_like(gain_grad_ref)

    inner = jnp.zeros((rows, HEAD_DIM), jnp.float32)
    for h in range(HEADS):
        at = slice(h * HEAD_DIM, (h + 1) * HEAD_DIM)
        ref = low_ref if h < HEADS // 2 else high_ref
        here = slice(h % (HEADS // 2) * HEAD_DIM, (h % (HEADS // 2) + 1) * HEAD_DIM)
        grad = turn(ref[:, here].astype(jnp.float32), cosine, sine)
        product = grad * lin_ref[:, at]
        gain = gain_ref[:, at]
        gain_grad_ref[:, at] += jnp.sum(product * scale, axis=0, keepdims=True)
        inner += product * gain
        kept[:, at] = grad * gain * scale
    inner = jnp.sum(inner, axis=1, keepdims=True) * (1.0 / (HEADS * HEAD_DIM))
    inner = jnp.broadcast_to(inner, (rows, HEAD_DIM)) * (scale * scale * scale)
    for h in range(HEADS):
        at = slice(h * HEAD_DIM, (h + 1) * HEAD_DIM)
        o_ref[:, at] = (kept[:, at] - lin_ref[:, at] * inner).astype(jnp.bfloat16)


def lin_back(low, high, lin, scale, gain, cosine, sine):
    rows, width = lin.shape
    tile = 256
    wide = pl.BlockSpec((tile, width), lambda i: (i, 0))
    one = pl.BlockSpec((1, width), lambda i: (0, 0))
    half = pl.BlockSpec((tile, width // 2), lambda i: (i, 0))
    table = pl.BlockSpec((tile, HEAD_DIM), lambda i: (i, 0))
    return kernel_call(
        lin_back_kernel,
        grid=(rows // tile,),
        in_specs=[half, half, wide, pl.BlockSpec((tile, 1), lambda i: (i, 0)), one, table, table],
        out_specs=[wide, one],
        scratch_shapes=[pltpu.VMEM((tile, width), jnp.float32)],
        out_shape=[
            jax.ShapeDtypeStruct((rows, width), jnp.bfloat16),
            jax.ShapeDtypeStruct((1, width), jnp.float32),
        ],
    )(low, high, lin, scale, gain, cosine, sine)


def flat(ref):
    return ref[...].reshape(-1, ref.shape[-1])


def gu_spec(weights):
    return pl.BlockSpec((2, weights.shape[1] // 3 * 2, weights.shape[2]), lambda i, *_: (0, 0, 0))


def d_spec(weights):
    return pl.BlockSpec((2, weights.shape[1] // 3, weights.shape[2]), lambda i, *_: (0, 2, 0))


def dynamic_block(index, block):
    return pl.ds(pl.multiple_of(index * block, block), block)


def experts_up_kernel(rank, x_ref, z_ref, ga, gb, ua, ub, g_ref, u_ref, my_ref, mx_ref, middle_ref):
    gate = matmul(x_ref[0], flat(ga)) + matmul(x_ref[1], flat(gb))
    up = matmul(z_ref[0], flat(ua)) + matmul(z_ref[1], flat(ub))
    g_ref[...] = gate
    u_ref[...] = up
    middle_ref[...] = (gate * jax.nn.sigmoid(gate) * up).astype(jnp.bfloat16)
    block = gate.shape[1] // 4
    for j in range(4):
        piece = middle_ref[:, dynamic_block(rank[0] ^ j, block)]
        dy, dx = j // 2, j % 2
        my_ref[dy, :, dx * block : (dx + 1) * block] = piece
        mx_ref[dx, :, dy * block : (dy + 1) * block] = piece


def experts_up(rank, by_y, by_x, weights):
    _, rows, depth = by_y.shape
    hidden = weights[0].shape[2]
    tile = 256
    x_spec = pl.BlockSpec((2, tile, depth), lambda i, rank: (0, i, 0))
    w_spec = gu_spec(weights[0])
    wide = pl.BlockSpec((tile, hidden), lambda i, rank: (i, 0))
    half = pl.BlockSpec((2, tile, hidden // 2), lambda i, rank: (0, i, 0))
    return kernel_call(
        experts_up_kernel,
        grid_spec=pltpu.PrefetchScalarGridSpec(
            num_scalar_prefetch=1,
            grid=(rows // tile,),
            in_specs=[x_spec, x_spec] + [w_spec] * 4,
            out_specs=[wide, wide, half, half],
            scratch_shapes=[pltpu.VMEM((tile, hidden), jnp.bfloat16)],
        ),
        out_shape=[jax.ShapeDtypeStruct((rows, hidden), jnp.float32)] * 2
        + [jax.ShapeDtypeStruct((2, rows, hidden // 2), jnp.bfloat16)] * 2,
    )(rank, by_y, by_x, *weights)


def experts_down_kernel(*refs):
    gates, slots, outs = refs[:2], (refs[2:8], refs[8:14]), refs[14:]
    half = outs[0].shape[1] // 2
    mixtures = []
    for side in range(2):
        at = slice(side * half, (side + 1) * half)
        mixture = 0.0
        for slot, (my, mx, la, lb, ra, rb) in enumerate(slots):
            if side == 0:
                out = matmul(my[0], flat(la)) + matmul(my[1], flat(lb))
            else:
                out = matmul(mx[0], flat(ra)) + matmul(mx[1], flat(rb))
            out = out.astype(jnp.bfloat16)
            outs[slot][:, at] = out
            mixture += gates[slot][...] * out.astype(jnp.float32)
        mixtures.append(mixture)

    @pl.when(pl.program_id(0) < pl.num_programs(0) // 2)
    def _():
        outs[2][:, :half], outs[2][:, half:] = mixtures

    @pl.when(pl.program_id(0) >= pl.num_programs(0) // 2)
    def _():
        outs[3][:, :half], outs[3][:, half:] = mixtures


def experts_down(gates, slots):
    _, rows, depth = slots[0][0].shape
    half = slots[0][2].shape[2]
    tile = 256
    x_spec = pl.BlockSpec((2, tile, depth), lambda i: (0, i, 0))
    w_spec = d_spec(slots[0][2])
    wide = pl.BlockSpec((tile, 2 * half), lambda i: (i, 0))
    column = pl.BlockSpec((tile, 1), lambda i: (i, 0))
    steps = rows // tile // 2
    return kernel_call(
        experts_down_kernel,
        grid=(rows // tile,),
        in_specs=[column] * 2 + ([x_spec] * 2 + [w_spec] * 4) * 2,
        out_specs=[
            wide,
            wide,
            pl.BlockSpec((tile, 2 * half), lambda i: (jnp.minimum(i, steps - 1), 0)),
            pl.BlockSpec((tile, 2 * half), lambda i: (jnp.maximum(i - steps, 0), 0)),
        ],
        out_shape=[
            jax.ShapeDtypeStruct((rows, 2 * half), jnp.bfloat16),
            jax.ShapeDtypeStruct((rows, 2 * half), jnp.bfloat16),
            jax.ShapeDtypeStruct((rows // 2, 2 * half), jnp.float32),
            jax.ShapeDtypeStruct((rows // 2, 2 * half), jnp.float32),
        ],
    )(*gates, *slots[0], *slots[1])


def experts_back_kernel(
    rank, own_ref, other_ref, out_ref, gate_ref, g_ref, u_ref, la, lb, ra, rb, p_ref, dg_ref, du_ref, gg_ref
):
    own = pl.program_id(0) < pl.num_programs(0) // 2
    grad = jnp.where(own, own_ref[...], other_ref[...])
    gg_ref[...] = jnp.sum(grad * out_ref[...].astype(jnp.float32), axis=1, keepdims=True)
    p_ref[...] = (gate_ref[...] * grad).astype(jnp.bfloat16)
    half = grad.shape[1] // 2
    left, right = p_ref[:, :half], p_ref[:, half:]
    block = la.shape[1]
    for j in range(4):
        dy, dx = j // 2, j % 2
        left_w = (la, lb)[dy][dx]
        right_w = (ra, rb)[dx][dy]
        middle_grad = dot_t(left, left_w) + dot_t(right, right_w)
        at = dynamic_block(rank[0] ^ j, block)
        gate_pre, up_pre = g_ref[:, at], u_ref[:, at]
        sigma = jax.nn.sigmoid(gate_pre)
        change = middle_grad * up_pre * sigma * (1.0 + gate_pre * (1.0 - sigma))
        dg_ref[:, at] = change.astype(jnp.bfloat16)
        du_ref[:, at] = (middle_grad * (gate_pre * sigma)).astype(jnp.bfloat16)


def experts_back(rank, own, other, out, gate, gate_pre, up_pre, weights):
    rows, width = out.shape
    hidden = gate_pre.shape[1]
    tile = 256
    wide = pl.BlockSpec((tile, width), lambda i, rank: (i, 0))
    narrow = pl.BlockSpec((tile, hidden), lambda i, rank: (i, 0))
    column = pl.BlockSpec((tile, 1), lambda i, rank: (i, 0))
    w_spec = d_spec(weights[0])
    steps = rows // tile // 2
    return kernel_call(
        experts_back_kernel,
        grid_spec=pltpu.PrefetchScalarGridSpec(
            num_scalar_prefetch=1,
            grid=(rows // tile,),
            in_specs=[
                pl.BlockSpec((tile, width), lambda i, rank: (jnp.minimum(i, steps - 1), 0)),
                pl.BlockSpec((tile, width), lambda i, rank: (jnp.maximum(i - steps, 0), 0)),
                wide, column, narrow, narrow
            ] + [w_spec] * 4,
            out_specs=[wide, narrow, narrow, column],
        ),
        out_shape=[
            jax.ShapeDtypeStruct((rows, width), jnp.bfloat16),
            jax.ShapeDtypeStruct((rows, hidden), jnp.bfloat16),
            jax.ShapeDtypeStruct((rows, hidden), jnp.bfloat16),
            jax.ShapeDtypeStruct((rows, 1), jnp.float32),
        ],
    )(rank, own, other, out, gate, gate_pre, up_pre, *weights)


def experts_input_kernel(*refs):
    totals = []
    for j in range(4):
        dy, dx = j // 2, j % 2
        total = 0.0
        for dg, du, ga, gb, ua, ub in (refs[:6], refs[6:12]):
            gate_w = (ga, gb)[dy][dx]
            up_w = (ua, ub)[dx][dy]
            part = dot_t(dg[...], gate_w) + dot_t(du[...], up_w)
            total += part.astype(jnp.bfloat16).astype(jnp.float32)
        totals.append(total)

    @pl.when(pl.program_id(0) < pl.num_programs(0) // 2)
    def _():
        for j in range(4):
            refs[-2][j] = totals[j]

    @pl.when(pl.program_id(0) >= pl.num_programs(0) // 2)
    def _():
        for j in range(4):
            refs[-1][j] = totals[j]


def experts_input(slots):
    rows, hidden = slots[0][0].shape
    depth = slots[0][2].shape[1] // 3 * 2
    tile = 256
    narrow = pl.BlockSpec((tile, hidden), lambda i: (i, 0))
    w_spec = gu_spec(slots[0][2])
    steps = rows // tile // 2
    return kernel_call(
        experts_input_kernel,
        grid=(rows // tile,),
        in_specs=([narrow] * 2 + [w_spec] * 4) * 2,
        out_specs=[
            pl.BlockSpec((4, tile, depth), lambda i: (0, jnp.minimum(i, steps - 1), 0)),
            pl.BlockSpec((4, tile, depth), lambda i: (0, jnp.maximum(i - steps, 0), 0)),
        ],
        out_shape=[jax.ShapeDtypeStruct((4, rows // 2, depth), jnp.float32)] * 2,
    )(*slots[0], *slots[1])


def residual_back_kernel(
    rank, a_ref, b_ref, lg_ref, wr_ref, x_ref, r_ref, scale_ref, gain_ref, o_ref, c_ref, gg_ref
):
    scale = scale_ref[...]
    block = a_ref.shape[2]

    @pl.when(pl.program_id(0) == 0)
    def _():
        gg_ref[...] = jnp.zeros_like(gg_ref)

    inner = jnp.zeros_like(scale)
    for j in range(4):
        at = dynamic_block(rank[0] ^ j, block)
        grad = a_ref[j] + b_ref[j]
        for e in range(wr_ref.shape[0]):
            grad += lg_ref[:, e : e + 1] * wr_ref[e : e + 1, at]
        o_ref[:, at] = grad
        product = grad * x_ref[:, at]
        inner += jnp.sum(product * gain_ref[:, at], axis=1, keepdims=True)
        gg_ref[:, at] += jnp.sum(product * scale, axis=0, keepdims=True)
    inner = inner * (1.0 / x_ref.shape[1]) * (scale * scale * scale)
    for j in range(4):
        at = slice(j * block, (j + 1) * block)
        value = scale * (o_ref[:, at] * gain_ref[:, at]) - x_ref[:, at] * inner
        value = r_ref[:, at] + value
        o_ref[:, at] = value
        c_ref[:, at] = value.astype(jnp.bfloat16)


def residual_back(rank, own, other, logit_grad, router, residual, result_grad, scale, gain):
    rows, width = residual.shape
    tile = 128
    wide = pl.BlockSpec((tile, width), lambda i, rank: (i, 0))
    piece = pl.BlockSpec((4, tile, width // 4), lambda i, rank: (0, i, 0))
    one = pl.BlockSpec((1, width), lambda i, rank: (0, 0))
    experts = logit_grad.shape[1]
    return kernel_call(
        residual_back_kernel,
        grid_spec=pltpu.PrefetchScalarGridSpec(
            num_scalar_prefetch=1,
            grid=(rows // tile,),
            in_specs=[
                piece,
                piece,
                pl.BlockSpec((tile, experts), lambda i, rank: (i, 0)),
                pl.BlockSpec((experts, width), lambda i, rank: (0, 0)),
                wide,
                wide,
                pl.BlockSpec((tile, 1), lambda i, rank: (i, 0)),
                one,
            ],
            out_specs=[wide, wide, one],
        ),
        out_shape=[
            jax.ShapeDtypeStruct((rows, width), jnp.float32),
            jax.ShapeDtypeStruct((rows, width), jnp.bfloat16),
            jax.ShapeDtypeStruct((1, width), jnp.float32),
        ],
    )(rank, own, other, logit_grad, router, residual, result_grad, scale, gain[None])


def experts_grad_kernel(x_ref, d_ref, m_ref, p_ref, *refs):
    o_ref = refs[-1]
    rows, down_rows = x_ref.shape[2], m_ref.shape[2]
    top, bottom = t_dot(x_ref[0], d_ref[...]), t_dot(m_ref[0], p_ref[...])
    if len(refs) == 2:
        top += refs[0][0, :rows].astype(jnp.float32)
        bottom += refs[0][0, rows:].astype(jnp.float32)
    o_ref[0, :rows] = top.astype(jnp.bfloat16)
    o_ref[0, rows:] = bottom.astype(jnp.bfloat16)


def experts_grad(inputs, pre_grad, middle, pair, part, side, got=()):
    _, rows, depth = inputs.shape
    hidden, down = pre_grad.shape[1], middle.shape[2]
    step = hidden // 2
    piece = pl.BlockSpec((1, (depth + down) // 2, step), lambda q, j: (q, 0, j))
    return kernel_call(
        experts_grad_kernel,
        grid=(2, 2),
        in_specs=[
            pl.BlockSpec((1, rows, depth // 2), lambda q, j: (part, 0, q)),
            pl.BlockSpec((rows, step), lambda q, j: (0, j)),
            pl.BlockSpec((1, rows, down // 2), lambda q, j: (part, 0, q)),
            pl.BlockSpec((rows, step), lambda q, j: (0, j + 2 * side)),
        ]
        + [piece] * len(got),
        out_specs=piece,
        out_shape=jax.ShapeDtypeStruct((2, (depth + down) // 2, hidden), jnp.bfloat16),
    )(inputs, pre_grad, middle, pair, *got)


def gain_grad_kernel(rank, g_ref, x_ref, scale_ref, o_ref, *, codes):
    half = len(codes) // 2
    block = x_ref.shape[1] // len(codes)

    @pl.when(pl.program_id(0) == 0)
    def _():
        o_ref[...] = jnp.zeros_like(o_ref)

    for place, code in enumerate(codes):
        columns = dynamic_block(rank[0] ^ code, block)
        grad = g_ref[place // half, :, place % half * block : (place % half + 1) * block]
        product = grad * (x_ref[:, columns].astype(jnp.float32) * scale_ref[...])
        o_ref[:, columns] += jnp.sum(product, axis=0, keepdims=True)


def gain_grad(rank, grad, value, scale, codes):
    rows, width = value.shape
    tile = 256
    return kernel_call(
        functools.partial(gain_grad_kernel, codes=codes),
        grid_spec=pltpu.PrefetchScalarGridSpec(
            num_scalar_prefetch=1,
            grid=(rows // tile,),
            in_specs=[
                pl.BlockSpec((2, tile, width // 2), lambda i, rank: (0, i, 0)),
                pl.BlockSpec((tile, width), lambda i, rank: (i, 0)),
                pl.BlockSpec((tile, 1), lambda i, rank: (i, 0)),
            ],
            out_specs=pl.BlockSpec((1, width), lambda i, rank: (0, 0)),
        ),
        out_shape=jax.ShapeDtypeStruct((1, width), jnp.float32),
    )(rank, grad, value, scale)


def chip_grad_kernel(x_ref, g_ref, *refs):
    total = t_dot(x_ref[0], g_ref[...])
    if len(refs) == 2:
        total += refs[0][...].astype(jnp.float32)
    refs[-1][...] = total.astype(jnp.bfloat16)


def chip_grad(halves, part, grad, start=0, got=()):
    depth = halves.shape[2]
    rows, width = grad.shape
    tile, step = 512, 512
    piece = pl.BlockSpec((tile, step), lambda i, j: (i, j))
    return kernel_call(
        chip_grad_kernel,
        grid=(depth // tile, width // step),
        in_specs=[
            pl.BlockSpec((1, rows, tile), lambda i, j: (part, start // rows, i)),
            pl.BlockSpec((rows, step), lambda i, j: (0, j)),
        ]
        + [piece] * len(got),
        out_specs=piece,
        out_shape=jax.ShapeDtypeStruct((depth, width), jnp.bfloat16),
    )(halves, grad, *got)


def mixed_back_kernel(g_ref, a_ref, b_ref, o_ref):
    for half, ref in enumerate((a_ref, b_ref)):
        o_ref[half] = dot_t(g_ref[...], ref[...]).astype(jnp.bfloat16)


def mixed_back(grad, weights):
    rows, width = grad.shape
    depth = weights[0].shape[0]
    step = 256
    weight = pl.BlockSpec((step, width), lambda j: (j, 0))
    return kernel_call(
        mixed_back_kernel,
        grid=(depth // step,),
        in_specs=[pl.BlockSpec((rows, width), lambda j: (0, 0)), weight, weight],
        out_specs=pl.BlockSpec((2, rows, step), lambda j: (0, 0, j)),
        out_shape=jax.ShapeDtypeStruct((2, rows, depth), jnp.bfloat16),
    )(grad, *weights)


def across(value, bit):
    count = lax.axis_size("rep")
    return lax.ppermute(value, "rep", [(place, place ^ bit) for place in range(count)])


def along(value, steps):
    count = lax.axis_size("ep")
    return lax.ppermute(value, "ep", [(place, (place + steps) % count) for place in range(count)])


def mirrored(value, moves):
    reps, count = lax.axis_size("rep"), lax.axis_size("ep")
    pairs = []
    for rep in range(reps):
        for source, target in moves:
            if rep % 2:
                source, target = count - 1 - source, count - 1 - target
            pairs.append((rep * count + source, rep * count + target))
    return lax.ppermute(value, ("rep", "ep"), pairs)


def pick(value, index, axis):
    return lax.dynamic_index_in_dim(value, index, axis, keepdims=False)


def in_order(own, other, bit, axis):
    return jnp.where(bit == 1, jnp.stack([other, own], axis), jnp.stack([own, other], axis))


def over_ep(value, place):
    shard = place[3]
    experts = lax.axis_size("ep")
    parts = jnp.zeros((experts,) + value.shape, value.dtype)
    parts = lax.dynamic_update_index_in_dim(parts, value, shard, 0)
    for steps in range(1, experts):
        parts = lax.dynamic_update_index_in_dim(
            parts, along(value, steps), lax.rem(shard - steps + experts, experts), 0
        )
    return parts


def hold(*values):
    return lax.optimization_barrier(values)


def both_ways(value):
    return across(value[0], 2), across(value[1], 4)


def other_ways(first, second):
    return across(first, 4), across(second, 2)


def add(left, right):
    return (left.astype(jnp.float32) + right.astype(jnp.float32)).astype(jnp.bfloat16)


def ep_sum(both):
    return lax.psum_scatter(both, "ep", scatter_dimension=1, tiled=True).astype(jnp.float32)


def body(
    tokens,
    teacher,
    segment_ids,
    valid_mask,
    routes,
    attn_gain,
    q_gain,
    k_gain,
    moe_gain,
    w_query,
    w_key,
    w_value,
    w_out,
    w_router,
    w_gate,
    w_up,
    w_down,
):
    bf16, f32 = jnp.bfloat16, jnp.float32
    local_rows, width = tokens.shape
    experts = lax.axis_size("ep")
    reps = lax.axis_size("rep")
    reach = min(-(-WINDOW // local_rows), experts - 1)
    shard = lax.axis_index("ep")
    rep = lax.axis_index("rep")
    place = (rep // 4, rep // 2 % 2, rep % 2, shard)
    core = rep % 2
    total_tokens = local_rows * reps * experts

    valid = valid_mask.reshape(local_rows).astype(f32)
    own_count = jnp.sum(valid_mask)
    counts = jnp.stack([own_count // 16, own_count % 16]).astype(bf16)
    small = jnp.concatenate(
        [
            jnp.stack([attn_gain, q_gain, k_gain, moe_gain], 1),
            w_router,
            jnp.broadcast_to(counts[None], (attn_gain.shape[0], 2)),
        ],
        1,
    )
    rank = rep.astype(jnp.int32)[None]
    quarter = rep // 2
    quarter_rank = quarter.astype(jnp.int32)[None]
    order = tuple(code_of(j, reps) for j in range(reps))
    half = width // 2
    behind = reach * local_rows
    all_rows = local_rows + behind
    m = jnp.where(core == 0, shard, experts - 1 - shard)
    quarter_rows = w_gate.shape[1] // 4
    quarter_down = w_down.shape[1] // 4

    def own_part(weight, rows):
        return lax.dynamic_slice_in_dim(weight[0], quarter * rows, rows, 0)

    down = own_part(w_down, quarter_down)
    own = jnp.stack(
        [
            jnp.concatenate([own_part(w_gate, quarter_rows), down[:, :half]], 0),
            jnp.concatenate([own_part(w_up, quarter_rows), down[:, half:]], 0),
        ]
    )
    segments = segment_ids.reshape(local_rows)
    shard_rows = w_key.shape[0]
    columns = small.shape[1]
    small = small.T

    small = over_ep(small, place)
    parts = over_ep(jnp.stack([w_key, w_value]), place)
    segments_1 = from_behind(segments, "ep", 1)
    parts, small, own, tokens_1, segments_1 = hold(parts, small, own, tokens, segments_1)
    qo = jnp.stack([w_query, w_out])

    qo, parts = hold(qo, parts)
    qo = lax.all_gather(qo, "ep", axis=0)
    block = shard_rows * experts
    k_w, v_w = parts[:, 0].reshape(block, width), parts[:, 1].reshape(block, width)
    e_1 = mirrored(own, [(0, 1), (1, 2)])
    small = small.reshape(-1)
    small = jnp.pad(small, (0, 16 * width - small.shape[0])).reshape(16, width)
    k_w = jnp.concatenate([k_w, small], 0)
    k_x, v_y = both_ways((k_w, v_w))
    segments_2 = from_behind(segments_1, "ep", 1)
    k_w, k_x, v_w, v_y, tokens_1, segments_2 = hold(k_w, k_x, v_w, v_y, tokens_1, segments_2)

    k_w = jnp.stack([k_w, k_x])
    k_y, v_x = other_ways(k_w, jnp.stack([v_w, v_y]))
    tokens_1 = from_behind(tokens_1, "ep", 1)
    qo, k_w, k_y, v_w, v_y, v_x, tokens_1 = hold(qo, k_w, k_y, v_w, v_y, v_x, tokens_1)

    small = jnp.concatenate([k_w[:, block : block + 2], k_y[:, block : block + 2]], 0)
    small = jnp.pad(small.reshape(-1, width), ((0, 8), (0, 0)))
    k_w = jnp.concatenate([k_w[0, :block], k_w[1, :block], k_y[0, :block], k_y[1, :block], small], 0)
    v_w = jnp.concatenate([v_w, v_x[0], v_y, v_x[1]], 0)
    key_w, value_w = (k_w, across(k_w, 1)), (v_w, across(v_w, 1))
    q_w, o_w = qo[:, 0].reshape(-1, width), qo[:, 1].reshape(-1, width)
    q_x, o_y = both_ways((q_w, o_w))
    tokens_2 = from_behind(tokens_1, "ep", 1)
    key_w, value_w, q_w, q_x, o_w, o_y, tokens_2, tokens_1, e_1, own = hold(
        key_w, value_w, q_w, q_x, o_w, o_y, tokens_2, tokens_1, e_1, own
    )

    q_w = jnp.concatenate([q_w, q_x], 0)
    q_y, o_x = other_ways(q_w, jnp.stack([o_w, o_y]))
    q_w = jnp.concatenate([q_w, q_y], 0)
    o_w = jnp.concatenate([o_w, o_x[0], o_y, o_x[1]], 0)
    e_2 = mirrored(jnp.where(m == 2, e_1, own), [(1, 0), (2, 3)])
    small = jnp.stack([weight[4 * block : 4 * block + 8] for weight in key_w])
    small = small.reshape(2, 2, 2, -1)[..., : experts * columns * shard_rows]
    for axis, bit in enumerate((core, place[0], place[1])):
        small = jnp.where(bit == 1, jnp.flip(small, axis), small)
    small = small.reshape(2, 2, 2, experts, columns, shard_rows)
    small = jnp.transpose(small, (4, 1, 2, 0, 3, 5)).reshape(columns, -1)
    gain_attn, gain_query, gain_key, gain_moe = [small[i].astype(f32) for i in range(4)]
    weight_router = small[4 : 4 + experts].T
    counts = small[4 + experts :, ::shard_rows].astype(f32)
    count = jnp.sum(counts[0]) * 16.0 + jnp.sum(counts[1])
    tokens_all = jnp.concatenate([tokens_2, tokens_1, tokens], 0)
    key_segments = jnp.concatenate([segments_2, segments_1, segments], 0)
    normed, scale_all = norm_rows(rank, tokens_all, gain_attn, order)
    key_lin, key_squares = project(normed, *key_w, f32)
    value_all, _ = project(normed, *value_w, bf16)
    q_w, o_w, e_2, e_1, own, normed, key_lin, value_all = hold(
        q_w, o_w, e_2, e_1, own, normed, key_lin, value_all
    )

    query_w, out_w = (q_w, across(q_w, 1)), (o_w, across(o_w, 1))
    e_b = jnp.where(m == 1, own, jnp.where(m == 2, e_1, e_2))
    b_x, b_y = both_ways(e_b)
    e_3 = mirrored(e_1, [(1, 2)])
    query_lin, query_squares = project(normed, *query_w, f32, behind)
    scale_key = lax.rsqrt(key_squares / width + norm_eps)
    scale_query = lax.rsqrt(query_squares / width + norm_eps)
    key_positions = (shard - reach) * local_rows + jnp.arange(all_rows, dtype=jnp.int32)
    half_head = HEAD_DIM // 2
    frequency = 10000.0 ** (-jnp.arange(half_head, dtype=f32) * 2.0 / HEAD_DIM)
    angles = key_positions[:, None].astype(f32) * frequency[None, :]
    cosine, sine = jnp.cos(angles), jnp.sin(angles)
    cosine, sine = jnp.concatenate([cosine, cosine], 1), jnp.concatenate([-sine, sine], 1)

    def mask_of(tile):
        span = behind + tile
        parts = []
        for start in range(0, local_rows, tile):
            keys = slice(start, start + span)
            queries = slice(behind + start, behind + start + tile)
            distance = key_positions[None, queries] - key_positions[keys, None]
            allowed = (
                (distance >= 0)
                & (distance < WINDOW)
                & (key_positions[keys, None] >= 0)
                & (key_segments[None, queries] == key_segments[keys, None])
            )
            parts.append(jnp.where(allowed, 0.0, -1e30).astype(f32))
        return jnp.stack(parts)

    operands = (
        query_lin,
        key_lin,
        value_all,
        scale_query,
        scale_key,
        gain_query[None],
        gain_key[None],
        cosine,
        sine,
    )
    bias_small = mask_of(local_rows // 4)
    mixed, lse_0 = attend(rank, operands, bias_small, 0)
    mixed, out_w, e_b, b_x, b_y, e_3, e_1, own = hold(mixed, out_w, e_b, b_x, b_y, e_3, e_1, own)

    b_0, b_1 = jnp.stack([e_b[0], b_x]), jnp.stack([e_b[1], b_y])
    b_2, b_3 = other_ways(b_0, b_1)
    e_4 = mirrored(e_3, [(2, 3)])
    mixed, lse_1 = attend(rank, operands, bias_small, HEADS // 2, (mixed,))
    branch, _ = project(mixed, *out_w, f32)
    residual = tokens.astype(f32) + branch
    moe, scale_moe = norm_rows(quarter_rank, residual, gain_moe, (0, 1, 2, 3))
    moe_y = jnp.concatenate([moe, across(moe, 1)], 1)
    piece = half // 2
    moe_x = jnp.stack(
        [
            jnp.concatenate([moe_y[0, :, i : i + piece], moe_y[1, :, i : i + piece]], 1)
            for i in (0, piece)
        ]
    )
    router_parts = weight_router.reshape(4, -1, experts)
    router_rel = jnp.concatenate([pick(router_parts, quarter ^ j, 0) for j in range(4)], 0)
    router_probs = jax.nn.softmax(
        matmul(moe[0], router_rel[:half]) + matmul(moe[1], router_rel[half:]), axis=-1
    )
    chosen = jnp.sum(
        (routes[:, :, None] == jnp.arange(experts, dtype=jnp.int32)).astype(f32), axis=1
    )
    gates = router_probs * chosen
    gates_both = jnp.concatenate([gates, across(gates, 1)], 0)
    gates_a = jnp.where(core == 0, gates_both[:, :1], gates_both[:, -1:])
    gates_b = jnp.where(core == 0, gates_both[:, 1:2], gates_both[:, -2:-1])
    b_0, b_1, b_2, b_3, e_4, e_3, e_1, own, moe_y, moe_x = hold(
        b_0, b_1, b_2, b_3, e_4, e_3, e_1, own, moe_y, moe_x
    )

    e_a = jnp.where(m == 0, own, jnp.where(m == 1, e_1, jnp.where(m == 2, e_3, e_4)))
    a_x, a_y = both_ways(e_a)
    weights_b = (b_0, b_2, b_1, b_3)
    gate_pre_b, up_pre_b, my_b, mx_b = experts_up(quarter_rank, moe_y, moe_x, weights_b)
    e_a, a_x, a_y, my_b, mx_b, moe_y, moe_x = hold(e_a, a_x, a_y, my_b, mx_b, moe_y, moe_x)

    a_0, a_1 = jnp.stack([e_a[0], a_x]), jnp.stack([e_a[1], a_y])
    a_2, a_3 = other_ways(a_0, a_1)
    weights_a = (a_0, a_2, a_1, a_3)
    gate_pre_a, up_pre_a, my_a, mx_a = experts_up(quarter_rank, moe_y, moe_x, weights_a)
    expert_out_a, expert_out_b, mixture, mixture_other = experts_down(
        (gates_a, gates_b), ((my_a, mx_a) + weights_a, (my_b, mx_b) + weights_b)
    )
    result = residual + (mixture + across(mixture_other, 1))
    output = result.astype(bf16)
    error = result - teacher.astype(f32)
    squares = jnp.sum(valid * jnp.sum(error * error, axis=1))
    result_grad = total_tokens / count * valid[:, None] * error
    result_other = across(result_grad, 1)

    pair_b, dg_b, du_b, gate_grad_b = experts_back(
        quarter_rank,
        result_grad,
        result_other,
        expert_out_b,
        gates_b,
        gate_pre_b,
        up_pre_b,
        weights_b,
    )
    sent_x = experts_grad(moe_x, dg_b, mx_b, pair_b, 1, 0)
    sent_y = experts_grad(moe_y, du_b, my_b, pair_b, 1, 1)
    sent_x, sent_y, expert_out_a = hold(sent_x, sent_y, expert_out_a)

    b_x, b_y = both_ways((sent_x, sent_y))
    pair_a, dg_a, du_a, gate_grad_a = experts_back(
        quarter_rank,
        result_grad,
        result_other,
        expert_out_a,
        gates_a,
        gate_pre_a,
        up_pre_a,
        weights_a,
    )
    sent_x = experts_grad(moe_x, dg_a, mx_a, pair_a, 1, 0)
    sent_y = experts_grad(moe_y, du_a, my_a, pair_a, 1, 1)
    input_grad, input_other = experts_input(
        ((dg_a, du_a) + weights_a, (dg_b, du_b) + weights_b)
    )
    slot_grads = jnp.concatenate([gate_grad_a, gate_grad_b], 1)
    own_slots, partner_slots = slot_grads[:local_rows], across(slot_grads[local_rows:], 1)
    from_low = jnp.where(core == 0, own_slots, partner_slots)
    from_high = jnp.where(core == 0, partner_slots, own_slots)
    prob_grad = chosen * jnp.concatenate([from_low, from_high[:, ::-1]], 1)
    logit_grad = router_probs * (
        prob_grad - jnp.sum(prob_grad * router_probs, axis=-1, keepdims=True)
    )
    b_x, b_y, sent_x, sent_y, input_grad, input_other, logit_grad = hold(
        b_x, b_y, sent_x, sent_y, input_grad, input_other, logit_grad
    )

    input_other = across(input_other, 1)
    a_x, a_y = both_ways((sent_x, sent_y))
    b_0 = experts_grad(moe_x, dg_b, mx_b, pair_b, 0, 0, (b_x,))
    b_1 = experts_grad(moe_y, du_b, my_b, pair_b, 0, 1, (b_y,))
    b_y, b_x = other_ways(b_0[1], b_1[1])
    router_local = jnp.concatenate(
        [
            jnp.dot(part.T.astype(f32), logit_grad, precision=highest, preferred_element_type=f32)
            for part in (moe[0], moe[1])
        ],
        0,
    )
    router_local = router_local.reshape(4, -1, experts)
    router_local = jnp.concatenate([pick(router_local, quarter ^ j, 0) for j in range(4)], 0)
    residual_grad, branch_grad, moe_gain_local = residual_back(
        quarter_rank,
        input_grad,
        input_other,
        logit_grad,
        weight_router.astype(f32).T,
        residual,
        result_grad,
        scale_moe,
        gain_moe,
    )
    out_sent = across(chip_grad(mixed, 1, branch_grad), 1)
    out_sum = chip_grad(mixed, 0, branch_grad, 0, (out_sent,)).reshape(2, 2, -1, width)
    mixed_grad = mixed_back(branch_grad, out_w)
    bias = mask_of(local_rows // 2)
    dq_0, dk_0, dv_0 = attend_back(rank, operands, bias, mixed_grad, lse_0, 0)
    dq_1, dk_1, dv_1 = attend_back(rank, operands, bias, mixed_grad, lse_1, HEADS // 2)
    a_x, a_y, b_0, b_1, b_x, b_y, out_sum, dq_0, dk_0, dv_0, dq_1, dk_1, dv_1 = hold(
        a_x, a_y, b_0, b_1, b_x, b_y, out_sum, dq_0, dk_0, dv_0, dq_1, dk_1, dv_1
    )

    a_0 = experts_grad(moe_x, dg_a, mx_a, pair_a, 0, 0, (a_x,))
    a_1 = experts_grad(moe_y, du_a, my_a, pair_a, 0, 1, (a_y,))
    a_y, a_x = other_ways(a_0[1], a_1[1])
    out_x, out_y = across(out_sum[:, 1, :, :half], 2), across(out_sum[1, :, :, half:], 4)
    b_end = jnp.stack([add(b_0[0], b_y), add(b_1[0], b_x)])
    b_got = mirrored(b_end, [(3, 2), (0, 1)])
    query_lin_grad, q_gain_local = lin_back(
        dq_0, dq_1, query_lin, scale_query, gain_query[None], cosine[behind:], sine[behind:]
    )
    key_lin_grad, k_gain_local = lin_back(
        dk_0, dk_1, key_lin, scale_key, gain_key[None], cosine, sine
    )
    value_sent = (chip_grad(normed, 1, dv_0), chip_grad(normed, 1, dv_1))
    (
        a_0, a_1, a_x, a_y, out_sum, out_x, out_y, b_end, b_got, query_lin_grad, key_lin_grad,
        value_sent, dv_0, dv_1,
    ) = hold(
        a_0, a_1, a_x, a_y, out_sum, out_x, out_y, b_end, b_got, query_lin_grad, key_lin_grad,
        value_sent, dv_0, dv_1,
    )

    out_a, out_b = add(out_sum[:, 0, :, :half], out_x), add(out_sum[0, :, :, half:], out_y)
    out_x, out_y = across(out_b[1], 2), across(out_a[1], 4)
    b_low = add(b_end, b_got)
    b_got_2 = mirrored(b_low, [(2, 1)])
    a_end = jnp.stack([add(a_0[0], a_y), add(a_1[0], a_x)])
    a_got = mirrored(a_end, [(3, 2)])
    normed_grad = project_back(
        key_lin_grad, dv_0, dv_1, query_lin_grad, key_w, value_w, query_w
    )
    out_a, out_b, out_x, out_y, normed_grad, value_sent, query_lin_grad, key_lin_grad = hold(
        out_a, out_b, out_x, out_y, normed_grad, value_sent, query_lin_grad, key_lin_grad
    )

    carried = from_behind(normed_grad[:, :local_rows].astype(bf16), "ep", -1)
    value_got = across(value_sent[0], 1), across(value_sent[1], 1)
    out_total = ep_sum(jnp.stack([add(out_a[0], out_y), add(out_b[0], out_x)]))
    attn_gain_local = gain_grad(rank, normed_grad, tokens_all, scale_all, order)
    query_sent = chip_grad(normed, 1, query_lin_grad, behind)
    key_sent = chip_grad(normed, 1, key_lin_grad)
    value_a = chip_grad(normed, 0, dv_0, 0, (value_got[0],)).reshape(2, 2, -1, half)
    value_b = chip_grad(normed, 0, dv_1, 0, (value_got[1],)).reshape(2, 2, -1, half)
    packed = jnp.concatenate(
        [
            jnp.broadcast_to(squares, (1, width)),
            attn_gain_local,
            q_gain_local,
            k_gain_local,
            moe_gain_local,
            router_local.T,
        ],
        0,
    )
    carried, value_a, value_b, query_sent, key_sent, query_lin_grad, key_lin_grad, packed = hold(
        carried, value_a, value_b, query_sent, key_sent, query_lin_grad, key_lin_grad, packed
    )

    query_got, key_got = across(query_sent, 1), across(key_sent, 1)
    value_x, value_y = across(value_a[:, 1], 2), across(value_b[1], 4)
    for back in range(1, reach):
        here = normed_grad[:, back * local_rows : (back + 1) * local_rows] + carried.astype(f32)
        carried = from_behind(here.astype(bf16), "ep", -1)
    query_sum = chip_grad(normed, 0, query_lin_grad, behind, (query_got,))
    key_sum = chip_grad(normed, 0, key_lin_grad, 0, (key_got,))
    query_sum = query_sum.reshape(2, 2, -1, width)
    key_sum = key_sum.reshape(2, 2, -1, width)
    packed = packed + across(packed, 1)
    carried, value_a, value_b, value_x, value_y, query_sum, key_sum, packed, a_end, a_got = hold(
        carried, value_a, value_b, value_x, value_y, query_sum, key_sum, packed, a_end, a_got
    )

    query_x, key_y = across(query_sum[:, 1], 2), across(key_sum[1], 4)
    value_a, value_b = add(value_a[:, 0], value_x), add(value_b[0], value_y)
    value_x, value_y = across(value_b[1], 2), across(value_a[1], 4)
    a_low = add(a_end, a_got)
    a_got = mirrored(a_low, [(2, 1)])
    packed = packed + across(packed, 2)
    tokens_grad = tokens_back(
        rank, normed_grad, carried, tokens, residual_grad, scale_all, gain_attn, reps
    )
    query_sum, key_sum, query_x, key_y, value_a, value_b, value_x, value_y, packed, a_low, a_got = hold(
        query_sum, key_sum, query_x, key_y, value_a, value_b, value_x, value_y, packed, a_low, a_got
    )

    query_sum, key_sum = add(query_sum[:, 0], query_x), add(key_sum[0], key_y)
    query_y, key_x = across(query_sum[1], 4), across(key_sum[1], 2)
    value_total = ep_sum(jnp.stack([add(value_a[0], value_y), add(value_b[0], value_x)]))
    packed = packed + across(packed, 4)
    a_low = a_low.astype(f32) + a_got.astype(f32)
    a_got = mirrored(a_low.astype(bf16), [(1, 0)])
    query_sum, key_sum, query_y, key_x, packed, a_low, a_got = hold(
        query_sum, key_sum, query_y, key_x, packed, a_low, a_got
    )

    qk_total = ep_sum(jnp.stack([add(query_sum[0], query_y), add(key_sum[0], key_x)]))
    packed = jnp.sum(over_ep(packed, place), axis=0)
    b_total = b_end.astype(f32) + b_got.astype(f32) + b_got_2.astype(f32)
    mine = jnp.where(m == 0, a_low + a_got.astype(f32), b_total)

    def own_half(piece):
        return piece.reshape(2, 2, -1, piece.shape[2])

    tops, bottoms = own_half(mine[:, :quarter_rows]), own_half(mine[:, quarter_rows:])
    halves = jnp.concatenate([tops, bottoms], 2)
    other = across(pick(halves, 1 - core, 1), 1)
    mine = jnp.where(m < 2, pick(halves, core, 1), other)
    top = quarter_rows // 2
    down_out = jnp.concatenate([mine[0, top:], mine[1, top:]], 1)
    out_out = jnp.concatenate([out_total[0], out_total[1]], 1)
    value_out = jnp.concatenate([value_total[0], value_total[1]], 1)
    loss = packed[0, 0] / (2.0 * count * width)
    shares = lax.dynamic_slice_in_dim(
        packed, (rep * experts + shard) * shard_rows, shard_rows, 1
    )
    return (
        output,
        loss,
        tokens_grad,
        shares[1],
        shares[2],
        shares[3],
        shares[4],
        qk_total[0],
        qk_total[1],
        value_out,
        out_out,
        shares[5:].T,
        mine[0, :top][None],
        mine[1, :top][None],
        down_out[None],
    )


def solution(mesh):
    placed = (
        P(("rep", "ep"), None),
        P(("rep", "ep"), None),
        P("rep", "ep"),
        P("rep", "ep"),
        P(("rep", "ep"), None),
        P(("rep", "ep")),
        P(("rep", "ep")),
        P(("rep", "ep")),
        P(("rep", "ep")),
        P(("rep", "ep"), None),
        P(("rep", "ep"), None),
        P(("rep", "ep"), None),
        P(("rep", "ep"), None),
        P(("rep", "ep"), None),
        P("ep", None, None),
        P("ep", None, None),
        P("ep", None, None),
    )
    chips = mesh.shape["rep"] == 8 and mesh.shape["ep"] == 4
    return jax.shard_map(
        body if chips else body_plain,
        mesh=mesh,
        in_specs=placed,
        out_specs=(
            P(("rep", "ep"), None),
            P(),
            P(("rep", "ep"), None),
            P(("rep", "ep")),
            P(("rep", "ep")),
            P(("rep", "ep")),
            P(("rep", "ep")),
            P(("rep", "ep"), None),
            P(("rep", "ep"), None),
            P(("rep", "ep"), None),
            P(("rep", "ep"), None),
            P(("rep", "ep"), None),
            P("ep", "rep", None),
            P("ep", "rep", None),
            P("ep", "rep", None),
        ),
        check_vma=False,
    )
```

```python
import functools

import jax
import jax.numpy as jnp
from jax import lax
from jax.experimental import pallas as pl
from jax.experimental.pallas import tpu as pltpu
from jax.sharding import PartitionSpec as P

HEADS = 16
HEAD_DIM = 128
WINDOW = 1024
TOP = 2
VMEM_LIMIT = 56 * 1024 * 1024


norm_eps = 1e-05
highest = lax.Precision.HIGHEST


def from_behind(value, axis, steps):
    count = lax.axis_size(axis)
    leading, last = (max(0, -steps), min(count, count - steps))
    return lax.ppermute(value, axis, [(source, source + steps) for source in range(leading, last)])


def matmul(left, right):
    return jnp.dot(left, right, preferred_element_type=jnp.float32)


def rms_scale(value):
    return lax.rsqrt(jnp.mean(value * value, axis=-1, keepdims=True) + norm_eps)


def norm_back(value, scale, gain, grad):
    weighted = grad * gain
    inner = jnp.mean(weighted * value, axis=-1, keepdims=True)
    return (
        scale * weighted - value * (scale * scale * scale) * inner,
        jnp.sum(grad * value * scale, axis=0),
    )


def rounded(value):
    return lax.optimization_barrier(value.astype(jnp.bfloat16)).astype(jnp.float32)


def rotary_tables(positions, head_size):
    half = head_size // 2
    frequency = 10000.0 ** (-jnp.arange(half, dtype=jnp.float32) * 2.0 / head_size)
    angles = positions[:, None].astype(jnp.float32) * frequency[None, :]
    cosine = jnp.cos(angles)
    sine = jnp.sin(angles)
    return (
        jnp.concatenate([cosine, cosine], -1)[:, None, :],
        jnp.concatenate([sine, sine], -1)[:, None, :],
    )


def rotate(value, cosine, sine):
    half = value.shape[-1] // 2
    turned = jnp.concatenate([-value[..., half:], value[..., :half]], -1)
    return value * cosine + turned * sine


def rotate_back(grad, cosine, sine):
    half = grad.shape[-1] // 2
    scaled = grad * sine
    turned = jnp.concatenate([scaled[..., half:], -scaled[..., :half]], -1)
    return grad * cosine + turned


def unpack(everything):
    gains = [everything[index].astype(jnp.float32) for index in range(4)]
    return (gains, everything[4], everything[5], everything[6], everything[7], everything[8])


def body_plain(
    tokens,
    teacher,
    segment_ids,
    valid_mask,
    routes,
    attn_gain,
    q_gain,
    k_gain,
    moe_gain,
    w_query,
    w_key,
    w_value,
    w_out,
    w_router,
    w_gate,
    w_up,
    w_down,
):
    local_rows, width = tokens.shape
    experts = lax.axis_size("ep")
    pairs = local_rows * TOP
    capacity = 5 * pairs // (4 * experts)
    reach = min(-(-WINDOW // local_rows), experts - 1)
    group = min(HEADS, 4)
    score_scale = HEAD_DIM ** (-0.5)
    shard = lax.axis_index("ep")
    total_tokens = local_rows * lax.axis_size("rep") * experts
    everything = (
        lax.all_gather(attn_gain, ("rep", "ep"), axis=0, tiled=True),
        lax.all_gather(q_gain, ("rep", "ep"), axis=0, tiled=True),
        lax.all_gather(k_gain, ("rep", "ep"), axis=0, tiled=True),
        lax.all_gather(moe_gain, ("rep", "ep"), axis=0, tiled=True),
        lax.all_gather(w_query, ("rep", "ep"), axis=0, tiled=True),
        lax.all_gather(w_key, ("rep", "ep"), axis=0, tiled=True),
        lax.all_gather(w_value, ("rep", "ep"), axis=0, tiled=True),
        lax.all_gather(w_out, ("rep", "ep"), axis=0, tiled=True),
        lax.all_gather(w_router, ("rep", "ep"), axis=0, tiled=True),
    )
    gains, weight_query, weight_key, weight_value, weight_out, weight_router = unpack(everything)
    gain_attn, gain_query, gain_key, gain_moe = gains
    inputs = tokens.astype(jnp.float32)
    scale_attn = rms_scale(inputs)
    normed = (inputs * scale_attn * gain_attn).astype(jnp.bfloat16)
    query_lin = matmul(normed, weight_query)
    key_lin = matmul(normed, weight_key)
    value_rows = (
        matmul(normed, weight_value).astype(jnp.bfloat16).reshape(local_rows, HEADS, HEAD_DIM)
    )
    scale_query = rms_scale(query_lin)
    scale_key = rms_scale(key_lin)
    positions = shard * local_rows + jnp.arange(local_rows, dtype=jnp.int32)
    cosine, sine = rotary_tables(positions, HEAD_DIM)
    query_rows = rotate(
        (query_lin * scale_query * gain_query).reshape(local_rows, HEADS, HEAD_DIM), cosine, sine
    ).astype(jnp.bfloat16)
    key_rows = rotate(
        (key_lin * scale_key * gain_key).reshape(local_rows, HEADS, HEAD_DIM), cosine, sine
    ).astype(jnp.bfloat16)
    segments = segment_ids.reshape(local_rows)
    key_parts, value_parts, segment_parts = ([], [], [])
    for back in range(reach, 0, -1):
        moved = from_behind((key_rows, value_rows, segments.astype(jnp.bfloat16)), "ep", back)
        key_parts.append(moved[0])
        value_parts.append(moved[1])
        segment_parts.append(moved[2].astype(jnp.int32))
    all_keys = jnp.concatenate(key_parts + [key_rows], 0)
    all_values = jnp.concatenate(value_parts + [value_rows], 0)
    key_segments = jnp.concatenate(segment_parts + [segments], 0)
    key_positions = (shard - reach) * local_rows + jnp.arange(
        (reach + 1) * local_rows, dtype=jnp.int32
    )
    distance = positions[:, None] - key_positions[None, :]
    allowed = (
        (distance >= 0)
        & (distance < WINDOW)
        & (key_positions[None, :] >= 0)
        & (segments[:, None] == key_segments[None, :])
    )

    def by_group(value):
        return jnp.moveaxis(value.reshape(value.shape[0], HEADS // group, group, HEAD_DIM), 1, 0)

    def from_group(value):
        return jnp.moveaxis(value, 0, 1).reshape(value.shape[1], HEADS * HEAD_DIM)

    def scores_of(query_group, key_group):
        raw = (
            jnp.einsum("qhd,khd->hqk", query_group, key_group, preferred_element_type=jnp.float32)
            * score_scale
        )
        return jnp.where(allowed[None], raw, -1e30)

    def attend_forward(item):
        query_group, key_group, value_group = item
        scores = scores_of(query_group, key_group)
        peak = jnp.max(scores, axis=-1, keepdims=True)
        shifted = jnp.exp(scores - peak)
        total = jnp.sum(shifted, axis=-1, keepdims=True)
        weights = (shifted / total).astype(jnp.bfloat16)
        mixed = jnp.einsum("hqk,khd->qhd", weights, value_group, preferred_element_type=jnp.float32)
        return (mixed, peak, total)

    query_groups = by_group(query_rows)
    key_groups = by_group(all_keys)
    value_groups = by_group(all_values)
    mixed, peaks, totals = lax.map(attend_forward, (query_groups, key_groups, value_groups))
    mixed_rows = from_group(mixed).astype(jnp.bfloat16)
    residual = inputs + matmul(mixed_rows, weight_out)
    scale_moe = rms_scale(residual)
    normed_moe = (residual * scale_moe * gain_moe).astype(jnp.bfloat16)
    router_probs = jax.nn.softmax(matmul(normed_moe, weight_router), axis=-1)
    flat_routes = routes.reshape(pairs)
    choose = (flat_routes[:, None] == jnp.arange(experts, dtype=jnp.int32)[None, :]).astype(
        jnp.int32
    )
    rank = jnp.sum((jnp.cumsum(choose, axis=0) - choose) * choose, axis=1)
    slots = flat_routes * capacity + rank
    pair_source = (
        jnp.full((experts * capacity,), pairs, jnp.int32)
        .at[slots]
        .set(jnp.arange(pairs, dtype=jnp.int32))
    )
    token_source = jnp.where(pair_source < pairs, pair_source // TOP, local_rows)
    zero_row = jnp.zeros((1, width), jnp.bfloat16)
    outgoing = jnp.concatenate([normed_moe, zero_row], 0)[token_source].reshape(
        experts, capacity, width
    )
    choose_float = choose.reshape(local_rows, TOP, experts).astype(jnp.float32)
    gate_value = jnp.sum(choose_float * router_probs[:, None, :], axis=2)
    gate_weight = w_gate[0]
    up_weight = w_up[0]
    down_weight = w_down[0]
    piece = lax.all_to_all(outgoing, "ep", split_axis=0, concat_axis=0, tiled=True)
    flat = piece.reshape(-1, width)
    gate_pre = matmul(flat, gate_weight)
    up_pre = matmul(flat, up_weight)
    middle = (jax.nn.silu(gate_pre) * up_pre).astype(jnp.bfloat16)
    expert_out = matmul(middle, down_weight).astype(jnp.bfloat16)
    lead = piece.shape[:2]
    returned = expert_out.reshape(piece.shape)
    gate_kept = gate_pre.reshape(lead + (-1,))
    up_kept = up_pre.reshape(lead + (-1,))
    arrived = lax.all_to_all(returned, "ep", split_axis=0, concat_axis=0, tiled=True)
    expert_rows = arrived.reshape(experts * capacity, width)[slots].reshape(local_rows, TOP, width)
    result = residual + jnp.sum(gate_value[:, :, None] * expert_rows, axis=1)
    output = result.astype(jnp.bfloat16)
    valid = valid_mask.reshape(local_rows).astype(jnp.float32)
    error = result - teacher.astype(jnp.float32)
    squares = jnp.sum(valid * jnp.sum(error * error, axis=1))
    total_squares, count = lax.psum((squares, jnp.sum(valid)), ("rep", "ep"))
    loss = total_squares / (2.0 * count * width)
    result_grad = total_tokens / count * valid[:, None] * error
    gate_value_grad = jnp.sum(result_grad[:, None, :] * expert_rows, axis=2)
    pair_grad = (
        (gate_value[:, :, None] * result_grad[:, None, :])
        .astype(jnp.bfloat16)
        .reshape(pairs, width)
    )
    grad_outgoing = jnp.concatenate([pair_grad, zero_row], 0)[pair_source].reshape(
        experts, capacity, width
    )
    grad_in = lax.all_to_all(grad_outgoing, "ep", split_axis=0, concat_axis=0, tiled=True)
    rows_in = piece.reshape(-1, width)
    gate_pre = gate_kept.reshape(rows_in.shape[0], -1)
    up_pre = up_kept.reshape(rows_in.shape[0], -1)
    flat_grad = grad_in.reshape(-1, width)
    sigma = jax.nn.sigmoid(gate_pre)
    active = gate_pre * sigma
    middle = (active * up_pre).astype(jnp.bfloat16)
    down_local = matmul(middle.T, flat_grad)
    middle_grad = matmul(flat_grad, down_weight.T)
    gate_pre_grad = (middle_grad * up_pre * sigma * (1.0 + gate_pre * (1.0 - sigma))).astype(
        jnp.bfloat16
    )
    up_pre_grad = (middle_grad * active).astype(jnp.bfloat16)
    gate_local = matmul(rows_in.T, gate_pre_grad)
    up_local = matmul(rows_in.T, up_pre_grad)
    input_grad = (matmul(gate_pre_grad, gate_weight.T) + matmul(up_pre_grad, up_weight.T)).astype(
        jnp.bfloat16
    )
    back_rows = lax.all_to_all(
        input_grad.reshape(experts, capacity, width), "ep", split_axis=0, concat_axis=0, tiled=True
    )
    pair_back = back_rows.reshape(experts * capacity, width)[slots].reshape(local_rows, TOP, width)
    everything = (
        lax.all_gather(attn_gain, ("rep", "ep"), axis=0, tiled=True),
        lax.all_gather(q_gain, ("rep", "ep"), axis=0, tiled=True),
        lax.all_gather(k_gain, ("rep", "ep"), axis=0, tiled=True),
        lax.all_gather(moe_gain, ("rep", "ep"), axis=0, tiled=True),
        lax.all_gather(w_query, ("rep", "ep"), axis=0, tiled=True),
        lax.all_gather(w_key, ("rep", "ep"), axis=0, tiled=True),
        lax.all_gather(w_value, ("rep", "ep"), axis=0, tiled=True),
        lax.all_gather(w_out, ("rep", "ep"), axis=0, tiled=True),
        lax.all_gather(w_router, ("rep", "ep"), axis=0, tiled=True),
    )
    gains, weight_query, weight_key, weight_value, weight_out, weight_router = unpack(everything)
    gain_attn, gain_query, gain_key, gain_moe = gains
    prob_grad = jnp.sum(choose_float * gate_value_grad[:, :, None], axis=1)
    logit_grad = router_probs * (
        prob_grad - jnp.sum(prob_grad * router_probs, axis=-1, keepdims=True)
    )
    router_local = jnp.dot(
        normed_moe.T, logit_grad, precision=highest, preferred_element_type=jnp.float32
    )
    normed_moe_grad = jnp.sum(pair_back.astype(jnp.float32), axis=1) + jnp.dot(
        logit_grad, weight_router.T, precision=highest, preferred_element_type=jnp.float32
    )
    residual_part, moe_gain_local = norm_back(residual, scale_moe, gain_moe, normed_moe_grad)
    residual_grad = result_grad + residual_part
    branch_grad = residual_grad.astype(jnp.bfloat16)
    out_local = matmul(mixed_rows.T, branch_grad)
    mixed_grad = (
        matmul(branch_grad, weight_out.T).astype(jnp.bfloat16).reshape(local_rows, HEADS, HEAD_DIM)
    )

    def attend_backward(item):
        query_group, key_group, value_group, grad_group, peak, total = item
        scores = scores_of(query_group, key_group)
        probs = jnp.exp(scores - peak) / total
        weights = probs.astype(jnp.bfloat16)
        value_part = jnp.einsum(
            "hqk,qhd->khd", weights, grad_group, preferred_element_type=jnp.float32
        )
        probs_grad = jnp.einsum(
            "qhd,khd->hqk", grad_group, value_group, preferred_element_type=jnp.float32
        )
        inner = jnp.sum(probs * probs_grad, axis=-1, keepdims=True)
        score_grad = (probs * (probs_grad - inner)).astype(jnp.bfloat16)
        query_part = (
            jnp.einsum("hqk,khd->qhd", score_grad, key_group, preferred_element_type=jnp.float32)
            * score_scale
        )
        key_part = (
            jnp.einsum("hqk,qhd->khd", score_grad, query_group, preferred_element_type=jnp.float32)
            * score_scale
        )
        return (query_part, key_part, value_part)

    query_parts, key_parts_grad, value_parts_grad = lax.map(
        attend_backward,
        (query_groups, key_groups, value_groups, by_group(mixed_grad), peaks, totals),
    )
    query_row_grad = from_group(query_parts)
    key_all_grad = from_group(key_parts_grad)
    value_all_grad = from_group(value_parts_grad)
    own_keys = key_all_grad[reach * local_rows :]
    own_values = value_all_grad[reach * local_rows :]
    for back in range(1, reach + 1):
        start = (reach - back) * local_rows
        moved = from_behind(
            (key_all_grad[start : start + local_rows], value_all_grad[start : start + local_rows]),
            "ep",
            -back,
        )
        own_keys = own_keys + moved[0]
        own_values = own_values + moved[1]
    query_turned = rotate_back(
        rounded(query_row_grad).reshape(local_rows, HEADS, HEAD_DIM), cosine, sine
    ).reshape(local_rows, width)
    key_turned = rotate_back(
        rounded(own_keys).reshape(local_rows, HEADS, HEAD_DIM), cosine, sine
    ).reshape(local_rows, width)
    query_lin_grad, q_gain_local = norm_back(query_lin, scale_query, gain_query, query_turned)
    key_lin_grad, k_gain_local = norm_back(key_lin, scale_key, gain_key, key_turned)
    query_lin_grad = query_lin_grad.astype(jnp.bfloat16)
    key_lin_grad = key_lin_grad.astype(jnp.bfloat16)
    value_row_grad = own_values.astype(jnp.bfloat16)
    query_local = matmul(normed.T, query_lin_grad)
    key_local = matmul(normed.T, key_lin_grad)
    value_local = matmul(normed.T, value_row_grad)
    normed_grad = (
        matmul(query_lin_grad, weight_query.T)
        + matmul(key_lin_grad, weight_key.T)
        + matmul(value_row_grad, weight_value.T)
    )
    inputs_part, attn_gain_local = norm_back(inputs, scale_attn, gain_attn, normed_grad)
    tokens_grad = residual_grad + inputs_part
    summed = (
        lax.psum_scatter(attn_gain_local, ("rep", "ep"), scatter_dimension=0, tiled=True),
        lax.psum_scatter(q_gain_local, ("rep", "ep"), scatter_dimension=0, tiled=True),
        lax.psum_scatter(k_gain_local, ("rep", "ep"), scatter_dimension=0, tiled=True),
        lax.psum_scatter(moe_gain_local, ("rep", "ep"), scatter_dimension=0, tiled=True),
        lax.psum_scatter(query_local, ("rep", "ep"), scatter_dimension=0, tiled=True),
        lax.psum_scatter(key_local, ("rep", "ep"), scatter_dimension=0, tiled=True),
        lax.psum_scatter(value_local, ("rep", "ep"), scatter_dimension=0, tiled=True),
        lax.psum_scatter(out_local, ("rep", "ep"), scatter_dimension=0, tiled=True),
        lax.psum_scatter(router_local, ("rep", "ep"), scatter_dimension=0, tiled=True),
    )
    expert_summed = (
        lax.psum_scatter(gate_local[None], "rep", scatter_dimension=1, tiled=True),
        lax.psum_scatter(up_local[None], "rep", scatter_dimension=1, tiled=True),
        lax.psum_scatter(down_local[None], "rep", scatter_dimension=1, tiled=True),
    )
    return (
        output,
        loss,
        tokens_grad,
        summed[0],
        summed[1],
        summed[2],
        summed[3],
        summed[4],
        summed[5],
        summed[6],
        summed[7],
        summed[8],
        expert_summed[0],
        expert_summed[1],
        expert_summed[2],
    )


def dot_t(left, right):
    return lax.dot_general(left, right, (((1,), (1,)), ((), ())), preferred_element_type=jnp.float32)


def t_dot(left, right):
    return lax.dot_general(left, right, (((0,), (0,)), ((), ())), preferred_element_type=jnp.float32)


def kernel_call(kernel, **options):
    return pl.pallas_call(
        kernel,
        compiler_params=pltpu.CompilerParams(vmem_limit_bytes=VMEM_LIMIT),
        **options,
    )


def turn(value, cosine, sine):
    return value * cosine + pltpu.roll(value, HEAD_DIM // 2, 1) * sine


def code_of(place, blocks):
    return place % (blocks // 2) * 2 + place // (blocks // 2)


def place_of(code, blocks):
    return code % 2 * (blocks // 2) + code // 2


def norm_kernel(rank, x_ref, gain_ref, o_ref, scale_ref, *, codes):
    value = x_ref[...].astype(jnp.float32)
    scale = lax.rsqrt(jnp.mean(value * value, axis=1, keepdims=True) + norm_eps)
    scale_ref[...] = scale
    half = len(codes) // 2
    block = x_ref.shape[1] // len(codes)
    for place, code in enumerate(codes):
        start = pl.multiple_of((rank[0] ^ code) * block, block)
        piece = x_ref[:, pl.ds(start, block)].astype(jnp.float32)
        piece = piece * scale * gain_ref[:, pl.ds(start, block)]
        at = place % half * block
        o_ref[place // half, :, at : at + block] = piece.astype(jnp.bfloat16)


def norm_rows(rank, value, gain, codes):
    rows, width = value.shape
    tile = 256
    return kernel_call(
        functools.partial(norm_kernel, codes=codes),
        grid_spec=pltpu.PrefetchScalarGridSpec(
            num_scalar_prefetch=1,
            grid=(rows // tile,),
            in_specs=[
                pl.BlockSpec((tile, width), lambda i, rank: (i, 0)),
                pl.BlockSpec((1, width), lambda i, rank: (0, 0)),
            ],
            out_specs=[
                pl.BlockSpec((2, tile, width // 2), lambda i, rank: (0, i, 0)),
                pl.BlockSpec((tile, 1), lambda i, rank: (i, 0)),
            ],
        ),
        out_shape=[
            jax.ShapeDtypeStruct((2, rows, width // 2), jnp.bfloat16),
            jax.ShapeDtypeStruct((rows, 1), jnp.float32),
        ],
    )(rank, value, gain[None])


def project_kernel(low_ref, high_ref, a_ref, b_ref, o_ref, s_ref):
    total = matmul(low_ref[0], a_ref[...]) + matmul(high_ref[0], b_ref[...])
    o_ref[...] = total.astype(o_ref.dtype)
    s_ref[...] = jnp.sum(total * total, axis=1, keepdims=True)


def project(halves, a, b, dtype, start=0):
    _, rows, depth = halves.shape
    rows = rows - start
    width = a.shape[1]
    tile = 256
    first = start // tile
    weight = pl.BlockSpec((depth, width), lambda i: (0, 0))
    return kernel_call(
        project_kernel,
        grid=(rows // tile,),
        in_specs=[
            pl.BlockSpec((1, tile, depth), lambda i: (0, i + first, 0)),
            pl.BlockSpec((1, tile, depth), lambda i: (1, i + first, 0)),
            weight,
            weight,
        ],
        out_specs=[
            pl.BlockSpec((tile, width), lambda i: (i, 0)),
            pl.BlockSpec((tile, 1), lambda i: (i, 0)),
        ],
        out_shape=[
            jax.ShapeDtypeStruct((rows, width), dtype),
            jax.ShapeDtypeStruct((rows, 1), jnp.float32),
        ],
    )(halves, halves, a, b)


def project_back_kernel(k_ref, v_ref, w_ref, q_ref, ka, kb, va, vb, qa, qb, o_ref, *, tile):
    j = pl.program_id(0)
    half = pl.num_programs(0) // 2
    half_width = v_ref.shape[1]
    own = k_ref.shape[0] - q_ref.shape[0]

    def part(key, value, query):
        for start in range(0, k_ref.shape[0], tile):
            at = slice(start, start + tile)
            total = dot_t(k_ref[at, :], key[...]) + dot_t(v_ref[at, :], value[:, :half_width])
            total += dot_t(w_ref[at, :], value[:, half_width:])
            if start >= own:
                total += dot_t(q_ref[start - own : start - own + tile, :], query[...])
            o_ref[0, at, :] = total

    @pl.when(j < half)
    def _():
        part(ka, va, qa)

    @pl.when(j >= half)
    def _():
        part(kb, vb, qb)


def project_back(key, value, value_high, query, key_w, value_w, query_w):
    rows, width = key.shape
    depth = value_w[0].shape[0]
    step = 256
    half = depth // step
    whole = lambda value: pl.BlockSpec(value.shape, lambda j: (0, 0), pipeline_mode=pl.Buffered(1))
    low = pl.BlockSpec((step, width), lambda j: (jnp.minimum(j, half - 1), 0))
    high = pl.BlockSpec((step, width), lambda j: (jnp.maximum(j - half, 0), 0))
    return kernel_call(
        functools.partial(project_back_kernel, tile=512),
        grid=(2 * half,),
        in_specs=[whole(key), whole(value), whole(value_high), whole(query)] + [low, high] * 3,
        out_specs=pl.BlockSpec((1, rows, step), lambda j: (j // half, 0, j % half)),
        out_shape=jax.ShapeDtypeStruct((2, rows, depth), jnp.float32),
    )(key, value, value_high, query, *key_w, *value_w, *query_w)


def tokens_back_kernel(
    rank, g_ref, c_ref, x_ref, res_ref, scale_ref, gain_ref, o_ref, *, blocks
):
    scale = scale_ref[...]
    block = x_ref.shape[1] // blocks
    half = blocks // 2

    def pieces(place):
        start = pl.multiple_of((rank[0] ^ code_of(place, blocks)) * block, block)
        at = slice(place % half * block, place % half * block + block)
        grad = g_ref[place // half, :, at] + c_ref[place // half, :, at].astype(jnp.float32)
        columns = pl.ds(start, block)
        return columns, grad, x_ref[:, columns].astype(jnp.float32), gain_ref[:, columns]

    inner = jnp.zeros_like(scale)
    for place in range(blocks):
        columns, grad, value, gain = pieces(place)
        inner += jnp.sum(grad * value * gain, axis=1, keepdims=True)
    inner = inner * (1.0 / x_ref.shape[1]) * (scale * scale * scale)
    for place in range(blocks):
        columns, grad, value, gain = pieces(place)
        o_ref[:, columns] = res_ref[:, columns] + (scale * (grad * gain) - value * inner)


def tokens_back(rank, grad, carried, tokens, residual_grad, scale, gain, blocks):
    rows, width = tokens.shape
    tile = 128
    first = (grad.shape[1] - rows) // tile
    wide = pl.BlockSpec((tile, width), lambda i, rank: (i, 0))
    one = pl.BlockSpec((1, width), lambda i, rank: (0, 0))
    return kernel_call(
        functools.partial(tokens_back_kernel, blocks=blocks),
        grid_spec=pltpu.PrefetchScalarGridSpec(
            num_scalar_prefetch=1,
            grid=(rows // tile,),
            in_specs=[
                pl.BlockSpec((2, tile, width // 2), lambda i, rank: (0, i + first, 0)),
                pl.BlockSpec((2, tile, width // 2), lambda i, rank: (0, i, 0)),
                wide,
                wide,
                pl.BlockSpec((tile, 1), lambda i, rank: (i + first, 0)),
                one,
            ],
            out_specs=wide,
        ),
        out_shape=jax.ShapeDtypeStruct((rows, width), jnp.float32),
    )(rank, grad, carried, tokens, residual_grad, scale, gain[None])


def head_rows(lin, scale, gain, cosine, sine):
    return turn(lin * scale * gain, cosine, sine).astype(jnp.bfloat16)


def moved_head(head, rank):
    place = place_of((head // 2) ^ rank[0], HEADS // 2) * 2 + head % 2
    return place // (HEADS // 2), 0, place % (HEADS // 2)


def attention_specs(rows, all_rows, bias, first=0):
    head = lambda h, rank: (0, h + first)
    fixed = lambda h, rank: (0, 0)
    return [
        pl.BlockSpec((rows, HEAD_DIM), head),
        pl.BlockSpec((all_rows, HEAD_DIM), head),
        pl.BlockSpec((all_rows, HEAD_DIM), head),
        pl.BlockSpec((rows, 1), fixed),
        pl.BlockSpec((all_rows, 1), fixed),
        pl.BlockSpec((1, HEAD_DIM), head),
        pl.BlockSpec((1, HEAD_DIM), head),
        pl.BlockSpec((all_rows, HEAD_DIM), fixed),
        pl.BlockSpec((all_rows, HEAD_DIM), fixed),
        pl.BlockSpec(bias.shape, lambda h, rank: (0, 0, 0)),
    ]


def attend_kernel(
    rank,
    q_ref,
    k_ref,
    v_ref,
    sq_ref,
    sk_ref,
    gq_ref,
    gk_ref,
    cos_ref,
    sin_ref,
    bias_ref,
    *refs,
    behind,
    tile,
    span,
):
    o_ref, lse_ref = refs[-2:]
    rows = q_ref.shape[0]
    cosine, sine = cos_ref[...], sin_ref[...]
    keys = head_rows(k_ref[...], sk_ref[...], gk_ref[...], cosine, sine)
    queries = head_rows(q_ref[...], sq_ref[...], gq_ref[...], cosine[behind:], sine[behind:])
    for t in range(rows // tile):
        at = slice(t * tile, (t + 1) * tile)
        seen = slice(t * tile, t * tile + span)
        scores = dot_t(keys[seen], queries[at])
        scores = scores * HEAD_DIM ** (-0.5) + bias_ref[t].astype(jnp.float32)
        peak = jnp.max(scores, axis=0, keepdims=True)
        shifted = jnp.exp(scores - peak)
        total = jnp.sum(shifted, axis=0, keepdims=True)
        weights = (shifted * (1.0 / total)).astype(jnp.bfloat16)
        o_ref[0, at, :] = t_dot(weights, v_ref[seen, :]).astype(jnp.bfloat16)
        lse_ref[0, :, at] = peak + jnp.log(total)


def attend(rank, operands, bias, first, into=()):
    rows, width = operands[0].shape
    all_rows = operands[1].shape[0]
    tiles, span, tile = bias.shape
    return kernel_call(
        functools.partial(attend_kernel, behind=all_rows - rows, tile=tile, span=span),
        grid_spec=pltpu.PrefetchScalarGridSpec(
            num_scalar_prefetch=1,
            grid=(HEADS // 2,),
            in_specs=attention_specs(rows, all_rows, bias, first)
            + [pl.BlockSpec(memory_space=pl.ANY)] * len(into),
            out_specs=[
                pl.BlockSpec((1, rows, HEAD_DIM), lambda h, rank: moved_head(h + first, rank)),
                pl.BlockSpec((1, 1, rows), lambda h, rank: (h, 0, 0)),
            ],
        ),
        input_output_aliases={2 + len(operands): 0} if into else {},
        out_shape=[
            jax.ShapeDtypeStruct((2, rows, width // 2), jnp.bfloat16),
            jax.ShapeDtypeStruct((HEADS // 2, 1, rows), jnp.float32),
        ],
    )(rank, *operands, bias, *into)


def attend_back_kernel(
    rank,
    q_ref,
    k_ref,
    v_ref,
    sq_ref,
    sk_ref,
    gq_ref,
    gk_ref,
    cos_ref,
    sin_ref,
    bias_ref,
    g_ref,
    lse_ref,
    dq_ref,
    dk_ref,
    dv_ref,
    key_total,
    value_total,
    *,
    behind,
    tile,
    span,
):
    rows = q_ref.shape[0]
    score_scale = HEAD_DIM ** (-0.5)
    cosine, sine = cos_ref[...], sin_ref[...]
    keys = head_rows(k_ref[...], sk_ref[...], gk_ref[...], cosine, sine)
    queries = head_rows(q_ref[...], sq_ref[...], gq_ref[...], cosine[behind:], sine[behind:])
    key_total[...] = jnp.zeros_like(key_total)
    value_total[...] = jnp.zeros_like(value_total)
    for t in range(rows // tile):
        at = slice(t * tile, (t + 1) * tile)
        seen = slice(t * tile, t * tile + span)
        scores = dot_t(keys[seen], queries[at])
        scores = scores * score_scale + bias_ref[t].astype(jnp.float32)
        probs = jnp.exp(scores - lse_ref[0, :, at])
        grad = g_ref[0, at, :]
        value_total[seen, :] += matmul(probs.astype(jnp.bfloat16), grad)
        probs_grad = dot_t(v_ref[seen, :], grad)
        inner = jnp.sum(probs * probs_grad, axis=0, keepdims=True)
        score_grad = (probs * (probs_grad - inner)).astype(jnp.bfloat16)
        dq_ref[at, :] = (t_dot(score_grad, keys[seen]) * score_scale).astype(jnp.bfloat16)
        key_total[seen, :] += matmul(score_grad, queries[at])
    dk_ref[...] = (key_total[...] * score_scale).astype(jnp.bfloat16)
    dv_ref[...] = value_total[...].astype(jnp.bfloat16)


def attend_back(rank, operands, bias, grad, lse, first):
    rows, width = operands[0].shape
    width = width // 2
    all_rows = operands[1].shape[0]
    tiles, span, tile = bias.shape
    head = lambda h, rank: (0, h)
    return kernel_call(
        functools.partial(attend_back_kernel, behind=all_rows - rows, tile=tile, span=span),
        grid_spec=pltpu.PrefetchScalarGridSpec(
            num_scalar_prefetch=1,
            grid=(HEADS // 2,),
            in_specs=attention_specs(rows, all_rows, bias, first)
            + [
                pl.BlockSpec((1, rows, HEAD_DIM), lambda h, rank: moved_head(h + first, rank)),
                pl.BlockSpec((1, 1, rows), lambda h, rank: (h, 0, 0)),
            ],
            out_specs=[
                pl.BlockSpec((rows, HEAD_DIM), head),
                pl.BlockSpec((all_rows, HEAD_DIM), head),
                pl.BlockSpec((all_rows, HEAD_DIM), head),
            ],
            scratch_shapes=[
                pltpu.VMEM((all_rows, HEAD_DIM), jnp.float32),
                pltpu.VMEM((all_rows, HEAD_DIM), jnp.float32),
            ],
        ),
        out_shape=[
            jax.ShapeDtypeStruct((rows, width), jnp.bfloat16),
            jax.ShapeDtypeStruct((all_rows, width), jnp.bfloat16),
            jax.ShapeDtypeStruct((all_rows, width), jnp.bfloat16),
        ],
    )(rank, *operands, bias, grad, lse)


def lin_back_kernel(
    low_ref, high_ref, lin_ref, scale_ref, gain_ref, cos_ref, sin_ref, o_ref, gain_grad_ref, kept
):
    rows = scale_ref.shape[0]
    scale = jnp.broadcast_to(scale_ref[...], (rows, HEAD_DIM))
    cosine, sine = cos_ref[...], -sin_ref[...]

    @pl.when(pl.program_id(0) == 0)
    def _():
        gain_grad_ref[...] = jnp.zeros_like(gain_grad_ref)

    inner = jnp.zeros((rows, HEAD_DIM), jnp.float32)
    for h in range(HEADS):
        at = slice(h * HEAD_DIM, (h + 1) * HEAD_DIM)
        ref = low_ref if h < HEADS // 2 else high_ref
        here = slice(h % (HEADS // 2) * HEAD_DIM, (h % (HEADS // 2) + 1) * HEAD_DIM)
        grad = turn(ref[:, here].astype(jnp.float32), cosine, sine)
        product = grad * lin_ref[:, at]
        gain = gain_ref[:, at]
        gain_grad_ref[:, at] += jnp.sum(product * scale, axis=0, keepdims=True)
        inner += product * gain
        kept[:, at] = grad * gain * scale
    inner = jnp.sum(inner, axis=1, keepdims=True) * (1.0 / (HEADS * HEAD_DIM))
    inner = jnp.broadcast_to(inner, (rows, HEAD_DIM)) * (scale * scale * scale)
    for h in range(HEADS):
        at = slice(h * HEAD_DIM, (h + 1) * HEAD_DIM)
        o_ref[:, at] = (kept[:, at] - lin_ref[:, at] * inner).astype(jnp.bfloat16)


def lin_back(low, high, lin, scale, gain, cosine, sine):
    rows, width = lin.shape
    tile = 256
    wide = pl.BlockSpec((tile, width), lambda i: (i, 0))
    one = pl.BlockSpec((1, width), lambda i: (0, 0))
    half = pl.BlockSpec((tile, width // 2), lambda i: (i, 0))
    table = pl.BlockSpec((tile, HEAD_DIM), lambda i: (i, 0))
    return kernel_call(
        lin_back_kernel,
        grid=(rows // tile,),
        in_specs=[half, half, wide, pl.BlockSpec((tile, 1), lambda i: (i, 0)), one, table, table],
        out_specs=[wide, one],
        scratch_shapes=[pltpu.VMEM((tile, width), jnp.float32)],
        out_shape=[
            jax.ShapeDtypeStruct((rows, width), jnp.bfloat16),
            jax.ShapeDtypeStruct((1, width), jnp.float32),
        ],
    )(low, high, lin, scale, gain, cosine, sine)


def flat(ref):
    return ref[...].reshape(-1, ref.shape[-1])


def gu_spec(weights, rows):
    return pl.BlockSpec((2, rows, weights.shape[2]), lambda i, *_: (0, 0, 0))


def d_spec(weights, rows):
    last = weights.shape[1] // rows - 1
    return pl.BlockSpec((2, rows, weights.shape[2]), lambda i, *_: (0, last, 0))


def dynamic_block(index, block):
    return pl.ds(pl.multiple_of(index * block, block), block)


def experts_up_kernel(rank, x_ref, z_ref, ga, gb, ua, ub, g_ref, u_ref, my_ref, mx_ref, middle_ref):
    gate = matmul(x_ref[0], flat(ga)) + matmul(x_ref[1], flat(gb))
    up = matmul(z_ref[0], flat(ua)) + matmul(z_ref[1], flat(ub))
    g_ref[...] = gate
    u_ref[...] = up
    middle_ref[...] = (gate * jax.nn.sigmoid(gate) * up).astype(jnp.bfloat16)
    block = gate.shape[1] // 4
    for j in range(4):
        piece = middle_ref[:, dynamic_block(rank[0] ^ j, block)]
        dy, dx = j // 2, j % 2
        my_ref[dy, :, dx * block : (dx + 1) * block] = piece
        mx_ref[dx, :, dy * block : (dy + 1) * block] = piece


def experts_up(rank, by_y, by_x, weights):
    _, rows, depth = by_y.shape
    hidden = weights[0].shape[2]
    tile = 256
    x_spec = pl.BlockSpec((2, tile, depth), lambda i, rank: (0, i, 0))
    w_specs = [gu_spec(weight, depth // 2) for weight in weights]
    wide = pl.BlockSpec((tile, hidden), lambda i, rank: (i, 0))
    half = pl.BlockSpec((2, tile, hidden // 2), lambda i, rank: (0, i, 0))
    return kernel_call(
        experts_up_kernel,
        grid_spec=pltpu.PrefetchScalarGridSpec(
            num_scalar_prefetch=1,
            grid=(rows // tile,),
            in_specs=[x_spec, x_spec] + w_specs,
            out_specs=[wide, wide, half, half],
            scratch_shapes=[pltpu.VMEM((tile, hidden), jnp.bfloat16)],
        ),
        out_shape=[jax.ShapeDtypeStruct((rows, hidden), jnp.float32)] * 2
        + [jax.ShapeDtypeStruct((2, rows, hidden // 2), jnp.bfloat16)] * 2,
    )(rank, by_y, by_x, *weights)


def experts_down_kernel(*refs):
    gates, slots, outs = refs[:2], (refs[2:8], refs[8:14]), refs[14:]
    half = outs[0].shape[1] // 2
    mixtures = []
    for side in range(2):
        at = slice(side * half, (side + 1) * half)
        mixture = 0.0
        for slot, (my, mx, la, lb, ra, rb) in enumerate(slots):
            if side == 0:
                out = matmul(my[0], flat(la)) + matmul(my[1], flat(lb))
            else:
                out = matmul(mx[0], flat(ra)) + matmul(mx[1], flat(rb))
            out = out.astype(jnp.bfloat16)
            outs[slot][:, at] = out
            mixture += gates[slot][...] * out.astype(jnp.float32)
        mixtures.append(mixture)

    @pl.when(pl.program_id(0) < pl.num_programs(0) // 2)
    def _():
        outs[2][:, :half], outs[2][:, half:] = mixtures

    @pl.when(pl.program_id(0) >= pl.num_programs(0) // 2)
    def _():
        outs[3][:, :half], outs[3][:, half:] = mixtures


def experts_down(gates, slots):
    _, rows, depth = slots[0][0].shape
    half = slots[0][2].shape[2]
    tile = 256
    x_spec = pl.BlockSpec((2, tile, depth), lambda i: (0, i, 0))
    w_specs = [d_spec(weight, depth // 2) for weight in slots[0][2:]]
    wide = pl.BlockSpec((tile, 2 * half), lambda i: (i, 0))
    column = pl.BlockSpec((tile, 1), lambda i: (i, 0))
    steps = rows // tile // 2
    return kernel_call(
        experts_down_kernel,
        grid=(rows // tile,),
        in_specs=[column] * 2 + ([x_spec] * 2 + w_specs) * 2,
        out_specs=[
            wide,
            wide,
            pl.BlockSpec((tile, 2 * half), lambda i: (jnp.minimum(i, steps - 1), 0)),
            pl.BlockSpec((tile, 2 * half), lambda i: (jnp.maximum(i - steps, 0), 0)),
        ],
        out_shape=[
            jax.ShapeDtypeStruct((rows, 2 * half), jnp.bfloat16),
            jax.ShapeDtypeStruct((rows, 2 * half), jnp.bfloat16),
            jax.ShapeDtypeStruct((rows // 2, 2 * half), jnp.float32),
            jax.ShapeDtypeStruct((rows // 2, 2 * half), jnp.float32),
        ],
    )(*gates, *slots[0], *slots[1])


def experts_back_kernel(
    rank, own_ref, other_ref, out_ref, gate_ref, g_ref, u_ref, la, lb, ra, rb, p_ref, dg_ref, du_ref, gg_ref
):
    own = pl.program_id(0) < pl.num_programs(0) // 2
    grad = jnp.where(own, own_ref[...], other_ref[...])
    gg_ref[...] = jnp.sum(grad * out_ref[...].astype(jnp.float32), axis=1, keepdims=True)
    p_ref[...] = (gate_ref[...] * grad).astype(jnp.bfloat16)
    half = grad.shape[1] // 2
    left, right = p_ref[:, :half], p_ref[:, half:]
    block = la.shape[1]
    for j in range(4):
        dy, dx = j // 2, j % 2
        left_w = (la, lb)[dy][dx]
        right_w = (ra, rb)[dx][dy]
        middle_grad = dot_t(left, left_w) + dot_t(right, right_w)
        at = dynamic_block(rank[0] ^ j, block)
        gate_pre, up_pre = g_ref[:, at], u_ref[:, at]
        sigma = jax.nn.sigmoid(gate_pre)
        change = middle_grad * up_pre * sigma * (1.0 + gate_pre * (1.0 - sigma))
        dg_ref[:, at] = change.astype(jnp.bfloat16)
        du_ref[:, at] = (middle_grad * (gate_pre * sigma)).astype(jnp.bfloat16)


def experts_back(rank, own, other, out, gate, gate_pre, up_pre, weights):
    rows, width = out.shape
    hidden = gate_pre.shape[1]
    tile = 256
    wide = pl.BlockSpec((tile, width), lambda i, rank: (i, 0))
    narrow = pl.BlockSpec((tile, hidden), lambda i, rank: (i, 0))
    column = pl.BlockSpec((tile, 1), lambda i, rank: (i, 0))
    w_specs = [d_spec(weight, hidden // 4) for weight in weights]
    steps = rows // tile // 2
    return kernel_call(
        experts_back_kernel,
        grid_spec=pltpu.PrefetchScalarGridSpec(
            num_scalar_prefetch=1,
            grid=(rows // tile,),
            in_specs=[
                pl.BlockSpec((tile, width), lambda i, rank: (jnp.minimum(i, steps - 1), 0)),
                pl.BlockSpec((tile, width), lambda i, rank: (jnp.maximum(i - steps, 0), 0)),
                wide, column, narrow, narrow
            ] + w_specs,
            out_specs=[wide, narrow, narrow, column],
        ),
        out_shape=[
            jax.ShapeDtypeStruct((rows, width), jnp.bfloat16),
            jax.ShapeDtypeStruct((rows, hidden), jnp.bfloat16),
            jax.ShapeDtypeStruct((rows, hidden), jnp.bfloat16),
            jax.ShapeDtypeStruct((rows, 1), jnp.float32),
        ],
    )(rank, own, other, out, gate, gate_pre, up_pre, *weights)


def experts_input_kernel(*refs):
    totals = []
    for j in range(4):
        dy, dx = j // 2, j % 2
        total = 0.0
        for dg, du, ga, gb, ua, ub in (refs[:6], refs[6:12]):
            gate_w = (ga, gb)[dy][dx]
            up_w = (ua, ub)[dx][dy]
            part = dot_t(dg[...], gate_w) + dot_t(du[...], up_w)
            total += part.astype(jnp.bfloat16).astype(jnp.float32)
        totals.append(total)

    @pl.when(pl.program_id(0) < pl.num_programs(0) // 2)
    def _():
        for j in range(4):
            refs[-2][j] = totals[j]

    @pl.when(pl.program_id(0) >= pl.num_programs(0) // 2)
    def _():
        for j in range(4):
            refs[-1][j] = totals[j]


def experts_input(slots):
    rows, hidden = slots[0][0].shape
    depth = slots[0][2].shape[1] // 3 * 2
    tile = 256
    narrow = pl.BlockSpec((tile, hidden), lambda i: (i, 0))
    w_specs = [gu_spec(weight, depth) for weight in slots[0][2:]]
    steps = rows // tile // 2
    return kernel_call(
        experts_input_kernel,
        grid=(rows // tile,),
        in_specs=([narrow] * 2 + w_specs) * 2,
        out_specs=[
            pl.BlockSpec((4, tile, depth), lambda i: (0, jnp.minimum(i, steps - 1), 0)),
            pl.BlockSpec((4, tile, depth), lambda i: (0, jnp.maximum(i - steps, 0), 0)),
        ],
        out_shape=[jax.ShapeDtypeStruct((4, rows // 2, depth), jnp.float32)] * 2,
    )(*slots[0], *slots[1])


def residual_back_kernel(
    rank, a_ref, b_ref, lg_ref, wr_ref, x_ref, r_ref, scale_ref, gain_ref, o_ref, c_ref, gg_ref
):
    scale = scale_ref[...]
    block = a_ref.shape[2]

    @pl.when(pl.program_id(0) == 0)
    def _():
        gg_ref[...] = jnp.zeros_like(gg_ref)

    inner = jnp.zeros_like(scale)
    for j in range(4):
        at = dynamic_block(rank[0] ^ j, block)
        grad = a_ref[j] + b_ref[j]
        for e in range(wr_ref.shape[0]):
            grad += lg_ref[:, e : e + 1] * wr_ref[e : e + 1, at]
        o_ref[:, at] = grad
        product = grad * x_ref[:, at]
        inner += jnp.sum(product * gain_ref[:, at], axis=1, keepdims=True)
        gg_ref[:, at] += jnp.sum(product * scale, axis=0, keepdims=True)
    inner = inner * (1.0 / x_ref.shape[1]) * (scale * scale * scale)
    for j in range(4):
        at = slice(j * block, (j + 1) * block)
        value = scale * (o_ref[:, at] * gain_ref[:, at]) - x_ref[:, at] * inner
        value = r_ref[:, at] + value
        o_ref[:, at] = value
        c_ref[:, at] = value.astype(jnp.bfloat16)


def residual_back(rank, own, other, logit_grad, router, residual, result_grad, scale, gain):
    rows, width = residual.shape
    tile = 128
    wide = pl.BlockSpec((tile, width), lambda i, rank: (i, 0))
    piece = pl.BlockSpec((4, tile, width // 4), lambda i, rank: (0, i, 0))
    one = pl.BlockSpec((1, width), lambda i, rank: (0, 0))
    experts = logit_grad.shape[1]
    return kernel_call(
        residual_back_kernel,
        grid_spec=pltpu.PrefetchScalarGridSpec(
            num_scalar_prefetch=1,
            grid=(rows // tile,),
            in_specs=[
                piece,
                piece,
                pl.BlockSpec((tile, experts), lambda i, rank: (i, 0)),
                pl.BlockSpec((experts, width), lambda i, rank: (0, 0)),
                wide,
                wide,
                pl.BlockSpec((tile, 1), lambda i, rank: (i, 0)),
                one,
            ],
            out_specs=[wide, wide, one],
        ),
        out_shape=[
            jax.ShapeDtypeStruct((rows, width), jnp.float32),
            jax.ShapeDtypeStruct((rows, width), jnp.bfloat16),
            jax.ShapeDtypeStruct((1, width), jnp.float32),
        ],
    )(rank, own, other, logit_grad, router, residual, result_grad, scale, gain[None])


def experts_grad_kernel(x_ref, d_ref, m_ref, p_ref, *refs):
    o_ref = refs[-1]
    rows, down_rows = x_ref.shape[2], m_ref.shape[2]
    top, bottom = t_dot(x_ref[0], d_ref[...]), t_dot(m_ref[0], p_ref[...])
    if len(refs) == 2:
        top += refs[0][0, :rows].astype(jnp.float32)
        bottom += refs[0][0, rows:].astype(jnp.float32)
    o_ref[0, :rows] = top.astype(jnp.bfloat16)
    o_ref[0, rows:] = bottom.astype(jnp.bfloat16)


def experts_grad(inputs, pre_grad, middle, pair, part, side, got=()):
    _, rows, depth = inputs.shape
    hidden, down = pre_grad.shape[1], middle.shape[2]
    piece = pl.BlockSpec((1, (depth + down) // 2, hidden), lambda q: (q, 0, 0))
    return kernel_call(
        experts_grad_kernel,
        grid=(2,),
        in_specs=[
            pl.BlockSpec((1, rows, depth // 2), lambda q: (part, 0, q)),
            pl.BlockSpec((rows, hidden), lambda q: (0, 0)),
            pl.BlockSpec((1, rows, down // 2), lambda q: (part, 0, q)),
            pl.BlockSpec((rows, hidden), lambda q: (0, side)),
        ]
        + [piece] * len(got),
        out_specs=piece,
        out_shape=jax.ShapeDtypeStruct((2, (depth + down) // 2, hidden), jnp.bfloat16),
    )(inputs, pre_grad, middle, pair, *got)


def chip_grad_kernel(x_ref, *refs, count):
    o_ref = refs[-1]
    width = o_ref.shape[1] // count
    for i in range(count):
        at = slice(i * width, (i + 1) * width)
        total = t_dot(x_ref[0], refs[i][...])
        if len(refs) > count + 1:
            total += refs[count][:, at].astype(jnp.float32)
        o_ref[:, at] = total.astype(jnp.bfloat16)


def chip_grad(halves, part, grads, start=0, got=()):
    depth = halves.shape[2]
    rows = grads[0].shape[0]
    width = sum(grad.shape[1] for grad in grads)
    tile = 256
    piece = pl.BlockSpec((tile, width), lambda i: (i, 0))
    return kernel_call(
        functools.partial(chip_grad_kernel, count=len(grads)),
        grid=(depth // tile,),
        in_specs=[pl.BlockSpec((1, rows, tile), lambda i: (part, start // rows, i))]
        + [pl.BlockSpec(grad.shape, lambda i: (0, 0)) for grad in grads]
        + [piece] * len(got),
        out_specs=piece,
        out_shape=jax.ShapeDtypeStruct((depth, width), jnp.bfloat16),
    )(halves, *grads, *got)


def mixed_back_kernel(g_ref, a_ref, b_ref, o_ref):
    for half, ref in enumerate((a_ref, b_ref)):
        o_ref[half] = dot_t(g_ref[...], ref[...]).astype(jnp.bfloat16)


def mixed_back(grad, weights):
    rows, width = grad.shape
    depth = weights[0].shape[0]
    step = 256
    weight = pl.BlockSpec((step, width), lambda j: (j, 0))
    return kernel_call(
        mixed_back_kernel,
        grid=(depth // step,),
        in_specs=[pl.BlockSpec((rows, width), lambda j: (0, 0)), weight, weight],
        out_specs=pl.BlockSpec((2, rows, step), lambda j: (0, 0, j)),
        out_shape=jax.ShapeDtypeStruct((2, rows, depth), jnp.bfloat16),
    )(grad, *weights)


def across(value, bit):
    count = lax.axis_size("rep")
    return lax.ppermute(value, "rep", [(place, place ^ bit) for place in range(count)])


def along(value, steps):
    count = lax.axis_size("ep")
    return lax.ppermute(value, "ep", [(place, (place + steps) % count) for place in range(count)])


def mirrored(value, moves):
    reps, count = lax.axis_size("rep"), lax.axis_size("ep")
    pairs = []
    for rep in range(reps):
        for source, target in moves:
            if rep % 2:
                source, target = count - 1 - source, count - 1 - target
            pairs.append((rep * count + source, rep * count + target))
    return lax.ppermute(value, ("rep", "ep"), pairs)


def pick(value, index, axis):
    return lax.dynamic_index_in_dim(value, index, axis, keepdims=False)


def in_order(own, other, bit, axis):
    return jnp.where(bit == 1, jnp.stack([other, own], axis), jnp.stack([own, other], axis))


def over_ep(value, place):
    shard = place[3]
    experts = lax.axis_size("ep")
    parts = jnp.zeros((experts,) + value.shape, value.dtype)
    parts = lax.dynamic_update_index_in_dim(parts, value, shard, 0)
    for steps in range(1, experts):
        parts = lax.dynamic_update_index_in_dim(
            parts, along(value, steps), lax.rem(shard - steps + experts, experts), 0
        )
    return parts


def hold(*values):
    return lax.optimization_barrier(values)


def both_ways(value):
    return across(value[0], 2), across(value[1], 4)


def other_ways(first, second):
    return across(first, 4), across(second, 2)


def add(left, right):
    return (left.astype(jnp.float32) + right.astype(jnp.float32)).astype(jnp.bfloat16)


def ep_sum(both):
    return lax.psum_scatter(both, "ep", scatter_dimension=1, tiled=True).astype(jnp.float32)


def body(
    tokens,
    teacher,
    segment_ids,
    valid_mask,
    routes,
    attn_gain,
    q_gain,
    k_gain,
    moe_gain,
    w_query,
    w_key,
    w_value,
    w_out,
    w_router,
    w_gate,
    w_up,
    w_down,
):
    bf16, f32 = jnp.bfloat16, jnp.float32
    local_rows, width = tokens.shape
    experts = lax.axis_size("ep")
    reps = lax.axis_size("rep")
    reach = min(-(-WINDOW // local_rows), experts - 1)
    shard = lax.axis_index("ep")
    rep = lax.axis_index("rep")
    place = (rep // 4, rep // 2 % 2, rep % 2, shard)
    core = rep % 2
    total_tokens = local_rows * reps * experts

    valid = valid_mask.reshape(local_rows).astype(f32)
    own_count = jnp.sum(valid_mask)
    counts = jnp.stack([own_count // 16, own_count % 16]).astype(bf16)
    small = jnp.concatenate(
        [
            jnp.stack([attn_gain, q_gain, k_gain, moe_gain], 1),
            w_router,
            jnp.broadcast_to(counts[None], (attn_gain.shape[0], 2)),
        ],
        1,
    )
    rank = rep.astype(jnp.int32)[None]
    quarter = rep // 2
    quarter_rank = quarter.astype(jnp.int32)[None]
    order = tuple(code_of(j, reps) for j in range(reps))
    half = width // 2
    behind = reach * local_rows
    all_rows = local_rows + behind
    m = jnp.where(core == 0, shard, experts - 1 - shard)
    quarter_rows = w_gate.shape[1] // 4
    quarter_down = w_down.shape[1] // 4

    def own_part(weight, rows):
        return lax.dynamic_slice_in_dim(weight[0], quarter * rows, rows, 0)

    down = own_part(w_down, quarter_down)
    own = jnp.stack(
        [
            jnp.concatenate([own_part(w_gate, quarter_rows), down[:, :half]], 0),
            jnp.concatenate([own_part(w_up, quarter_rows), down[:, half:]], 0),
        ]
    )
    segments = segment_ids.reshape(local_rows)
    shard_rows = w_key.shape[0]
    columns = small.shape[1]
    small = small.T

    small = over_ep(small, place)
    parts = over_ep(jnp.stack([w_key, w_value]), place)
    segments_1 = from_behind(segments, "ep", 1)
    parts, small, own, tokens_1, segments_1 = hold(parts, small, own, tokens, segments_1)
    qo = jnp.stack([w_query, w_out])

    qo, parts = hold(qo, parts)
    qo = lax.all_gather(qo, "ep", axis=0)
    block = shard_rows * experts
    k_w, v_w = parts[:, 0].reshape(block, width), parts[:, 1].reshape(block, width)
    e_1 = mirrored(own, [(0, 1), (1, 2)])
    small = small.reshape(-1)
    small = jnp.pad(small, (0, 16 * width - small.shape[0])).reshape(16, width)
    k_w = jnp.concatenate([k_w, small], 0)
    k_x, v_y = both_ways((k_w, v_w))
    segments_2 = from_behind(segments_1, "ep", 1)
    k_w, k_x, v_w, v_y, tokens_1, segments_2 = hold(k_w, k_x, v_w, v_y, tokens_1, segments_2)

    k_w = jnp.stack([k_w, k_x])
    k_y, v_x = other_ways(k_w, jnp.stack([v_w, v_y]))
    tokens_1 = from_behind(tokens_1, "ep", 1)
    qo, k_w, k_y, v_w, v_y, v_x, tokens_1 = hold(qo, k_w, k_y, v_w, v_y, v_x, tokens_1)

    small = jnp.concatenate([k_w[:, block : block + 2], k_y[:, block : block + 2]], 0)
    small = jnp.pad(small.reshape(-1, width), ((0, 8), (0, 0)))
    k_w = jnp.concatenate([k_w[0, :block], k_w[1, :block], k_y[0, :block], k_y[1, :block], small], 0)
    v_w = jnp.concatenate([v_w, v_x[0], v_y, v_x[1]], 0)
    key_w, value_w = (k_w, across(k_w, 1)), (v_w, across(v_w, 1))
    q_w, o_w = qo[:, 0].reshape(-1, width), qo[:, 1].reshape(-1, width)
    q_x, o_y = both_ways((q_w, o_w))
    tokens_2 = from_behind(tokens_1, "ep", 1)
    key_w, value_w, q_w, q_x, o_w, o_y, tokens_2, tokens_1, e_1, own = hold(
        key_w, value_w, q_w, q_x, o_w, o_y, tokens_2, tokens_1, e_1, own
    )

    q_w = jnp.concatenate([q_w, q_x], 0)
    q_y, o_x = other_ways(q_w, jnp.stack([o_w, o_y]))
    q_w = jnp.concatenate([q_w, q_y], 0)
    o_w = jnp.concatenate([o_w, o_x[0], o_y, o_x[1]], 0)
    e_2 = mirrored(jnp.where(m == 2, e_1, own), [(1, 0), (2, 3)])
    small = jnp.stack([weight[4 * block : 4 * block + 8] for weight in key_w])
    small = small.reshape(2, 2, 2, -1)[..., : experts * columns * shard_rows]
    for axis, bit in enumerate((core, place[0], place[1])):
        small = jnp.where(bit == 1, jnp.flip(small, axis), small)
    small = small.reshape(2, 2, 2, experts, columns, shard_rows)
    small = jnp.transpose(small, (4, 1, 2, 0, 3, 5)).reshape(columns, -1)
    gain_attn, gain_query, gain_key, gain_moe = [small[i].astype(f32) for i in range(4)]
    weight_router = small[4 : 4 + experts].T
    counts = small[4 + experts :, ::shard_rows].astype(f32)
    count = jnp.sum(counts[0]) * 16.0 + jnp.sum(counts[1])
    tokens_all = jnp.concatenate([tokens_2, tokens_1, tokens], 0)
    key_segments = jnp.concatenate([segments_2, segments_1, segments], 0)
    normed, scale_all = norm_rows(rank, tokens_all, gain_attn, order)
    key_lin, key_squares = project(normed, *key_w, f32)
    value_all, _ = project(normed, *value_w, bf16)
    q_w, o_w, e_2, e_1, own, normed, key_lin, value_all = hold(
        q_w, o_w, e_2, e_1, own, normed, key_lin, value_all
    )

    query_w, out_w = (q_w, across(q_w, 1)), (o_w, across(o_w, 1))
    e_b = jnp.where(m == 1, own, jnp.where(m == 2, e_1, e_2))
    b_x, b_y = both_ways(e_b)
    e_3 = mirrored(e_1, [(1, 2)])
    query_lin, query_squares = project(normed, *query_w, f32, behind)
    scale_key = lax.rsqrt(key_squares / width + norm_eps)
    scale_query = lax.rsqrt(query_squares / width + norm_eps)
    key_positions = (shard - reach) * local_rows + jnp.arange(all_rows, dtype=jnp.int32)
    half_head = HEAD_DIM // 2
    frequency = 10000.0 ** (-jnp.arange(half_head, dtype=f32) * 2.0 / HEAD_DIM)
    angles = key_positions[:, None].astype(f32) * frequency[None, :]
    cosine, sine = jnp.cos(angles), jnp.sin(angles)
    cosine, sine = jnp.concatenate([cosine, cosine], 1), jnp.concatenate([-sine, sine], 1)

    def mask_of(tile):
        span = behind + tile
        parts = []
        for start in range(0, local_rows, tile):
            keys = slice(start, start + span)
            queries = slice(behind + start, behind + start + tile)
            distance = key_positions[None, queries] - key_positions[keys, None]
            allowed = (
                (distance >= 0)
                & (distance < WINDOW)
                & (key_positions[keys, None] >= 0)
                & (key_segments[None, queries] == key_segments[keys, None])
            )
            parts.append(jnp.where(allowed, 0.0, -1e30).astype(f32))
        return jnp.stack(parts)

    operands = (
        query_lin,
        key_lin,
        value_all,
        scale_query,
        scale_key,
        gain_query[None],
        gain_key[None],
        cosine,
        sine,
    )
    bias_small = mask_of(local_rows // 4)
    mixed, lse_0 = attend(rank, operands, bias_small, 0)
    mixed, out_w, e_b, b_x, b_y, e_3, e_1, own = hold(mixed, out_w, e_b, b_x, b_y, e_3, e_1, own)

    b_0, b_1 = jnp.stack([e_b[0], b_x]), jnp.stack([e_b[1], b_y])
    b_2, b_3 = other_ways(b_0[:, :quarter_rows], b_1[:, :quarter_rows])
    e_4 = mirrored(e_3, [(2, 3)])
    mixed, lse_1 = attend(rank, operands, bias_small, HEADS // 2, (mixed,))
    branch, _ = project(mixed, *out_w, f32)
    residual = tokens.astype(f32) + branch
    moe, scale_moe = norm_rows(quarter_rank, residual, gain_moe, (0, 1, 2, 3))
    moe_y = jnp.concatenate([moe, across(moe, 1)], 1)
    piece = half // 2
    moe_x = jnp.stack(
        [
            jnp.concatenate([moe_y[0, :, i : i + piece], moe_y[1, :, i : i + piece]], 1)
            for i in (0, piece)
        ]
    )
    router_parts = weight_router.reshape(4, -1, experts)
    router_rel = jnp.concatenate([pick(router_parts, quarter ^ j, 0) for j in range(4)], 0)
    router_probs = jax.nn.softmax(
        matmul(moe[0], router_rel[:half]) + matmul(moe[1], router_rel[half:]), axis=-1
    )
    chosen = jnp.sum(
        (routes[:, :, None] == jnp.arange(experts, dtype=jnp.int32)).astype(f32), axis=1
    )
    gates = router_probs * chosen
    gates_both = jnp.concatenate([gates, across(gates, 1)], 0)
    gates_a = jnp.where(core == 0, gates_both[:, :1], gates_both[:, -1:])
    gates_b = jnp.where(core == 0, gates_both[:, 1:2], gates_both[:, -2:-1])
    b_0, b_1, b_2, b_3, e_4, e_3, e_1, own, moe_y, moe_x = hold(
        b_0, b_1, b_2, b_3, e_4, e_3, e_1, own, moe_y, moe_x
    )

    e_a = jnp.where(m == 0, own, jnp.where(m == 1, e_1, jnp.where(m == 2, e_3, e_4)))
    a_x, a_y = both_ways(e_a)
    b_4, b_5 = other_ways(b_0[:, quarter_rows:], b_1[:, quarter_rows:])
    up_weights_b, down_weights_b = (b_0, b_2, b_1, b_3), (b_0, b_4, b_1, b_5)
    gate_pre_b, up_pre_b, my_b, mx_b = experts_up(quarter_rank, moe_y, moe_x, up_weights_b)
    e_a, a_x, a_y, my_b, mx_b, moe_y, moe_x = hold(e_a, a_x, a_y, my_b, mx_b, moe_y, moe_x)

    a_0, a_1 = jnp.stack([e_a[0], a_x]), jnp.stack([e_a[1], a_y])
    a_2, a_3 = other_ways(a_0[:, :quarter_rows], a_1[:, :quarter_rows])
    a_0, a_1, a_2, a_3 = hold(a_0, a_1, a_2, a_3)

    a_4, a_5 = other_ways(a_0[:, quarter_rows:], a_1[:, quarter_rows:])
    up_weights_a, down_weights_a = (a_0, a_2, a_1, a_3), (a_0, a_4, a_1, a_5)
    gate_pre_a, up_pre_a, my_a, mx_a = experts_up(quarter_rank, moe_y, moe_x, up_weights_a)
    expert_out_a, expert_out_b, mixture, mixture_other = experts_down(
        (gates_a, gates_b), ((my_a, mx_a) + down_weights_a, (my_b, mx_b) + down_weights_b)
    )
    result = residual + (mixture + across(mixture_other, 1))
    output = result.astype(bf16)
    error = result - teacher.astype(f32)
    squares = jnp.sum(valid * jnp.sum(error * error, axis=1))
    result_grad = total_tokens / count * valid[:, None] * error
    result_other = across(result_grad, 1)

    pair_b, dg_b, du_b, gate_grad_b = experts_back(
        quarter_rank,
        result_grad,
        result_other,
        expert_out_b,
        gates_b,
        gate_pre_b,
        up_pre_b,
        down_weights_b,
    )
    sent_x = experts_grad(moe_x, dg_b, mx_b, pair_b, 1, 0)
    sent_y = experts_grad(moe_y, du_b, my_b, pair_b, 1, 1)
    sent_x, sent_y, expert_out_a = hold(sent_x, sent_y, expert_out_a)

    b_x, b_y = both_ways((sent_x, sent_y))
    pair_a, dg_a, du_a, gate_grad_a = experts_back(
        quarter_rank,
        result_grad,
        result_other,
        expert_out_a,
        gates_a,
        gate_pre_a,
        up_pre_a,
        down_weights_a,
    )
    sent_x = experts_grad(moe_x, dg_a, mx_a, pair_a, 1, 0)
    sent_y = experts_grad(moe_y, du_a, my_a, pair_a, 1, 1)
    input_grad, input_other = experts_input(
        ((dg_a, du_a) + up_weights_a, (dg_b, du_b) + up_weights_b)
    )
    slot_grads = jnp.concatenate([gate_grad_a, gate_grad_b], 1)
    own_slots, partner_slots = slot_grads[:local_rows], across(slot_grads[local_rows:], 1)
    from_low = jnp.where(core == 0, own_slots, partner_slots)
    from_high = jnp.where(core == 0, partner_slots, own_slots)
    prob_grad = chosen * jnp.concatenate([from_low, from_high[:, ::-1]], 1)
    logit_grad = router_probs * (
        prob_grad - jnp.sum(prob_grad * router_probs, axis=-1, keepdims=True)
    )
    b_x, b_y, sent_x, sent_y, input_grad, input_other, logit_grad = hold(
        b_x, b_y, sent_x, sent_y, input_grad, input_other, logit_grad
    )

    input_other = across(input_other, 1)
    a_x, a_y = both_ways((sent_x, sent_y))
    b_0 = experts_grad(moe_x, dg_b, mx_b, pair_b, 0, 0, (b_x,))
    b_1 = experts_grad(moe_y, du_b, my_b, pair_b, 0, 1, (b_y,))
    router_local = jnp.concatenate(
        [
            jnp.dot(part.T.astype(f32), logit_grad, precision=highest, preferred_element_type=f32)
            for part in (moe[0], moe[1])
        ],
        0,
    )
    router_local = router_local.reshape(4, -1, experts)
    router_local = jnp.concatenate([pick(router_local, quarter ^ j, 0) for j in range(4)], 0)
    residual_grad, branch_grad, moe_gain_local = residual_back(
        quarter_rank,
        input_grad,
        input_other,
        logit_grad,
        weight_router.astype(f32).T,
        residual,
        result_grad,
        scale_moe,
        gain_moe,
    )
    out_sent = across(chip_grad(mixed, 1, (branch_grad,)), 1)
    out_sum = chip_grad(mixed, 0, (branch_grad,), 0, (out_sent,)).reshape(2, 2, -1, width)
    mixed_grad = mixed_back(branch_grad, out_w)
    b_0, b_1, out_sum, mixed_grad, branch_grad = hold(b_0, b_1, out_sum, mixed_grad, branch_grad)

    b_y, b_x = other_ways(b_0[1], b_1[1])
    out_x, out_y = across(out_sum[:, 1, :, :half], 2), across(out_sum[1, :, :, half:], 4)
    bias = mask_of(local_rows // 2)
    dq_0, dk_0, dv_0 = attend_back(rank, operands, bias, mixed_grad, lse_0, 0)
    dq_1, dk_1, dv_1 = attend_back(rank, operands, bias, mixed_grad, lse_1, HEADS // 2)
    a_x, a_y, b_0, b_1, b_x, b_y, out_sum, out_x, out_y, dq_0, dk_0, dv_0, dq_1, dk_1, dv_1 = hold(
        a_x, a_y, b_0, b_1, b_x, b_y, out_sum, out_x, out_y, dq_0, dk_0, dv_0, dq_1, dk_1, dv_1
    )

    a_0 = experts_grad(moe_x, dg_a, mx_a, pair_a, 0, 0, (a_x,))
    a_1 = experts_grad(moe_y, du_a, my_a, pair_a, 0, 1, (a_y,))
    a_y, a_x = other_ways(a_0[1], a_1[1])
    out_a, out_b = add(out_sum[:, 0, :, :half], out_x), add(out_sum[0, :, :, half:], out_y)
    out_x, out_y = across(out_b[1], 2), across(out_a[1], 4)
    b_end = jnp.stack([add(b_0[0], b_y), add(b_1[0], b_x)])
    b_got = mirrored(b_end, [(3, 2), (0, 1)])
    value_sent = chip_grad(normed, 1, (dv_0, dv_1))
    value_got = across(value_sent, 1)
    value_sum = chip_grad(normed, 0, (dv_0, dv_1), 0, (value_got,)).reshape(2, 2, -1, width)
    value_x = across(value_sum[:, 1, :, :half], 2)
    value_y = across(value_sum[1, :, :, half:], 4)
    query_lin_grad, q_gain_local = lin_back(
        dq_0, dq_1, query_lin, scale_query, gain_query[None], cosine[behind:], sine[behind:]
    )
    key_lin_grad, k_gain_local = lin_back(
        dk_0, dk_1, key_lin, scale_key, gain_key[None], cosine, sine
    )
    query_sent = chip_grad(normed, 1, (query_lin_grad,), behind)
    key_sent = chip_grad(normed, 1, (key_lin_grad,))
    packed = jnp.concatenate(
        [
            jnp.broadcast_to(squares, (1, width)),
            q_gain_local,
            k_gain_local,
            moe_gain_local,
            router_local.T,
        ],
        0,
    )
    (
        a_0, a_1, a_x, a_y, out_a, out_b, out_x, out_y, b_end, b_got, query_lin_grad, key_lin_grad,
        value_sum, value_x, value_y, query_sent, key_sent, packed,
    ) = hold(
        a_0, a_1, a_x, a_y, out_a, out_b, out_x, out_y, b_end, b_got, query_lin_grad, key_lin_grad,
        value_sum, value_x, value_y, query_sent, key_sent, packed,
    )

    query_got, key_got = across(query_sent, 1), across(key_sent, 1)
    value_a = add(value_sum[:, 0, :, :half], value_x)
    value_b = add(value_sum[0, :, :, half:], value_y)
    for link in (1, 2, 4):
        packed = packed + across(packed, link)
    value_a, value_b, packed = hold(value_a, value_b, packed)
    value_x, value_y = across(value_b[1], 2), across(value_a[1], 4)
    out_total = ep_sum(jnp.stack([add(out_a[0], out_y), add(out_b[0], out_x)]))
    b_low = add(b_end, b_got)
    b_got_2 = mirrored(b_low, [(2, 1)])
    a_end = jnp.stack([add(a_0[0], a_y), add(a_1[0], a_x)])
    a_got = mirrored(a_end, [(3, 2)])
    normed_grad = project_back(
        key_lin_grad, dv_0, dv_1, query_lin_grad, key_w, value_w, query_w
    )
    query_sum = chip_grad(normed, 0, (query_lin_grad,), behind, (query_got,))
    key_sum = chip_grad(normed, 0, (key_lin_grad,), 0, (key_got,))
    (
        normed_grad, query_sum, key_sum, value_a, value_b, value_x, value_y, b_got_2, a_end, a_got,
        packed,
    ) = hold(
        normed_grad, query_sum, key_sum, value_a, value_b, value_x, value_y, b_got_2, a_end, a_got,
        packed,
    )

    query_sum = query_sum.reshape(2, 2, -1, width)
    key_sum = key_sum.reshape(2, 2, -1, width)
    query_x, key_y = across(query_sum[:, 1], 2), across(key_sum[1], 4)
    carried = from_behind(normed_grad[:, :local_rows].astype(bf16), "ep", -1)
    a_low = add(a_end, a_got)
    a_got = mirrored(a_low, [(2, 1)])
    value_total = ep_sum(jnp.stack([add(value_a[0], value_y), add(value_b[0], value_x)]))
    b_total = (b_end.astype(f32) + b_got.astype(f32) + b_got_2.astype(f32)).astype(bf16)
    query_sum, key_sum, query_x, key_y, carried, a_low, a_got, packed, b_total = hold(
        query_sum, key_sum, query_x, key_y, carried, a_low, a_got, packed, b_total
    )

    query_sum, key_sum = add(query_sum[:, 0], query_x), add(key_sum[0], key_y)
    query_y, key_x = across(query_sum[1], 4), across(key_sum[1], 2)
    for back in range(1, reach):
        here = normed_grad[:, back * local_rows : (back + 1) * local_rows] + carried.astype(f32)
        carried = from_behind(here.astype(bf16), "ep", -1)
    a_low = add(a_low, a_got)
    a_got = mirrored(a_low, [(1, 0)])
    query_sum, key_sum, query_y, key_x, carried, packed, a_low, a_got = hold(
        query_sum, key_sum, query_y, key_x, carried, packed, a_low, a_got
    )

    qk_total = ep_sum(jnp.stack([add(query_sum[0], query_y), add(key_sum[0], key_x)]))
    packed = jnp.sum(over_ep(packed, place), axis=0)
    tokens_grad = tokens_back(
        rank, normed_grad, carried, tokens, residual_grad, scale_all, gain_attn, reps
    )
    mine = jnp.where(m == 0, add(a_low, a_got), b_total)

    def own_half(piece):
        return piece.reshape(2, 2, -1, piece.shape[2])

    tops, bottoms = own_half(mine[:, :quarter_rows]), own_half(mine[:, quarter_rows:])
    halves = jnp.concatenate([tops, bottoms], 2)
    other = across(pick(halves, 1 - core, 1), 1)
    mine = jnp.where(m < 2, pick(halves, core, 1), other).astype(f32)
    top = quarter_rows // 2
    down_out = jnp.concatenate([mine[0, top:], mine[1, top:]], 1)
    out_out = jnp.concatenate([out_total[0], out_total[1]], 1)
    value_out = jnp.concatenate([value_total[0], value_total[1]], 1)
    loss = packed[0, 0] / (2.0 * count * width)
    attn_gain_out = (
        jnp.sum(w_query.astype(f32) * qk_total[0], axis=1)
        + jnp.sum(w_key.astype(f32) * qk_total[1], axis=1)
        + jnp.sum(w_value.astype(f32) * value_out, axis=1)
    ) / attn_gain.astype(f32)
    shares = lax.dynamic_slice_in_dim(
        packed, (rep * experts + shard) * shard_rows, shard_rows, 1
    )
    return (
        output,
        loss,
        tokens_grad,
        attn_gain_out,
        shares[1],
        shares[2],
        shares[3],
        qk_total[0],
        qk_total[1],
        value_out,
        out_out,
        shares[4:].T,
        mine[0, :top][None],
        mine[1, :top][None],
        down_out[None],
    )


def solution(mesh):
    placed = (
        P(("rep", "ep"), None),
        P(("rep", "ep"), None),
        P("rep", "ep"),
        P("rep", "ep"),
        P(("rep", "ep"), None),
        P(("rep", "ep")),
        P(("rep", "ep")),
        P(("rep", "ep")),
        P(("rep", "ep")),
        P(("rep", "ep"), None),
        P(("rep", "ep"), None),
        P(("rep", "ep"), None),
        P(("rep", "ep"), None),
        P(("rep", "ep"), None),
        P("ep", None, None),
        P("ep", None, None),
        P("ep", None, None),
    )
    chips = mesh.shape["rep"] == 8 and mesh.shape["ep"] == 4
    return jax.shard_map(
        body if chips else body_plain,
        mesh=mesh,
        in_specs=placed,
        out_specs=(
            P(("rep", "ep"), None),
            P(),
            P(("rep", "ep"), None),
            P(("rep", "ep")),
            P(("rep", "ep")),
            P(("rep", "ep")),
            P(("rep", "ep")),
            P(("rep", "ep"), None),
            P(("rep", "ep"), None),
            P(("rep", "ep"), None),
            P(("rep", "ep"), None),
            P(("rep", "ep"), None),
            P("ep", "rep", None),
            P("ep", "rep", None),
            P("ep", "rep", None),
        ),
        check_vma=False,
    )
```

```python
import functools

import jax
import jax.numpy as jnp
from jax import lax
from jax.experimental import pallas as pl
from jax.experimental.pallas import tpu as pltpu
from jax.sharding import PartitionSpec as P

HEADS = 16
HEAD_DIM = 128
WINDOW = 1024
TOP = 2
VMEM_LIMIT = 56 * 1024 * 1024


norm_eps = 1e-05
highest = lax.Precision.HIGHEST


def from_behind(value, axis, steps):
    count = lax.axis_size(axis)
    leading, last = (max(0, -steps), min(count, count - steps))
    return lax.ppermute(value, axis, [(source, source + steps) for source in range(leading, last)])


def matmul(left, right):
    return jnp.dot(left, right, preferred_element_type=jnp.float32)


def rms_scale(value):
    return lax.rsqrt(jnp.mean(value * value, axis=-1, keepdims=True) + norm_eps)


def norm_back(value, scale, gain, grad):
    weighted = grad * gain
    inner = jnp.mean(weighted * value, axis=-1, keepdims=True)
    return (
        scale * weighted - value * (scale * scale * scale) * inner,
        jnp.sum(grad * value * scale, axis=0),
    )


def rounded(value):
    return lax.optimization_barrier(value.astype(jnp.bfloat16)).astype(jnp.float32)


def rotary_tables(positions, head_size):
    half = head_size // 2
    frequency = 10000.0 ** (-jnp.arange(half, dtype=jnp.float32) * 2.0 / head_size)
    angles = positions[:, None].astype(jnp.float32) * frequency[None, :]
    cosine = jnp.cos(angles)
    sine = jnp.sin(angles)
    return (
        jnp.concatenate([cosine, cosine], -1)[:, None, :],
        jnp.concatenate([sine, sine], -1)[:, None, :],
    )


def rotate(value, cosine, sine):
    half = value.shape[-1] // 2
    turned = jnp.concatenate([-value[..., half:], value[..., :half]], -1)
    return value * cosine + turned * sine


def rotate_back(grad, cosine, sine):
    half = grad.shape[-1] // 2
    scaled = grad * sine
    turned = jnp.concatenate([scaled[..., half:], -scaled[..., :half]], -1)
    return grad * cosine + turned


def unpack(everything):
    gains = [everything[index].astype(jnp.float32) for index in range(4)]
    return (gains, everything[4], everything[5], everything[6], everything[7], everything[8])


def body_plain(
    tokens,
    teacher,
    segment_ids,
    valid_mask,
    routes,
    attn_gain,
    q_gain,
    k_gain,
    moe_gain,
    w_query,
    w_key,
    w_value,
    w_out,
    w_router,
    w_gate,
    w_up,
    w_down,
):
    local_rows, width = tokens.shape
    experts = lax.axis_size("ep")
    pairs = local_rows * TOP
    capacity = 5 * pairs // (4 * experts)
    reach = min(-(-WINDOW // local_rows), experts - 1)
    group = min(HEADS, 4)
    score_scale = HEAD_DIM ** (-0.5)
    shard = lax.axis_index("ep")
    total_tokens = local_rows * lax.axis_size("rep") * experts
    everything = (
        lax.all_gather(attn_gain, ("rep", "ep"), axis=0, tiled=True),
        lax.all_gather(q_gain, ("rep", "ep"), axis=0, tiled=True),
        lax.all_gather(k_gain, ("rep", "ep"), axis=0, tiled=True),
        lax.all_gather(moe_gain, ("rep", "ep"), axis=0, tiled=True),
        lax.all_gather(w_query, ("rep", "ep"), axis=0, tiled=True),
        lax.all_gather(w_key, ("rep", "ep"), axis=0, tiled=True),
        lax.all_gather(w_value, ("rep", "ep"), axis=0, tiled=True),
        lax.all_gather(w_out, ("rep", "ep"), axis=0, tiled=True),
        lax.all_gather(w_router, ("rep", "ep"), axis=0, tiled=True),
    )
    gains, weight_query, weight_key, weight_value, weight_out, weight_router = unpack(everything)
    gain_attn, gain_query, gain_key, gain_moe = gains
    inputs = tokens.astype(jnp.float32)
    scale_attn = rms_scale(inputs)
    normed = (inputs * scale_attn * gain_attn).astype(jnp.bfloat16)
    query_lin = matmul(normed, weight_query)
    key_lin = matmul(normed, weight_key)
    value_rows = (
        matmul(normed, weight_value).astype(jnp.bfloat16).reshape(local_rows, HEADS, HEAD_DIM)
    )
    scale_query = rms_scale(query_lin)
    scale_key = rms_scale(key_lin)
    positions = shard * local_rows + jnp.arange(local_rows, dtype=jnp.int32)
    cosine, sine = rotary_tables(positions, HEAD_DIM)
    query_rows = rotate(
        (query_lin * scale_query * gain_query).reshape(local_rows, HEADS, HEAD_DIM), cosine, sine
    ).astype(jnp.bfloat16)
    key_rows = rotate(
        (key_lin * scale_key * gain_key).reshape(local_rows, HEADS, HEAD_DIM), cosine, sine
    ).astype(jnp.bfloat16)
    segments = segment_ids.reshape(local_rows)
    key_parts, value_parts, segment_parts = ([], [], [])
    for back in range(reach, 0, -1):
        moved = from_behind((key_rows, value_rows, segments.astype(jnp.bfloat16)), "ep", back)
        key_parts.append(moved[0])
        value_parts.append(moved[1])
        segment_parts.append(moved[2].astype(jnp.int32))
    all_keys = jnp.concatenate(key_parts + [key_rows], 0)
    all_values = jnp.concatenate(value_parts + [value_rows], 0)
    key_segments = jnp.concatenate(segment_parts + [segments], 0)
    key_positions = (shard - reach) * local_rows + jnp.arange(
        (reach + 1) * local_rows, dtype=jnp.int32
    )
    distance = positions[:, None] - key_positions[None, :]
    allowed = (
        (distance >= 0)
        & (distance < WINDOW)
        & (key_positions[None, :] >= 0)
        & (segments[:, None] == key_segments[None, :])
    )

    def by_group(value):
        return jnp.moveaxis(value.reshape(value.shape[0], HEADS // group, group, HEAD_DIM), 1, 0)

    def from_group(value):
        return jnp.moveaxis(value, 0, 1).reshape(value.shape[1], HEADS * HEAD_DIM)

    def scores_of(query_group, key_group):
        raw = (
            jnp.einsum("qhd,khd->hqk", query_group, key_group, preferred_element_type=jnp.float32)
            * score_scale
        )
        return jnp.where(allowed[None], raw, -1e30)

    def attend_forward(item):
        query_group, key_group, value_group = item
        scores = scores_of(query_group, key_group)
        peak = jnp.max(scores, axis=-1, keepdims=True)
        shifted = jnp.exp(scores - peak)
        total = jnp.sum(shifted, axis=-1, keepdims=True)
        weights = (shifted / total).astype(jnp.bfloat16)
        mixed = jnp.einsum("hqk,khd->qhd", weights, value_group, preferred_element_type=jnp.float32)
        return (mixed, peak, total)

    query_groups = by_group(query_rows)
    key_groups = by_group(all_keys)
    value_groups = by_group(all_values)
    mixed, peaks, totals = lax.map(attend_forward, (query_groups, key_groups, value_groups))
    mixed_rows = from_group(mixed).astype(jnp.bfloat16)
    residual = inputs + matmul(mixed_rows, weight_out)
    scale_moe = rms_scale(residual)
    normed_moe = (residual * scale_moe * gain_moe).astype(jnp.bfloat16)
    router_probs = jax.nn.softmax(matmul(normed_moe, weight_router), axis=-1)
    flat_routes = routes.reshape(pairs)
    choose = (flat_routes[:, None] == jnp.arange(experts, dtype=jnp.int32)[None, :]).astype(
        jnp.int32
    )
    rank = jnp.sum((jnp.cumsum(choose, axis=0) - choose) * choose, axis=1)
    slots = flat_routes * capacity + rank
    pair_source = (
        jnp.full((experts * capacity,), pairs, jnp.int32)
        .at[slots]
        .set(jnp.arange(pairs, dtype=jnp.int32))
    )
    token_source = jnp.where(pair_source < pairs, pair_source // TOP, local_rows)
    zero_row = jnp.zeros((1, width), jnp.bfloat16)
    outgoing = jnp.concatenate([normed_moe, zero_row], 0)[token_source].reshape(
        experts, capacity, width
    )
    choose_float = choose.reshape(local_rows, TOP, experts).astype(jnp.float32)
    gate_value = jnp.sum(choose_float * router_probs[:, None, :], axis=2)
    gate_weight = w_gate[0]
    up_weight = w_up[0]
    down_weight = w_down[0]
    piece = lax.all_to_all(outgoing, "ep", split_axis=0, concat_axis=0, tiled=True)
    flat = piece.reshape(-1, width)
    gate_pre = matmul(flat, gate_weight)
    up_pre = matmul(flat, up_weight)
    middle = (jax.nn.silu(gate_pre) * up_pre).astype(jnp.bfloat16)
    expert_out = matmul(middle, down_weight).astype(jnp.bfloat16)
    lead = piece.shape[:2]
    returned = expert_out.reshape(piece.shape)
    gate_kept = gate_pre.reshape(lead + (-1,))
    up_kept = up_pre.reshape(lead + (-1,))
    arrived = lax.all_to_all(returned, "ep", split_axis=0, concat_axis=0, tiled=True)
    expert_rows = arrived.reshape(experts * capacity, width)[slots].reshape(local_rows, TOP, width)
    result = residual + jnp.sum(gate_value[:, :, None] * expert_rows, axis=1)
    output = result.astype(jnp.bfloat16)
    valid = valid_mask.reshape(local_rows).astype(jnp.float32)
    error = result - teacher.astype(jnp.float32)
    squares = jnp.sum(valid * jnp.sum(error * error, axis=1))
    total_squares, count = lax.psum((squares, jnp.sum(valid)), ("rep", "ep"))
    loss = total_squares / (2.0 * count * width)
    result_grad = total_tokens / count * valid[:, None] * error
    gate_value_grad = jnp.sum(result_grad[:, None, :] * expert_rows, axis=2)
    pair_grad = (
        (gate_value[:, :, None] * result_grad[:, None, :])
        .astype(jnp.bfloat16)
        .reshape(pairs, width)
    )
    grad_outgoing = jnp.concatenate([pair_grad, zero_row], 0)[pair_source].reshape(
        experts, capacity, width
    )
    grad_in = lax.all_to_all(grad_outgoing, "ep", split_axis=0, concat_axis=0, tiled=True)
    rows_in = piece.reshape(-1, width)
    gate_pre = gate_kept.reshape(rows_in.shape[0], -1)
    up_pre = up_kept.reshape(rows_in.shape[0], -1)
    flat_grad = grad_in.reshape(-1, width)
    sigma = jax.nn.sigmoid(gate_pre)
    active = gate_pre * sigma
    middle = (active * up_pre).astype(jnp.bfloat16)
    down_local = matmul(middle.T, flat_grad)
    middle_grad = matmul(flat_grad, down_weight.T)
    gate_pre_grad = (middle_grad * up_pre * sigma * (1.0 + gate_pre * (1.0 - sigma))).astype(
        jnp.bfloat16
    )
    up_pre_grad = (middle_grad * active).astype(jnp.bfloat16)
    gate_local = matmul(rows_in.T, gate_pre_grad)
    up_local = matmul(rows_in.T, up_pre_grad)
    input_grad = (matmul(gate_pre_grad, gate_weight.T) + matmul(up_pre_grad, up_weight.T)).astype(
        jnp.bfloat16
    )
    back_rows = lax.all_to_all(
        input_grad.reshape(experts, capacity, width), "ep", split_axis=0, concat_axis=0, tiled=True
    )
    pair_back = back_rows.reshape(experts * capacity, width)[slots].reshape(local_rows, TOP, width)
    everything = (
        lax.all_gather(attn_gain, ("rep", "ep"), axis=0, tiled=True),
        lax.all_gather(q_gain, ("rep", "ep"), axis=0, tiled=True),
        lax.all_gather(k_gain, ("rep", "ep"), axis=0, tiled=True),
        lax.all_gather(moe_gain, ("rep", "ep"), axis=0, tiled=True),
        lax.all_gather(w_query, ("rep", "ep"), axis=0, tiled=True),
        lax.all_gather(w_key, ("rep", "ep"), axis=0, tiled=True),
        lax.all_gather(w_value, ("rep", "ep"), axis=0, tiled=True),
        lax.all_gather(w_out, ("rep", "ep"), axis=0, tiled=True),
        lax.all_gather(w_router, ("rep", "ep"), axis=0, tiled=True),
    )
    gains, weight_query, weight_key, weight_value, weight_out, weight_router = unpack(everything)
    gain_attn, gain_query, gain_key, gain_moe = gains
    prob_grad = jnp.sum(choose_float * gate_value_grad[:, :, None], axis=1)
    logit_grad = router_probs * (
        prob_grad - jnp.sum(prob_grad * router_probs, axis=-1, keepdims=True)
    )
    router_local = jnp.dot(
        normed_moe.T, logit_grad, precision=highest, preferred_element_type=jnp.float32
    )
    normed_moe_grad = jnp.sum(pair_back.astype(jnp.float32), axis=1) + jnp.dot(
        logit_grad, weight_router.T, precision=highest, preferred_element_type=jnp.float32
    )
    residual_part, moe_gain_local = norm_back(residual, scale_moe, gain_moe, normed_moe_grad)
    residual_grad = result_grad + residual_part
    branch_grad = residual_grad.astype(jnp.bfloat16)
    out_local = matmul(mixed_rows.T, branch_grad)
    mixed_grad = (
        matmul(branch_grad, weight_out.T).astype(jnp.bfloat16).reshape(local_rows, HEADS, HEAD_DIM)
    )

    def attend_backward(item):
        query_group, key_group, value_group, grad_group, peak, total = item
        scores = scores_of(query_group, key_group)
        probs = jnp.exp(scores - peak) / total
        weights = probs.astype(jnp.bfloat16)
        value_part = jnp.einsum(
            "hqk,qhd->khd", weights, grad_group, preferred_element_type=jnp.float32
        )
        probs_grad = jnp.einsum(
            "qhd,khd->hqk", grad_group, value_group, preferred_element_type=jnp.float32
        )
        inner = jnp.sum(probs * probs_grad, axis=-1, keepdims=True)
        score_grad = (probs * (probs_grad - inner)).astype(jnp.bfloat16)
        query_part = (
            jnp.einsum("hqk,khd->qhd", score_grad, key_group, preferred_element_type=jnp.float32)
            * score_scale
        )
        key_part = (
            jnp.einsum("hqk,qhd->khd", score_grad, query_group, preferred_element_type=jnp.float32)
            * score_scale
        )
        return (query_part, key_part, value_part)

    query_parts, key_parts_grad, value_parts_grad = lax.map(
        attend_backward,
        (query_groups, key_groups, value_groups, by_group(mixed_grad), peaks, totals),
    )
    query_row_grad = from_group(query_parts)
    key_all_grad = from_group(key_parts_grad)
    value_all_grad = from_group(value_parts_grad)
    own_keys = key_all_grad[reach * local_rows :]
    own_values = value_all_grad[reach * local_rows :]
    for back in range(1, reach + 1):
        start = (reach - back) * local_rows
        moved = from_behind(
            (key_all_grad[start : start + local_rows], value_all_grad[start : start + local_rows]),
            "ep",
            -back,
        )
        own_keys = own_keys + moved[0]
        own_values = own_values + moved[1]
    query_turned = rotate_back(
        rounded(query_row_grad).reshape(local_rows, HEADS, HEAD_DIM), cosine, sine
    ).reshape(local_rows, width)
    key_turned = rotate_back(
        rounded(own_keys).reshape(local_rows, HEADS, HEAD_DIM), cosine, sine
    ).reshape(local_rows, width)
    query_lin_grad, q_gain_local = norm_back(query_lin, scale_query, gain_query, query_turned)
    key_lin_grad, k_gain_local = norm_back(key_lin, scale_key, gain_key, key_turned)
    query_lin_grad = query_lin_grad.astype(jnp.bfloat16)
    key_lin_grad = key_lin_grad.astype(jnp.bfloat16)
    value_row_grad = own_values.astype(jnp.bfloat16)
    query_local = matmul(normed.T, query_lin_grad)
    key_local = matmul(normed.T, key_lin_grad)
    value_local = matmul(normed.T, value_row_grad)
    normed_grad = (
        matmul(query_lin_grad, weight_query.T)
        + matmul(key_lin_grad, weight_key.T)
        + matmul(value_row_grad, weight_value.T)
    )
    inputs_part, attn_gain_local = norm_back(inputs, scale_attn, gain_attn, normed_grad)
    tokens_grad = residual_grad + inputs_part
    summed = (
        lax.psum_scatter(attn_gain_local, ("rep", "ep"), scatter_dimension=0, tiled=True),
        lax.psum_scatter(q_gain_local, ("rep", "ep"), scatter_dimension=0, tiled=True),
        lax.psum_scatter(k_gain_local, ("rep", "ep"), scatter_dimension=0, tiled=True),
        lax.psum_scatter(moe_gain_local, ("rep", "ep"), scatter_dimension=0, tiled=True),
        lax.psum_scatter(query_local, ("rep", "ep"), scatter_dimension=0, tiled=True),
        lax.psum_scatter(key_local, ("rep", "ep"), scatter_dimension=0, tiled=True),
        lax.psum_scatter(value_local, ("rep", "ep"), scatter_dimension=0, tiled=True),
        lax.psum_scatter(out_local, ("rep", "ep"), scatter_dimension=0, tiled=True),
        lax.psum_scatter(router_local, ("rep", "ep"), scatter_dimension=0, tiled=True),
    )
    expert_summed = (
        lax.psum_scatter(gate_local[None], "rep", scatter_dimension=1, tiled=True),
        lax.psum_scatter(up_local[None], "rep", scatter_dimension=1, tiled=True),
        lax.psum_scatter(down_local[None], "rep", scatter_dimension=1, tiled=True),
    )
    return (
        output,
        loss,
        tokens_grad,
        summed[0],
        summed[1],
        summed[2],
        summed[3],
        summed[4],
        summed[5],
        summed[6],
        summed[7],
        summed[8],
        expert_summed[0],
        expert_summed[1],
        expert_summed[2],
    )


def dot_t(left, right):
    return lax.dot_general(left, right, (((1,), (1,)), ((), ())), preferred_element_type=jnp.float32)


def t_dot(left, right):
    return lax.dot_general(left, right, (((0,), (0,)), ((), ())), preferred_element_type=jnp.float32)


def kernel_call(kernel, **options):
    return pl.pallas_call(
        kernel,
        compiler_params=pltpu.CompilerParams(vmem_limit_bytes=VMEM_LIMIT),
        **options,
    )


def turn(value, cosine, sine):
    return value * cosine + pltpu.roll(value, HEAD_DIM // 2, 1) * sine


def code_of(place, blocks):
    return place % (blocks // 2) * 2 + place // (blocks // 2)


def place_of(code, blocks):
    return code % 2 * (blocks // 2) + code // 2


def norm_kernel(rank, x_ref, gain_ref, o_ref, scale_ref, *, codes):
    value = x_ref[...].astype(jnp.float32)
    scale = lax.rsqrt(jnp.mean(value * value, axis=1, keepdims=True) + norm_eps)
    scale_ref[...] = scale
    half = len(codes) // 2
    block = x_ref.shape[1] // len(codes)
    for place, code in enumerate(codes):
        start = pl.multiple_of((rank[0] ^ code) * block, block)
        piece = x_ref[:, pl.ds(start, block)].astype(jnp.float32)
        piece = piece * scale * gain_ref[:, pl.ds(start, block)]
        at = place % half * block
        o_ref[place // half, :, at : at + block] = piece.astype(jnp.bfloat16)


def norm_rows(rank, value, gain, codes):
    rows, width = value.shape
    tile = 256
    return kernel_call(
        functools.partial(norm_kernel, codes=codes),
        grid_spec=pltpu.PrefetchScalarGridSpec(
            num_scalar_prefetch=1,
            grid=(rows // tile,),
            in_specs=[
                pl.BlockSpec((tile, width), lambda i, rank: (i, 0)),
                pl.BlockSpec((1, width), lambda i, rank: (0, 0)),
            ],
            out_specs=[
                pl.BlockSpec((2, tile, width // 2), lambda i, rank: (0, i, 0)),
                pl.BlockSpec((tile, 1), lambda i, rank: (i, 0)),
            ],
        ),
        out_shape=[
            jax.ShapeDtypeStruct((2, rows, width // 2), jnp.bfloat16),
            jax.ShapeDtypeStruct((rows, 1), jnp.float32),
        ],
    )(rank, value, gain[None])


def project_kernel(low_ref, high_ref, a_ref, b_ref, o_ref, s_ref):
    total = matmul(low_ref[0], a_ref[...]) + matmul(high_ref[0], b_ref[...])
    o_ref[...] = total.astype(o_ref.dtype)
    s_ref[...] = jnp.sum(total * total, axis=1, keepdims=True)


def project(halves, a, b, dtype, start=0):
    _, rows, depth = halves.shape
    rows = rows - start
    width = a.shape[1]
    tile = 256
    first = start // tile
    weight = pl.BlockSpec((depth, width), lambda i: (0, 0))
    return kernel_call(
        project_kernel,
        grid=(rows // tile,),
        in_specs=[
            pl.BlockSpec((1, tile, depth), lambda i: (0, i + first, 0)),
            pl.BlockSpec((1, tile, depth), lambda i: (1, i + first, 0)),
            weight,
            weight,
        ],
        out_specs=[
            pl.BlockSpec((tile, width), lambda i: (i, 0)),
            pl.BlockSpec((tile, 1), lambda i: (i, 0)),
        ],
        out_shape=[
            jax.ShapeDtypeStruct((rows, width), dtype),
            jax.ShapeDtypeStruct((rows, 1), jnp.float32),
        ],
    )(halves, halves, a, b)


def project_back_kernel(k_ref, v_ref, w_ref, q_ref, ka, kb, va, vb, qa, qb, o_ref, *, tile):
    j = pl.program_id(0)
    half = pl.num_programs(0) // 2
    half_width = v_ref.shape[1]
    own = k_ref.shape[0] - q_ref.shape[0]

    def part(key, value, query):
        for start in range(0, k_ref.shape[0], tile):
            at = slice(start, start + tile)
            total = dot_t(k_ref[at, :], key[...]) + dot_t(v_ref[at, :], value[:, :half_width])
            total += dot_t(w_ref[at, :], value[:, half_width:])
            if start >= own:
                total += dot_t(q_ref[start - own : start - own + tile, :], query[...])
            o_ref[0, at, :] = total

    @pl.when(j < half)
    def _():
        part(ka, va, qa)

    @pl.when(j >= half)
    def _():
        part(kb, vb, qb)


def project_back(key, value, value_high, query, key_w, value_w, query_w):
    rows, width = key.shape
    depth = value_w[0].shape[0]
    step = 256
    half = depth // step
    whole = lambda value: pl.BlockSpec(value.shape, lambda j: (0, 0), pipeline_mode=pl.Buffered(1))
    low = pl.BlockSpec((step, width), lambda j: (jnp.minimum(j, half - 1), 0))
    high = pl.BlockSpec((step, width), lambda j: (jnp.maximum(j - half, 0), 0))
    return kernel_call(
        functools.partial(project_back_kernel, tile=512),
        grid=(2 * half,),
        in_specs=[whole(key), whole(value), whole(value_high), whole(query)] + [low, high] * 3,
        out_specs=pl.BlockSpec((1, rows, step), lambda j: (j // half, 0, j % half)),
        out_shape=jax.ShapeDtypeStruct((2, rows, depth), jnp.float32),
    )(key, value, value_high, query, *key_w, *value_w, *query_w)


def tokens_back_kernel(
    rank, g_ref, c_ref, x_ref, res_ref, scale_ref, gain_ref, o_ref, *, blocks
):
    scale = scale_ref[...]
    block = x_ref.shape[1] // blocks
    half = blocks // 2

    def pieces(place):
        start = pl.multiple_of((rank[0] ^ code_of(place, blocks)) * block, block)
        at = slice(place % half * block, place % half * block + block)
        grad = g_ref[place // half, :, at] + c_ref[place // half, :, at].astype(jnp.float32)
        columns = pl.ds(start, block)
        return columns, grad, x_ref[:, columns].astype(jnp.float32), gain_ref[:, columns]

    inner = jnp.zeros_like(scale)
    for place in range(blocks):
        columns, grad, value, gain = pieces(place)
        inner += jnp.sum(grad * value * gain, axis=1, keepdims=True)
    inner = inner * (1.0 / x_ref.shape[1]) * (scale * scale * scale)
    for place in range(blocks):
        columns, grad, value, gain = pieces(place)
        o_ref[:, columns] = res_ref[:, columns] + (scale * (grad * gain) - value * inner)


def tokens_back(rank, grad, carried, tokens, residual_grad, scale, gain, blocks):
    rows, width = tokens.shape
    tile = 128
    first = (grad.shape[1] - rows) // tile
    wide = pl.BlockSpec((tile, width), lambda i, rank: (i, 0))
    one = pl.BlockSpec((1, width), lambda i, rank: (0, 0))
    return kernel_call(
        functools.partial(tokens_back_kernel, blocks=blocks),
        grid_spec=pltpu.PrefetchScalarGridSpec(
            num_scalar_prefetch=1,
            grid=(rows // tile,),
            in_specs=[
                pl.BlockSpec((2, tile, width // 2), lambda i, rank: (0, i + first, 0)),
                pl.BlockSpec((2, tile, width // 2), lambda i, rank: (0, i, 0)),
                wide,
                wide,
                pl.BlockSpec((tile, 1), lambda i, rank: (i + first, 0)),
                one,
            ],
            out_specs=wide,
        ),
        out_shape=jax.ShapeDtypeStruct((rows, width), jnp.float32),
    )(rank, grad, carried, tokens, residual_grad, scale, gain[None])


def head_rows(lin, scale, gain, cosine, sine):
    return turn(lin * scale * gain, cosine, sine).astype(jnp.bfloat16)


def moved_head(head, rank):
    place = place_of((head // 2) ^ rank[0], HEADS // 2) * 2 + head % 2
    return place // (HEADS // 2), 0, place % (HEADS // 2)


def attention_specs(rows, all_rows, bias, first=0):
    head = lambda h, rank: (0, h + first)
    fixed = lambda h, rank: (0, 0)
    return [
        pl.BlockSpec((rows, HEAD_DIM), head),
        pl.BlockSpec((all_rows, HEAD_DIM), head),
        pl.BlockSpec((all_rows, HEAD_DIM), head),
        pl.BlockSpec((rows, 1), fixed),
        pl.BlockSpec((all_rows, 1), fixed),
        pl.BlockSpec((1, HEAD_DIM), head),
        pl.BlockSpec((1, HEAD_DIM), head),
        pl.BlockSpec((all_rows, HEAD_DIM), fixed),
        pl.BlockSpec((all_rows, HEAD_DIM), fixed),
        pl.BlockSpec(bias.shape, lambda h, rank: (0, 0, 0)),
    ]


def attend_kernel(
    rank,
    q_ref,
    k_ref,
    v_ref,
    sq_ref,
    sk_ref,
    gq_ref,
    gk_ref,
    cos_ref,
    sin_ref,
    bias_ref,
    *refs,
    behind,
    tile,
    span,
):
    o_ref, lse_ref = refs[-2:]
    rows = q_ref.shape[0]
    cosine, sine = cos_ref[...], sin_ref[...]
    keys = head_rows(k_ref[...], sk_ref[...], gk_ref[...], cosine, sine)
    queries = head_rows(q_ref[...], sq_ref[...], gq_ref[...], cosine[behind:], sine[behind:])
    for t in range(rows // tile):
        at = slice(t * tile, (t + 1) * tile)
        seen = slice(t * tile, t * tile + span)
        scores = dot_t(keys[seen], queries[at])
        scores = scores * HEAD_DIM ** (-0.5) + bias_ref[t].astype(jnp.float32)
        peak = jnp.max(scores, axis=0, keepdims=True)
        shifted = jnp.exp(scores - peak)
        total = jnp.sum(shifted, axis=0, keepdims=True)
        weights = (shifted * (1.0 / total)).astype(jnp.bfloat16)
        o_ref[0, at, :] = t_dot(weights, v_ref[seen, :]).astype(jnp.bfloat16)
        lse_ref[0, :, at] = peak + jnp.log(total)


def attend(rank, operands, bias, first, into=()):
    rows, width = operands[0].shape
    all_rows = operands[1].shape[0]
    tiles, span, tile = bias.shape
    return kernel_call(
        functools.partial(attend_kernel, behind=all_rows - rows, tile=tile, span=span),
        grid_spec=pltpu.PrefetchScalarGridSpec(
            num_scalar_prefetch=1,
            grid=(HEADS // 2,),
            in_specs=attention_specs(rows, all_rows, bias, first)
            + [pl.BlockSpec(memory_space=pl.ANY)] * len(into),
            out_specs=[
                pl.BlockSpec((1, rows, HEAD_DIM), lambda h, rank: moved_head(h + first, rank)),
                pl.BlockSpec((1, 1, rows), lambda h, rank: (h, 0, 0)),
            ],
        ),
        input_output_aliases={2 + len(operands): 0} if into else {},
        out_shape=[
            jax.ShapeDtypeStruct((2, rows, width // 2), jnp.bfloat16),
            jax.ShapeDtypeStruct((HEADS // 2, 1, rows), jnp.float32),
        ],
    )(rank, *operands, bias, *into)


def attend_back_kernel(
    rank,
    q_ref,
    k_ref,
    v_ref,
    sq_ref,
    sk_ref,
    gq_ref,
    gk_ref,
    cos_ref,
    sin_ref,
    bias_ref,
    g_ref,
    lse_ref,
    dq_ref,
    dk_ref,
    dv_ref,
    key_total,
    value_total,
    *,
    behind,
    tile,
    span,
):
    rows = q_ref.shape[0]
    score_scale = HEAD_DIM ** (-0.5)
    cosine, sine = cos_ref[...], sin_ref[...]
    keys = head_rows(k_ref[...], sk_ref[...], gk_ref[...], cosine, sine)
    queries = head_rows(q_ref[...], sq_ref[...], gq_ref[...], cosine[behind:], sine[behind:])
    key_total[...] = jnp.zeros_like(key_total)
    value_total[...] = jnp.zeros_like(value_total)
    for t in range(rows // tile):
        at = slice(t * tile, (t + 1) * tile)
        seen = slice(t * tile, t * tile + span)
        scores = dot_t(keys[seen], queries[at])
        scores = scores * score_scale + bias_ref[t].astype(jnp.float32)
        probs = jnp.exp(scores - lse_ref[0, :, at])
        grad = g_ref[0, at, :]
        value_total[seen, :] += matmul(probs.astype(jnp.bfloat16), grad)
        probs_grad = dot_t(v_ref[seen, :], grad)
        inner = jnp.sum(probs * probs_grad, axis=0, keepdims=True)
        score_grad = (probs * (probs_grad - inner)).astype(jnp.bfloat16)
        dq_ref[at, :] = (t_dot(score_grad, keys[seen]) * score_scale).astype(jnp.bfloat16)
        key_total[seen, :] += matmul(score_grad, queries[at])
    dk_ref[...] = (key_total[...] * score_scale).astype(jnp.bfloat16)
    dv_ref[...] = value_total[...].astype(jnp.bfloat16)


def attend_back(rank, operands, bias, grad, lse, first):
    rows, width = operands[0].shape
    width = width // 2
    all_rows = operands[1].shape[0]
    tiles, span, tile = bias.shape
    head = lambda h, rank: (0, h)
    return kernel_call(
        functools.partial(attend_back_kernel, behind=all_rows - rows, tile=tile, span=span),
        grid_spec=pltpu.PrefetchScalarGridSpec(
            num_scalar_prefetch=1,
            grid=(HEADS // 2,),
            in_specs=attention_specs(rows, all_rows, bias, first)
            + [
                pl.BlockSpec((1, rows, HEAD_DIM), lambda h, rank: moved_head(h + first, rank)),
                pl.BlockSpec((1, 1, rows), lambda h, rank: (h, 0, 0)),
            ],
            out_specs=[
                pl.BlockSpec((rows, HEAD_DIM), head),
                pl.BlockSpec((all_rows, HEAD_DIM), head),
                pl.BlockSpec((all_rows, HEAD_DIM), head),
            ],
            scratch_shapes=[
                pltpu.VMEM((all_rows, HEAD_DIM), jnp.float32),
                pltpu.VMEM((all_rows, HEAD_DIM), jnp.float32),
            ],
        ),
        out_shape=[
            jax.ShapeDtypeStruct((rows, width), jnp.bfloat16),
            jax.ShapeDtypeStruct((all_rows, width), jnp.bfloat16),
            jax.ShapeDtypeStruct((all_rows, width), jnp.bfloat16),
        ],
    )(rank, *operands, bias, grad, lse)


def lin_back_kernel(
    low_ref, high_ref, lin_ref, scale_ref, gain_ref, cos_ref, sin_ref, o_ref, gain_grad_ref, kept
):
    rows = scale_ref.shape[0]
    scale = jnp.broadcast_to(scale_ref[...], (rows, HEAD_DIM))
    cosine, sine = cos_ref[...], -sin_ref[...]

    @pl.when(pl.program_id(0) == 0)
    def _():
        gain_grad_ref[...] = jnp.zeros_like(gain_grad_ref)

    inner = jnp.zeros((rows, HEAD_DIM), jnp.float32)
    for h in range(HEADS):
        at = slice(h * HEAD_DIM, (h + 1) * HEAD_DIM)
        ref = low_ref if h < HEADS // 2 else high_ref
        here = slice(h % (HEADS // 2) * HEAD_DIM, (h % (HEADS // 2) + 1) * HEAD_DIM)
        grad = turn(ref[:, here].astype(jnp.float32), cosine, sine)
        product = grad * lin_ref[:, at]
        gain = gain_ref[:, at]
        gain_grad_ref[:, at] += jnp.sum(product * scale, axis=0, keepdims=True)
        inner += product * gain
        kept[:, at] = grad * gain * scale
    inner = jnp.sum(inner, axis=1, keepdims=True) * (1.0 / (HEADS * HEAD_DIM))
    inner = jnp.broadcast_to(inner, (rows, HEAD_DIM)) * (scale * scale * scale)
    for h in range(HEADS):
        at = slice(h * HEAD_DIM, (h + 1) * HEAD_DIM)
        o_ref[:, at] = (kept[:, at] - lin_ref[:, at] * inner).astype(jnp.bfloat16)


def lin_back(low, high, lin, scale, gain, cosine, sine):
    rows, width = lin.shape
    tile = 256
    wide = pl.BlockSpec((tile, width), lambda i: (i, 0))
    one = pl.BlockSpec((1, width), lambda i: (0, 0))
    half = pl.BlockSpec((tile, width // 2), lambda i: (i, 0))
    table = pl.BlockSpec((tile, HEAD_DIM), lambda i: (i, 0))
    return kernel_call(
        lin_back_kernel,
        grid=(rows // tile,),
        in_specs=[half, half, wide, pl.BlockSpec((tile, 1), lambda i: (i, 0)), one, table, table],
        out_specs=[wide, one],
        scratch_shapes=[pltpu.VMEM((tile, width), jnp.float32)],
        out_shape=[
            jax.ShapeDtypeStruct((rows, width), jnp.bfloat16),
            jax.ShapeDtypeStruct((1, width), jnp.float32),
        ],
    )(low, high, lin, scale, gain, cosine, sine)


def flat(ref):
    return ref[...].reshape(-1, ref.shape[-1])


def gu_spec(weights, rows):
    return pl.BlockSpec((2, rows, weights.shape[2]), lambda i, *_: (0, 0, 0))


def d_spec(weights, rows):
    last = weights.shape[1] // rows - 1
    return pl.BlockSpec((2, rows, weights.shape[2]), lambda i, *_: (0, last, 0))


def dynamic_block(index, block):
    return pl.ds(pl.multiple_of(index * block, block), block)


def experts_up_kernel(rank, x_ref, z_ref, ga, gb, ua, ub, g_ref, u_ref, my_ref, mx_ref, middle_ref):
    gate = matmul(x_ref[0], flat(ga)) + matmul(x_ref[1], flat(gb))
    up = matmul(z_ref[0], flat(ua)) + matmul(z_ref[1], flat(ub))
    g_ref[...] = gate
    u_ref[...] = up
    middle_ref[...] = (gate * jax.nn.sigmoid(gate) * up).astype(jnp.bfloat16)
    block = gate.shape[1] // 4
    for j in range(4):
        piece = middle_ref[:, dynamic_block(rank[0] ^ j, block)]
        dy, dx = j // 2, j % 2
        my_ref[dy, :, dx * block : (dx + 1) * block] = piece
        mx_ref[dx, :, dy * block : (dy + 1) * block] = piece


def experts_up(rank, by_y, by_x, weights):
    _, rows, depth = by_y.shape
    hidden = weights[0].shape[2]
    tile = 256
    x_spec = pl.BlockSpec((2, tile, depth), lambda i, rank: (0, i, 0))
    w_specs = [gu_spec(weight, depth // 2) for weight in weights]
    wide = pl.BlockSpec((tile, hidden), lambda i, rank: (i, 0))
    half = pl.BlockSpec((2, tile, hidden // 2), lambda i, rank: (0, i, 0))
    return kernel_call(
        experts_up_kernel,
        grid_spec=pltpu.PrefetchScalarGridSpec(
            num_scalar_prefetch=1,
            grid=(rows // tile,),
            in_specs=[x_spec, x_spec] + w_specs,
            out_specs=[wide, wide, half, half],
            scratch_shapes=[pltpu.VMEM((tile, hidden), jnp.bfloat16)],
        ),
        out_shape=[jax.ShapeDtypeStruct((rows, hidden), jnp.float32)] * 2
        + [jax.ShapeDtypeStruct((2, rows, hidden // 2), jnp.bfloat16)] * 2,
    )(rank, by_y, by_x, *weights)


def experts_down_kernel(*refs):
    gates, slots, outs = refs[:2], (refs[2:8], refs[8:14]), refs[14:]
    half = outs[0].shape[1] // 2
    mixtures = []
    for side in range(2):
        at = slice(side * half, (side + 1) * half)
        mixture = 0.0
        for slot, (my, mx, la, lb, ra, rb) in enumerate(slots):
            if side == 0:
                out = matmul(my[0], flat(la)) + matmul(my[1], flat(lb))
            else:
                out = matmul(mx[0], flat(ra)) + matmul(mx[1], flat(rb))
            out = out.astype(jnp.bfloat16)
            outs[slot][:, at] = out
            mixture += gates[slot][...] * out.astype(jnp.float32)
        mixtures.append(mixture)

    @pl.when(pl.program_id(0) < pl.num_programs(0) // 2)
    def _():
        outs[2][:, :half], outs[2][:, half:] = mixtures

    @pl.when(pl.program_id(0) >= pl.num_programs(0) // 2)
    def _():
        outs[3][:, :half], outs[3][:, half:] = mixtures


def experts_down(gates, slots):
    _, rows, depth = slots[0][0].shape
    half = slots[0][2].shape[2]
    tile = 256
    x_spec = pl.BlockSpec((2, tile, depth), lambda i: (0, i, 0))
    w_specs = [d_spec(weight, depth // 2) for weight in slots[0][2:]]
    wide = pl.BlockSpec((tile, 2 * half), lambda i: (i, 0))
    column = pl.BlockSpec((tile, 1), lambda i: (i, 0))
    steps = rows // tile // 2
    return kernel_call(
        experts_down_kernel,
        grid=(rows // tile,),
        in_specs=[column] * 2 + ([x_spec] * 2 + w_specs) * 2,
        out_specs=[
            wide,
            wide,
            pl.BlockSpec((tile, 2 * half), lambda i: (jnp.minimum(i, steps - 1), 0)),
            pl.BlockSpec((tile, 2 * half), lambda i: (jnp.maximum(i - steps, 0), 0)),
        ],
        out_shape=[
            jax.ShapeDtypeStruct((rows, 2 * half), jnp.bfloat16),
            jax.ShapeDtypeStruct((rows, 2 * half), jnp.bfloat16),
            jax.ShapeDtypeStruct((rows // 2, 2 * half), jnp.float32),
            jax.ShapeDtypeStruct((rows // 2, 2 * half), jnp.float32),
        ],
    )(*gates, *slots[0], *slots[1])


def experts_back_kernel(
    rank, own_ref, other_ref, out_ref, gate_ref, g_ref, u_ref, la, lb, ra, rb, p_ref, dg_ref, du_ref, gg_ref
):
    own = pl.program_id(0) < pl.num_programs(0) // 2
    grad = jnp.where(own, own_ref[...], other_ref[...])
    gg_ref[...] = jnp.sum(grad * out_ref[...].astype(jnp.float32), axis=1, keepdims=True)
    p_ref[...] = (gate_ref[...] * grad).astype(jnp.bfloat16)
    half = grad.shape[1] // 2
    left, right = p_ref[:, :half], p_ref[:, half:]
    block = la.shape[1]
    for j in range(4):
        dy, dx = j // 2, j % 2
        left_w = (la, lb)[dy][dx]
        right_w = (ra, rb)[dx][dy]
        middle_grad = dot_t(left, left_w) + dot_t(right, right_w)
        at = dynamic_block(rank[0] ^ j, block)
        gate_pre, up_pre = g_ref[:, at], u_ref[:, at]
        sigma = jax.nn.sigmoid(gate_pre)
        change = middle_grad * up_pre * sigma * (1.0 + gate_pre * (1.0 - sigma))
        dg_ref[:, at] = change.astype(jnp.bfloat16)
        du_ref[:, at] = (middle_grad * (gate_pre * sigma)).astype(jnp.bfloat16)


def experts_back(rank, own, other, out, gate, gate_pre, up_pre, weights):
    rows, width = out.shape
    hidden = gate_pre.shape[1]
    tile = 256
    wide = pl.BlockSpec((tile, width), lambda i, rank: (i, 0))
    narrow = pl.BlockSpec((tile, hidden), lambda i, rank: (i, 0))
    column = pl.BlockSpec((tile, 1), lambda i, rank: (i, 0))
    w_specs = [d_spec(weight, hidden // 4) for weight in weights]
    steps = rows // tile // 2
    return kernel_call(
        experts_back_kernel,
        grid_spec=pltpu.PrefetchScalarGridSpec(
            num_scalar_prefetch=1,
            grid=(rows // tile,),
            in_specs=[
                pl.BlockSpec((tile, width), lambda i, rank: (jnp.minimum(i, steps - 1), 0)),
                pl.BlockSpec((tile, width), lambda i, rank: (jnp.maximum(i - steps, 0), 0)),
                wide, column, narrow, narrow
            ] + w_specs,
            out_specs=[wide, narrow, narrow, column],
        ),
        out_shape=[
            jax.ShapeDtypeStruct((rows, width), jnp.bfloat16),
            jax.ShapeDtypeStruct((rows, hidden), jnp.bfloat16),
            jax.ShapeDtypeStruct((rows, hidden), jnp.bfloat16),
            jax.ShapeDtypeStruct((rows, 1), jnp.float32),
        ],
    )(rank, own, other, out, gate, gate_pre, up_pre, *weights)


def experts_input_kernel(*refs):
    totals = []
    for j in range(4):
        dy, dx = j // 2, j % 2
        total = 0.0
        for dg, du, ga, gb, ua, ub in (refs[:6], refs[6:12]):
            gate_w = (ga, gb)[dy][dx]
            up_w = (ua, ub)[dx][dy]
            part = dot_t(dg[...], gate_w) + dot_t(du[...], up_w)
            total += part.astype(jnp.bfloat16).astype(jnp.float32)
        totals.append(total)

    @pl.when(pl.program_id(0) < pl.num_programs(0) // 2)
    def _():
        for j in range(4):
            refs[-2][j] = totals[j]

    @pl.when(pl.program_id(0) >= pl.num_programs(0) // 2)
    def _():
        for j in range(4):
            refs[-1][j] = totals[j]


def experts_input(slots):
    rows, hidden = slots[0][0].shape
    depth = slots[0][2].shape[1] // 3 * 2
    tile = 256
    narrow = pl.BlockSpec((tile, hidden), lambda i: (i, 0))
    w_specs = [gu_spec(weight, depth) for weight in slots[0][2:]]
    steps = rows // tile // 2
    return kernel_call(
        experts_input_kernel,
        grid=(rows // tile,),
        in_specs=([narrow] * 2 + w_specs) * 2,
        out_specs=[
            pl.BlockSpec((4, tile, depth), lambda i: (0, jnp.minimum(i, steps - 1), 0)),
            pl.BlockSpec((4, tile, depth), lambda i: (0, jnp.maximum(i - steps, 0), 0)),
        ],
        out_shape=[jax.ShapeDtypeStruct((4, rows // 2, depth), jnp.float32)] * 2,
    )(*slots[0], *slots[1])


def residual_back_kernel(
    rank, a_ref, b_ref, lg_ref, wr_ref, x_ref, r_ref, scale_ref, gain_ref, o_ref, c_ref, gg_ref
):
    scale = scale_ref[...]
    block = a_ref.shape[2]

    @pl.when(pl.program_id(0) == 0)
    def _():
        gg_ref[...] = jnp.zeros_like(gg_ref)

    inner = jnp.zeros_like(scale)
    for j in range(4):
        at = dynamic_block(rank[0] ^ j, block)
        grad = a_ref[j] + b_ref[j]
        for e in range(wr_ref.shape[0]):
            grad += lg_ref[:, e : e + 1] * wr_ref[e : e + 1, at]
        o_ref[:, at] = grad
        product = grad * x_ref[:, at]
        inner += jnp.sum(product * gain_ref[:, at], axis=1, keepdims=True)
        gg_ref[:, at] += jnp.sum(product * scale, axis=0, keepdims=True)
    inner = inner * (1.0 / x_ref.shape[1]) * (scale * scale * scale)
    for j in range(4):
        at = slice(j * block, (j + 1) * block)
        value = scale * (o_ref[:, at] * gain_ref[:, at]) - x_ref[:, at] * inner
        value = r_ref[:, at] + value
        o_ref[:, at] = value
        c_ref[:, at] = value.astype(jnp.bfloat16)


def residual_back(rank, own, other, logit_grad, router, residual, result_grad, scale, gain):
    rows, width = residual.shape
    tile = 128
    wide = pl.BlockSpec((tile, width), lambda i, rank: (i, 0))
    piece = pl.BlockSpec((4, tile, width // 4), lambda i, rank: (0, i, 0))
    one = pl.BlockSpec((1, width), lambda i, rank: (0, 0))
    experts = logit_grad.shape[1]
    return kernel_call(
        residual_back_kernel,
        grid_spec=pltpu.PrefetchScalarGridSpec(
            num_scalar_prefetch=1,
            grid=(rows // tile,),
            in_specs=[
                piece,
                piece,
                pl.BlockSpec((tile, experts), lambda i, rank: (i, 0)),
                pl.BlockSpec((experts, width), lambda i, rank: (0, 0)),
                wide,
                wide,
                pl.BlockSpec((tile, 1), lambda i, rank: (i, 0)),
                one,
            ],
            out_specs=[wide, wide, one],
        ),
        out_shape=[
            jax.ShapeDtypeStruct((rows, width), jnp.float32),
            jax.ShapeDtypeStruct((rows, width), jnp.bfloat16),
            jax.ShapeDtypeStruct((1, width), jnp.float32),
        ],
    )(rank, own, other, logit_grad, router, residual, result_grad, scale, gain[None])


def experts_grad_kernel(x_ref, d_ref, m_ref, p_ref, *refs):
    o_ref = refs[-1]
    rows, down_rows = x_ref.shape[2], m_ref.shape[2]
    top, bottom = t_dot(x_ref[0], d_ref[...]), t_dot(m_ref[0], p_ref[...])
    if len(refs) == 2:
        top += refs[0][0, :rows].astype(jnp.float32)
        bottom += refs[0][0, rows:].astype(jnp.float32)
    o_ref[0, :rows] = top.astype(jnp.bfloat16)
    o_ref[0, rows:] = bottom.astype(jnp.bfloat16)


def experts_grad(inputs, pre_grad, middle, pair, part, side, got=()):
    _, rows, depth = inputs.shape
    hidden, down = pre_grad.shape[1], middle.shape[2]
    piece = pl.BlockSpec((1, (depth + down) // 2, hidden), lambda q: (q, 0, 0))
    return kernel_call(
        experts_grad_kernel,
        grid=(2,),
        in_specs=[
            pl.BlockSpec((1, rows, depth // 2), lambda q: (part, 0, q)),
            pl.BlockSpec((rows, hidden), lambda q: (0, 0)),
            pl.BlockSpec((1, rows, down // 2), lambda q: (part, 0, q)),
            pl.BlockSpec((rows, hidden), lambda q: (0, side)),
        ]
        + [piece] * len(got),
        out_specs=piece,
        out_shape=jax.ShapeDtypeStruct((2, (depth + down) // 2, hidden), jnp.bfloat16),
    )(inputs, pre_grad, middle, pair, *got)


def chip_grad_kernel(x_ref, *refs, count):
    o_ref = refs[-1]
    width = o_ref.shape[1] // count
    for i in range(count):
        at = slice(i * width, (i + 1) * width)
        total = t_dot(x_ref[0], refs[i][...])
        if len(refs) > count + 1:
            total += refs[count][:, at].astype(jnp.float32)
        o_ref[:, at] = total.astype(jnp.bfloat16)


def chip_grad(halves, part, grads, start=0, got=()):
    depth = halves.shape[2]
    rows = grads[0].shape[0]
    width = sum(grad.shape[1] for grad in grads)
    tile = 256
    piece = pl.BlockSpec((tile, width), lambda i: (i, 0))
    return kernel_call(
        functools.partial(chip_grad_kernel, count=len(grads)),
        grid=(depth // tile,),
        in_specs=[pl.BlockSpec((1, rows, tile), lambda i: (part, start // rows, i))]
        + [pl.BlockSpec(grad.shape, lambda i: (0, 0)) for grad in grads]
        + [piece] * len(got),
        out_specs=piece,
        out_shape=jax.ShapeDtypeStruct((depth, width), jnp.bfloat16),
    )(halves, *grads, *got)


def mixed_back_kernel(g_ref, a_ref, b_ref, o_ref):
    for half, ref in enumerate((a_ref, b_ref)):
        o_ref[half] = dot_t(g_ref[...], ref[...]).astype(jnp.bfloat16)


def mixed_back(grad, weights):
    rows, width = grad.shape
    depth = weights[0].shape[0]
    step = 256
    weight = pl.BlockSpec((step, width), lambda j: (j, 0))
    return kernel_call(
        mixed_back_kernel,
        grid=(depth // step,),
        in_specs=[pl.BlockSpec((rows, width), lambda j: (0, 0)), weight, weight],
        out_specs=pl.BlockSpec((2, rows, step), lambda j: (0, 0, j)),
        out_shape=jax.ShapeDtypeStruct((2, rows, depth), jnp.bfloat16),
    )(grad, *weights)


def across(value, bit):
    count = lax.axis_size("rep")
    return lax.ppermute(value, "rep", [(place, place ^ bit) for place in range(count)])


def along(value, steps):
    count = lax.axis_size("ep")
    return lax.ppermute(value, "ep", [(place, (place + steps) % count) for place in range(count)])


def mirrored(value, moves):
    reps, count = lax.axis_size("rep"), lax.axis_size("ep")
    pairs = []
    for rep in range(reps):
        for source, target in moves:
            if rep % 2:
                source, target = count - 1 - source, count - 1 - target
            pairs.append((rep * count + source, rep * count + target))
    return lax.ppermute(value, ("rep", "ep"), pairs)


def pick(value, index, axis):
    return lax.dynamic_index_in_dim(value, index, axis, keepdims=False)


def in_order(own, other, bit, axis):
    return jnp.where(bit == 1, jnp.stack([other, own], axis), jnp.stack([own, other], axis))


def over_ep(value, place):
    shard = place[3]
    experts = lax.axis_size("ep")
    parts = jnp.zeros((experts,) + value.shape, value.dtype)
    parts = lax.dynamic_update_index_in_dim(parts, value, shard, 0)
    for steps in range(1, experts):
        parts = lax.dynamic_update_index_in_dim(
            parts, along(value, steps), lax.rem(shard - steps + experts, experts), 0
        )
    return parts


def hold(*values):
    return lax.optimization_barrier(values)


def both_ways(value):
    return across(value[0], 2), across(value[1], 4)


def other_ways(first, second):
    return across(first, 4), across(second, 2)


def add(left, right):
    return (left.astype(jnp.float32) + right.astype(jnp.float32)).astype(jnp.bfloat16)


def ep_sum(both):
    return lax.psum_scatter(both, "ep", scatter_dimension=1, tiled=True).astype(jnp.float32)


def body(
    tokens,
    teacher,
    segment_ids,
    valid_mask,
    routes,
    attn_gain,
    q_gain,
    k_gain,
    moe_gain,
    w_query,
    w_key,
    w_value,
    w_out,
    w_router,
    w_gate,
    w_up,
    w_down,
):
    bf16, f32 = jnp.bfloat16, jnp.float32
    local_rows, width = tokens.shape
    experts = lax.axis_size("ep")
    reps = lax.axis_size("rep")
    reach = min(-(-WINDOW // local_rows), experts - 1)
    shard = lax.axis_index("ep")
    rep = lax.axis_index("rep")
    place = (rep // 4, rep // 2 % 2, rep % 2, shard)
    core = rep % 2
    total_tokens = local_rows * reps * experts

    valid = valid_mask.reshape(local_rows).astype(f32)
    own_count = jnp.sum(valid_mask)
    counts = jnp.stack([own_count // 16, own_count % 16]).astype(bf16)
    small = jnp.concatenate(
        [
            jnp.stack([attn_gain, q_gain, k_gain, moe_gain], 1),
            w_router,
            jnp.broadcast_to(counts[None], (attn_gain.shape[0], 2)),
        ],
        1,
    )
    rank = rep.astype(jnp.int32)[None]
    quarter = rep // 2
    quarter_rank = quarter.astype(jnp.int32)[None]
    order = tuple(code_of(j, reps) for j in range(reps))
    half = width // 2
    behind = reach * local_rows
    all_rows = local_rows + behind
    m = jnp.where(core == 0, shard, experts - 1 - shard)
    quarter_rows = w_gate.shape[1] // 4
    quarter_down = w_down.shape[1] // 4

    def own_part(weight, rows):
        return lax.dynamic_slice_in_dim(weight[0], quarter * rows, rows, 0)

    down = own_part(w_down, quarter_down)
    own = jnp.stack(
        [
            jnp.concatenate([own_part(w_gate, quarter_rows), down[:, :half]], 0),
            jnp.concatenate([own_part(w_up, quarter_rows), down[:, half:]], 0),
        ]
    )
    segments = segment_ids.reshape(local_rows)
    shard_rows = w_key.shape[0]
    columns = small.shape[1]
    small = small.T

    small = over_ep(small, place)
    parts = over_ep(jnp.stack([w_key, w_value]), place)
    segments_1 = from_behind(segments, "ep", 1)
    parts, small, own, tokens_1, segments_1 = hold(parts, small, own, tokens, segments_1)
    qo = jnp.stack([w_query, w_out])

    qo, parts = hold(qo, parts)
    qo = lax.all_gather(qo, "ep", axis=0)
    block = shard_rows * experts
    k_w, v_w = parts[:, 0].reshape(block, width), parts[:, 1].reshape(block, width)
    e_1 = mirrored(own, [(0, 1), (1, 2)])
    small = small.reshape(-1)
    small = jnp.pad(small, (0, 16 * width - small.shape[0])).reshape(16, width)
    k_w = jnp.concatenate([k_w, small], 0)
    k_x, v_y = both_ways((k_w, v_w))
    segments_2 = from_behind(segments_1, "ep", 1)
    k_w, k_x, v_w, v_y, tokens_1, segments_2 = hold(k_w, k_x, v_w, v_y, tokens_1, segments_2)

    k_w = jnp.stack([k_w, k_x])
    k_y, v_x = other_ways(k_w, jnp.stack([v_w, v_y]))
    tokens_1 = from_behind(tokens_1, "ep", 1)
    qo, k_w, k_y, v_w, v_y, v_x, tokens_1 = hold(qo, k_w, k_y, v_w, v_y, v_x, tokens_1)

    small = jnp.concatenate([k_w[:, block : block + 2], k_y[:, block : block + 2]], 0)
    small = jnp.pad(small.reshape(-1, width), ((0, 8), (0, 0)))
    k_w = jnp.concatenate([k_w[0, :block], k_w[1, :block], k_y[0, :block], k_y[1, :block], small], 0)
    v_w = jnp.concatenate([v_w, v_x[0], v_y, v_x[1]], 0)
    key_w, value_w = (k_w, across(k_w, 1)), (v_w, across(v_w, 1))
    q_w, o_w = qo[:, 0].reshape(-1, width), qo[:, 1].reshape(-1, width)
    q_x, o_y = both_ways((q_w, o_w))
    tokens_2 = from_behind(tokens_1, "ep", 1)
    key_w, value_w, q_w, q_x, o_w, o_y, tokens_2, tokens_1, e_1, own = hold(
        key_w, value_w, q_w, q_x, o_w, o_y, tokens_2, tokens_1, e_1, own
    )

    q_w = jnp.concatenate([q_w, q_x], 0)
    q_y, o_x = other_ways(q_w, jnp.stack([o_w, o_y]))
    q_w = jnp.concatenate([q_w, q_y], 0)
    o_w = jnp.concatenate([o_w, o_x[0], o_y, o_x[1]], 0)
    e_2 = mirrored(jnp.where(m == 2, e_1, own), [(1, 0), (2, 3)])
    small = jnp.stack([weight[4 * block : 4 * block + 8] for weight in key_w])
    small = small.reshape(2, 2, 2, -1)[..., : experts * columns * shard_rows]
    for axis, bit in enumerate((core, place[0], place[1])):
        small = jnp.where(bit == 1, jnp.flip(small, axis), small)
    small = small.reshape(2, 2, 2, experts, columns, shard_rows)
    small = jnp.transpose(small, (4, 1, 2, 0, 3, 5)).reshape(columns, -1)
    gain_attn, gain_query, gain_key, gain_moe = [small[i].astype(f32) for i in range(4)]
    weight_router = small[4 : 4 + experts].T
    counts = small[4 + experts :, ::shard_rows].astype(f32)
    count = jnp.sum(counts[0]) * 16.0 + jnp.sum(counts[1])
    tokens_all = jnp.concatenate([tokens_2, tokens_1, tokens], 0)
    key_segments = jnp.concatenate([segments_2, segments_1, segments], 0)
    normed, scale_all = norm_rows(rank, tokens_all, gain_attn, order)
    key_lin, key_squares = project(normed, *key_w, f32)
    value_all, _ = project(normed, *value_w, bf16)
    q_w, o_w, e_2, e_1, own, normed, key_lin, value_all = hold(
        q_w, o_w, e_2, e_1, own, normed, key_lin, value_all
    )

    query_w, out_w = (q_w, across(q_w, 1)), (o_w, across(o_w, 1))
    e_b = jnp.where(m == 1, own, jnp.where(m == 2, e_1, e_2))
    b_x, b_y = both_ways(e_b)
    e_3 = mirrored(e_1, [(1, 2)])
    query_lin, query_squares = project(normed, *query_w, f32, behind)
    scale_key = lax.rsqrt(key_squares / width + norm_eps)
    scale_query = lax.rsqrt(query_squares / width + norm_eps)
    key_positions = (shard - reach) * local_rows + jnp.arange(all_rows, dtype=jnp.int32)
    half_head = HEAD_DIM // 2
    frequency = 10000.0 ** (-jnp.arange(half_head, dtype=f32) * 2.0 / HEAD_DIM)
    angles = key_positions[:, None].astype(f32) * frequency[None, :]
    cosine, sine = jnp.cos(angles), jnp.sin(angles)
    cosine, sine = jnp.concatenate([cosine, cosine], 1), jnp.concatenate([-sine, sine], 1)

    def mask_of(tile):
        span = behind + tile
        parts = []
        for start in range(0, local_rows, tile):
            keys = slice(start, start + span)
            queries = slice(behind + start, behind + start + tile)
            distance = key_positions[None, queries] - key_positions[keys, None]
            allowed = (
                (distance >= 0)
                & (distance < WINDOW)
                & (key_positions[keys, None] >= 0)
                & (key_segments[None, queries] == key_segments[keys, None])
            )
            parts.append(jnp.where(allowed, 0.0, -1e30).astype(f32))
        return jnp.stack(parts)

    operands = (
        query_lin,
        key_lin,
        value_all,
        scale_query,
        scale_key,
        gain_query[None],
        gain_key[None],
        cosine,
        sine,
    )
    bias_small = mask_of(local_rows // 4)
    mixed, lse_0 = attend(rank, operands, bias_small, 0)
    mixed, out_w, e_b, b_x, b_y, e_3, e_1, own = hold(mixed, out_w, e_b, b_x, b_y, e_3, e_1, own)

    b_0, b_1 = jnp.stack([e_b[0], b_x]), jnp.stack([e_b[1], b_y])
    b_2, b_3 = other_ways(b_0[:, :quarter_rows], b_1[:, :quarter_rows])
    e_4 = mirrored(e_3, [(2, 3)])
    mixed, lse_1 = attend(rank, operands, bias_small, HEADS // 2, (mixed,))
    branch, _ = project(mixed, *out_w, f32)
    residual = tokens.astype(f32) + branch
    moe, scale_moe = norm_rows(quarter_rank, residual, gain_moe, (0, 1, 2, 3))
    moe_y = jnp.concatenate([moe, across(moe, 1)], 1)
    piece = half // 2
    moe_x = jnp.stack(
        [
            jnp.concatenate([moe_y[0, :, i : i + piece], moe_y[1, :, i : i + piece]], 1)
            for i in (0, piece)
        ]
    )
    router_parts = weight_router.reshape(4, -1, experts)
    router_rel = jnp.concatenate([pick(router_parts, quarter ^ j, 0) for j in range(4)], 0)
    router_probs = jax.nn.softmax(
        matmul(moe[0], router_rel[:half]) + matmul(moe[1], router_rel[half:]), axis=-1
    )
    chosen = jnp.sum(
        (routes[:, :, None] == jnp.arange(experts, dtype=jnp.int32)).astype(f32), axis=1
    )
    gates = router_probs * chosen
    gates_both = jnp.concatenate([gates, across(gates, 1)], 0)
    gates_a = jnp.where(core == 0, gates_both[:, :1], gates_both[:, -1:])
    gates_b = jnp.where(core == 0, gates_both[:, 1:2], gates_both[:, -2:-1])
    b_0, b_1, b_2, b_3, e_4, e_3, e_1, own, moe_y, moe_x = hold(
        b_0, b_1, b_2, b_3, e_4, e_3, e_1, own, moe_y, moe_x
    )

    e_a = jnp.where(m == 0, own, jnp.where(m == 1, e_1, jnp.where(m == 2, e_3, e_4)))
    a_x, a_y = both_ways(e_a)
    b_4, b_5 = other_ways(b_0[:, quarter_rows:], b_1[:, quarter_rows:])
    up_weights_b, down_weights_b = (b_0, b_2, b_1, b_3), (b_0, b_4, b_1, b_5)
    gate_pre_b, up_pre_b, my_b, mx_b = experts_up(quarter_rank, moe_y, moe_x, up_weights_b)
    e_a, a_x, a_y, my_b, mx_b, moe_y, moe_x = hold(e_a, a_x, a_y, my_b, mx_b, moe_y, moe_x)

    a_0, a_1 = jnp.stack([e_a[0], a_x]), jnp.stack([e_a[1], a_y])
    a_2, a_3 = other_ways(a_0[:, :quarter_rows], a_1[:, :quarter_rows])
    a_0, a_1, a_2, a_3 = hold(a_0, a_1, a_2, a_3)

    a_4, a_5 = other_ways(a_0[:, quarter_rows:], a_1[:, quarter_rows:])
    up_weights_a, down_weights_a = (a_0, a_2, a_1, a_3), (a_0, a_4, a_1, a_5)
    gate_pre_a, up_pre_a, my_a, mx_a = experts_up(quarter_rank, moe_y, moe_x, up_weights_a)
    expert_out_a, expert_out_b, mixture, mixture_other = experts_down(
        (gates_a, gates_b), ((my_a, mx_a) + down_weights_a, (my_b, mx_b) + down_weights_b)
    )
    result = residual + (mixture + across(mixture_other, 1))
    output = result.astype(bf16)
    error = result - teacher.astype(f32)
    squares = jnp.sum(valid * jnp.sum(error * error, axis=1))
    result_grad = total_tokens / count * valid[:, None] * error
    result_other = across(result_grad, 1)

    pair_a, dg_a, du_a, gate_grad_a = experts_back(
        quarter_rank,
        result_grad,
        result_other,
        expert_out_a,
        gates_a,
        gate_pre_a,
        up_pre_a,
        down_weights_a,
    )
    sent_x = experts_grad(moe_x, dg_a, mx_a, pair_a, 1, 0)
    sent_y = experts_grad(moe_y, du_a, my_a, pair_a, 1, 1)
    sent_x, sent_y, expert_out_b = hold(sent_x, sent_y, expert_out_b)

    a_x, a_y = both_ways((sent_x, sent_y))
    pair_b, dg_b, du_b, gate_grad_b = experts_back(
        quarter_rank,
        result_grad,
        result_other,
        expert_out_b,
        gates_b,
        gate_pre_b,
        up_pre_b,
        down_weights_b,
    )
    sent_x = experts_grad(moe_x, dg_b, mx_b, pair_b, 1, 0)
    sent_y = experts_grad(moe_y, du_b, my_b, pair_b, 1, 1)
    input_grad, input_other = experts_input(
        ((dg_b, du_b) + up_weights_b, (dg_a, du_a) + up_weights_a)
    )
    slot_grads = jnp.concatenate([gate_grad_a, gate_grad_b], 1)
    own_slots, partner_slots = slot_grads[:local_rows], across(slot_grads[local_rows:], 1)
    from_low = jnp.where(core == 0, own_slots, partner_slots)
    from_high = jnp.where(core == 0, partner_slots, own_slots)
    prob_grad = chosen * jnp.concatenate([from_low, from_high[:, ::-1]], 1)
    logit_grad = router_probs * (
        prob_grad - jnp.sum(prob_grad * router_probs, axis=-1, keepdims=True)
    )
    a_x, a_y, sent_x, sent_y, input_grad, input_other, logit_grad = hold(
        a_x, a_y, sent_x, sent_y, input_grad, input_other, logit_grad
    )

    input_other = across(input_other, 1)
    b_x, b_y = both_ways((sent_x, sent_y))
    a_0 = experts_grad(moe_x, dg_a, mx_a, pair_a, 0, 0, (a_x,))
    a_1 = experts_grad(moe_y, du_a, my_a, pair_a, 0, 1, (a_y,))
    router_local = jnp.concatenate(
        [
            jnp.dot(part.T.astype(f32), logit_grad, precision=highest, preferred_element_type=f32)
            for part in (moe[0], moe[1])
        ],
        0,
    )
    router_local = router_local.reshape(4, -1, experts)
    router_local = jnp.concatenate([pick(router_local, quarter ^ j, 0) for j in range(4)], 0)
    residual_grad, branch_grad, moe_gain_local = residual_back(
        quarter_rank,
        input_grad,
        input_other,
        logit_grad,
        weight_router.astype(f32).T,
        residual,
        result_grad,
        scale_moe,
        gain_moe,
    )
    out_sent = across(chip_grad(mixed, 1, (branch_grad,)), 1)
    out_sum = chip_grad(mixed, 0, (branch_grad,), 0, (out_sent,)).reshape(2, 2, -1, width)
    mixed_grad = mixed_back(branch_grad, out_w)
    a_y, a_x = other_ways(a_0[1], a_1[1])
    bias = mask_of(local_rows // 2)
    dq_0, dk_0, dv_0 = attend_back(rank, operands, bias, mixed_grad, lse_0, 0)
    dq_1, dk_1, dv_1 = attend_back(rank, operands, bias, mixed_grad, lse_1, HEADS // 2)
    b_x, b_y, a_0, a_1, a_x, a_y, out_sum, dq_0, dk_0, dv_0, dq_1, dk_1, dv_1 = hold(
        b_x, b_y, a_0, a_1, a_x, a_y, out_sum, dq_0, dk_0, dv_0, dq_1, dk_1, dv_1
    )

    b_0 = experts_grad(moe_x, dg_b, mx_b, pair_b, 0, 0, (b_x,))
    b_1 = experts_grad(moe_y, du_b, my_b, pair_b, 0, 1, (b_y,))
    b_y, b_x = other_ways(b_0[1], b_1[1])
    out_x, out_y = across(out_sum[:, 1, :, :half], 2), across(out_sum[1, :, :, half:], 4)
    a_end = jnp.stack([add(a_0[0], a_y), add(a_1[0], a_x)])
    a_got = mirrored(a_end, [(3, 2)])
    value_sent = chip_grad(normed, 1, (dv_0, dv_1))
    value_got = across(value_sent, 1)
    value_sum = chip_grad(normed, 0, (dv_0, dv_1), 0, (value_got,)).reshape(2, 2, -1, width)
    value_x = across(value_sum[:, 1, :, :half], 2)
    value_y = across(value_sum[1, :, :, half:], 4)
    query_lin_grad, q_gain_local = lin_back(
        dq_0, dq_1, query_lin, scale_query, gain_query[None], cosine[behind:], sine[behind:]
    )
    key_lin_grad, k_gain_local = lin_back(
        dk_0, dk_1, key_lin, scale_key, gain_key[None], cosine, sine
    )
    query_sent = chip_grad(normed, 1, (query_lin_grad,), behind)
    key_sent = chip_grad(normed, 1, (key_lin_grad,))
    packed = jnp.concatenate(
        [
            jnp.broadcast_to(squares, (1, width)),
            q_gain_local,
            k_gain_local,
            moe_gain_local,
            router_local.T,
        ],
        0,
    )
    (
        b_0, b_1, b_x, b_y, out_sum, out_x, out_y, a_end, a_got, query_lin_grad, key_lin_grad,
        value_sum, value_x, value_y, query_sent, key_sent, packed,
    ) = hold(
        b_0, b_1, b_x, b_y, out_sum, out_x, out_y, a_end, a_got, query_lin_grad, key_lin_grad,
        value_sum, value_x, value_y, query_sent, key_sent, packed,
    )

    query_got, key_got = across(query_sent, 1), across(key_sent, 1)
    value_a = add(value_sum[:, 0, :, :half], value_x)
    value_b = add(value_sum[0, :, :, half:], value_y)
    for link in (1, 2, 4):
        packed = packed + across(packed, link)
    out_a, out_b = add(out_sum[:, 0, :, :half], out_x), add(out_sum[0, :, :, half:], out_y)
    value_a, value_b, packed, out_a, out_b = hold(value_a, value_b, packed, out_a, out_b)
    moved_x = across(jnp.stack([value_b[1], out_b[1]]), 2)
    moved_y = across(jnp.stack([value_a[1], out_a[1]]), 4)
    value_x, value_y, out_x, out_y = moved_x[0], moved_y[0], moved_x[1], moved_y[1]
    four = [add(out_a[0], out_y), add(out_b[0], out_x)]
    four += [add(value_a[0], value_y), add(value_b[0], value_x)]
    four = ep_sum(jnp.stack(four))
    out_total, value_total = four[:2], four[2:]
    a_low = add(a_end, a_got)
    a_got = mirrored(a_low, [(2, 1)])
    b_end = jnp.stack([add(b_0[0], b_y), add(b_1[0], b_x)])
    b_got = mirrored(b_end, [(3, 2), (0, 1)])
    normed_grad = project_back(
        key_lin_grad, dv_0, dv_1, query_lin_grad, key_w, value_w, query_w
    )
    query_sum = chip_grad(normed, 0, (query_lin_grad,), behind, (query_got,))
    key_sum = chip_grad(normed, 0, (key_lin_grad,), 0, (key_got,))
    (
        normed_grad, query_sum, key_sum, out_total, value_total, a_low, a_got, b_end, b_got, packed,
    ) = hold(
        normed_grad, query_sum, key_sum, out_total, value_total, a_low, a_got, b_end, b_got, packed,
    )

    query_sum = query_sum.reshape(2, 2, -1, width)
    key_sum = key_sum.reshape(2, 2, -1, width)
    query_x, key_y = across(query_sum[:, 1], 2), across(key_sum[1], 4)
    carried = from_behind(normed_grad[:, :local_rows].astype(bf16), "ep", -1)
    a_low = add(a_low, a_got)
    a_got = mirrored(a_low, [(1, 0)])
    b_got_2 = mirrored(add(b_end, b_got), [(2, 1)])
    query_sum, key_sum, query_x, key_y, carried, a_low, a_got, packed, b_got_2 = hold(
        query_sum, key_sum, query_x, key_y, carried, a_low, a_got, packed, b_got_2
    )

    query_sum, key_sum = add(query_sum[:, 0], query_x), add(key_sum[0], key_y)
    query_y, key_x = across(query_sum[1], 4), across(key_sum[1], 2)
    for back in range(1, reach):
        here = normed_grad[:, back * local_rows : (back + 1) * local_rows] + carried.astype(f32)
        carried = from_behind(here.astype(bf16), "ep", -1)
    b_total = (b_end.astype(f32) + b_got.astype(f32) + b_got_2.astype(f32)).astype(bf16)
    mine = jnp.where(m == 0, add(a_low, a_got), b_total)

    def own_half(piece):
        return piece.reshape(2, 2, -1, piece.shape[2])

    tops, bottoms = own_half(mine[:, :quarter_rows]), own_half(mine[:, quarter_rows:])
    halves = jnp.concatenate([tops, bottoms], 2)
    other = across(pick(halves, 1 - core, 1), 1)
    query_sum, key_sum, query_y, key_x, carried, packed, other = hold(
        query_sum, key_sum, query_y, key_x, carried, packed, other
    )

    qk_total = ep_sum(jnp.stack([add(query_sum[0], query_y), add(key_sum[0], key_x)]))
    packed = jnp.sum(over_ep(packed, place), axis=0)
    tokens_grad = tokens_back(
        rank, normed_grad, carried, tokens, residual_grad, scale_all, gain_attn, reps
    )
    mine = jnp.where(m < 2, pick(halves, core, 1), other).astype(f32)
    top = quarter_rows // 2
    down_out = jnp.concatenate([mine[0, top:], mine[1, top:]], 1)
    out_out = jnp.concatenate([out_total[0], out_total[1]], 1)
    value_out = jnp.concatenate([value_total[0], value_total[1]], 1)
    loss = packed[0, 0] / (2.0 * count * width)
    attn_gain_out = (
        jnp.sum(w_query.astype(f32) * qk_total[0], axis=1)
        + jnp.sum(w_key.astype(f32) * qk_total[1], axis=1)
        + jnp.sum(w_value.astype(f32) * value_out, axis=1)
    ) / attn_gain.astype(f32)
    shares = lax.dynamic_slice_in_dim(
        packed, (rep * experts + shard) * shard_rows, shard_rows, 1
    )
    return (
        output,
        loss,
        tokens_grad,
        attn_gain_out,
        shares[1],
        shares[2],
        shares[3],
        qk_total[0],
        qk_total[1],
        value_out,
        out_out,
        shares[4:].T,
        mine[0, :top][None],
        mine[1, :top][None],
        down_out[None],
    )


def solution(mesh):
    placed = (
        P(("rep", "ep"), None),
        P(("rep", "ep"), None),
        P("rep", "ep"),
        P("rep", "ep"),
        P(("rep", "ep"), None),
        P(("rep", "ep")),
        P(("rep", "ep")),
        P(("rep", "ep")),
        P(("rep", "ep")),
        P(("rep", "ep"), None),
        P(("rep", "ep"), None),
        P(("rep", "ep"), None),
        P(("rep", "ep"), None),
        P(("rep", "ep"), None),
        P("ep", None, None),
        P("ep", None, None),
        P("ep", None, None),
    )
    chips = mesh.shape["rep"] == 8 and mesh.shape["ep"] == 4
    return jax.shard_map(
        body if chips else body_plain,
        mesh=mesh,
        in_specs=placed,
        out_specs=(
            P(("rep", "ep"), None),
            P(),
            P(("rep", "ep"), None),
            P(("rep", "ep")),
            P(("rep", "ep")),
            P(("rep", "ep")),
            P(("rep", "ep")),
            P(("rep", "ep"), None),
            P(("rep", "ep"), None),
            P(("rep", "ep"), None),
            P(("rep", "ep"), None),
            P(("rep", "ep"), None),
            P("ep", "rep", None),
            P("ep", "rep", None),
            P("ep", "rep", None),
        ),
        check_vma=False,
    )
```

```python
import functools

import jax
import jax.numpy as jnp
from jax import lax
from jax.experimental import pallas as pl
from jax.experimental.pallas import tpu as pltpu
from jax.sharding import PartitionSpec as P

HEADS = 16
HEAD_DIM = 128
WINDOW = 1024
TOP = 2
VMEM_LIMIT = 56 * 1024 * 1024


norm_eps = 1e-05
highest = lax.Precision.HIGHEST


def from_behind(value, axis, steps):
    count = lax.axis_size(axis)
    leading, last = (max(0, -steps), min(count, count - steps))
    return lax.ppermute(value, axis, [(source, source + steps) for source in range(leading, last)])


def matmul(left, right):
    return jnp.dot(left, right, preferred_element_type=jnp.float32)


def rms_scale(value):
    return lax.rsqrt(jnp.mean(value * value, axis=-1, keepdims=True) + norm_eps)


def norm_back(value, scale, gain, grad):
    weighted = grad * gain
    inner = jnp.mean(weighted * value, axis=-1, keepdims=True)
    return (
        scale * weighted - value * (scale * scale * scale) * inner,
        jnp.sum(grad * value * scale, axis=0),
    )


def rounded(value):
    return lax.optimization_barrier(value.astype(jnp.bfloat16)).astype(jnp.float32)


def rotary_tables(positions, head_size):
    half = head_size // 2
    frequency = 10000.0 ** (-jnp.arange(half, dtype=jnp.float32) * 2.0 / head_size)
    angles = positions[:, None].astype(jnp.float32) * frequency[None, :]
    cosine = jnp.cos(angles)
    sine = jnp.sin(angles)
    return (
        jnp.concatenate([cosine, cosine], -1)[:, None, :],
        jnp.concatenate([sine, sine], -1)[:, None, :],
    )


def rotate(value, cosine, sine):
    half = value.shape[-1] // 2
    turned = jnp.concatenate([-value[..., half:], value[..., :half]], -1)
    return value * cosine + turned * sine


def rotate_back(grad, cosine, sine):
    half = grad.shape[-1] // 2
    scaled = grad * sine
    turned = jnp.concatenate([scaled[..., half:], -scaled[..., :half]], -1)
    return grad * cosine + turned


def unpack(everything):
    gains = [everything[index].astype(jnp.float32) for index in range(4)]
    return (gains, everything[4], everything[5], everything[6], everything[7], everything[8])


def body_plain(
    tokens,
    teacher,
    segment_ids,
    valid_mask,
    routes,
    attn_gain,
    q_gain,
    k_gain,
    moe_gain,
    w_query,
    w_key,
    w_value,
    w_out,
    w_router,
    w_gate,
    w_up,
    w_down,
):
    local_rows, width = tokens.shape
    experts = lax.axis_size("ep")
    pairs = local_rows * TOP
    capacity = 5 * pairs // (4 * experts)
    reach = min(-(-WINDOW // local_rows), experts - 1)
    group = min(HEADS, 4)
    score_scale = HEAD_DIM ** (-0.5)
    shard = lax.axis_index("ep")
    total_tokens = local_rows * lax.axis_size("rep") * experts
    everything = (
        lax.all_gather(attn_gain, ("rep", "ep"), axis=0, tiled=True),
        lax.all_gather(q_gain, ("rep", "ep"), axis=0, tiled=True),
        lax.all_gather(k_gain, ("rep", "ep"), axis=0, tiled=True),
        lax.all_gather(moe_gain, ("rep", "ep"), axis=0, tiled=True),
        lax.all_gather(w_query, ("rep", "ep"), axis=0, tiled=True),
        lax.all_gather(w_key, ("rep", "ep"), axis=0, tiled=True),
        lax.all_gather(w_value, ("rep", "ep"), axis=0, tiled=True),
        lax.all_gather(w_out, ("rep", "ep"), axis=0, tiled=True),
        lax.all_gather(w_router, ("rep", "ep"), axis=0, tiled=True),
    )
    gains, weight_query, weight_key, weight_value, weight_out, weight_router = unpack(everything)
    gain_attn, gain_query, gain_key, gain_moe = gains
    inputs = tokens.astype(jnp.float32)
    scale_attn = rms_scale(inputs)
    normed = (inputs * scale_attn * gain_attn).astype(jnp.bfloat16)
    query_lin = matmul(normed, weight_query)
    key_lin = matmul(normed, weight_key)
    value_rows = (
        matmul(normed, weight_value).astype(jnp.bfloat16).reshape(local_rows, HEADS, HEAD_DIM)
    )
    scale_query = rms_scale(query_lin)
    scale_key = rms_scale(key_lin)
    positions = shard * local_rows + jnp.arange(local_rows, dtype=jnp.int32)
    cosine, sine = rotary_tables(positions, HEAD_DIM)
    query_rows = rotate(
        (query_lin * scale_query * gain_query).reshape(local_rows, HEADS, HEAD_DIM), cosine, sine
    ).astype(jnp.bfloat16)
    key_rows = rotate(
        (key_lin * scale_key * gain_key).reshape(local_rows, HEADS, HEAD_DIM), cosine, sine
    ).astype(jnp.bfloat16)
    segments = segment_ids.reshape(local_rows)
    key_parts, value_parts, segment_parts = ([], [], [])
    for back in range(reach, 0, -1):
        moved = from_behind((key_rows, value_rows, segments.astype(jnp.bfloat16)), "ep", back)
        key_parts.append(moved[0])
        value_parts.append(moved[1])
        segment_parts.append(moved[2].astype(jnp.int32))
    all_keys = jnp.concatenate(key_parts + [key_rows], 0)
    all_values = jnp.concatenate(value_parts + [value_rows], 0)
    key_segments = jnp.concatenate(segment_parts + [segments], 0)
    key_positions = (shard - reach) * local_rows + jnp.arange(
        (reach + 1) * local_rows, dtype=jnp.int32
    )
    distance = positions[:, None] - key_positions[None, :]
    allowed = (
        (distance >= 0)
        & (distance < WINDOW)
        & (key_positions[None, :] >= 0)
        & (segments[:, None] == key_segments[None, :])
    )

    def by_group(value):
        return jnp.moveaxis(value.reshape(value.shape[0], HEADS // group, group, HEAD_DIM), 1, 0)

    def from_group(value):
        return jnp.moveaxis(value, 0, 1).reshape(value.shape[1], HEADS * HEAD_DIM)

    def scores_of(query_group, key_group):
        raw = (
            jnp.einsum("qhd,khd->hqk", query_group, key_group, preferred_element_type=jnp.float32)
            * score_scale
        )
        return jnp.where(allowed[None], raw, -1e30)

    def attend_forward(item):
        query_group, key_group, value_group = item
        scores = scores_of(query_group, key_group)
        peak = jnp.max(scores, axis=-1, keepdims=True)
        shifted = jnp.exp(scores - peak)
        total = jnp.sum(shifted, axis=-1, keepdims=True)
        weights = (shifted / total).astype(jnp.bfloat16)
        mixed = jnp.einsum("hqk,khd->qhd", weights, value_group, preferred_element_type=jnp.float32)
        return (mixed, peak, total)

    query_groups = by_group(query_rows)
    key_groups = by_group(all_keys)
    value_groups = by_group(all_values)
    mixed, peaks, totals = lax.map(attend_forward, (query_groups, key_groups, value_groups))
    mixed_rows = from_group(mixed).astype(jnp.bfloat16)
    residual = inputs + matmul(mixed_rows, weight_out)
    scale_moe = rms_scale(residual)
    normed_moe = (residual * scale_moe * gain_moe).astype(jnp.bfloat16)
    router_probs = jax.nn.softmax(matmul(normed_moe, weight_router), axis=-1)
    flat_routes = routes.reshape(pairs)
    choose = (flat_routes[:, None] == jnp.arange(experts, dtype=jnp.int32)[None, :]).astype(
        jnp.int32
    )
    rank = jnp.sum((jnp.cumsum(choose, axis=0) - choose) * choose, axis=1)
    slots = flat_routes * capacity + rank
    pair_source = (
        jnp.full((experts * capacity,), pairs, jnp.int32)
        .at[slots]
        .set(jnp.arange(pairs, dtype=jnp.int32))
    )
    token_source = jnp.where(pair_source < pairs, pair_source // TOP, local_rows)
    zero_row = jnp.zeros((1, width), jnp.bfloat16)
    outgoing = jnp.concatenate([normed_moe, zero_row], 0)[token_source].reshape(
        experts, capacity, width
    )
    choose_float = choose.reshape(local_rows, TOP, experts).astype(jnp.float32)
    gate_value = jnp.sum(choose_float * router_probs[:, None, :], axis=2)
    gate_weight = w_gate[0]
    up_weight = w_up[0]
    down_weight = w_down[0]
    piece = lax.all_to_all(outgoing, "ep", split_axis=0, concat_axis=0, tiled=True)
    flat = piece.reshape(-1, width)
    gate_pre = matmul(flat, gate_weight)
    up_pre = matmul(flat, up_weight)
    middle = (jax.nn.silu(gate_pre) * up_pre).astype(jnp.bfloat16)
    expert_out = matmul(middle, down_weight).astype(jnp.bfloat16)
    lead = piece.shape[:2]
    returned = expert_out.reshape(piece.shape)
    gate_kept = gate_pre.reshape(lead + (-1,))
    up_kept = up_pre.reshape(lead + (-1,))
    arrived = lax.all_to_all(returned, "ep", split_axis=0, concat_axis=0, tiled=True)
    expert_rows = arrived.reshape(experts * capacity, width)[slots].reshape(local_rows, TOP, width)
    result = residual + jnp.sum(gate_value[:, :, None] * expert_rows, axis=1)
    output = result.astype(jnp.bfloat16)
    valid = valid_mask.reshape(local_rows).astype(jnp.float32)
    error = result - teacher.astype(jnp.float32)
    squares = jnp.sum(valid * jnp.sum(error * error, axis=1))
    total_squares, count = lax.psum((squares, jnp.sum(valid)), ("rep", "ep"))
    loss = total_squares / (2.0 * count * width)
    result_grad = total_tokens / count * valid[:, None] * error
    gate_value_grad = jnp.sum(result_grad[:, None, :] * expert_rows, axis=2)
    pair_grad = (
        (gate_value[:, :, None] * result_grad[:, None, :])
        .astype(jnp.bfloat16)
        .reshape(pairs, width)
    )
    grad_outgoing = jnp.concatenate([pair_grad, zero_row], 0)[pair_source].reshape(
        experts, capacity, width
    )
    grad_in = lax.all_to_all(grad_outgoing, "ep", split_axis=0, concat_axis=0, tiled=True)
    rows_in = piece.reshape(-1, width)
    gate_pre = gate_kept.reshape(rows_in.shape[0], -1)
    up_pre = up_kept.reshape(rows_in.shape[0], -1)
    flat_grad = grad_in.reshape(-1, width)
    sigma = jax.nn.sigmoid(gate_pre)
    active = gate_pre * sigma
    middle = (active * up_pre).astype(jnp.bfloat16)
    down_local = matmul(middle.T, flat_grad)
    middle_grad = matmul(flat_grad, down_weight.T)
    gate_pre_grad = (middle_grad * up_pre * sigma * (1.0 + gate_pre * (1.0 - sigma))).astype(
        jnp.bfloat16
    )
    up_pre_grad = (middle_grad * active).astype(jnp.bfloat16)
    gate_local = matmul(rows_in.T, gate_pre_grad)
    up_local = matmul(rows_in.T, up_pre_grad)
    input_grad = (matmul(gate_pre_grad, gate_weight.T) + matmul(up_pre_grad, up_weight.T)).astype(
        jnp.bfloat16
    )
    back_rows = lax.all_to_all(
        input_grad.reshape(experts, capacity, width), "ep", split_axis=0, concat_axis=0, tiled=True
    )
    pair_back = back_rows.reshape(experts * capacity, width)[slots].reshape(local_rows, TOP, width)
    everything = (
        lax.all_gather(attn_gain, ("rep", "ep"), axis=0, tiled=True),
        lax.all_gather(q_gain, ("rep", "ep"), axis=0, tiled=True),
        lax.all_gather(k_gain, ("rep", "ep"), axis=0, tiled=True),
        lax.all_gather(moe_gain, ("rep", "ep"), axis=0, tiled=True),
        lax.all_gather(w_query, ("rep", "ep"), axis=0, tiled=True),
        lax.all_gather(w_key, ("rep", "ep"), axis=0, tiled=True),
        lax.all_gather(w_value, ("rep", "ep"), axis=0, tiled=True),
        lax.all_gather(w_out, ("rep", "ep"), axis=0, tiled=True),
        lax.all_gather(w_router, ("rep", "ep"), axis=0, tiled=True),
    )
    gains, weight_query, weight_key, weight_value, weight_out, weight_router = unpack(everything)
    gain_attn, gain_query, gain_key, gain_moe = gains
    prob_grad = jnp.sum(choose_float * gate_value_grad[:, :, None], axis=1)
    logit_grad = router_probs * (
        prob_grad - jnp.sum(prob_grad * router_probs, axis=-1, keepdims=True)
    )
    router_local = jnp.dot(
        normed_moe.T, logit_grad, precision=highest, preferred_element_type=jnp.float32
    )
    normed_moe_grad = jnp.sum(pair_back.astype(jnp.float32), axis=1) + jnp.dot(
        logit_grad, weight_router.T, precision=highest, preferred_element_type=jnp.float32
    )
    residual_part, moe_gain_local = norm_back(residual, scale_moe, gain_moe, normed_moe_grad)
    residual_grad = result_grad + residual_part
    branch_grad = residual_grad.astype(jnp.bfloat16)
    out_local = matmul(mixed_rows.T, branch_grad)
    mixed_grad = (
        matmul(branch_grad, weight_out.T).astype(jnp.bfloat16).reshape(local_rows, HEADS, HEAD_DIM)
    )

    def attend_backward(item):
        query_group, key_group, value_group, grad_group, peak, total = item
        scores = scores_of(query_group, key_group)
        probs = jnp.exp(scores - peak) / total
        weights = probs.astype(jnp.bfloat16)
        value_part = jnp.einsum(
            "hqk,qhd->khd", weights, grad_group, preferred_element_type=jnp.float32
        )
        probs_grad = jnp.einsum(
            "qhd,khd->hqk", grad_group, value_group, preferred_element_type=jnp.float32
        )
        inner = jnp.sum(probs * probs_grad, axis=-1, keepdims=True)
        score_grad = (probs * (probs_grad - inner)).astype(jnp.bfloat16)
        query_part = (
            jnp.einsum("hqk,khd->qhd", score_grad, key_group, preferred_element_type=jnp.float32)
            * score_scale
        )
        key_part = (
            jnp.einsum("hqk,qhd->khd", score_grad, query_group, preferred_element_type=jnp.float32)
            * score_scale
        )
        return (query_part, key_part, value_part)

    query_parts, key_parts_grad, value_parts_grad = lax.map(
        attend_backward,
        (query_groups, key_groups, value_groups, by_group(mixed_grad), peaks, totals),
    )
    query_row_grad = from_group(query_parts)
    key_all_grad = from_group(key_parts_grad)
    value_all_grad = from_group(value_parts_grad)
    own_keys = key_all_grad[reach * local_rows :]
    own_values = value_all_grad[reach * local_rows :]
    for back in range(1, reach + 1):
        start = (reach - back) * local_rows
        moved = from_behind(
            (key_all_grad[start : start + local_rows], value_all_grad[start : start + local_rows]),
            "ep",
            -back,
        )
        own_keys = own_keys + moved[0]
        own_values = own_values + moved[1]
    query_turned = rotate_back(
        rounded(query_row_grad).reshape(local_rows, HEADS, HEAD_DIM), cosine, sine
    ).reshape(local_rows, width)
    key_turned = rotate_back(
        rounded(own_keys).reshape(local_rows, HEADS, HEAD_DIM), cosine, sine
    ).reshape(local_rows, width)
    query_lin_grad, q_gain_local = norm_back(query_lin, scale_query, gain_query, query_turned)
    key_lin_grad, k_gain_local = norm_back(key_lin, scale_key, gain_key, key_turned)
    query_lin_grad = query_lin_grad.astype(jnp.bfloat16)
    key_lin_grad = key_lin_grad.astype(jnp.bfloat16)
    value_row_grad = own_values.astype(jnp.bfloat16)
    query_local = matmul(normed.T, query_lin_grad)
    key_local = matmul(normed.T, key_lin_grad)
    value_local = matmul(normed.T, value_row_grad)
    normed_grad = (
        matmul(query_lin_grad, weight_query.T)
        + matmul(key_lin_grad, weight_key.T)
        + matmul(value_row_grad, weight_value.T)
    )
    inputs_part, attn_gain_local = norm_back(inputs, scale_attn, gain_attn, normed_grad)
    tokens_grad = residual_grad + inputs_part
    summed = (
        lax.psum_scatter(attn_gain_local, ("rep", "ep"), scatter_dimension=0, tiled=True),
        lax.psum_scatter(q_gain_local, ("rep", "ep"), scatter_dimension=0, tiled=True),
        lax.psum_scatter(k_gain_local, ("rep", "ep"), scatter_dimension=0, tiled=True),
        lax.psum_scatter(moe_gain_local, ("rep", "ep"), scatter_dimension=0, tiled=True),
        lax.psum_scatter(query_local, ("rep", "ep"), scatter_dimension=0, tiled=True),
        lax.psum_scatter(key_local, ("rep", "ep"), scatter_dimension=0, tiled=True),
        lax.psum_scatter(value_local, ("rep", "ep"), scatter_dimension=0, tiled=True),
        lax.psum_scatter(out_local, ("rep", "ep"), scatter_dimension=0, tiled=True),
        lax.psum_scatter(router_local, ("rep", "ep"), scatter_dimension=0, tiled=True),
    )
    expert_summed = (
        lax.psum_scatter(gate_local[None], "rep", scatter_dimension=1, tiled=True),
        lax.psum_scatter(up_local[None], "rep", scatter_dimension=1, tiled=True),
        lax.psum_scatter(down_local[None], "rep", scatter_dimension=1, tiled=True),
    )
    return (
        output,
        loss,
        tokens_grad,
        summed[0],
        summed[1],
        summed[2],
        summed[3],
        summed[4],
        summed[5],
        summed[6],
        summed[7],
        summed[8],
        expert_summed[0],
        expert_summed[1],
        expert_summed[2],
    )


def dot_t(left, right):
    return lax.dot_general(left, right, (((1,), (1,)), ((), ())), preferred_element_type=jnp.float32)


def t_dot(left, right):
    return lax.dot_general(left, right, (((0,), (0,)), ((), ())), preferred_element_type=jnp.float32)


def kernel_call(kernel, **options):
    return pl.pallas_call(
        kernel,
        compiler_params=pltpu.CompilerParams(vmem_limit_bytes=VMEM_LIMIT),
        **options,
    )


def turn(value, cosine, sine):
    return value * cosine + pltpu.roll(value, HEAD_DIM // 2, 1) * sine


def code_of(place, blocks):
    return place % (blocks // 2) * 2 + place // (blocks // 2)


def place_of(code, blocks):
    return code % 2 * (blocks // 2) + code // 2


def norm_kernel(rank, x_ref, gain_ref, o_ref, scale_ref, *, codes):
    value = x_ref[...].astype(jnp.float32)
    scale = lax.rsqrt(jnp.mean(value * value, axis=1, keepdims=True) + norm_eps)
    scale_ref[...] = scale
    half = len(codes) // 2
    block = x_ref.shape[1] // len(codes)
    for place, code in enumerate(codes):
        start = pl.multiple_of((rank[0] ^ code) * block, block)
        piece = x_ref[:, pl.ds(start, block)].astype(jnp.float32)
        piece = piece * scale * gain_ref[:, pl.ds(start, block)]
        at = place % half * block
        o_ref[place // half, :, at : at + block] = piece.astype(jnp.bfloat16)


def norm_rows(rank, value, gain, codes):
    rows, width = value.shape
    tile = 256
    return kernel_call(
        functools.partial(norm_kernel, codes=codes),
        grid_spec=pltpu.PrefetchScalarGridSpec(
            num_scalar_prefetch=1,
            grid=(rows // tile,),
            in_specs=[
                pl.BlockSpec((tile, width), lambda i, rank: (i, 0)),
                pl.BlockSpec((1, width), lambda i, rank: (0, 0)),
            ],
            out_specs=[
                pl.BlockSpec((2, tile, width // 2), lambda i, rank: (0, i, 0)),
                pl.BlockSpec((tile, 1), lambda i, rank: (i, 0)),
            ],
        ),
        out_shape=[
            jax.ShapeDtypeStruct((2, rows, width // 2), jnp.bfloat16),
            jax.ShapeDtypeStruct((rows, 1), jnp.float32),
        ],
    )(rank, value, gain[None])


def project_kernel(low_ref, high_ref, a_ref, b_ref, o_ref, s_ref):
    total = matmul(low_ref[0], a_ref[...]) + matmul(high_ref[0], b_ref[...])
    o_ref[...] = total.astype(o_ref.dtype)
    s_ref[...] = jnp.sum(total * total, axis=1, keepdims=True)


def project(halves, a, b, dtype, start=0):
    _, rows, depth = halves.shape
    rows = rows - start
    width = a.shape[1]
    tile = 256
    first = start // tile
    weight = pl.BlockSpec((depth, width), lambda i: (0, 0))
    return kernel_call(
        project_kernel,
        grid=(rows // tile,),
        in_specs=[
            pl.BlockSpec((1, tile, depth), lambda i: (0, i + first, 0)),
            pl.BlockSpec((1, tile, depth), lambda i: (1, i + first, 0)),
            weight,
            weight,
        ],
        out_specs=[
            pl.BlockSpec((tile, width), lambda i: (i, 0)),
            pl.BlockSpec((tile, 1), lambda i: (i, 0)),
        ],
        out_shape=[
            jax.ShapeDtypeStruct((rows, width), dtype),
            jax.ShapeDtypeStruct((rows, 1), jnp.float32),
        ],
    )(halves, halves, a, b)


def project_back_kernel(k_ref, v_ref, w_ref, q_ref, ka, kb, va, vb, qa, qb, o_ref, *, tile):
    j = pl.program_id(0)
    half = pl.num_programs(0) // 2
    half_width = v_ref.shape[1]
    own = k_ref.shape[0] - q_ref.shape[0]

    def part(key, value, query):
        for start in range(0, k_ref.shape[0], tile):
            at = slice(start, start + tile)
            total = dot_t(k_ref[at, :], key[...]) + dot_t(v_ref[at, :], value[:, :half_width])
            total += dot_t(w_ref[at, :], value[:, half_width:])
            if start >= own:
                total += dot_t(q_ref[start - own : start - own + tile, :], query[...])
            o_ref[0, at, :] = total

    @pl.when(j < half)
    def _():
        part(ka, va, qa)

    @pl.when(j >= half)
    def _():
        part(kb, vb, qb)


def project_back(key, value, value_high, query, key_w, value_w, query_w):
    rows, width = key.shape
    depth = value_w[0].shape[0]
    step = 256
    half = depth // step
    whole = lambda value: pl.BlockSpec(value.shape, lambda j: (0, 0), pipeline_mode=pl.Buffered(1))
    low = pl.BlockSpec((step, width), lambda j: (jnp.minimum(j, half - 1), 0))
    high = pl.BlockSpec((step, width), lambda j: (jnp.maximum(j - half, 0), 0))
    return kernel_call(
        functools.partial(project_back_kernel, tile=512),
        grid=(2 * half,),
        in_specs=[whole(key), whole(value), whole(value_high), whole(query)] + [low, high] * 3,
        out_specs=pl.BlockSpec((1, rows, step), lambda j: (j // half, 0, j % half)),
        out_shape=jax.ShapeDtypeStruct((2, rows, depth), jnp.float32),
    )(key, value, value_high, query, *key_w, *value_w, *query_w)


def tokens_back_kernel(
    rank, g_ref, c_ref, x_ref, res_ref, scale_ref, gain_ref, o_ref, *, blocks
):
    scale = scale_ref[...]
    block = x_ref.shape[1] // blocks
    half = blocks // 2

    def pieces(place):
        start = pl.multiple_of((rank[0] ^ code_of(place, blocks)) * block, block)
        at = slice(place % half * block, place % half * block + block)
        grad = g_ref[place // half, :, at] + c_ref[place // half, :, at].astype(jnp.float32)
        columns = pl.ds(start, block)
        return columns, grad, x_ref[:, columns].astype(jnp.float32), gain_ref[:, columns]

    inner = jnp.zeros_like(scale)
    for place in range(blocks):
        columns, grad, value, gain = pieces(place)
        inner += jnp.sum(grad * value * gain, axis=1, keepdims=True)
    inner = inner * (1.0 / x_ref.shape[1]) * (scale * scale * scale)
    for place in range(blocks):
        columns, grad, value, gain = pieces(place)
        o_ref[:, columns] = res_ref[:, columns] + (scale * (grad * gain) - value * inner)


def tokens_back(rank, grad, carried, tokens, residual_grad, scale, gain, blocks):
    rows, width = tokens.shape
    tile = 128
    first = (grad.shape[1] - rows) // tile
    wide = pl.BlockSpec((tile, width), lambda i, rank: (i, 0))
    one = pl.BlockSpec((1, width), lambda i, rank: (0, 0))
    return kernel_call(
        functools.partial(tokens_back_kernel, blocks=blocks),
        grid_spec=pltpu.PrefetchScalarGridSpec(
            num_scalar_prefetch=1,
            grid=(rows // tile,),
            in_specs=[
                pl.BlockSpec((2, tile, width // 2), lambda i, rank: (0, i + first, 0)),
                pl.BlockSpec((2, tile, width // 2), lambda i, rank: (0, i, 0)),
                wide,
                wide,
                pl.BlockSpec((tile, 1), lambda i, rank: (i + first, 0)),
                one,
            ],
            out_specs=wide,
        ),
        out_shape=jax.ShapeDtypeStruct((rows, width), jnp.float32),
    )(rank, grad, carried, tokens, residual_grad, scale, gain[None])


def head_rows(lin, scale, gain, cosine, sine):
    return turn(lin * scale * gain, cosine, sine).astype(jnp.bfloat16)


def moved_head(head, rank):
    place = place_of((head // 2) ^ rank[0], HEADS // 2) * 2 + head % 2
    return place // (HEADS // 2), 0, place % (HEADS // 2)


def attention_specs(rows, all_rows, bias, first=0):
    head = lambda h, rank: (0, h + first)
    fixed = lambda h, rank: (0, 0)
    return [
        pl.BlockSpec((rows, HEAD_DIM), head),
        pl.BlockSpec((all_rows, HEAD_DIM), head),
        pl.BlockSpec((all_rows, HEAD_DIM), head),
        pl.BlockSpec((rows, 1), fixed),
        pl.BlockSpec((all_rows, 1), fixed),
        pl.BlockSpec((1, HEAD_DIM), head),
        pl.BlockSpec((1, HEAD_DIM), head),
        pl.BlockSpec((all_rows, HEAD_DIM), fixed),
        pl.BlockSpec((all_rows, HEAD_DIM), fixed),
        pl.BlockSpec(bias.shape, lambda h, rank: (0, 0, 0)),
    ]


def attend_kernel(
    rank,
    q_ref,
    k_ref,
    v_ref,
    sq_ref,
    sk_ref,
    gq_ref,
    gk_ref,
    cos_ref,
    sin_ref,
    bias_ref,
    *refs,
    behind,
    tile,
    span,
):
    o_ref, lse_ref = refs[-2:]
    rows = q_ref.shape[0]
    cosine, sine = cos_ref[...], sin_ref[...]
    keys = head_rows(k_ref[...], sk_ref[...], gk_ref[...], cosine, sine)
    queries = head_rows(q_ref[...], sq_ref[...], gq_ref[...], cosine[behind:], sine[behind:])
    for t in range(rows // tile):
        at = slice(t * tile, (t + 1) * tile)
        seen = slice(t * tile, t * tile + span)
        scores = dot_t(keys[seen], queries[at])
        scores = scores * HEAD_DIM ** (-0.5) + bias_ref[t].astype(jnp.float32)
        peak = jnp.max(scores, axis=0, keepdims=True)
        shifted = jnp.exp(scores - peak)
        total = jnp.sum(shifted, axis=0, keepdims=True)
        weights = (shifted * (1.0 / total)).astype(jnp.bfloat16)
        o_ref[0, at, :] = t_dot(weights, v_ref[seen, :]).astype(jnp.bfloat16)
        lse_ref[0, :, at] = peak + jnp.log(total)


def attend(rank, operands, bias, first, into=()):
    rows, width = operands[0].shape
    all_rows = operands[1].shape[0]
    tiles, span, tile = bias.shape
    return kernel_call(
        functools.partial(attend_kernel, behind=all_rows - rows, tile=tile, span=span),
        grid_spec=pltpu.PrefetchScalarGridSpec(
            num_scalar_prefetch=1,
            grid=(HEADS // 2,),
            in_specs=attention_specs(rows, all_rows, bias, first)
            + [pl.BlockSpec(memory_space=pl.ANY)] * len(into),
            out_specs=[
                pl.BlockSpec((1, rows, HEAD_DIM), lambda h, rank: moved_head(h + first, rank)),
                pl.BlockSpec((1, 1, rows), lambda h, rank: (h, 0, 0)),
            ],
        ),
        input_output_aliases={2 + len(operands): 0} if into else {},
        out_shape=[
            jax.ShapeDtypeStruct((2, rows, width // 2), jnp.bfloat16),
            jax.ShapeDtypeStruct((HEADS // 2, 1, rows), jnp.float32),
        ],
    )(rank, *operands, bias, *into)


def attend_back_kernel(
    rank,
    q_ref,
    k_ref,
    v_ref,
    sq_ref,
    sk_ref,
    gq_ref,
    gk_ref,
    cos_ref,
    sin_ref,
    bias_ref,
    g_ref,
    lse_ref,
    dq_ref,
    dk_ref,
    dv_ref,
    key_total,
    value_total,
    *,
    behind,
    tile,
    span,
):
    rows = q_ref.shape[0]
    score_scale = HEAD_DIM ** (-0.5)
    cosine, sine = cos_ref[...], sin_ref[...]
    keys = head_rows(k_ref[...], sk_ref[...], gk_ref[...], cosine, sine)
    queries = head_rows(q_ref[...], sq_ref[...], gq_ref[...], cosine[behind:], sine[behind:])
    key_total[...] = jnp.zeros_like(key_total)
    value_total[...] = jnp.zeros_like(value_total)
    for t in range(rows // tile):
        at = slice(t * tile, (t + 1) * tile)
        seen = slice(t * tile, t * tile + span)
        scores = dot_t(keys[seen], queries[at])
        scores = scores * score_scale + bias_ref[t].astype(jnp.float32)
        probs = jnp.exp(scores - lse_ref[0, :, at])
        grad = g_ref[0, at, :]
        value_total[seen, :] += matmul(probs.astype(jnp.bfloat16), grad)
        probs_grad = dot_t(v_ref[seen, :], grad)
        inner = jnp.sum(probs * probs_grad, axis=0, keepdims=True)
        score_grad = (probs * (probs_grad - inner)).astype(jnp.bfloat16)
        dq_ref[at, :] = (t_dot(score_grad, keys[seen]) * score_scale).astype(jnp.bfloat16)
        key_total[seen, :] += matmul(score_grad, queries[at])
    dk_ref[...] = (key_total[...] * score_scale).astype(jnp.bfloat16)
    dv_ref[...] = value_total[...].astype(jnp.bfloat16)


def attend_back(rank, operands, bias, grad, lse, first):
    rows, width = operands[0].shape
    width = width // 2
    all_rows = operands[1].shape[0]
    tiles, span, tile = bias.shape
    head = lambda h, rank: (0, h)
    return kernel_call(
        functools.partial(attend_back_kernel, behind=all_rows - rows, tile=tile, span=span),
        grid_spec=pltpu.PrefetchScalarGridSpec(
            num_scalar_prefetch=1,
            grid=(HEADS // 2,),
            in_specs=attention_specs(rows, all_rows, bias, first)
            + [
                pl.BlockSpec((1, rows, HEAD_DIM), lambda h, rank: moved_head(h + first, rank)),
                pl.BlockSpec((1, 1, rows), lambda h, rank: (h, 0, 0)),
            ],
            out_specs=[
                pl.BlockSpec((rows, HEAD_DIM), head),
                pl.BlockSpec((all_rows, HEAD_DIM), head),
                pl.BlockSpec((all_rows, HEAD_DIM), head),
            ],
            scratch_shapes=[
                pltpu.VMEM((all_rows, HEAD_DIM), jnp.float32),
                pltpu.VMEM((all_rows, HEAD_DIM), jnp.float32),
            ],
        ),
        out_shape=[
            jax.ShapeDtypeStruct((rows, width), jnp.bfloat16),
            jax.ShapeDtypeStruct((all_rows, width), jnp.bfloat16),
            jax.ShapeDtypeStruct((all_rows, width), jnp.bfloat16),
        ],
    )(rank, *operands, bias, grad, lse)


def lin_back_kernel(
    low_ref, high_ref, lin_ref, scale_ref, gain_ref, cos_ref, sin_ref, o_ref, gain_grad_ref, kept
):
    rows = scale_ref.shape[0]
    scale = jnp.broadcast_to(scale_ref[...], (rows, HEAD_DIM))
    cosine, sine = cos_ref[...], -sin_ref[...]

    @pl.when(pl.program_id(0) == 0)
    def _():
        gain_grad_ref[...] = jnp.zeros_like(gain_grad_ref)

    inner = jnp.zeros((rows, HEAD_DIM), jnp.float32)
    for h in range(HEADS):
        at = slice(h * HEAD_DIM, (h + 1) * HEAD_DIM)
        ref = low_ref if h < HEADS // 2 else high_ref
        here = slice(h % (HEADS // 2) * HEAD_DIM, (h % (HEADS // 2) + 1) * HEAD_DIM)
        grad = turn(ref[:, here].astype(jnp.float32), cosine, sine)
        product = grad * lin_ref[:, at]
        gain = gain_ref[:, at]
        gain_grad_ref[:, at] += jnp.sum(product * scale, axis=0, keepdims=True)
        inner += product * gain
        kept[:, at] = grad * gain * scale
    inner = jnp.sum(inner, axis=1, keepdims=True) * (1.0 / (HEADS * HEAD_DIM))
    inner = jnp.broadcast_to(inner, (rows, HEAD_DIM)) * (scale * scale * scale)
    for h in range(HEADS):
        at = slice(h * HEAD_DIM, (h + 1) * HEAD_DIM)
        o_ref[:, at] = (kept[:, at] - lin_ref[:, at] * inner).astype(jnp.bfloat16)


def lin_back(low, high, lin, scale, gain, cosine, sine):
    rows, width = lin.shape
    tile = 256
    wide = pl.BlockSpec((tile, width), lambda i: (i, 0))
    one = pl.BlockSpec((1, width), lambda i: (0, 0))
    half = pl.BlockSpec((tile, width // 2), lambda i: (i, 0))
    table = pl.BlockSpec((tile, HEAD_DIM), lambda i: (i, 0))
    return kernel_call(
        lin_back_kernel,
        grid=(rows // tile,),
        in_specs=[half, half, wide, pl.BlockSpec((tile, 1), lambda i: (i, 0)), one, table, table],
        out_specs=[wide, one],
        scratch_shapes=[pltpu.VMEM((tile, width), jnp.float32)],
        out_shape=[
            jax.ShapeDtypeStruct((rows, width), jnp.bfloat16),
            jax.ShapeDtypeStruct((1, width), jnp.float32),
        ],
    )(low, high, lin, scale, gain, cosine, sine)


def flat(ref):
    return ref[...].reshape(-1, ref.shape[-1])


def gu_spec(weights, rows):
    return pl.BlockSpec((2, rows, weights.shape[2]), lambda i, *_: (0, 0, 0))


def d_spec(weights, rows):
    last = weights.shape[1] // rows - 1
    return pl.BlockSpec((2, rows, weights.shape[2]), lambda i, *_: (0, last, 0))


def dynamic_block(index, block):
    return pl.ds(pl.multiple_of(index * block, block), block)


def experts_up_kernel(rank, x_ref, z_ref, ga, gb, ua, ub, g_ref, u_ref, my_ref, mx_ref, middle_ref):
    gate = matmul(x_ref[0], flat(ga)) + matmul(x_ref[1], flat(gb))
    up = matmul(z_ref[0], flat(ua)) + matmul(z_ref[1], flat(ub))
    g_ref[...] = gate
    u_ref[...] = up
    middle_ref[...] = (gate * jax.nn.sigmoid(gate) * up).astype(jnp.bfloat16)
    block = gate.shape[1] // 4
    for j in range(4):
        piece = middle_ref[:, dynamic_block(rank[0] ^ j, block)]
        dy, dx = j // 2, j % 2
        my_ref[dy, :, dx * block : (dx + 1) * block] = piece
        mx_ref[dx, :, dy * block : (dy + 1) * block] = piece


def experts_up(rank, by_y, by_x, weights):
    _, rows, depth = by_y.shape
    hidden = weights[0].shape[2]
    tile = 256
    x_spec = pl.BlockSpec((2, tile, depth), lambda i, rank: (0, i, 0))
    w_specs = [gu_spec(weight, depth // 2) for weight in weights]
    wide = pl.BlockSpec((tile, hidden), lambda i, rank: (i, 0))
    half = pl.BlockSpec((2, tile, hidden // 2), lambda i, rank: (0, i, 0))
    return kernel_call(
        experts_up_kernel,
        grid_spec=pltpu.PrefetchScalarGridSpec(
            num_scalar_prefetch=1,
            grid=(rows // tile,),
            in_specs=[x_spec, x_spec] + w_specs,
            out_specs=[wide, wide, half, half],
            scratch_shapes=[pltpu.VMEM((tile, hidden), jnp.bfloat16)],
        ),
        out_shape=[jax.ShapeDtypeStruct((rows, hidden), jnp.float32)] * 2
        + [jax.ShapeDtypeStruct((2, rows, hidden // 2), jnp.bfloat16)] * 2,
    )(rank, by_y, by_x, *weights)


def experts_down_kernel(*refs):
    gates, slots, outs = refs[:2], (refs[2:8], refs[8:14]), refs[14:]
    half = outs[0].shape[1] // 2
    mixtures = []
    for side in range(2):
        at = slice(side * half, (side + 1) * half)
        mixture = 0.0
        for slot, (my, mx, la, lb, ra, rb) in enumerate(slots):
            if side == 0:
                out = matmul(my[0], flat(la)) + matmul(my[1], flat(lb))
            else:
                out = matmul(mx[0], flat(ra)) + matmul(mx[1], flat(rb))
            out = out.astype(jnp.bfloat16)
            outs[slot][:, at] = out
            mixture += gates[slot][...] * out.astype(jnp.float32)
        mixtures.append(mixture)

    @pl.when(pl.program_id(0) < pl.num_programs(0) // 2)
    def _():
        outs[2][:, :half], outs[2][:, half:] = mixtures

    @pl.when(pl.program_id(0) >= pl.num_programs(0) // 2)
    def _():
        outs[3][:, :half], outs[3][:, half:] = mixtures


def experts_down(gates, slots):
    _, rows, depth = slots[0][0].shape
    half = slots[0][2].shape[2]
    tile = 256
    x_spec = pl.BlockSpec((2, tile, depth), lambda i: (0, i, 0))
    w_specs = [d_spec(weight, depth // 2) for weight in slots[0][2:]]
    wide = pl.BlockSpec((tile, 2 * half), lambda i: (i, 0))
    column = pl.BlockSpec((tile, 1), lambda i: (i, 0))
    steps = rows // tile // 2
    return kernel_call(
        experts_down_kernel,
        grid=(rows // tile,),
        in_specs=[column] * 2 + ([x_spec] * 2 + w_specs) * 2,
        out_specs=[
            wide,
            wide,
            pl.BlockSpec((tile, 2 * half), lambda i: (jnp.minimum(i, steps - 1), 0)),
            pl.BlockSpec((tile, 2 * half), lambda i: (jnp.maximum(i - steps, 0), 0)),
        ],
        out_shape=[
            jax.ShapeDtypeStruct((rows, 2 * half), jnp.bfloat16),
            jax.ShapeDtypeStruct((rows, 2 * half), jnp.bfloat16),
            jax.ShapeDtypeStruct((rows // 2, 2 * half), jnp.float32),
            jax.ShapeDtypeStruct((rows // 2, 2 * half), jnp.float32),
        ],
    )(*gates, *slots[0], *slots[1])


def experts_back_kernel(
    rank, own_ref, other_ref, out_ref, gate_ref, g_ref, u_ref, la, lb, ra, rb, p_ref, dg_ref, du_ref, gg_ref
):
    own = pl.program_id(0) < pl.num_programs(0) // 2
    grad = jnp.where(own, own_ref[...], other_ref[...])
    gg_ref[...] = jnp.sum(grad * out_ref[...].astype(jnp.float32), axis=1, keepdims=True)
    p_ref[...] = (gate_ref[...] * grad).astype(jnp.bfloat16)
    half = grad.shape[1] // 2
    left, right = p_ref[:, :half], p_ref[:, half:]
    block = la.shape[1]
    for j in range(4):
        dy, dx = j // 2, j % 2
        left_w = (la, lb)[dy][dx]
        right_w = (ra, rb)[dx][dy]
        middle_grad = dot_t(left, left_w) + dot_t(right, right_w)
        at = dynamic_block(rank[0] ^ j, block)
        gate_pre, up_pre = g_ref[:, at], u_ref[:, at]
        sigma = jax.nn.sigmoid(gate_pre)
        change = middle_grad * up_pre * sigma * (1.0 + gate_pre * (1.0 - sigma))
        dg_ref[:, at] = change.astype(jnp.bfloat16)
        du_ref[:, at] = (middle_grad * (gate_pre * sigma)).astype(jnp.bfloat16)


def experts_back(rank, own, other, out, gate, gate_pre, up_pre, weights):
    rows, width = out.shape
    hidden = gate_pre.shape[1]
    tile = 256
    wide = pl.BlockSpec((tile, width), lambda i, rank: (i, 0))
    narrow = pl.BlockSpec((tile, hidden), lambda i, rank: (i, 0))
    column = pl.BlockSpec((tile, 1), lambda i, rank: (i, 0))
    w_specs = [d_spec(weight, hidden // 4) for weight in weights]
    steps = rows // tile // 2
    return kernel_call(
        experts_back_kernel,
        grid_spec=pltpu.PrefetchScalarGridSpec(
            num_scalar_prefetch=1,
            grid=(rows // tile,),
            in_specs=[
                pl.BlockSpec((tile, width), lambda i, rank: (jnp.minimum(i, steps - 1), 0)),
                pl.BlockSpec((tile, width), lambda i, rank: (jnp.maximum(i - steps, 0), 0)),
                wide, column, narrow, narrow
            ] + w_specs,
            out_specs=[wide, narrow, narrow, column],
        ),
        out_shape=[
            jax.ShapeDtypeStruct((rows, width), jnp.bfloat16),
            jax.ShapeDtypeStruct((rows, hidden), jnp.bfloat16),
            jax.ShapeDtypeStruct((rows, hidden), jnp.bfloat16),
            jax.ShapeDtypeStruct((rows, 1), jnp.float32),
        ],
    )(rank, own, other, out, gate, gate_pre, up_pre, *weights)


def experts_input_kernel(*refs):
    totals = []
    for j in range(4):
        dy, dx = j // 2, j % 2
        total = 0.0
        for dg, du, ga, gb, ua, ub in (refs[:6], refs[6:12]):
            gate_w = (ga, gb)[dy][dx]
            up_w = (ua, ub)[dx][dy]
            part = dot_t(dg[...], gate_w) + dot_t(du[...], up_w)
            total += part.astype(jnp.bfloat16).astype(jnp.float32)
        totals.append(total)

    @pl.when(pl.program_id(0) < pl.num_programs(0) // 2)
    def _():
        for j in range(4):
            refs[-2][j] = totals[j]

    @pl.when(pl.program_id(0) >= pl.num_programs(0) // 2)
    def _():
        for j in range(4):
            refs[-1][j] = totals[j]


def experts_input(slots):
    rows, hidden = slots[0][0].shape
    depth = slots[0][2].shape[1] // 3 * 2
    tile = 256
    narrow = pl.BlockSpec((tile, hidden), lambda i: (i, 0))
    w_specs = [gu_spec(weight, depth) for weight in slots[0][2:]]
    steps = rows // tile // 2
    return kernel_call(
        experts_input_kernel,
        grid=(rows // tile,),
        in_specs=([narrow] * 2 + w_specs) * 2,
        out_specs=[
            pl.BlockSpec((4, tile, depth), lambda i: (0, jnp.minimum(i, steps - 1), 0)),
            pl.BlockSpec((4, tile, depth), lambda i: (0, jnp.maximum(i - steps, 0), 0)),
        ],
        out_shape=[jax.ShapeDtypeStruct((4, rows // 2, depth), jnp.float32)] * 2,
    )(*slots[0], *slots[1])


def residual_back_kernel(
    rank, a_ref, b_ref, lg_ref, wr_ref, x_ref, r_ref, scale_ref, gain_ref, o_ref, c_ref, gg_ref
):
    scale = scale_ref[...]
    block = a_ref.shape[2]

    @pl.when(pl.program_id(0) == 0)
    def _():
        gg_ref[...] = jnp.zeros_like(gg_ref)

    inner = jnp.zeros_like(scale)
    for j in range(4):
        at = dynamic_block(rank[0] ^ j, block)
        grad = a_ref[j] + b_ref[j]
        for e in range(wr_ref.shape[0]):
            grad += lg_ref[:, e : e + 1] * wr_ref[e : e + 1, at]
        o_ref[:, at] = grad
        product = grad * x_ref[:, at]
        inner += jnp.sum(product * gain_ref[:, at], axis=1, keepdims=True)
        gg_ref[:, at] += jnp.sum(product * scale, axis=0, keepdims=True)
    inner = inner * (1.0 / x_ref.shape[1]) * (scale * scale * scale)
    for j in range(4):
        at = slice(j * block, (j + 1) * block)
        value = scale * (o_ref[:, at] * gain_ref[:, at]) - x_ref[:, at] * inner
        value = r_ref[:, at] + value
        o_ref[:, at] = value
        c_ref[:, at] = value.astype(jnp.bfloat16)


def residual_back(rank, own, other, logit_grad, router, residual, result_grad, scale, gain):
    rows, width = residual.shape
    tile = 128
    wide = pl.BlockSpec((tile, width), lambda i, rank: (i, 0))
    piece = pl.BlockSpec((4, tile, width // 4), lambda i, rank: (0, i, 0))
    one = pl.BlockSpec((1, width), lambda i, rank: (0, 0))
    experts = logit_grad.shape[1]
    return kernel_call(
        residual_back_kernel,
        grid_spec=pltpu.PrefetchScalarGridSpec(
            num_scalar_prefetch=1,
            grid=(rows // tile,),
            in_specs=[
                piece,
                piece,
                pl.BlockSpec((tile, experts), lambda i, rank: (i, 0)),
                pl.BlockSpec((experts, width), lambda i, rank: (0, 0)),
                wide,
                wide,
                pl.BlockSpec((tile, 1), lambda i, rank: (i, 0)),
                one,
            ],
            out_specs=[wide, wide, one],
        ),
        out_shape=[
            jax.ShapeDtypeStruct((rows, width), jnp.float32),
            jax.ShapeDtypeStruct((rows, width), jnp.bfloat16),
            jax.ShapeDtypeStruct((1, width), jnp.float32),
        ],
    )(rank, own, other, logit_grad, router, residual, result_grad, scale, gain[None])


def experts_grad_kernel(x_ref, d_ref, m_ref, p_ref, *refs):
    o_ref = refs[-1]
    rows, down_rows = x_ref.shape[2], m_ref.shape[2]
    top, bottom = t_dot(x_ref[0], d_ref[...]), t_dot(m_ref[0], p_ref[...])
    if len(refs) == 2:
        top += refs[0][0, :rows].astype(jnp.float32)
        bottom += refs[0][0, rows:].astype(jnp.float32)
    o_ref[0, :rows] = top.astype(jnp.bfloat16)
    o_ref[0, rows:] = bottom.astype(jnp.bfloat16)


def experts_grad(inputs, pre_grad, middle, pair, part, side, got=()):
    _, rows, depth = inputs.shape
    hidden, down = pre_grad.shape[1], middle.shape[2]
    piece = pl.BlockSpec((1, (depth + down) // 2, hidden), lambda q: (q, 0, 0))
    return kernel_call(
        experts_grad_kernel,
        grid=(2,),
        in_specs=[
            pl.BlockSpec((1, rows, depth // 2), lambda q: (part, 0, q)),
            pl.BlockSpec((rows, hidden), lambda q: (0, 0)),
            pl.BlockSpec((1, rows, down // 2), lambda q: (part, 0, q)),
            pl.BlockSpec((rows, hidden), lambda q: (0, side)),
        ]
        + [piece] * len(got),
        out_specs=piece,
        out_shape=jax.ShapeDtypeStruct((2, (depth + down) // 2, hidden), jnp.bfloat16),
    )(inputs, pre_grad, middle, pair, *got)


def chip_grad_kernel(x_ref, *refs, count):
    o_ref = refs[-1]
    width = o_ref.shape[1] // count
    for i in range(count):
        at = slice(i * width, (i + 1) * width)
        total = t_dot(x_ref[0], refs[i][...])
        if len(refs) > count + 1:
            total += refs[count][:, at].astype(jnp.float32)
        o_ref[:, at] = total.astype(jnp.bfloat16)


def chip_grad(halves, part, grads, start=0, got=()):
    depth = halves.shape[2]
    rows = grads[0].shape[0]
    width = sum(grad.shape[1] for grad in grads)
    tile = 256
    piece = pl.BlockSpec((tile, width), lambda i: (i, 0))
    return kernel_call(
        functools.partial(chip_grad_kernel, count=len(grads)),
        grid=(depth // tile,),
        in_specs=[pl.BlockSpec((1, rows, tile), lambda i: (part, start // rows, i))]
        + [pl.BlockSpec(grad.shape, lambda i: (0, 0)) for grad in grads]
        + [piece] * len(got),
        out_specs=piece,
        out_shape=jax.ShapeDtypeStruct((depth, width), jnp.bfloat16),
    )(halves, *grads, *got)


def mixed_back_kernel(g_ref, a_ref, b_ref, o_ref):
    for half, ref in enumerate((a_ref, b_ref)):
        o_ref[half] = dot_t(g_ref[...], ref[...]).astype(jnp.bfloat16)


def mixed_back(grad, weights):
    rows, width = grad.shape
    depth = weights[0].shape[0]
    step = 256
    weight = pl.BlockSpec((step, width), lambda j: (j, 0))
    return kernel_call(
        mixed_back_kernel,
        grid=(depth // step,),
        in_specs=[pl.BlockSpec((rows, width), lambda j: (0, 0)), weight, weight],
        out_specs=pl.BlockSpec((2, rows, step), lambda j: (0, 0, j)),
        out_shape=jax.ShapeDtypeStruct((2, rows, depth), jnp.bfloat16),
    )(grad, *weights)


def across(value, bit):
    count = lax.axis_size("rep")
    return lax.ppermute(value, "rep", [(place, place ^ bit) for place in range(count)])


def along(value, steps):
    count = lax.axis_size("ep")
    return lax.ppermute(value, "ep", [(place, (place + steps) % count) for place in range(count)])


def mirrored(value, moves):
    reps, count = lax.axis_size("rep"), lax.axis_size("ep")
    pairs = []
    for rep in range(reps):
        for source, target in moves:
            if rep % 2:
                source, target = count - 1 - source, count - 1 - target
            pairs.append((rep * count + source, rep * count + target))
    return lax.ppermute(value, ("rep", "ep"), pairs)


def pick(value, index, axis):
    return lax.dynamic_index_in_dim(value, index, axis, keepdims=False)


def in_order(own, other, bit, axis):
    return jnp.where(bit == 1, jnp.stack([other, own], axis), jnp.stack([own, other], axis))


def over_ep(value, place):
    shard = place[3]
    experts = lax.axis_size("ep")
    parts = jnp.zeros((experts,) + value.shape, value.dtype)
    parts = lax.dynamic_update_index_in_dim(parts, value, shard, 0)
    for steps in range(1, experts):
        parts = lax.dynamic_update_index_in_dim(
            parts, along(value, steps), lax.rem(shard - steps + experts, experts), 0
        )
    return parts


def hold(*values):
    return lax.optimization_barrier(values)


def both_ways(value):
    return across(value[0], 2), across(value[1], 4)


def other_ways(first, second):
    return across(first, 4), across(second, 2)


def add(left, right):
    return (left.astype(jnp.float32) + right.astype(jnp.float32)).astype(jnp.bfloat16)


def ep_sum(both):
    return lax.psum_scatter(both, "ep", scatter_dimension=1, tiled=True).astype(jnp.float32)


def body(
    tokens,
    teacher,
    segment_ids,
    valid_mask,
    routes,
    attn_gain,
    q_gain,
    k_gain,
    moe_gain,
    w_query,
    w_key,
    w_value,
    w_out,
    w_router,
    w_gate,
    w_up,
    w_down,
):
    bf16, f32 = jnp.bfloat16, jnp.float32
    local_rows, width = tokens.shape
    experts = lax.axis_size("ep")
    reps = lax.axis_size("rep")
    reach = min(-(-WINDOW // local_rows), experts - 1)
    shard = lax.axis_index("ep")
    rep = lax.axis_index("rep")
    place = (rep // 4, rep // 2 % 2, rep % 2, shard)
    core = rep % 2
    total_tokens = local_rows * reps * experts

    valid = valid_mask.reshape(local_rows).astype(f32)
    own_count = jnp.sum(valid_mask)
    counts = jnp.stack([own_count // 16, own_count % 16]).astype(bf16)
    small = jnp.concatenate(
        [
            jnp.stack([attn_gain, q_gain, k_gain, moe_gain], 1),
            w_router,
            jnp.broadcast_to(counts[None], (attn_gain.shape[0], 2)),
        ],
        1,
    )
    rank = rep.astype(jnp.int32)[None]
    quarter = rep // 2
    quarter_rank = quarter.astype(jnp.int32)[None]
    order = tuple(code_of(j, reps) for j in range(reps))
    half = width // 2
    behind = reach * local_rows
    all_rows = local_rows + behind
    m = jnp.where(core == 0, shard, experts - 1 - shard)
    quarter_rows = w_gate.shape[1] // 4
    quarter_down = w_down.shape[1] // 4

    def own_part(weight, rows):
        return lax.dynamic_slice_in_dim(weight[0], quarter * rows, rows, 0)

    down = own_part(w_down, quarter_down)
    own = jnp.stack(
        [
            jnp.concatenate([own_part(w_gate, quarter_rows), down[:, :half]], 0),
            jnp.concatenate([own_part(w_up, quarter_rows), down[:, half:]], 0),
        ]
    )
    segments = segment_ids.reshape(local_rows)
    shard_rows = w_key.shape[0]
    columns = small.shape[1]
    small = small.T

    small = over_ep(small, place)
    parts = over_ep(jnp.stack([w_key, w_value]), place)
    segments_1 = from_behind(segments, "ep", 1)
    parts, small, own, tokens_1, segments_1 = hold(parts, small, own, tokens, segments_1)
    qo = jnp.stack([w_query, w_out])

    qo, parts = hold(qo, parts)
    qo = lax.all_gather(qo, "ep", axis=0)
    block = shard_rows * experts
    k_w, v_w = parts[:, 0].reshape(block, width), parts[:, 1].reshape(block, width)
    e_1 = mirrored(own, [(0, 1), (1, 2)])
    small = small.reshape(-1)
    small = jnp.pad(small, (0, 16 * width - small.shape[0])).reshape(16, width)
    k_w = jnp.concatenate([k_w, small], 0)
    k_x, v_y = both_ways((k_w, v_w))
    segments_2 = from_behind(segments_1, "ep", 1)
    k_w, k_x, v_w, v_y, tokens_1, segments_2 = hold(k_w, k_x, v_w, v_y, tokens_1, segments_2)

    k_w = jnp.stack([k_w, k_x])
    k_y, v_x = other_ways(k_w, jnp.stack([v_w, v_y]))
    tokens_1 = from_behind(tokens_1, "ep", 1)
    qo, k_w, k_y, v_w, v_y, v_x, tokens_1 = hold(qo, k_w, k_y, v_w, v_y, v_x, tokens_1)

    small = jnp.concatenate([k_w[:, block : block + 2], k_y[:, block : block + 2]], 0)
    small = jnp.pad(small.reshape(-1, width), ((0, 8), (0, 0)))
    k_w = jnp.concatenate([k_w[0, :block], k_w[1, :block], k_y[0, :block], k_y[1, :block], small], 0)
    v_w = jnp.concatenate([v_w, v_x[0], v_y, v_x[1]], 0)
    key_w, value_w = (k_w, across(k_w, 1)), (v_w, across(v_w, 1))
    q_w, o_w = qo[:, 0].reshape(-1, width), qo[:, 1].reshape(-1, width)
    q_x, o_y = both_ways((q_w, o_w))
    tokens_2 = from_behind(tokens_1, "ep", 1)
    key_w, value_w, q_w, q_x, o_w, o_y, tokens_2, tokens_1, e_1, own = hold(
        key_w, value_w, q_w, q_x, o_w, o_y, tokens_2, tokens_1, e_1, own
    )

    q_w = jnp.concatenate([q_w, q_x], 0)
    q_y, o_x = other_ways(q_w, jnp.stack([o_w, o_y]))
    q_w = jnp.concatenate([q_w, q_y], 0)
    o_w = jnp.concatenate([o_w, o_x[0], o_y, o_x[1]], 0)
    e_2 = mirrored(jnp.where(m == 2, e_1, own), [(1, 0), (2, 3)])
    small = jnp.stack([weight[4 * block : 4 * block + 8] for weight in key_w])
    small = small.reshape(2, 2, 2, -1)[..., : experts * columns * shard_rows]
    for axis, bit in enumerate((core, place[0], place[1])):
        small = jnp.where(bit == 1, jnp.flip(small, axis), small)
    small = small.reshape(2, 2, 2, experts, columns, shard_rows)
    small = jnp.transpose(small, (4, 1, 2, 0, 3, 5)).reshape(columns, -1)
    gain_attn, gain_query, gain_key, gain_moe = [small[i].astype(f32) for i in range(4)]
    weight_router = small[4 : 4 + experts].T
    counts = small[4 + experts :, ::shard_rows].astype(f32)
    count = jnp.sum(counts[0]) * 16.0 + jnp.sum(counts[1])
    tokens_all = jnp.concatenate([tokens_2, tokens_1, tokens], 0)
    key_segments = jnp.concatenate([segments_2, segments_1, segments], 0)
    normed, scale_all = norm_rows(rank, tokens_all, gain_attn, order)
    key_lin, key_squares = project(normed, *key_w, f32)
    value_all, _ = project(normed, *value_w, bf16)
    q_w, o_w, e_2, e_1, own, normed, key_lin, value_all = hold(
        q_w, o_w, e_2, e_1, own, normed, key_lin, value_all
    )

    query_w, out_w = (q_w, across(q_w, 1)), (o_w, across(o_w, 1))
    e_b = jnp.where(m == 1, own, jnp.where(m == 2, e_1, e_2))
    b_x, b_y = both_ways(e_b)
    e_3 = mirrored(e_1, [(1, 2)])
    query_lin, query_squares = project(normed, *query_w, f32, behind)
    scale_key = lax.rsqrt(key_squares / width + norm_eps)
    scale_query = lax.rsqrt(query_squares / width + norm_eps)
    key_positions = (shard - reach) * local_rows + jnp.arange(all_rows, dtype=jnp.int32)
    half_head = HEAD_DIM // 2
    frequency = 10000.0 ** (-jnp.arange(half_head, dtype=f32) * 2.0 / HEAD_DIM)
    angles = key_positions[:, None].astype(f32) * frequency[None, :]
    cosine, sine = jnp.cos(angles), jnp.sin(angles)
    cosine, sine = jnp.concatenate([cosine, cosine], 1), jnp.concatenate([-sine, sine], 1)

    def mask_of(tile):
        span = behind + tile
        parts = []
        for start in range(0, local_rows, tile):
            keys = slice(start, start + span)
            queries = slice(behind + start, behind + start + tile)
            distance = key_positions[None, queries] - key_positions[keys, None]
            allowed = (
                (distance >= 0)
                & (distance < WINDOW)
                & (key_positions[keys, None] >= 0)
                & (key_segments[None, queries] == key_segments[keys, None])
            )
            parts.append(jnp.where(allowed, 0.0, -1e30).astype(f32))
        return jnp.stack(parts)

    operands = (
        query_lin,
        key_lin,
        value_all,
        scale_query,
        scale_key,
        gain_query[None],
        gain_key[None],
        cosine,
        sine,
    )
    bias_small = mask_of(local_rows // 4)
    mixed, lse_0 = attend(rank, operands, bias_small, 0)
    mixed, out_w, e_b, b_x, b_y, e_3, e_1, own = hold(mixed, out_w, e_b, b_x, b_y, e_3, e_1, own)

    b_0, b_1 = jnp.stack([e_b[0], b_x]), jnp.stack([e_b[1], b_y])
    b_2, b_3 = other_ways(b_0[:, :quarter_rows], b_1[:, :quarter_rows])
    e_4 = mirrored(e_3, [(2, 3)])
    mixed, lse_1 = attend(rank, operands, bias_small, HEADS // 2, (mixed,))
    branch, _ = project(mixed, *out_w, f32)
    residual = tokens.astype(f32) + branch
    moe, scale_moe = norm_rows(quarter_rank, residual, gain_moe, (0, 1, 2, 3))
    moe_y = jnp.concatenate([moe, across(moe, 1)], 1)
    piece = half // 2
    moe_x = jnp.stack(
        [
            jnp.concatenate([moe_y[0, :, i : i + piece], moe_y[1, :, i : i + piece]], 1)
            for i in (0, piece)
        ]
    )
    router_parts = weight_router.reshape(4, -1, experts)
    router_rel = jnp.concatenate([pick(router_parts, quarter ^ j, 0) for j in range(4)], 0)
    router_probs = jax.nn.softmax(
        matmul(moe[0], router_rel[:half]) + matmul(moe[1], router_rel[half:]), axis=-1
    )
    chosen = jnp.sum(
        (routes[:, :, None] == jnp.arange(experts, dtype=jnp.int32)).astype(f32), axis=1
    )
    gates = router_probs * chosen
    gates_both = jnp.concatenate([gates, across(gates, 1)], 0)
    gates_a = jnp.where(core == 0, gates_both[:, :1], gates_both[:, -1:])
    gates_b = jnp.where(core == 0, gates_both[:, 1:2], gates_both[:, -2:-1])
    b_0, b_1, b_2, b_3, e_4, e_3, e_1, own, moe_y, moe_x = hold(
        b_0, b_1, b_2, b_3, e_4, e_3, e_1, own, moe_y, moe_x
    )

    e_a = jnp.where(m == 0, own, jnp.where(m == 1, e_1, jnp.where(m == 2, e_3, e_4)))
    a_x, a_y = both_ways(e_a)
    b_4, b_5 = other_ways(b_0[:, quarter_rows:], b_1[:, quarter_rows:])
    up_weights_b, down_weights_b = (b_0, b_2, b_1, b_3), (b_0, b_4, b_1, b_5)
    gate_pre_b, up_pre_b, my_b, mx_b = experts_up(quarter_rank, moe_y, moe_x, up_weights_b)
    e_a, a_x, a_y, my_b, mx_b, moe_y, moe_x = hold(e_a, a_x, a_y, my_b, mx_b, moe_y, moe_x)

    a_0, a_1 = jnp.stack([e_a[0], a_x]), jnp.stack([e_a[1], a_y])
    a_2, a_3 = other_ways(a_0[:, :quarter_rows], a_1[:, :quarter_rows])
    a_0, a_1, a_2, a_3 = hold(a_0, a_1, a_2, a_3)

    a_4, a_5 = other_ways(a_0[:, quarter_rows:], a_1[:, quarter_rows:])
    up_weights_a, down_weights_a = (a_0, a_2, a_1, a_3), (a_0, a_4, a_1, a_5)
    gate_pre_a, up_pre_a, my_a, mx_a = experts_up(quarter_rank, moe_y, moe_x, up_weights_a)
    expert_out_a, expert_out_b, mixture, mixture_other = experts_down(
        (gates_a, gates_b), ((my_a, mx_a) + down_weights_a, (my_b, mx_b) + down_weights_b)
    )
    result = residual + (mixture + across(mixture_other, 1))
    output = result.astype(bf16)
    error = result - teacher.astype(f32)
    squares = jnp.sum(valid * jnp.sum(error * error, axis=1))
    result_grad = total_tokens / count * valid[:, None] * error
    result_other = across(result_grad, 1)

    pair_b, dg_b, du_b, gate_grad_b = experts_back(
        quarter_rank,
        result_grad,
        result_other,
        expert_out_b,
        gates_b,
        gate_pre_b,
        up_pre_b,
        down_weights_b,
    )
    sent_x = experts_grad(moe_x, dg_b, mx_b, pair_b, 1, 0)
    sent_y = experts_grad(moe_y, du_b, my_b, pair_b, 1, 1)
    sent_x, sent_y, expert_out_a = hold(sent_x, sent_y, expert_out_a)

    b_x, b_y = both_ways((sent_x, sent_y))
    pair_a, dg_a, du_a, gate_grad_a = experts_back(
        quarter_rank,
        result_grad,
        result_other,
        expert_out_a,
        gates_a,
        gate_pre_a,
        up_pre_a,
        down_weights_a,
    )
    sent_x = experts_grad(moe_x, dg_a, mx_a, pair_a, 1, 0)
    sent_y = experts_grad(moe_y, du_a, my_a, pair_a, 1, 1)
    input_grad, input_other = experts_input(
        ((dg_a, du_a) + up_weights_a, (dg_b, du_b) + up_weights_b)
    )
    slot_grads = jnp.concatenate([gate_grad_a, gate_grad_b], 1)
    own_slots, partner_slots = slot_grads[:local_rows], across(slot_grads[local_rows:], 1)
    from_low = jnp.where(core == 0, own_slots, partner_slots)
    from_high = jnp.where(core == 0, partner_slots, own_slots)
    prob_grad = chosen * jnp.concatenate([from_low, from_high[:, ::-1]], 1)
    logit_grad = router_probs * (
        prob_grad - jnp.sum(prob_grad * router_probs, axis=-1, keepdims=True)
    )
    b_x, b_y, sent_x, sent_y, input_grad, input_other, logit_grad = hold(
        b_x, b_y, sent_x, sent_y, input_grad, input_other, logit_grad
    )

    input_other = across(input_other, 1)
    a_x, a_y = both_ways((sent_x, sent_y))
    b_0 = experts_grad(moe_x, dg_b, mx_b, pair_b, 0, 0, (b_x,))
    b_1 = experts_grad(moe_y, du_b, my_b, pair_b, 0, 1, (b_y,))
    router_local = jnp.concatenate(
        [
            jnp.dot(part.T.astype(f32), logit_grad, precision=highest, preferred_element_type=f32)
            for part in (moe[0], moe[1])
        ],
        0,
    )
    router_local = router_local.reshape(4, -1, experts)
    router_local = jnp.concatenate([pick(router_local, quarter ^ j, 0) for j in range(4)], 0)
    residual_grad, branch_grad, moe_gain_local = residual_back(
        quarter_rank,
        input_grad,
        input_other,
        logit_grad,
        weight_router.astype(f32).T,
        residual,
        result_grad,
        scale_moe,
        gain_moe,
    )
    out_sent = across(chip_grad(mixed, 1, (branch_grad,)), 1)
    out_sum = chip_grad(mixed, 0, (branch_grad,), 0, (out_sent,)).reshape(2, 2, -1, width)
    mixed_grad = mixed_back(branch_grad, out_w)
    b_y, b_x = other_ways(b_0[1], b_1[1])
    bias = mask_of(local_rows // 2)
    dq_0, dk_0, dv_0 = attend_back(rank, operands, bias, mixed_grad, lse_0, 0)
    dq_1, dk_1, dv_1 = attend_back(rank, operands, bias, mixed_grad, lse_1, HEADS // 2)
    a_x, a_y, b_0, b_1, b_x, b_y, out_sum, dq_0, dk_0, dv_0, dq_1, dk_1, dv_1 = hold(
        a_x, a_y, b_0, b_1, b_x, b_y, out_sum, dq_0, dk_0, dv_0, dq_1, dk_1, dv_1
    )

    a_0 = experts_grad(moe_x, dg_a, mx_a, pair_a, 0, 0, (a_x,))
    a_1 = experts_grad(moe_y, du_a, my_a, pair_a, 0, 1, (a_y,))
    a_y, a_x = other_ways(a_0[1], a_1[1])
    out_x, out_y = across(out_sum[:, 1, :, :half], 2), across(out_sum[1, :, :, half:], 4)
    b_end = jnp.stack([add(b_0[0], b_y), add(b_1[0], b_x)])
    b_got = mirrored(b_end, [(3, 2), (0, 1)])
    value_sent = chip_grad(normed, 1, (dv_0, dv_1))
    value_got = across(value_sent, 1)
    value_sum = chip_grad(normed, 0, (dv_0, dv_1), 0, (value_got,)).reshape(2, 2, -1, width)
    value_x = across(value_sum[:, 1, :, :half], 2)
    value_y = across(value_sum[1, :, :, half:], 4)
    query_lin_grad, q_gain_local = lin_back(
        dq_0, dq_1, query_lin, scale_query, gain_query[None], cosine[behind:], sine[behind:]
    )
    key_lin_grad, k_gain_local = lin_back(
        dk_0, dk_1, key_lin, scale_key, gain_key[None], cosine, sine
    )
    query_sent = chip_grad(normed, 1, (query_lin_grad,), behind)
    key_sent = chip_grad(normed, 1, (key_lin_grad,))
    packed = jnp.concatenate(
        [
            jnp.broadcast_to(squares, (1, width)),
            q_gain_local,
            k_gain_local,
            moe_gain_local,
            router_local.T,
        ],
        0,
    )
    (
        a_0, a_1, a_x, a_y, out_sum, out_x, out_y, b_end, b_got, query_lin_grad, key_lin_grad,
        value_sum, value_x, value_y, query_sent, key_sent, packed,
    ) = hold(
        a_0, a_1, a_x, a_y, out_sum, out_x, out_y, b_end, b_got, query_lin_grad, key_lin_grad,
        value_sum, value_x, value_y, query_sent, key_sent, packed,
    )

    query_got, key_got = across(query_sent, 1), across(key_sent, 1)
    value_a = add(value_sum[:, 0, :, :half], value_x)
    value_b = add(value_sum[0, :, :, half:], value_y)
    for link in (1, 2, 4):
        packed = packed + across(packed, link)
    out_a, out_b = add(out_sum[:, 0, :, :half], out_x), add(out_sum[0, :, :, half:], out_y)
    value_a, value_b, packed, out_a, out_b = hold(value_a, value_b, packed, out_a, out_b)
    moved_x = across(jnp.stack([value_b[1], out_b[1]]), 2)
    moved_y = across(jnp.stack([value_a[1], out_a[1]]), 4)
    value_x, value_y, out_x, out_y = moved_x[0], moved_y[0], moved_x[1], moved_y[1]
    four = [add(out_a[0], out_y), add(out_b[0], out_x)]
    four += [add(value_a[0], value_y), add(value_b[0], value_x)]
    four = ep_sum(jnp.stack(four))
    out_total, value_total = four[:2], four[2:]
    b_low = add(b_end, b_got)
    b_got_2 = mirrored(b_low, [(2, 1)])
    a_end = jnp.stack([add(a_0[0], a_y), add(a_1[0], a_x)])
    a_got = mirrored(a_end, [(3, 2)])
    normed_grad = project_back(
        key_lin_grad, dv_0, dv_1, query_lin_grad, key_w, value_w, query_w
    )
    query_sum = chip_grad(normed, 0, (query_lin_grad,), behind, (query_got,))
    key_sum = chip_grad(normed, 0, (key_lin_grad,), 0, (key_got,))
    (
        normed_grad, query_sum, key_sum, out_total, value_total, b_got_2, a_end, a_got, packed,
    ) = hold(
        normed_grad, query_sum, key_sum, out_total, value_total, b_got_2, a_end, a_got, packed,
    )

    query_sum = query_sum.reshape(2, 2, -1, width)
    key_sum = key_sum.reshape(2, 2, -1, width)
    query_x, key_y = across(query_sum[:, 1], 2), across(key_sum[1], 4)
    carried = from_behind(normed_grad[:, :local_rows].astype(bf16), "ep", -1)
    a_low = add(a_end, a_got)
    a_got = mirrored(a_low, [(2, 1)])
    b_total = (b_end.astype(f32) + b_got.astype(f32) + b_got_2.astype(f32)).astype(bf16)
    query_sum, key_sum, query_x, key_y, carried, a_low, a_got, packed, b_total = hold(
        query_sum, key_sum, query_x, key_y, carried, a_low, a_got, packed, b_total
    )

    query_sum, key_sum = add(query_sum[:, 0], query_x), add(key_sum[0], key_y)
    query_y, key_x = across(query_sum[1], 4), across(key_sum[1], 2)
    for back in range(1, reach):
        here = normed_grad[:, back * local_rows : (back + 1) * local_rows] + carried.astype(f32)
        carried = from_behind(here.astype(bf16), "ep", -1)
    a_low = add(a_low, a_got)
    a_got = mirrored(a_low, [(1, 0)])
    query_sum, key_sum, query_y, key_x, carried, packed, a_low, a_got = hold(
        query_sum, key_sum, query_y, key_x, carried, packed, a_low, a_got
    )

    qk_total = ep_sum(jnp.stack([add(query_sum[0], query_y), add(key_sum[0], key_x)]))
    packed = jnp.sum(over_ep(packed, place), axis=0)
    tokens_grad = tokens_back(
        rank, normed_grad, carried, tokens, residual_grad, scale_all, gain_attn, reps
    )
    mine = jnp.where(m == 0, add(a_low, a_got), b_total)

    def own_half(piece):
        return piece.reshape(2, 2, -1, piece.shape[2])

    tops, bottoms = own_half(mine[:, :quarter_rows]), own_half(mine[:, quarter_rows:])
    halves = jnp.concatenate([tops, bottoms], 2)
    other = across(pick(halves, 1 - core, 1), 1)
    mine = jnp.where(m < 2, pick(halves, core, 1), other).astype(f32)
    top = quarter_rows // 2
    down_out = jnp.concatenate([mine[0, top:], mine[1, top:]], 1)
    out_out = jnp.concatenate([out_total[0], out_total[1]], 1)
    value_out = jnp.concatenate([value_total[0], value_total[1]], 1)
    loss = packed[0, 0] / (2.0 * count * width)
    attn_gain_out = (
        jnp.sum(w_query.astype(f32) * qk_total[0], axis=1)
        + jnp.sum(w_key.astype(f32) * qk_total[1], axis=1)
        + jnp.sum(w_value.astype(f32) * value_out, axis=1)
    ) / attn_gain.astype(f32)
    shares = lax.dynamic_slice_in_dim(
        packed, (rep * experts + shard) * shard_rows, shard_rows, 1
    )
    return (
        output,
        loss,
        tokens_grad,
        attn_gain_out,
        shares[1],
        shares[2],
        shares[3],
        qk_total[0],
        qk_total[1],
        value_out,
        out_out,
        shares[4:].T,
        mine[0, :top][None],
        mine[1, :top][None],
        down_out[None],
    )


def solution(mesh):
    placed = (
        P(("rep", "ep"), None),
        P(("rep", "ep"), None),
        P("rep", "ep"),
        P("rep", "ep"),
        P(("rep", "ep"), None),
        P(("rep", "ep")),
        P(("rep", "ep")),
        P(("rep", "ep")),
        P(("rep", "ep")),
        P(("rep", "ep"), None),
        P(("rep", "ep"), None),
        P(("rep", "ep"), None),
        P(("rep", "ep"), None),
        P(("rep", "ep"), None),
        P("ep", None, None),
        P("ep", None, None),
        P("ep", None, None),
    )
    chips = mesh.shape["rep"] == 8 and mesh.shape["ep"] == 4
    return jax.shard_map(
        body if chips else body_plain,
        mesh=mesh,
        in_specs=placed,
        out_specs=(
            P(("rep", "ep"), None),
            P(),
            P(("rep", "ep"), None),
            P(("rep", "ep")),
            P(("rep", "ep")),
            P(("rep", "ep")),
            P(("rep", "ep")),
            P(("rep", "ep"), None),
            P(("rep", "ep"), None),
            P(("rep", "ep"), None),
            P(("rep", "ep"), None),
            P(("rep", "ep"), None),
            P("ep", "rep", None),
            P("ep", "rep", None),
            P("ep", "rep", None),
        ),
        check_vma=False,
    )
```

```python
import functools

import jax
import jax.numpy as jnp
from jax import lax
from jax.experimental import pallas as pl
from jax.experimental.pallas import tpu as pltpu
from jax.sharding import PartitionSpec as P

HEADS = 16
HEAD_DIM = 128
WINDOW = 1024
TOP = 2
VMEM_LIMIT = 56 * 1024 * 1024


norm_eps = 1e-05
highest = lax.Precision.HIGHEST


def from_behind(value, axis, steps):
    count = lax.axis_size(axis)
    leading, last = (max(0, -steps), min(count, count - steps))
    return lax.ppermute(value, axis, [(source, source + steps) for source in range(leading, last)])


def matmul(left, right):
    return jnp.dot(left, right, preferred_element_type=jnp.float32)


def rms_scale(value):
    return lax.rsqrt(jnp.mean(value * value, axis=-1, keepdims=True) + norm_eps)


def norm_back(value, scale, gain, grad):
    weighted = grad * gain
    inner = jnp.mean(weighted * value, axis=-1, keepdims=True)
    return (
        scale * weighted - value * (scale * scale * scale) * inner,
        jnp.sum(grad * value * scale, axis=0),
    )


def rounded(value):
    return lax.optimization_barrier(value.astype(jnp.bfloat16)).astype(jnp.float32)


def rotary_tables(positions, head_size):
    half = head_size // 2
    frequency = 10000.0 ** (-jnp.arange(half, dtype=jnp.float32) * 2.0 / head_size)
    angles = positions[:, None].astype(jnp.float32) * frequency[None, :]
    cosine = jnp.cos(angles)
    sine = jnp.sin(angles)
    return (
        jnp.concatenate([cosine, cosine], -1)[:, None, :],
        jnp.concatenate([sine, sine], -1)[:, None, :],
    )


def rotate(value, cosine, sine):
    half = value.shape[-1] // 2
    turned = jnp.concatenate([-value[..., half:], value[..., :half]], -1)
    return value * cosine + turned * sine


def rotate_back(grad, cosine, sine):
    half = grad.shape[-1] // 2
    scaled = grad * sine
    turned = jnp.concatenate([scaled[..., half:], -scaled[..., :half]], -1)
    return grad * cosine + turned


def unpack(everything):
    gains = [everything[index].astype(jnp.float32) for index in range(4)]
    return (gains, everything[4], everything[5], everything[6], everything[7], everything[8])


def body_plain(
    tokens,
    teacher,
    segment_ids,
    valid_mask,
    routes,
    attn_gain,
    q_gain,
    k_gain,
    moe_gain,
    w_query,
    w_key,
    w_value,
    w_out,
    w_router,
    w_gate,
    w_up,
    w_down,
):
    local_rows, width = tokens.shape
    experts = lax.axis_size("ep")
    pairs = local_rows * TOP
    capacity = 5 * pairs // (4 * experts)
    reach = min(-(-WINDOW // local_rows), experts - 1)
    group = min(HEADS, 4)
    score_scale = HEAD_DIM ** (-0.5)
    shard = lax.axis_index("ep")
    total_tokens = local_rows * lax.axis_size("rep") * experts
    everything = (
        lax.all_gather(attn_gain, ("rep", "ep"), axis=0, tiled=True),
        lax.all_gather(q_gain, ("rep", "ep"), axis=0, tiled=True),
        lax.all_gather(k_gain, ("rep", "ep"), axis=0, tiled=True),
        lax.all_gather(moe_gain, ("rep", "ep"), axis=0, tiled=True),
        lax.all_gather(w_query, ("rep", "ep"), axis=0, tiled=True),
        lax.all_gather(w_key, ("rep", "ep"), axis=0, tiled=True),
        lax.all_gather(w_value, ("rep", "ep"), axis=0, tiled=True),
        lax.all_gather(w_out, ("rep", "ep"), axis=0, tiled=True),
        lax.all_gather(w_router, ("rep", "ep"), axis=0, tiled=True),
    )
    gains, weight_query, weight_key, weight_value, weight_out, weight_router = unpack(everything)
    gain_attn, gain_query, gain_key, gain_moe = gains
    inputs = tokens.astype(jnp.float32)
    scale_attn = rms_scale(inputs)
    normed = (inputs * scale_attn * gain_attn).astype(jnp.bfloat16)
    query_lin = matmul(normed, weight_query)
    key_lin = matmul(normed, weight_key)
    value_rows = (
        matmul(normed, weight_value).astype(jnp.bfloat16).reshape(local_rows, HEADS, HEAD_DIM)
    )
    scale_query = rms_scale(query_lin)
    scale_key = rms_scale(key_lin)
    positions = shard * local_rows + jnp.arange(local_rows, dtype=jnp.int32)
    cosine, sine = rotary_tables(positions, HEAD_DIM)
    query_rows = rotate(
        (query_lin * scale_query * gain_query).reshape(local_rows, HEADS, HEAD_DIM), cosine, sine
    ).astype(jnp.bfloat16)
    key_rows = rotate(
        (key_lin * scale_key * gain_key).reshape(local_rows, HEADS, HEAD_DIM), cosine, sine
    ).astype(jnp.bfloat16)
    segments = segment_ids.reshape(local_rows)
    key_parts, value_parts, segment_parts = ([], [], [])
    for back in range(reach, 0, -1):
        moved = from_behind((key_rows, value_rows, segments.astype(jnp.bfloat16)), "ep", back)
        key_parts.append(moved[0])
        value_parts.append(moved[1])
        segment_parts.append(moved[2].astype(jnp.int32))
    all_keys = jnp.concatenate(key_parts + [key_rows], 0)
    all_values = jnp.concatenate(value_parts + [value_rows], 0)
    key_segments = jnp.concatenate(segment_parts + [segments], 0)
    key_positions = (shard - reach) * local_rows + jnp.arange(
        (reach + 1) * local_rows, dtype=jnp.int32
    )
    distance = positions[:, None] - key_positions[None, :]
    allowed = (
        (distance >= 0)
        & (distance < WINDOW)
        & (key_positions[None, :] >= 0)
        & (segments[:, None] == key_segments[None, :])
    )

    def by_group(value):
        return jnp.moveaxis(value.reshape(value.shape[0], HEADS // group, group, HEAD_DIM), 1, 0)

    def from_group(value):
        return jnp.moveaxis(value, 0, 1).reshape(value.shape[1], HEADS * HEAD_DIM)

    def scores_of(query_group, key_group):
        raw = (
            jnp.einsum("qhd,khd->hqk", query_group, key_group, preferred_element_type=jnp.float32)
            * score_scale
        )
        return jnp.where(allowed[None], raw, -1e30)

    def attend_forward(item):
        query_group, key_group, value_group = item
        scores = scores_of(query_group, key_group)
        peak = jnp.max(scores, axis=-1, keepdims=True)
        shifted = jnp.exp(scores - peak)
        total = jnp.sum(shifted, axis=-1, keepdims=True)
        weights = (shifted / total).astype(jnp.bfloat16)
        mixed = jnp.einsum("hqk,khd->qhd", weights, value_group, preferred_element_type=jnp.float32)
        return (mixed, peak, total)

    query_groups = by_group(query_rows)
    key_groups = by_group(all_keys)
    value_groups = by_group(all_values)
    mixed, peaks, totals = lax.map(attend_forward, (query_groups, key_groups, value_groups))
    mixed_rows = from_group(mixed).astype(jnp.bfloat16)
    residual = inputs + matmul(mixed_rows, weight_out)
    scale_moe = rms_scale(residual)
    normed_moe = (residual * scale_moe * gain_moe).astype(jnp.bfloat16)
    router_probs = jax.nn.softmax(matmul(normed_moe, weight_router), axis=-1)
    flat_routes = routes.reshape(pairs)
    choose = (flat_routes[:, None] == jnp.arange(experts, dtype=jnp.int32)[None, :]).astype(
        jnp.int32
    )
    rank = jnp.sum((jnp.cumsum(choose, axis=0) - choose) * choose, axis=1)
    slots = flat_routes * capacity + rank
    pair_source = (
        jnp.full((experts * capacity,), pairs, jnp.int32)
        .at[slots]
        .set(jnp.arange(pairs, dtype=jnp.int32))
    )
    token_source = jnp.where(pair_source < pairs, pair_source // TOP, local_rows)
    zero_row = jnp.zeros((1, width), jnp.bfloat16)
    outgoing = jnp.concatenate([normed_moe, zero_row], 0)[token_source].reshape(
        experts, capacity, width
    )
    choose_float = choose.reshape(local_rows, TOP, experts).astype(jnp.float32)
    gate_value = jnp.sum(choose_float * router_probs[:, None, :], axis=2)
    gate_weight = w_gate[0]
    up_weight = w_up[0]
    down_weight = w_down[0]
    piece = lax.all_to_all(outgoing, "ep", split_axis=0, concat_axis=0, tiled=True)
    flat = piece.reshape(-1, width)
    gate_pre = matmul(flat, gate_weight)
    up_pre = matmul(flat, up_weight)
    middle = (jax.nn.silu(gate_pre) * up_pre).astype(jnp.bfloat16)
    expert_out = matmul(middle, down_weight).astype(jnp.bfloat16)
    lead = piece.shape[:2]
    returned = expert_out.reshape(piece.shape)
    gate_kept = gate_pre.reshape(lead + (-1,))
    up_kept = up_pre.reshape(lead + (-1,))
    arrived = lax.all_to_all(returned, "ep", split_axis=0, concat_axis=0, tiled=True)
    expert_rows = arrived.reshape(experts * capacity, width)[slots].reshape(local_rows, TOP, width)
    result = residual + jnp.sum(gate_value[:, :, None] * expert_rows, axis=1)
    output = result.astype(jnp.bfloat16)
    valid = valid_mask.reshape(local_rows).astype(jnp.float32)
    error = result - teacher.astype(jnp.float32)
    squares = jnp.sum(valid * jnp.sum(error * error, axis=1))
    total_squares, count = lax.psum((squares, jnp.sum(valid)), ("rep", "ep"))
    loss = total_squares / (2.0 * count * width)
    result_grad = total_tokens / count * valid[:, None] * error
    gate_value_grad = jnp.sum(result_grad[:, None, :] * expert_rows, axis=2)
    pair_grad = (
        (gate_value[:, :, None] * result_grad[:, None, :])
        .astype(jnp.bfloat16)
        .reshape(pairs, width)
    )
    grad_outgoing = jnp.concatenate([pair_grad, zero_row], 0)[pair_source].reshape(
        experts, capacity, width
    )
    grad_in = lax.all_to_all(grad_outgoing, "ep", split_axis=0, concat_axis=0, tiled=True)
    rows_in = piece.reshape(-1, width)
    gate_pre = gate_kept.reshape(rows_in.shape[0], -1)
    up_pre = up_kept.reshape(rows_in.shape[0], -1)
    flat_grad = grad_in.reshape(-1, width)
    sigma = jax.nn.sigmoid(gate_pre)
    active = gate_pre * sigma
    middle = (active * up_pre).astype(jnp.bfloat16)
    down_local = matmul(middle.T, flat_grad)
    middle_grad = matmul(flat_grad, down_weight.T)
    gate_pre_grad = (middle_grad * up_pre * sigma * (1.0 + gate_pre * (1.0 - sigma))).astype(
        jnp.bfloat16
    )
    up_pre_grad = (middle_grad * active).astype(jnp.bfloat16)
    gate_local = matmul(rows_in.T, gate_pre_grad)
    up_local = matmul(rows_in.T, up_pre_grad)
    input_grad = (matmul(gate_pre_grad, gate_weight.T) + matmul(up_pre_grad, up_weight.T)).astype(
        jnp.bfloat16
    )
    back_rows = lax.all_to_all(
        input_grad.reshape(experts, capacity, width), "ep", split_axis=0, concat_axis=0, tiled=True
    )
    pair_back = back_rows.reshape(experts * capacity, width)[slots].reshape(local_rows, TOP, width)
    everything = (
        lax.all_gather(attn_gain, ("rep", "ep"), axis=0, tiled=True),
        lax.all_gather(q_gain, ("rep", "ep"), axis=0, tiled=True),
        lax.all_gather(k_gain, ("rep", "ep"), axis=0, tiled=True),
        lax.all_gather(moe_gain, ("rep", "ep"), axis=0, tiled=True),
        lax.all_gather(w_query, ("rep", "ep"), axis=0, tiled=True),
        lax.all_gather(w_key, ("rep", "ep"), axis=0, tiled=True),
        lax.all_gather(w_value, ("rep", "ep"), axis=0, tiled=True),
        lax.all_gather(w_out, ("rep", "ep"), axis=0, tiled=True),
        lax.all_gather(w_router, ("rep", "ep"), axis=0, tiled=True),
    )
    gains, weight_query, weight_key, weight_value, weight_out, weight_router = unpack(everything)
    gain_attn, gain_query, gain_key, gain_moe = gains
    prob_grad = jnp.sum(choose_float * gate_value_grad[:, :, None], axis=1)
    logit_grad = router_probs * (
        prob_grad - jnp.sum(prob_grad * router_probs, axis=-1, keepdims=True)
    )
    router_local = jnp.dot(
        normed_moe.T, logit_grad, precision=highest, preferred_element_type=jnp.float32
    )
    normed_moe_grad = jnp.sum(pair_back.astype(jnp.float32), axis=1) + jnp.dot(
        logit_grad, weight_router.T, precision=highest, preferred_element_type=jnp.float32
    )
    residual_part, moe_gain_local = norm_back(residual, scale_moe, gain_moe, normed_moe_grad)
    residual_grad = result_grad + residual_part
    branch_grad = residual_grad.astype(jnp.bfloat16)
    out_local = matmul(mixed_rows.T, branch_grad)
    mixed_grad = (
        matmul(branch_grad, weight_out.T).astype(jnp.bfloat16).reshape(local_rows, HEADS, HEAD_DIM)
    )

    def attend_backward(item):
        query_group, key_group, value_group, grad_group, peak, total = item
        scores = scores_of(query_group, key_group)
        probs = jnp.exp(scores - peak) / total
        weights = probs.astype(jnp.bfloat16)
        value_part = jnp.einsum(
            "hqk,qhd->khd", weights, grad_group, preferred_element_type=jnp.float32
        )
        probs_grad = jnp.einsum(
            "qhd,khd->hqk", grad_group, value_group, preferred_element_type=jnp.float32
        )
        inner = jnp.sum(probs * probs_grad, axis=-1, keepdims=True)
        score_grad = (probs * (probs_grad - inner)).astype(jnp.bfloat16)
        query_part = (
            jnp.einsum("hqk,khd->qhd", score_grad, key_group, preferred_element_type=jnp.float32)
            * score_scale
        )
        key_part = (
            jnp.einsum("hqk,qhd->khd", score_grad, query_group, preferred_element_type=jnp.float32)
            * score_scale
        )
        return (query_part, key_part, value_part)

    query_parts, key_parts_grad, value_parts_grad = lax.map(
        attend_backward,
        (query_groups, key_groups, value_groups, by_group(mixed_grad), peaks, totals),
    )
    query_row_grad = from_group(query_parts)
    key_all_grad = from_group(key_parts_grad)
    value_all_grad = from_group(value_parts_grad)
    own_keys = key_all_grad[reach * local_rows :]
    own_values = value_all_grad[reach * local_rows :]
    for back in range(1, reach + 1):
        start = (reach - back) * local_rows
        moved = from_behind(
            (key_all_grad[start : start + local_rows], value_all_grad[start : start + local_rows]),
            "ep",
            -back,
        )
        own_keys = own_keys + moved[0]
        own_values = own_values + moved[1]
    query_turned = rotate_back(
        rounded(query_row_grad).reshape(local_rows, HEADS, HEAD_DIM), cosine, sine
    ).reshape(local_rows, width)
    key_turned = rotate_back(
        rounded(own_keys).reshape(local_rows, HEADS, HEAD_DIM), cosine, sine
    ).reshape(local_rows, width)
    query_lin_grad, q_gain_local = norm_back(query_lin, scale_query, gain_query, query_turned)
    key_lin_grad, k_gain_local = norm_back(key_lin, scale_key, gain_key, key_turned)
    query_lin_grad = query_lin_grad.astype(jnp.bfloat16)
    key_lin_grad = key_lin_grad.astype(jnp.bfloat16)
    value_row_grad = own_values.astype(jnp.bfloat16)
    query_local = matmul(normed.T, query_lin_grad)
    key_local = matmul(normed.T, key_lin_grad)
    value_local = matmul(normed.T, value_row_grad)
    normed_grad = (
        matmul(query_lin_grad, weight_query.T)
        + matmul(key_lin_grad, weight_key.T)
        + matmul(value_row_grad, weight_value.T)
    )
    inputs_part, attn_gain_local = norm_back(inputs, scale_attn, gain_attn, normed_grad)
    tokens_grad = residual_grad + inputs_part
    summed = (
        lax.psum_scatter(attn_gain_local, ("rep", "ep"), scatter_dimension=0, tiled=True),
        lax.psum_scatter(q_gain_local, ("rep", "ep"), scatter_dimension=0, tiled=True),
        lax.psum_scatter(k_gain_local, ("rep", "ep"), scatter_dimension=0, tiled=True),
        lax.psum_scatter(moe_gain_local, ("rep", "ep"), scatter_dimension=0, tiled=True),
        lax.psum_scatter(query_local, ("rep", "ep"), scatter_dimension=0, tiled=True),
        lax.psum_scatter(key_local, ("rep", "ep"), scatter_dimension=0, tiled=True),
        lax.psum_scatter(value_local, ("rep", "ep"), scatter_dimension=0, tiled=True),
        lax.psum_scatter(out_local, ("rep", "ep"), scatter_dimension=0, tiled=True),
        lax.psum_scatter(router_local, ("rep", "ep"), scatter_dimension=0, tiled=True),
    )
    expert_summed = (
        lax.psum_scatter(gate_local[None], "rep", scatter_dimension=1, tiled=True),
        lax.psum_scatter(up_local[None], "rep", scatter_dimension=1, tiled=True),
        lax.psum_scatter(down_local[None], "rep", scatter_dimension=1, tiled=True),
    )
    return (
        output,
        loss,
        tokens_grad,
        summed[0],
        summed[1],
        summed[2],
        summed[3],
        summed[4],
        summed[5],
        summed[6],
        summed[7],
        summed[8],
        expert_summed[0],
        expert_summed[1],
        expert_summed[2],
    )


def dot_t(left, right):
    return lax.dot_general(left, right, (((1,), (1,)), ((), ())), preferred_element_type=jnp.float32)


def t_dot(left, right):
    return lax.dot_general(left, right, (((0,), (0,)), ((), ())), preferred_element_type=jnp.float32)


def kernel_call(kernel, **options):
    return pl.pallas_call(
        kernel,
        compiler_params=pltpu.CompilerParams(vmem_limit_bytes=VMEM_LIMIT),
        **options,
    )


def turn(value, cosine, sine):
    return value * cosine + pltpu.roll(value, HEAD_DIM // 2, 1) * sine


def code_of(place, blocks):
    return place % (blocks // 2) * 2 + place // (blocks // 2)


def place_of(code, blocks):
    return code % 2 * (blocks // 2) + code // 2


def norm_kernel(rank, *refs, codes, tiles):
    gain_ref, o_ref, scale_ref, x_ref = refs[-4:]
    for k, ref in enumerate(refs[:-4]):

        @pl.when(pl.program_id(0) // tiles == k)
        def _(ref=ref):
            x_ref[...] = ref[...].astype(jnp.float32)

    value = x_ref[...]
    scale = lax.rsqrt(jnp.mean(value * value, axis=1, keepdims=True) + norm_eps)
    scale_ref[...] = scale
    half = len(codes) // 2
    block = x_ref.shape[1] // len(codes)
    for place, code in enumerate(codes):
        columns = dynamic_block(rank[0] ^ code, block)
        piece = x_ref[:, columns] * scale * gain_ref[:, columns]
        at = place % half * block
        o_ref[place // half, :, at : at + block] = piece.astype(jnp.bfloat16)


def norm_rows(rank, parts, gain, codes):
    rows, width = parts[0].shape
    tile = 256
    tiles = rows // tile
    rows = rows * len(parts)

    def spec(k):
        return pl.BlockSpec(
            (tile, width), lambda i, rank: (jnp.clip(i - k * tiles, 0, tiles - 1), 0)
        )

    return kernel_call(
        functools.partial(norm_kernel, codes=codes, tiles=tiles),
        grid_spec=pltpu.PrefetchScalarGridSpec(
            num_scalar_prefetch=1,
            grid=(rows // tile,),
            in_specs=[spec(k) for k in range(len(parts))]
            + [pl.BlockSpec((1, width), lambda i, rank: (0, 0))],
            out_specs=[
                pl.BlockSpec((2, tile, width // 2), lambda i, rank: (0, i, 0)),
                pl.BlockSpec((tile, 1), lambda i, rank: (i, 0)),
            ],
            scratch_shapes=[pltpu.VMEM((tile, width), jnp.float32)],
        ),
        out_shape=[
            jax.ShapeDtypeStruct((2, rows, width // 2), jnp.bfloat16),
            jax.ShapeDtypeStruct((rows, 1), jnp.float32),
        ],
    )(rank, *parts, gain[None])


def project_kernel(low_ref, high_ref, a_ref, b_ref, o_ref, s_ref):
    total = matmul(low_ref[0], a_ref[...]) + matmul(high_ref[0], b_ref[...])
    o_ref[...] = total.astype(o_ref.dtype)
    s_ref[...] = jnp.sum(total * total, axis=1, keepdims=True)


def project(halves, a, b, dtype, start=0):
    _, rows, depth = halves.shape
    rows = rows - start
    width = a.shape[1]
    tile = 256
    first = start // tile
    weight = pl.BlockSpec((depth, width), lambda i: (0, 0))
    return kernel_call(
        project_kernel,
        grid=(rows // tile,),
        in_specs=[
            pl.BlockSpec((1, tile, depth), lambda i: (0, i + first, 0)),
            pl.BlockSpec((1, tile, depth), lambda i: (1, i + first, 0)),
            weight,
            weight,
        ],
        out_specs=[
            pl.BlockSpec((tile, width), lambda i: (i, 0)),
            pl.BlockSpec((tile, 1), lambda i: (i, 0)),
        ],
        out_shape=[
            jax.ShapeDtypeStruct((rows, width), dtype),
            jax.ShapeDtypeStruct((rows, 1), jnp.float32),
        ],
    )(halves, halves, a, b)


def project_back_kernel(k_ref, v_ref, w_ref, q_ref, ka, kb, va, vb, qa, qb, o_ref, *, tile):
    j = pl.program_id(0)
    half = pl.num_programs(0) // 2
    half_width = v_ref.shape[1]
    own = k_ref.shape[0] - q_ref.shape[0]

    def part(key, value, query):
        for start in range(0, k_ref.shape[0], tile):
            at = slice(start, start + tile)
            total = dot_t(k_ref[at, :], key[...]) + dot_t(v_ref[at, :], value[:, :half_width])
            total += dot_t(w_ref[at, :], value[:, half_width:])
            if start >= own:
                total += dot_t(q_ref[start - own : start - own + tile, :], query[...])
            o_ref[0, at, :] = total

    @pl.when(j < half)
    def _():
        part(ka, va, qa)

    @pl.when(j >= half)
    def _():
        part(kb, vb, qb)


def project_back(key, value, value_high, query, key_w, value_w, query_w):
    rows, width = key.shape
    depth = value_w[0].shape[0]
    step = 256
    half = depth // step
    whole = lambda value: pl.BlockSpec(value.shape, lambda j: (0, 0), pipeline_mode=pl.Buffered(1))
    low = pl.BlockSpec((step, width), lambda j: (jnp.minimum(j, half - 1), 0))
    high = pl.BlockSpec((step, width), lambda j: (jnp.maximum(j - half, 0), 0))
    return kernel_call(
        functools.partial(project_back_kernel, tile=512),
        grid=(2 * half,),
        in_specs=[whole(key), whole(value), whole(value_high), whole(query)] + [low, high] * 3,
        out_specs=pl.BlockSpec((1, rows, step), lambda j: (j // half, 0, j % half)),
        out_shape=jax.ShapeDtypeStruct((2, rows, depth), jnp.float32),
    )(key, value, value_high, query, *key_w, *value_w, *query_w)


def tokens_back_kernel(
    rank, g_ref, c_ref, x_ref, res_ref, scale_ref, gain_ref, o_ref, *, blocks
):
    scale = scale_ref[...]
    block = x_ref.shape[1] // blocks
    half = blocks // 2

    def pieces(place):
        start = pl.multiple_of((rank[0] ^ code_of(place, blocks)) * block, block)
        at = slice(place % half * block, place % half * block + block)
        grad = g_ref[place // half, :, at] + c_ref[place // half, :, at].astype(jnp.float32)
        columns = pl.ds(start, block)
        return columns, grad, x_ref[:, columns].astype(jnp.float32), gain_ref[:, columns]

    inner = jnp.zeros_like(scale)
    for place in range(blocks):
        columns, grad, value, gain = pieces(place)
        inner += jnp.sum(grad * value * gain, axis=1, keepdims=True)
    inner = inner * (1.0 / x_ref.shape[1]) * (scale * scale * scale)
    for place in range(blocks):
        columns, grad, value, gain = pieces(place)
        o_ref[:, columns] = res_ref[:, columns] + (scale * (grad * gain) - value * inner)


def tokens_back(rank, grad, carried, tokens, residual_grad, scale, gain, blocks):
    rows, width = tokens.shape
    tile = 128
    first = (grad.shape[1] - rows) // tile
    wide = pl.BlockSpec((tile, width), lambda i, rank: (i, 0))
    one = pl.BlockSpec((1, width), lambda i, rank: (0, 0))
    return kernel_call(
        functools.partial(tokens_back_kernel, blocks=blocks),
        grid_spec=pltpu.PrefetchScalarGridSpec(
            num_scalar_prefetch=1,
            grid=(rows // tile,),
            in_specs=[
                pl.BlockSpec((2, tile, width // 2), lambda i, rank: (0, i + first, 0)),
                pl.BlockSpec((2, tile, width // 2), lambda i, rank: (0, i, 0)),
                wide,
                wide,
                pl.BlockSpec((tile, 1), lambda i, rank: (i + first, 0)),
                one,
            ],
            out_specs=wide,
        ),
        out_shape=jax.ShapeDtypeStruct((rows, width), jnp.float32),
    )(rank, grad, carried, tokens, residual_grad, scale, gain[None])


def head_rows(lin, scale, gain, cosine, sine):
    return turn(lin * scale * gain, cosine, sine).astype(jnp.bfloat16)


def moved_head(head, rank):
    place = place_of((head // 2) ^ rank[0], HEADS // 2) * 2 + head % 2
    return place // (HEADS // 2), 0, place % (HEADS // 2)


def attention_specs(rows, all_rows, bias, first=0):
    head = lambda h, rank: (0, h + first)
    fixed = lambda h, rank: (0, 0)
    return [
        pl.BlockSpec((rows, HEAD_DIM), head),
        pl.BlockSpec((all_rows, HEAD_DIM), head),
        pl.BlockSpec((all_rows, HEAD_DIM), head),
        pl.BlockSpec((rows, 1), fixed),
        pl.BlockSpec((all_rows, 1), fixed),
        pl.BlockSpec((1, HEAD_DIM), head),
        pl.BlockSpec((1, HEAD_DIM), head),
        pl.BlockSpec((all_rows, HEAD_DIM), fixed),
        pl.BlockSpec((all_rows, HEAD_DIM), fixed),
        pl.BlockSpec(bias.shape, lambda h, rank: (0, 0, 0)),
    ]


def attend_kernel(
    rank,
    q_ref,
    k_ref,
    v_ref,
    sq_ref,
    sk_ref,
    gq_ref,
    gk_ref,
    cos_ref,
    sin_ref,
    bias_ref,
    *refs,
    behind,
    tile,
    span,
):
    o_ref, lse_ref = refs[-2:]
    rows = q_ref.shape[0]
    cosine, sine = cos_ref[...], sin_ref[...]
    keys = head_rows(k_ref[...], sk_ref[...], gk_ref[...], cosine, sine)
    queries = head_rows(q_ref[...], sq_ref[...], gq_ref[...], cosine[behind:], sine[behind:])
    for t in range(rows // tile):
        at = slice(t * tile, (t + 1) * tile)
        seen = slice(t * tile, t * tile + span)
        scores = dot_t(keys[seen], queries[at])
        scores = scores * HEAD_DIM ** (-0.5) + bias_ref[t].astype(jnp.float32)
        peak = jnp.max(scores, axis=0, keepdims=True)
        shifted = jnp.exp(scores - peak)
        total = jnp.sum(shifted, axis=0, keepdims=True)
        weights = (shifted * (1.0 / total)).astype(jnp.bfloat16)
        o_ref[0, at, :] = t_dot(weights, v_ref[seen, :]).astype(jnp.bfloat16)
        lse_ref[0, :, at] = peak + jnp.log(total)


def attend(rank, operands, bias, first, into=()):
    rows, width = operands[0].shape
    all_rows = operands[1].shape[0]
    tiles, span, tile = bias.shape
    return kernel_call(
        functools.partial(attend_kernel, behind=all_rows - rows, tile=tile, span=span),
        grid_spec=pltpu.PrefetchScalarGridSpec(
            num_scalar_prefetch=1,
            grid=(HEADS // 2,),
            in_specs=attention_specs(rows, all_rows, bias, first)
            + [pl.BlockSpec(memory_space=pl.ANY)] * len(into),
            out_specs=[
                pl.BlockSpec((1, rows, HEAD_DIM), lambda h, rank: moved_head(h + first, rank)),
                pl.BlockSpec((1, 1, rows), lambda h, rank: (h, 0, 0)),
            ],
        ),
        input_output_aliases={2 + len(operands): 0} if into else {},
        out_shape=[
            jax.ShapeDtypeStruct((2, rows, width // 2), jnp.bfloat16),
            jax.ShapeDtypeStruct((HEADS // 2, 1, rows), jnp.float32),
        ],
    )(rank, *operands, bias, *into)


def attend_back_kernel(
    rank,
    q_ref,
    k_ref,
    v_ref,
    sq_ref,
    sk_ref,
    gq_ref,
    gk_ref,
    cos_ref,
    sin_ref,
    bias_ref,
    g_ref,
    lse_ref,
    dq_ref,
    dk_ref,
    dv_ref,
    key_total,
    value_total,
    *,
    behind,
    tile,
    span,
):
    rows = q_ref.shape[0]
    score_scale = HEAD_DIM ** (-0.5)
    cosine, sine = cos_ref[...], sin_ref[...]
    keys = head_rows(k_ref[...], sk_ref[...], gk_ref[...], cosine, sine)
    queries = head_rows(q_ref[...], sq_ref[...], gq_ref[...], cosine[behind:], sine[behind:])
    key_total[...] = jnp.zeros_like(key_total)
    value_total[...] = jnp.zeros_like(value_total)
    for t in range(rows // tile):
        at = slice(t * tile, (t + 1) * tile)
        seen = slice(t * tile, t * tile + span)
        scores = dot_t(keys[seen], queries[at])
        scores = scores * score_scale + bias_ref[t].astype(jnp.float32)
        probs = jnp.exp(scores - lse_ref[0, :, at])
        grad = g_ref[0, at, :]
        value_total[seen, :] += matmul(probs.astype(jnp.bfloat16), grad)
        probs_grad = dot_t(v_ref[seen, :], grad)
        inner = jnp.sum(probs * probs_grad, axis=0, keepdims=True)
        score_grad = (probs * (probs_grad - inner)).astype(jnp.bfloat16)
        dq_ref[at, :] = (t_dot(score_grad, keys[seen]) * score_scale).astype(jnp.bfloat16)
        key_total[seen, :] += matmul(score_grad, queries[at])
    dk_ref[...] = (key_total[...] * score_scale).astype(jnp.bfloat16)
    dv_ref[...] = value_total[...].astype(jnp.bfloat16)


def attend_back(rank, operands, bias, grad, lse, first):
    rows, width = operands[0].shape
    width = width // 2
    all_rows = operands[1].shape[0]
    tiles, span, tile = bias.shape
    head = lambda h, rank: (0, h)
    return kernel_call(
        functools.partial(attend_back_kernel, behind=all_rows - rows, tile=tile, span=span),
        grid_spec=pltpu.PrefetchScalarGridSpec(
            num_scalar_prefetch=1,
            grid=(HEADS // 2,),
            in_specs=attention_specs(rows, all_rows, bias, first)
            + [
                pl.BlockSpec((1, rows, HEAD_DIM), lambda h, rank: moved_head(h + first, rank)),
                pl.BlockSpec((1, 1, rows), lambda h, rank: (h, 0, 0)),
            ],
            out_specs=[
                pl.BlockSpec((rows, HEAD_DIM), head),
                pl.BlockSpec((all_rows, HEAD_DIM), head),
                pl.BlockSpec((all_rows, HEAD_DIM), head),
            ],
            scratch_shapes=[
                pltpu.VMEM((all_rows, HEAD_DIM), jnp.float32),
                pltpu.VMEM((all_rows, HEAD_DIM), jnp.float32),
            ],
        ),
        out_shape=[
            jax.ShapeDtypeStruct((rows, width), jnp.bfloat16),
            jax.ShapeDtypeStruct((all_rows, width), jnp.bfloat16),
            jax.ShapeDtypeStruct((all_rows, width), jnp.bfloat16),
        ],
    )(rank, *operands, bias, grad, lse)


def lin_back_kernel(
    low_ref, high_ref, lin_ref, scale_ref, gain_ref, cos_ref, sin_ref, o_ref, gain_grad_ref, kept
):
    rows = scale_ref.shape[0]
    scale = jnp.broadcast_to(scale_ref[...], (rows, HEAD_DIM))
    cosine, sine = cos_ref[...], -sin_ref[...]

    @pl.when(pl.program_id(0) == 0)
    def _():
        gain_grad_ref[...] = jnp.zeros_like(gain_grad_ref)

    inner = jnp.zeros((rows, HEAD_DIM), jnp.float32)
    for h in range(HEADS):
        at = slice(h * HEAD_DIM, (h + 1) * HEAD_DIM)
        ref = low_ref if h < HEADS // 2 else high_ref
        here = slice(h % (HEADS // 2) * HEAD_DIM, (h % (HEADS // 2) + 1) * HEAD_DIM)
        grad = turn(ref[:, here].astype(jnp.float32), cosine, sine)
        product = grad * lin_ref[:, at]
        gain = gain_ref[:, at]
        gain_grad_ref[:, at] += jnp.sum(product * scale, axis=0, keepdims=True)
        inner += product * gain
        kept[:, at] = grad * gain * scale
    inner = jnp.sum(inner, axis=1, keepdims=True) * (1.0 / (HEADS * HEAD_DIM))
    inner = jnp.broadcast_to(inner, (rows, HEAD_DIM)) * (scale * scale * scale)
    for h in range(HEADS):
        at = slice(h * HEAD_DIM, (h + 1) * HEAD_DIM)
        o_ref[:, at] = (kept[:, at] - lin_ref[:, at] * inner).astype(jnp.bfloat16)


def lin_back(low, high, lin, scale, gain, cosine, sine):
    rows, width = lin.shape
    tile = 256
    wide = pl.BlockSpec((tile, width), lambda i: (i, 0))
    one = pl.BlockSpec((1, width), lambda i: (0, 0))
    half = pl.BlockSpec((tile, width // 2), lambda i: (i, 0))
    table = pl.BlockSpec((tile, HEAD_DIM), lambda i: (i, 0))
    return kernel_call(
        lin_back_kernel,
        grid=(rows // tile,),
        in_specs=[half, half, wide, pl.BlockSpec((tile, 1), lambda i: (i, 0)), one, table, table],
        out_specs=[wide, one],
        scratch_shapes=[pltpu.VMEM((tile, width), jnp.float32)],
        out_shape=[
            jax.ShapeDtypeStruct((rows, width), jnp.bfloat16),
            jax.ShapeDtypeStruct((1, width), jnp.float32),
        ],
    )(low, high, lin, scale, gain, cosine, sine)


def flat(ref):
    return ref[...].reshape(-1, ref.shape[-1])


def gu_spec(weights, rows):
    return pl.BlockSpec((2, rows, weights.shape[2]), lambda i, *_: (0, 0, 0))


def d_spec(weights, rows):
    last = weights.shape[1] // rows - 1
    return pl.BlockSpec((2, rows, weights.shape[2]), lambda i, *_: (0, last, 0))


def dynamic_block(index, block):
    return pl.ds(pl.multiple_of(index * block, block), block)


def experts_up_kernel(rank, x_ref, z_ref, ga, gb, ua, ub, g_ref, u_ref, my_ref, mx_ref, middle_ref):
    gate = matmul(x_ref[0], flat(ga)) + matmul(x_ref[1], flat(gb))
    up = matmul(z_ref[0], flat(ua)) + matmul(z_ref[1], flat(ub))
    g_ref[...] = gate
    u_ref[...] = up
    middle_ref[...] = (gate * jax.nn.sigmoid(gate) * up).astype(jnp.bfloat16)
    block = gate.shape[1] // 4
    for j in range(4):
        piece = middle_ref[:, dynamic_block(rank[0] ^ j, block)]
        dy, dx = j // 2, j % 2
        my_ref[dy, :, dx * block : (dx + 1) * block] = piece
        mx_ref[dx, :, dy * block : (dy + 1) * block] = piece


def experts_up(rank, by_y, by_x, weights):
    _, rows, depth = by_y.shape
    hidden = weights[0].shape[2]
    tile = 256
    x_spec = pl.BlockSpec((2, tile, depth), lambda i, rank: (0, i, 0))
    w_specs = [gu_spec(weight, depth // 2) for weight in weights]
    wide = pl.BlockSpec((tile, hidden), lambda i, rank: (i, 0))
    half = pl.BlockSpec((2, tile, hidden // 2), lambda i, rank: (0, i, 0))
    return kernel_call(
        experts_up_kernel,
        grid_spec=pltpu.PrefetchScalarGridSpec(
            num_scalar_prefetch=1,
            grid=(rows // tile,),
            in_specs=[x_spec, x_spec] + w_specs,
            out_specs=[wide, wide, half, half],
            scratch_shapes=[pltpu.VMEM((tile, hidden), jnp.bfloat16)],
        ),
        out_shape=[jax.ShapeDtypeStruct((rows, hidden), jnp.float32)] * 2
        + [jax.ShapeDtypeStruct((2, rows, hidden // 2), jnp.bfloat16)] * 2,
    )(rank, by_y, by_x, *weights)


def experts_down_kernel(*refs):
    gates, slots, outs = refs[:2], (refs[2:8], refs[8:14]), refs[14:]
    half = outs[0].shape[1] // 2
    mixtures = []
    for side in range(2):
        at = slice(side * half, (side + 1) * half)
        mixture = 0.0
        for slot, (my, mx, la, lb, ra, rb) in enumerate(slots):
            if side == 0:
                out = matmul(my[0], flat(la)) + matmul(my[1], flat(lb))
            else:
                out = matmul(mx[0], flat(ra)) + matmul(mx[1], flat(rb))
            out = out.astype(jnp.bfloat16)
            outs[slot][:, at] = out
            mixture += gates[slot][...] * out.astype(jnp.float32)
        mixtures.append(mixture)

    @pl.when(pl.program_id(0) < pl.num_programs(0) // 2)
    def _():
        outs[2][:, :half], outs[2][:, half:] = mixtures

    @pl.when(pl.program_id(0) >= pl.num_programs(0) // 2)
    def _():
        outs[3][:, :half], outs[3][:, half:] = mixtures


def experts_down(gates, slots):
    _, rows, depth = slots[0][0].shape
    half = slots[0][2].shape[2]
    tile = 256
    x_spec = pl.BlockSpec((2, tile, depth), lambda i: (0, i, 0))
    w_specs = [d_spec(weight, depth // 2) for weight in slots[0][2:]]
    wide = pl.BlockSpec((tile, 2 * half), lambda i: (i, 0))
    column = pl.BlockSpec((tile, 1), lambda i: (i, 0))
    steps = rows // tile // 2
    return kernel_call(
        experts_down_kernel,
        grid=(rows // tile,),
        in_specs=[column] * 2 + ([x_spec] * 2 + w_specs) * 2,
        out_specs=[
            wide,
            wide,
            pl.BlockSpec((tile, 2 * half), lambda i: (jnp.minimum(i, steps - 1), 0)),
            pl.BlockSpec((tile, 2 * half), lambda i: (jnp.maximum(i - steps, 0), 0)),
        ],
        out_shape=[
            jax.ShapeDtypeStruct((rows, 2 * half), jnp.bfloat16),
            jax.ShapeDtypeStruct((rows, 2 * half), jnp.bfloat16),
            jax.ShapeDtypeStruct((rows // 2, 2 * half), jnp.float32),
            jax.ShapeDtypeStruct((rows // 2, 2 * half), jnp.float32),
        ],
    )(*gates, *slots[0], *slots[1])


def experts_back_kernel(
    rank, own_ref, other_ref, out_ref, gate_ref, g_ref, u_ref, la, lb, ra, rb, p_ref, dg_ref, du_ref, gg_ref
):
    own = pl.program_id(0) < pl.num_programs(0) // 2
    grad = jnp.where(own, own_ref[...], other_ref[...])
    gg_ref[...] = jnp.sum(grad * out_ref[...].astype(jnp.float32), axis=1, keepdims=True)
    p_ref[...] = (gate_ref[...] * grad).astype(jnp.bfloat16)
    half = grad.shape[1] // 2
    left, right = p_ref[:, :half], p_ref[:, half:]
    block = la.shape[1]
    for j in range(4):
        dy, dx = j // 2, j % 2
        left_w = (la, lb)[dy][dx]
        right_w = (ra, rb)[dx][dy]
        middle_grad = dot_t(left, left_w) + dot_t(right, right_w)
        at = dynamic_block(rank[0] ^ j, block)
        gate_pre, up_pre = g_ref[:, at], u_ref[:, at]
        sigma = jax.nn.sigmoid(gate_pre)
        change = middle_grad * up_pre * sigma * (1.0 + gate_pre * (1.0 - sigma))
        dg_ref[:, at] = change.astype(jnp.bfloat16)
        du_ref[:, at] = (middle_grad * (gate_pre * sigma)).astype(jnp.bfloat16)


def experts_back(rank, own, other, out, gate, gate_pre, up_pre, weights):
    rows, width = out.shape
    hidden = gate_pre.shape[1]
    tile = 256
    wide = pl.BlockSpec((tile, width), lambda i, rank: (i, 0))
    narrow = pl.BlockSpec((tile, hidden), lambda i, rank: (i, 0))
    column = pl.BlockSpec((tile, 1), lambda i, rank: (i, 0))
    w_specs = [d_spec(weight, hidden // 4) for weight in weights]
    steps = rows // tile // 2
    return kernel_call(
        experts_back_kernel,
        grid_spec=pltpu.PrefetchScalarGridSpec(
            num_scalar_prefetch=1,
            grid=(rows // tile,),
            in_specs=[
                pl.BlockSpec((tile, width), lambda i, rank: (jnp.minimum(i, steps - 1), 0)),
                pl.BlockSpec((tile, width), lambda i, rank: (jnp.maximum(i - steps, 0), 0)),
                wide, column, narrow, narrow
            ] + w_specs,
            out_specs=[wide, narrow, narrow, column],
        ),
        out_shape=[
            jax.ShapeDtypeStruct((rows, width), jnp.bfloat16),
            jax.ShapeDtypeStruct((rows, hidden), jnp.bfloat16),
            jax.ShapeDtypeStruct((rows, hidden), jnp.bfloat16),
            jax.ShapeDtypeStruct((rows, 1), jnp.float32),
        ],
    )(rank, own, other, out, gate, gate_pre, up_pre, *weights)


def experts_input_kernel(*refs):
    totals = []
    for j in range(4):
        dy, dx = j // 2, j % 2
        total = 0.0
        for dg, du, ga, gb, ua, ub in (refs[:6], refs[6:12]):
            gate_w = (ga, gb)[dy][dx]
            up_w = (ua, ub)[dx][dy]
            part = dot_t(dg[...], gate_w) + dot_t(du[...], up_w)
            total += part.astype(jnp.bfloat16).astype(jnp.float32)
        totals.append(total)

    @pl.when(pl.program_id(0) < pl.num_programs(0) // 2)
    def _():
        for j in range(4):
            refs[-2][j] = totals[j]

    @pl.when(pl.program_id(0) >= pl.num_programs(0) // 2)
    def _():
        for j in range(4):
            refs[-1][j] = totals[j]


def experts_input(slots):
    rows, hidden = slots[0][0].shape
    depth = slots[0][2].shape[1] // 3 * 2
    tile = 256
    narrow = pl.BlockSpec((tile, hidden), lambda i: (i, 0))
    w_specs = [gu_spec(weight, depth) for weight in slots[0][2:]]
    steps = rows // tile // 2
    return kernel_call(
        experts_input_kernel,
        grid=(rows // tile,),
        in_specs=([narrow] * 2 + w_specs) * 2,
        out_specs=[
            pl.BlockSpec((4, tile, depth), lambda i: (0, jnp.minimum(i, steps - 1), 0)),
            pl.BlockSpec((4, tile, depth), lambda i: (0, jnp.maximum(i - steps, 0), 0)),
        ],
        out_shape=[jax.ShapeDtypeStruct((4, rows // 2, depth), jnp.float32)] * 2,
    )(*slots[0], *slots[1])


def residual_back_kernel(
    rank, a_ref, b_ref, lg_ref, wr_ref, x_ref, r_ref, scale_ref, gain_ref, o_ref, c_ref, gg_ref
):
    scale = scale_ref[...]
    block = a_ref.shape[2]

    @pl.when(pl.program_id(0) == 0)
    def _():
        gg_ref[...] = jnp.zeros_like(gg_ref)

    inner = jnp.zeros_like(scale)
    for j in range(4):
        at = dynamic_block(rank[0] ^ j, block)
        grad = a_ref[j] + b_ref[j]
        for e in range(wr_ref.shape[0]):
            grad += lg_ref[:, e : e + 1] * wr_ref[e : e + 1, at]
        o_ref[:, at] = grad
        product = grad * x_ref[:, at]
        inner += jnp.sum(product * gain_ref[:, at], axis=1, keepdims=True)
        gg_ref[:, at] += jnp.sum(product * scale, axis=0, keepdims=True)
    inner = inner * (1.0 / x_ref.shape[1]) * (scale * scale * scale)
    for j in range(4):
        at = slice(j * block, (j + 1) * block)
        value = scale * (o_ref[:, at] * gain_ref[:, at]) - x_ref[:, at] * inner
        value = r_ref[:, at] + value
        o_ref[:, at] = value
        c_ref[:, at] = value.astype(jnp.bfloat16)


def residual_back(rank, own, other, logit_grad, router, residual, result_grad, scale, gain):
    rows, width = residual.shape
    tile = 128
    wide = pl.BlockSpec((tile, width), lambda i, rank: (i, 0))
    piece = pl.BlockSpec((4, tile, width // 4), lambda i, rank: (0, i, 0))
    one = pl.BlockSpec((1, width), lambda i, rank: (0, 0))
    experts = logit_grad.shape[1]
    return kernel_call(
        residual_back_kernel,
        grid_spec=pltpu.PrefetchScalarGridSpec(
            num_scalar_prefetch=1,
            grid=(rows // tile,),
            in_specs=[
                piece,
                piece,
                pl.BlockSpec((tile, experts), lambda i, rank: (i, 0)),
                pl.BlockSpec((experts, width), lambda i, rank: (0, 0)),
                wide,
                wide,
                pl.BlockSpec((tile, 1), lambda i, rank: (i, 0)),
                one,
            ],
            out_specs=[wide, wide, one],
        ),
        out_shape=[
            jax.ShapeDtypeStruct((rows, width), jnp.float32),
            jax.ShapeDtypeStruct((rows, width), jnp.bfloat16),
            jax.ShapeDtypeStruct((1, width), jnp.float32),
        ],
    )(rank, own, other, logit_grad, router, residual, result_grad, scale, gain[None])


def experts_grad_kernel(x_ref, d_ref, m_ref, p_ref, *refs):
    o_ref = refs[-1]
    rows, down_rows = x_ref.shape[2], m_ref.shape[2]
    top, bottom = t_dot(x_ref[0], d_ref[...]), t_dot(m_ref[0], p_ref[...])
    if len(refs) == 2:
        top += refs[0][0, :rows].astype(jnp.float32)
        bottom += refs[0][0, rows:].astype(jnp.float32)
    o_ref[0, :rows] = top.astype(jnp.bfloat16)
    o_ref[0, rows:] = bottom.astype(jnp.bfloat16)


def experts_grad(inputs, pre_grad, middle, pair, part, side, got=()):
    _, rows, depth = inputs.shape
    hidden, down = pre_grad.shape[1], middle.shape[2]
    piece = pl.BlockSpec((1, (depth + down) // 2, hidden), lambda q: (q, 0, 0))
    return kernel_call(
        experts_grad_kernel,
        grid=(2,),
        in_specs=[
            pl.BlockSpec((1, rows, depth // 2), lambda q: (part, 0, q)),
            pl.BlockSpec((rows, hidden), lambda q: (0, 0)),
            pl.BlockSpec((1, rows, down // 2), lambda q: (part, 0, q)),
            pl.BlockSpec((rows, hidden), lambda q: (0, side)),
        ]
        + [piece] * len(got),
        out_specs=piece,
        out_shape=jax.ShapeDtypeStruct((2, (depth + down) // 2, hidden), jnp.bfloat16),
    )(inputs, pre_grad, middle, pair, *got)


def chip_grad_kernel(x_ref, *refs, count):
    o_ref = refs[-1]
    width = o_ref.shape[1] // count
    for i in range(count):
        at = slice(i * width, (i + 1) * width)
        total = t_dot(x_ref[0], refs[i][...])
        if len(refs) > count + 1:
            total += refs[count][:, at].astype(jnp.float32)
        o_ref[:, at] = total.astype(jnp.bfloat16)


def chip_grad(halves, part, grads, start=0, got=()):
    depth = halves.shape[2]
    rows = grads[0].shape[0]
    width = sum(grad.shape[1] for grad in grads)
    tile = 256
    piece = pl.BlockSpec((tile, width), lambda i: (i, 0))
    return kernel_call(
        functools.partial(chip_grad_kernel, count=len(grads)),
        grid=(depth // tile,),
        in_specs=[pl.BlockSpec((1, rows, tile), lambda i: (part, start // rows, i))]
        + [pl.BlockSpec(grad.shape, lambda i: (0, 0)) for grad in grads]
        + [piece] * len(got),
        out_specs=piece,
        out_shape=jax.ShapeDtypeStruct((depth, width), jnp.bfloat16),
    )(halves, *grads, *got)


def mixed_back_kernel(g_ref, a_ref, b_ref, o_ref):
    for half, ref in enumerate((a_ref, b_ref)):
        o_ref[half] = dot_t(g_ref[...], ref[...]).astype(jnp.bfloat16)


def mixed_back(grad, weights):
    rows, width = grad.shape
    depth = weights[0].shape[0]
    step = 256
    weight = pl.BlockSpec((step, width), lambda j: (j, 0))
    return kernel_call(
        mixed_back_kernel,
        grid=(depth // step,),
        in_specs=[pl.BlockSpec((rows, width), lambda j: (0, 0)), weight, weight],
        out_specs=pl.BlockSpec((2, rows, step), lambda j: (0, 0, j)),
        out_shape=jax.ShapeDtypeStruct((2, rows, depth), jnp.bfloat16),
    )(grad, *weights)


def across(value, bit):
    count = lax.axis_size("rep")
    return lax.ppermute(value, "rep", [(place, place ^ bit) for place in range(count)])


def along(value, steps):
    count = lax.axis_size("ep")
    return lax.ppermute(value, "ep", [(place, (place + steps) % count) for place in range(count)])


def mirrored(value, moves):
    reps, count = lax.axis_size("rep"), lax.axis_size("ep")
    pairs = []
    for rep in range(reps):
        for source, target in moves:
            if rep % 2:
                source, target = count - 1 - source, count - 1 - target
            pairs.append((rep * count + source, rep * count + target))
    return lax.ppermute(value, ("rep", "ep"), pairs)


def pick(value, index, axis):
    return lax.dynamic_index_in_dim(value, index, axis, keepdims=False)


def in_order(own, other, bit, axis):
    return jnp.where(bit == 1, jnp.stack([other, own], axis), jnp.stack([own, other], axis))


def over_ep(value, place):
    shard = place[3]
    experts = lax.axis_size("ep")
    parts = jnp.zeros((experts,) + value.shape, value.dtype)
    parts = lax.dynamic_update_index_in_dim(parts, value, shard, 0)
    for steps in range(1, experts):
        parts = lax.dynamic_update_index_in_dim(
            parts, along(value, steps), lax.rem(shard - steps + experts, experts), 0
        )
    return parts


def hold(*values):
    return lax.optimization_barrier(values)


def both_ways(value):
    return across(value[0], 2), across(value[1], 4)


def other_ways(first, second):
    return across(first, 4), across(second, 2)


def add(left, right):
    return (left.astype(jnp.float32) + right.astype(jnp.float32)).astype(jnp.bfloat16)


def ep_sum(both):
    return lax.psum_scatter(both, "ep", scatter_dimension=1, tiled=True).astype(jnp.float32)


def body(
    tokens,
    teacher,
    segment_ids,
    valid_mask,
    routes,
    attn_gain,
    q_gain,
    k_gain,
    moe_gain,
    w_query,
    w_key,
    w_value,
    w_out,
    w_router,
    w_gate,
    w_up,
    w_down,
):
    bf16, f32 = jnp.bfloat16, jnp.float32
    local_rows, width = tokens.shape
    experts = lax.axis_size("ep")
    reps = lax.axis_size("rep")
    reach = min(-(-WINDOW // local_rows), experts - 1)
    shard = lax.axis_index("ep")
    rep = lax.axis_index("rep")
    place = (rep // 4, rep // 2 % 2, rep % 2, shard)
    core = rep % 2
    total_tokens = local_rows * reps * experts

    valid = valid_mask.reshape(local_rows).astype(f32)
    own_count = jnp.sum(valid_mask)
    counts = jnp.stack([own_count // 16, own_count % 16]).astype(bf16)
    small = jnp.concatenate(
        [
            jnp.stack([attn_gain, q_gain, k_gain, moe_gain], 1),
            w_router,
            jnp.broadcast_to(counts[None], (attn_gain.shape[0], 2)),
        ],
        1,
    )
    rank = rep.astype(jnp.int32)[None]
    quarter = rep // 2
    quarter_rank = quarter.astype(jnp.int32)[None]
    order = tuple(code_of(j, reps) for j in range(reps))
    half = width // 2
    behind = reach * local_rows
    all_rows = local_rows + behind
    m = jnp.where(core == 0, shard, experts - 1 - shard)
    quarter_rows = w_gate.shape[1] // 4
    quarter_down = w_down.shape[1] // 4

    def own_part(weight, rows):
        return lax.dynamic_slice_in_dim(weight[0], quarter * rows, rows, 0)

    down = own_part(w_down, quarter_down)
    own = jnp.stack(
        [
            jnp.concatenate([own_part(w_gate, quarter_rows), down[:, :half]], 0),
            jnp.concatenate([own_part(w_up, quarter_rows), down[:, half:]], 0),
        ]
    )
    segments = segment_ids.reshape(local_rows)
    shard_rows = w_key.shape[0]
    columns = small.shape[1]
    small = small.T

    small = over_ep(small, place)
    parts = over_ep(jnp.stack([w_key, w_value]), place)
    segments_1 = from_behind(segments, "ep", 1)
    parts, small, own, tokens_1, segments_1 = hold(parts, small, own, tokens, segments_1)
    qo = jnp.stack([w_query, w_out])

    qo, parts = hold(qo, parts)
    qo = lax.all_gather(qo, "ep", axis=0)
    block = shard_rows * experts
    k_w, v_w = parts[:, 0].reshape(block, width), parts[:, 1].reshape(block, width)
    e_1 = mirrored(own, [(0, 1), (1, 2)])
    small = small.reshape(-1)
    small = jnp.pad(small, (0, 16 * width - small.shape[0])).reshape(16, width)
    k_w = jnp.concatenate([k_w, small], 0)
    k_x, v_y = both_ways((k_w, v_w))
    segments_2 = from_behind(segments_1, "ep", 1)
    k_w, k_x, v_w, v_y, tokens_1, segments_2 = hold(k_w, k_x, v_w, v_y, tokens_1, segments_2)

    k_w = jnp.stack([k_w, k_x])
    k_y, v_x = other_ways(k_w, jnp.stack([v_w, v_y]))
    tokens_1 = from_behind(tokens_1, "ep", 1)
    qo, k_w, k_y, v_w, v_y, v_x, tokens_1 = hold(qo, k_w, k_y, v_w, v_y, v_x, tokens_1)

    small = jnp.concatenate([k_w[:, block : block + 2], k_y[:, block : block + 2]], 0)
    small = jnp.pad(small.reshape(-1, width), ((0, 8), (0, 0)))
    k_w = jnp.concatenate([k_w[0, :block], k_w[1, :block], k_y[0, :block], k_y[1, :block], small], 0)
    v_w = jnp.concatenate([v_w, v_x[0], v_y, v_x[1]], 0)
    key_w, value_w = (k_w, across(k_w, 1)), (v_w, across(v_w, 1))
    q_w, o_w = qo[:, 0].reshape(-1, width), qo[:, 1].reshape(-1, width)
    q_x, o_y = both_ways((q_w, o_w))
    tokens_2 = from_behind(tokens_1, "ep", 1)
    key_w, value_w, q_w, q_x, o_w, o_y, tokens_2, tokens_1, e_1, own = hold(
        key_w, value_w, q_w, q_x, o_w, o_y, tokens_2, tokens_1, e_1, own
    )

    q_w = jnp.concatenate([q_w, q_x], 0)
    q_y, o_x = other_ways(q_w, jnp.stack([o_w, o_y]))
    q_w = jnp.concatenate([q_w, q_y], 0)
    o_w = jnp.concatenate([o_w, o_x[0], o_y, o_x[1]], 0)
    e_2 = mirrored(jnp.where(m == 2, e_1, own), [(1, 0), (2, 3)])
    small = jnp.stack([weight[4 * block : 4 * block + 8] for weight in key_w])
    small = small.reshape(2, 2, 2, -1)[..., : experts * columns * shard_rows]
    for axis, bit in enumerate((core, place[0], place[1])):
        small = jnp.where(bit == 1, jnp.flip(small, axis), small)
    small = small.reshape(2, 2, 2, experts, columns, shard_rows)
    small = jnp.transpose(small, (4, 1, 2, 0, 3, 5)).reshape(columns, -1)
    gain_attn, gain_query, gain_key, gain_moe = [small[i].astype(f32) for i in range(4)]
    weight_router = small[4 : 4 + experts].T
    counts = small[4 + experts :, ::shard_rows].astype(f32)
    count = jnp.sum(counts[0]) * 16.0 + jnp.sum(counts[1])
    key_segments = jnp.concatenate([segments_2, segments_1, segments], 0)
    normed, scale_all = norm_rows(rank, (tokens_2, tokens_1, tokens), gain_attn, order)
    key_lin, key_squares = project(normed, *key_w, f32)
    value_all, _ = project(normed, *value_w, bf16)
    q_w, o_w, e_2, e_1, own, normed, key_lin, value_all = hold(
        q_w, o_w, e_2, e_1, own, normed, key_lin, value_all
    )

    query_w, out_w = (q_w, across(q_w, 1)), (o_w, across(o_w, 1))
    e_b = jnp.where(m == 1, own, jnp.where(m == 2, e_1, e_2))
    b_x, b_y = both_ways(e_b)
    e_3 = mirrored(e_1, [(1, 2)])
    query_lin, query_squares = project(normed, *query_w, f32, behind)
    scale_key = lax.rsqrt(key_squares / width + norm_eps)
    scale_query = lax.rsqrt(query_squares / width + norm_eps)
    key_positions = (shard - reach) * local_rows + jnp.arange(all_rows, dtype=jnp.int32)
    half_head = HEAD_DIM // 2
    frequency = 10000.0 ** (-jnp.arange(half_head, dtype=f32) * 2.0 / HEAD_DIM)
    angles = key_positions[:, None].astype(f32) * frequency[None, :]
    cosine, sine = jnp.cos(angles), jnp.sin(angles)
    cosine, sine = jnp.concatenate([cosine, cosine], 1), jnp.concatenate([-sine, sine], 1)

    def mask_of(tile):
        span = behind + tile
        parts = []
        for start in range(0, local_rows, tile):
            keys = slice(start, start + span)
            queries = slice(behind + start, behind + start + tile)
            distance = key_positions[None, queries] - key_positions[keys, None]
            allowed = (
                (distance >= 0)
                & (distance < WINDOW)
                & (key_positions[keys, None] >= 0)
                & (key_segments[None, queries] == key_segments[keys, None])
            )
            parts.append(jnp.where(allowed, 0.0, -1e30).astype(f32))
        return jnp.stack(parts)

    operands = (
        query_lin,
        key_lin,
        value_all,
        scale_query,
        scale_key,
        gain_query[None],
        gain_key[None],
        cosine,
        sine,
    )
    bias_small = mask_of(local_rows // 4)
    mixed, lse_0 = attend(rank, operands, bias_small, 0)
    mixed, out_w, e_b, b_x, b_y, e_3, e_1, own = hold(mixed, out_w, e_b, b_x, b_y, e_3, e_1, own)

    b_0, b_1 = jnp.stack([e_b[0], b_x]), jnp.stack([e_b[1], b_y])
    b_2, b_3 = other_ways(b_0[:, :quarter_rows], b_1[:, :quarter_rows])
    e_4 = mirrored(e_3, [(2, 3)])
    mixed, lse_1 = attend(rank, operands, bias_small, HEADS // 2, (mixed,))
    branch, _ = project(mixed, *out_w, f32)
    residual = tokens.astype(f32) + branch
    moe, scale_moe = norm_rows(quarter_rank, (residual,), gain_moe, (0, 1, 2, 3))
    moe_y = jnp.concatenate([moe, across(moe, 1)], 1)
    piece = half // 2
    moe_x = jnp.stack(
        [
            jnp.concatenate([moe_y[0, :, i : i + piece], moe_y[1, :, i : i + piece]], 1)
            for i in (0, piece)
        ]
    )
    router_parts = weight_router.reshape(4, -1, experts)
    router_rel = jnp.concatenate([pick(router_parts, quarter ^ j, 0) for j in range(4)], 0)
    router_probs = jax.nn.softmax(
        matmul(moe[0], router_rel[:half]) + matmul(moe[1], router_rel[half:]), axis=-1
    )
    chosen = jnp.sum(
        (routes[:, :, None] == jnp.arange(experts, dtype=jnp.int32)).astype(f32), axis=1
    )
    gates = router_probs * chosen
    gates_both = jnp.concatenate([gates, across(gates, 1)], 0)
    gates_a = jnp.where(core == 0, gates_both[:, :1], gates_both[:, -1:])
    gates_b = jnp.where(core == 0, gates_both[:, 1:2], gates_both[:, -2:-1])
    b_0, b_1, b_2, b_3, e_4, e_3, e_1, own, moe_y, moe_x = hold(
        b_0, b_1, b_2, b_3, e_4, e_3, e_1, own, moe_y, moe_x
    )

    e_a = jnp.where(m == 0, own, jnp.where(m == 1, e_1, jnp.where(m == 2, e_3, e_4)))
    a_x, a_y = both_ways(e_a)
    b_4, b_5 = other_ways(b_0[:, quarter_rows:], b_1[:, quarter_rows:])
    up_weights_b, down_weights_b = (b_0, b_2, b_1, b_3), (b_0, b_4, b_1, b_5)
    gate_pre_b, up_pre_b, my_b, mx_b = experts_up(quarter_rank, moe_y, moe_x, up_weights_b)
    e_a, a_x, a_y, my_b, mx_b, moe_y, moe_x = hold(e_a, a_x, a_y, my_b, mx_b, moe_y, moe_x)

    a_0, a_1 = jnp.stack([e_a[0], a_x]), jnp.stack([e_a[1], a_y])
    a_2, a_3 = other_ways(a_0[:, :quarter_rows], a_1[:, :quarter_rows])
    a_0, a_1, a_2, a_3 = hold(a_0, a_1, a_2, a_3)

    a_4, a_5 = other_ways(a_0[:, quarter_rows:], a_1[:, quarter_rows:])
    up_weights_a, down_weights_a = (a_0, a_2, a_1, a_3), (a_0, a_4, a_1, a_5)
    gate_pre_a, up_pre_a, my_a, mx_a = experts_up(quarter_rank, moe_y, moe_x, up_weights_a)
    expert_out_a, expert_out_b, mixture, mixture_other = experts_down(
        (gates_a, gates_b), ((my_a, mx_a) + down_weights_a, (my_b, mx_b) + down_weights_b)
    )
    result = residual + (mixture + across(mixture_other, 1))
    output = result.astype(bf16)
    error = result - teacher.astype(f32)
    squares = jnp.sum(valid * jnp.sum(error * error, axis=1))
    result_grad = total_tokens / count * valid[:, None] * error
    result_other = across(result_grad, 1)

    pair_b, dg_b, du_b, gate_grad_b = experts_back(
        quarter_rank,
        result_grad,
        result_other,
        expert_out_b,
        gates_b,
        gate_pre_b,
        up_pre_b,
        down_weights_b,
    )
    sent_x = experts_grad(moe_x, dg_b, mx_b, pair_b, 1, 0)
    sent_y = experts_grad(moe_y, du_b, my_b, pair_b, 1, 1)
    sent_x, sent_y, expert_out_a = hold(sent_x, sent_y, expert_out_a)

    b_x, b_y = both_ways((sent_x, sent_y))
    pair_a, dg_a, du_a, gate_grad_a = experts_back(
        quarter_rank,
        result_grad,
        result_other,
        expert_out_a,
        gates_a,
        gate_pre_a,
        up_pre_a,
        down_weights_a,
    )
    sent_x = experts_grad(moe_x, dg_a, mx_a, pair_a, 1, 0)
    sent_y = experts_grad(moe_y, du_a, my_a, pair_a, 1, 1)
    input_grad, input_other = experts_input(
        ((dg_a, du_a) + up_weights_a, (dg_b, du_b) + up_weights_b)
    )
    slot_grads = jnp.concatenate([gate_grad_a, gate_grad_b], 1)
    own_slots, partner_slots = slot_grads[:local_rows], across(slot_grads[local_rows:], 1)
    from_low = jnp.where(core == 0, own_slots, partner_slots)
    from_high = jnp.where(core == 0, partner_slots, own_slots)
    prob_grad = chosen * jnp.concatenate([from_low, from_high[:, ::-1]], 1)
    logit_grad = router_probs * (
        prob_grad - jnp.sum(prob_grad * router_probs, axis=-1, keepdims=True)
    )
    b_x, b_y, sent_x, sent_y, input_grad, input_other, logit_grad = hold(
        b_x, b_y, sent_x, sent_y, input_grad, input_other, logit_grad
    )

    input_other = across(input_other, 1)
    a_x, a_y = both_ways((sent_x, sent_y))
    b_0 = experts_grad(moe_x, dg_b, mx_b, pair_b, 0, 0, (b_x,))
    b_1 = experts_grad(moe_y, du_b, my_b, pair_b, 0, 1, (b_y,))
    router_local = jnp.concatenate(
        [
            jnp.dot(part.T.astype(f32), logit_grad, precision=highest, preferred_element_type=f32)
            for part in (moe[0], moe[1])
        ],
        0,
    )
    router_local = router_local.reshape(4, -1, experts)
    router_local = jnp.concatenate([pick(router_local, quarter ^ j, 0) for j in range(4)], 0)
    residual_grad, branch_grad, moe_gain_local = residual_back(
        quarter_rank,
        input_grad,
        input_other,
        logit_grad,
        weight_router.astype(f32).T,
        residual,
        result_grad,
        scale_moe,
        gain_moe,
    )
    out_sent = across(chip_grad(mixed, 1, (branch_grad,)), 1)
    out_sum = chip_grad(mixed, 0, (branch_grad,), 0, (out_sent,)).reshape(2, 2, -1, width)
    mixed_grad = mixed_back(branch_grad, out_w)
    b_y, b_x = other_ways(b_0[1], b_1[1])
    bias = mask_of(local_rows // 2)
    dq_0, dk_0, dv_0 = attend_back(rank, operands, bias, mixed_grad, lse_0, 0)
    dq_1, dk_1, dv_1 = attend_back(rank, operands, bias, mixed_grad, lse_1, HEADS // 2)
    a_x, a_y, b_0, b_1, b_x, b_y, out_sum, dq_0, dk_0, dv_0, dq_1, dk_1, dv_1 = hold(
        a_x, a_y, b_0, b_1, b_x, b_y, out_sum, dq_0, dk_0, dv_0, dq_1, dk_1, dv_1
    )

    a_0 = experts_grad(moe_x, dg_a, mx_a, pair_a, 0, 0, (a_x,))
    a_1 = experts_grad(moe_y, du_a, my_a, pair_a, 0, 1, (a_y,))
    a_y, a_x = other_ways(a_0[1], a_1[1])
    out_x, out_y = across(out_sum[:, 1, :, :half], 2), across(out_sum[1, :, :, half:], 4)
    b_end = jnp.stack([add(b_0[0], b_y), add(b_1[0], b_x)])
    b_got = mirrored(b_end, [(3, 2), (0, 1)])
    value_sent = chip_grad(normed, 1, (dv_0, dv_1))
    value_got = across(value_sent, 1)
    value_sum = chip_grad(normed, 0, (dv_0, dv_1), 0, (value_got,)).reshape(2, 2, -1, width)
    value_x = across(value_sum[:, 1, :, :half], 2)
    value_y = across(value_sum[1, :, :, half:], 4)
    query_lin_grad, q_gain_local = lin_back(
        dq_0, dq_1, query_lin, scale_query, gain_query[None], cosine[behind:], sine[behind:]
    )
    key_lin_grad, k_gain_local = lin_back(
        dk_0, dk_1, key_lin, scale_key, gain_key[None], cosine, sine
    )
    query_sent = chip_grad(normed, 1, (query_lin_grad,), behind)
    key_sent = chip_grad(normed, 1, (key_lin_grad,))
    packed = jnp.concatenate(
        [
            jnp.broadcast_to(squares, (1, width)),
            q_gain_local,
            k_gain_local,
            moe_gain_local,
            router_local.T,
        ],
        0,
    )
    (
        a_0, a_1, a_x, a_y, out_sum, out_x, out_y, b_end, b_got, query_lin_grad, key_lin_grad,
        value_sum, value_x, value_y, query_sent, key_sent, packed,
    ) = hold(
        a_0, a_1, a_x, a_y, out_sum, out_x, out_y, b_end, b_got, query_lin_grad, key_lin_grad,
        value_sum, value_x, value_y, query_sent, key_sent, packed,
    )

    query_got, key_got = across(query_sent, 1), across(key_sent, 1)
    value_a = add(value_sum[:, 0, :, :half], value_x)
    value_b = add(value_sum[0, :, :, half:], value_y)
    for link in (1, 2, 4):
        packed = packed + across(packed, link)
    out_a, out_b = add(out_sum[:, 0, :, :half], out_x), add(out_sum[0, :, :, half:], out_y)
    value_a, value_b, packed, out_a, out_b = hold(value_a, value_b, packed, out_a, out_b)
    moved_x = across(jnp.stack([value_b[1], out_b[1]]), 2)
    moved_y = across(jnp.stack([value_a[1], out_a[1]]), 4)
    value_x, value_y, out_x, out_y = moved_x[0], moved_y[0], moved_x[1], moved_y[1]
    four = [add(out_a[0], out_y), add(out_b[0], out_x)]
    four += [add(value_a[0], value_y), add(value_b[0], value_x)]
    four = ep_sum(jnp.stack(four))
    out_total, value_total = four[:2], four[2:]
    b_low = add(b_end, b_got)
    b_got_2 = mirrored(b_low, [(2, 1)])
    a_end = jnp.stack([add(a_0[0], a_y), add(a_1[0], a_x)])
    a_got = mirrored(a_end, [(3, 2)])
    normed_grad = project_back(
        key_lin_grad, dv_0, dv_1, query_lin_grad, key_w, value_w, query_w
    )
    query_sum = chip_grad(normed, 0, (query_lin_grad,), behind, (query_got,))
    key_sum = chip_grad(normed, 0, (key_lin_grad,), 0, (key_got,))
    (
        normed_grad, query_sum, key_sum, out_total, value_total, b_got_2, a_end, a_got, packed,
    ) = hold(
        normed_grad, query_sum, key_sum, out_total, value_total, b_got_2, a_end, a_got, packed,
    )

    query_sum = query_sum.reshape(2, 2, -1, width)
    key_sum = key_sum.reshape(2, 2, -1, width)
    query_x, key_y = across(query_sum[:, 1], 2), across(key_sum[1], 4)
    carried = from_behind(normed_grad[:, :local_rows].astype(bf16), "ep", -1)
    a_low = add(a_end, a_got)
    a_got = mirrored(a_low, [(2, 1)])
    b_total = (b_end.astype(f32) + b_got.astype(f32) + b_got_2.astype(f32)).astype(bf16)
    query_sum, key_sum, query_x, key_y, carried, a_low, a_got, packed, b_total = hold(
        query_sum, key_sum, query_x, key_y, carried, a_low, a_got, packed, b_total
    )

    query_sum, key_sum = add(query_sum[:, 0], query_x), add(key_sum[0], key_y)
    query_y, key_x = across(query_sum[1], 4), across(key_sum[1], 2)
    for back in range(1, reach):
        here = normed_grad[:, back * local_rows : (back + 1) * local_rows] + carried.astype(f32)
        carried = from_behind(here.astype(bf16), "ep", -1)
    a_low = add(a_low, a_got)
    a_got = mirrored(a_low, [(1, 0)])
    query_sum, key_sum, query_y, key_x, carried, packed, a_low, a_got = hold(
        query_sum, key_sum, query_y, key_x, carried, packed, a_low, a_got
    )

    qk_total = ep_sum(jnp.stack([add(query_sum[0], query_y), add(key_sum[0], key_x)]))
    packed = jnp.sum(over_ep(packed, place), axis=0)
    tokens_grad = tokens_back(
        rank, normed_grad, carried, tokens, residual_grad, scale_all, gain_attn, reps
    )
    mine = jnp.where(m == 0, add(a_low, a_got), b_total)

    def own_half(piece):
        return piece.reshape(2, 2, -1, piece.shape[2])

    tops, bottoms = own_half(mine[:, :quarter_rows]), own_half(mine[:, quarter_rows:])
    halves = jnp.concatenate([tops, bottoms], 2)
    other = across(pick(halves, 1 - core, 1), 1)
    mine = jnp.where(m < 2, pick(halves, core, 1), other).astype(f32)
    top = quarter_rows // 2
    down_out = jnp.concatenate([mine[0, top:], mine[1, top:]], 1)
    out_out = jnp.concatenate([out_total[0], out_total[1]], 1)
    value_out = jnp.concatenate([value_total[0], value_total[1]], 1)
    loss = packed[0, 0] / (2.0 * count * width)
    attn_gain_out = (
        jnp.sum(w_query.astype(f32) * qk_total[0], axis=1)
        + jnp.sum(w_key.astype(f32) * qk_total[1], axis=1)
        + jnp.sum(w_value.astype(f32) * value_out, axis=1)
    ) / attn_gain.astype(f32)
    shares = lax.dynamic_slice_in_dim(
        packed, (rep * experts + shard) * shard_rows, shard_rows, 1
    )
    return (
        output,
        loss,
        tokens_grad,
        attn_gain_out,
        shares[1],
        shares[2],
        shares[3],
        qk_total[0],
        qk_total[1],
        value_out,
        out_out,
        shares[4:].T,
        mine[0, :top][None],
        mine[1, :top][None],
        down_out[None],
    )


def solution(mesh):
    placed = (
        P(("rep", "ep"), None),
        P(("rep", "ep"), None),
        P("rep", "ep"),
        P("rep", "ep"),
        P(("rep", "ep"), None),
        P(("rep", "ep")),
        P(("rep", "ep")),
        P(("rep", "ep")),
        P(("rep", "ep")),
        P(("rep", "ep"), None),
        P(("rep", "ep"), None),
        P(("rep", "ep"), None),
        P(("rep", "ep"), None),
        P(("rep", "ep"), None),
        P("ep", None, None),
        P("ep", None, None),
        P("ep", None, None),
    )
    chips = mesh.shape["rep"] == 8 and mesh.shape["ep"] == 4
    return jax.shard_map(
        body if chips else body_plain,
        mesh=mesh,
        in_specs=placed,
        out_specs=(
            P(("rep", "ep"), None),
            P(),
            P(("rep", "ep"), None),
            P(("rep", "ep")),
            P(("rep", "ep")),
            P(("rep", "ep")),
            P(("rep", "ep")),
            P(("rep", "ep"), None),
            P(("rep", "ep"), None),
            P(("rep", "ep"), None),
            P(("rep", "ep"), None),
            P(("rep", "ep"), None),
            P("ep", "rep", None),
            P("ep", "rep", None),
            P("ep", "rep", None),
        ),
        check_vma=False,
    )
```

```python
import functools

import jax
import jax.numpy as jnp
from jax import lax
from jax.experimental import pallas as pl
from jax.experimental.pallas import tpu as pltpu
from jax.sharding import PartitionSpec as P

HEADS = 16
HEAD_DIM = 128
WINDOW = 1024
TOP = 2
VMEM_LIMIT = 56 * 1024 * 1024


norm_eps = 1e-05
highest = lax.Precision.HIGHEST


def from_behind(value, axis, steps):
    count = lax.axis_size(axis)
    leading, last = (max(0, -steps), min(count, count - steps))
    return lax.ppermute(value, axis, [(source, source + steps) for source in range(leading, last)])


def matmul(left, right):
    return jnp.dot(left, right, preferred_element_type=jnp.float32)


def rms_scale(value):
    return lax.rsqrt(jnp.mean(value * value, axis=-1, keepdims=True) + norm_eps)


def norm_back(value, scale, gain, grad):
    weighted = grad * gain
    inner = jnp.mean(weighted * value, axis=-1, keepdims=True)
    return (
        scale * weighted - value * (scale * scale * scale) * inner,
        jnp.sum(grad * value * scale, axis=0),
    )


def rounded(value):
    return lax.optimization_barrier(value.astype(jnp.bfloat16)).astype(jnp.float32)


def rotary_tables(positions, head_size):
    half = head_size // 2
    frequency = 10000.0 ** (-jnp.arange(half, dtype=jnp.float32) * 2.0 / head_size)
    angles = positions[:, None].astype(jnp.float32) * frequency[None, :]
    cosine = jnp.cos(angles)
    sine = jnp.sin(angles)
    return (
        jnp.concatenate([cosine, cosine], -1)[:, None, :],
        jnp.concatenate([sine, sine], -1)[:, None, :],
    )


def rotate(value, cosine, sine):
    half = value.shape[-1] // 2
    turned = jnp.concatenate([-value[..., half:], value[..., :half]], -1)
    return value * cosine + turned * sine


def rotate_back(grad, cosine, sine):
    half = grad.shape[-1] // 2
    scaled = grad * sine
    turned = jnp.concatenate([scaled[..., half:], -scaled[..., :half]], -1)
    return grad * cosine + turned


def unpack(everything):
    gains = [everything[index].astype(jnp.float32) for index in range(4)]
    return (gains, everything[4], everything[5], everything[6], everything[7], everything[8])


def body_plain(
    tokens,
    teacher,
    segment_ids,
    valid_mask,
    routes,
    attn_gain,
    q_gain,
    k_gain,
    moe_gain,
    w_query,
    w_key,
    w_value,
    w_out,
    w_router,
    w_gate,
    w_up,
    w_down,
):
    local_rows, width = tokens.shape
    experts = lax.axis_size("ep")
    pairs = local_rows * TOP
    capacity = 5 * pairs // (4 * experts)
    reach = min(-(-WINDOW // local_rows), experts - 1)
    group = min(HEADS, 4)
    score_scale = HEAD_DIM ** (-0.5)
    shard = lax.axis_index("ep")
    total_tokens = local_rows * lax.axis_size("rep") * experts
    everything = (
        lax.all_gather(attn_gain, ("rep", "ep"), axis=0, tiled=True),
        lax.all_gather(q_gain, ("rep", "ep"), axis=0, tiled=True),
        lax.all_gather(k_gain, ("rep", "ep"), axis=0, tiled=True),
        lax.all_gather(moe_gain, ("rep", "ep"), axis=0, tiled=True),
        lax.all_gather(w_query, ("rep", "ep"), axis=0, tiled=True),
        lax.all_gather(w_key, ("rep", "ep"), axis=0, tiled=True),
        lax.all_gather(w_value, ("rep", "ep"), axis=0, tiled=True),
        lax.all_gather(w_out, ("rep", "ep"), axis=0, tiled=True),
        lax.all_gather(w_router, ("rep", "ep"), axis=0, tiled=True),
    )
    gains, weight_query, weight_key, weight_value, weight_out, weight_router = unpack(everything)
    gain_attn, gain_query, gain_key, gain_moe = gains
    inputs = tokens.astype(jnp.float32)
    scale_attn = rms_scale(inputs)
    normed = (inputs * scale_attn * gain_attn).astype(jnp.bfloat16)
    query_lin = matmul(normed, weight_query)
    key_lin = matmul(normed, weight_key)
    value_rows = (
        matmul(normed, weight_value).astype(jnp.bfloat16).reshape(local_rows, HEADS, HEAD_DIM)
    )
    scale_query = rms_scale(query_lin)
    scale_key = rms_scale(key_lin)
    positions = shard * local_rows + jnp.arange(local_rows, dtype=jnp.int32)
    cosine, sine = rotary_tables(positions, HEAD_DIM)
    query_rows = rotate(
        (query_lin * scale_query * gain_query).reshape(local_rows, HEADS, HEAD_DIM), cosine, sine
    ).astype(jnp.bfloat16)
    key_rows = rotate(
        (key_lin * scale_key * gain_key).reshape(local_rows, HEADS, HEAD_DIM), cosine, sine
    ).astype(jnp.bfloat16)
    segments = segment_ids.reshape(local_rows)
    key_parts, value_parts, segment_parts = ([], [], [])
    for back in range(reach, 0, -1):
        moved = from_behind((key_rows, value_rows, segments.astype(jnp.bfloat16)), "ep", back)
        key_parts.append(moved[0])
        value_parts.append(moved[1])
        segment_parts.append(moved[2].astype(jnp.int32))
    all_keys = jnp.concatenate(key_parts + [key_rows], 0)
    all_values = jnp.concatenate(value_parts + [value_rows], 0)
    key_segments = jnp.concatenate(segment_parts + [segments], 0)
    key_positions = (shard - reach) * local_rows + jnp.arange(
        (reach + 1) * local_rows, dtype=jnp.int32
    )
    distance = positions[:, None] - key_positions[None, :]
    allowed = (
        (distance >= 0)
        & (distance < WINDOW)
        & (key_positions[None, :] >= 0)
        & (segments[:, None] == key_segments[None, :])
    )

    def by_group(value):
        return jnp.moveaxis(value.reshape(value.shape[0], HEADS // group, group, HEAD_DIM), 1, 0)

    def from_group(value):
        return jnp.moveaxis(value, 0, 1).reshape(value.shape[1], HEADS * HEAD_DIM)

    def scores_of(query_group, key_group):
        raw = (
            jnp.einsum("qhd,khd->hqk", query_group, key_group, preferred_element_type=jnp.float32)
            * score_scale
        )
        return jnp.where(allowed[None], raw, -1e30)

    def attend_forward(item):
        query_group, key_group, value_group = item
        scores = scores_of(query_group, key_group)
        peak = jnp.max(scores, axis=-1, keepdims=True)
        shifted = jnp.exp(scores - peak)
        total = jnp.sum(shifted, axis=-1, keepdims=True)
        weights = (shifted / total).astype(jnp.bfloat16)
        mixed = jnp.einsum("hqk,khd->qhd", weights, value_group, preferred_element_type=jnp.float32)
        return (mixed, peak, total)

    query_groups = by_group(query_rows)
    key_groups = by_group(all_keys)
    value_groups = by_group(all_values)
    mixed, peaks, totals = lax.map(attend_forward, (query_groups, key_groups, value_groups))
    mixed_rows = from_group(mixed).astype(jnp.bfloat16)
    residual = inputs + matmul(mixed_rows, weight_out)
    scale_moe = rms_scale(residual)
    normed_moe = (residual * scale_moe * gain_moe).astype(jnp.bfloat16)
    router_probs = jax.nn.softmax(matmul(normed_moe, weight_router), axis=-1)
    flat_routes = routes.reshape(pairs)
    choose = (flat_routes[:, None] == jnp.arange(experts, dtype=jnp.int32)[None, :]).astype(
        jnp.int32
    )
    rank = jnp.sum((jnp.cumsum(choose, axis=0) - choose) * choose, axis=1)
    slots = flat_routes * capacity + rank
    pair_source = (
        jnp.full((experts * capacity,), pairs, jnp.int32)
        .at[slots]
        .set(jnp.arange(pairs, dtype=jnp.int32))
    )
    token_source = jnp.where(pair_source < pairs, pair_source // TOP, local_rows)
    zero_row = jnp.zeros((1, width), jnp.bfloat16)
    outgoing = jnp.concatenate([normed_moe, zero_row], 0)[token_source].reshape(
        experts, capacity, width
    )
    choose_float = choose.reshape(local_rows, TOP, experts).astype(jnp.float32)
    gate_value = jnp.sum(choose_float * router_probs[:, None, :], axis=2)
    gate_weight = w_gate[0]
    up_weight = w_up[0]
    down_weight = w_down[0]
    piece = lax.all_to_all(outgoing, "ep", split_axis=0, concat_axis=0, tiled=True)
    flat = piece.reshape(-1, width)
    gate_pre = matmul(flat, gate_weight)
    up_pre = matmul(flat, up_weight)
    middle = (jax.nn.silu(gate_pre) * up_pre).astype(jnp.bfloat16)
    expert_out = matmul(middle, down_weight).astype(jnp.bfloat16)
    lead = piece.shape[:2]
    returned = expert_out.reshape(piece.shape)
    gate_kept = gate_pre.reshape(lead + (-1,))
    up_kept = up_pre.reshape(lead + (-1,))
    arrived = lax.all_to_all(returned, "ep", split_axis=0, concat_axis=0, tiled=True)
    expert_rows = arrived.reshape(experts * capacity, width)[slots].reshape(local_rows, TOP, width)
    result = residual + jnp.sum(gate_value[:, :, None] * expert_rows, axis=1)
    output = result.astype(jnp.bfloat16)
    valid = valid_mask.reshape(local_rows).astype(jnp.float32)
    error = result - teacher.astype(jnp.float32)
    squares = jnp.sum(valid * jnp.sum(error * error, axis=1))
    total_squares, count = lax.psum((squares, jnp.sum(valid)), ("rep", "ep"))
    loss = total_squares / (2.0 * count * width)
    result_grad = total_tokens / count * valid[:, None] * error
    gate_value_grad = jnp.sum(result_grad[:, None, :] * expert_rows, axis=2)
    pair_grad = (
        (gate_value[:, :, None] * result_grad[:, None, :])
        .astype(jnp.bfloat16)
        .reshape(pairs, width)
    )
    grad_outgoing = jnp.concatenate([pair_grad, zero_row], 0)[pair_source].reshape(
        experts, capacity, width
    )
    grad_in = lax.all_to_all(grad_outgoing, "ep", split_axis=0, concat_axis=0, tiled=True)
    rows_in = piece.reshape(-1, width)
    gate_pre = gate_kept.reshape(rows_in.shape[0], -1)
    up_pre = up_kept.reshape(rows_in.shape[0], -1)
    flat_grad = grad_in.reshape(-1, width)
    sigma = jax.nn.sigmoid(gate_pre)
    active = gate_pre * sigma
    middle = (active * up_pre).astype(jnp.bfloat16)
    down_local = matmul(middle.T, flat_grad)
    middle_grad = matmul(flat_grad, down_weight.T)
    gate_pre_grad = (middle_grad * up_pre * sigma * (1.0 + gate_pre * (1.0 - sigma))).astype(
        jnp.bfloat16
    )
    up_pre_grad = (middle_grad * active).astype(jnp.bfloat16)
    gate_local = matmul(rows_in.T, gate_pre_grad)
    up_local = matmul(rows_in.T, up_pre_grad)
    input_grad = (matmul(gate_pre_grad, gate_weight.T) + matmul(up_pre_grad, up_weight.T)).astype(
        jnp.bfloat16
    )
    back_rows = lax.all_to_all(
        input_grad.reshape(experts, capacity, width), "ep", split_axis=0, concat_axis=0, tiled=True
    )
    pair_back = back_rows.reshape(experts * capacity, width)[slots].reshape(local_rows, TOP, width)
    everything = (
        lax.all_gather(attn_gain, ("rep", "ep"), axis=0, tiled=True),
        lax.all_gather(q_gain, ("rep", "ep"), axis=0, tiled=True),
        lax.all_gather(k_gain, ("rep", "ep"), axis=0, tiled=True),
        lax.all_gather(moe_gain, ("rep", "ep"), axis=0, tiled=True),
        lax.all_gather(w_query, ("rep", "ep"), axis=0, tiled=True),
        lax.all_gather(w_key, ("rep", "ep"), axis=0, tiled=True),
        lax.all_gather(w_value, ("rep", "ep"), axis=0, tiled=True),
        lax.all_gather(w_out, ("rep", "ep"), axis=0, tiled=True),
        lax.all_gather(w_router, ("rep", "ep"), axis=0, tiled=True),
    )
    gains, weight_query, weight_key, weight_value, weight_out, weight_router = unpack(everything)
    gain_attn, gain_query, gain_key, gain_moe = gains
    prob_grad = jnp.sum(choose_float * gate_value_grad[:, :, None], axis=1)
    logit_grad = router_probs * (
        prob_grad - jnp.sum(prob_grad * router_probs, axis=-1, keepdims=True)
    )
    router_local = jnp.dot(
        normed_moe.T, logit_grad, precision=highest, preferred_element_type=jnp.float32
    )
    normed_moe_grad = jnp.sum(pair_back.astype(jnp.float32), axis=1) + jnp.dot(
        logit_grad, weight_router.T, precision=highest, preferred_element_type=jnp.float32
    )
    residual_part, moe_gain_local = norm_back(residual, scale_moe, gain_moe, normed_moe_grad)
    residual_grad = result_grad + residual_part
    branch_grad = residual_grad.astype(jnp.bfloat16)
    out_local = matmul(mixed_rows.T, branch_grad)
    mixed_grad = (
        matmul(branch_grad, weight_out.T).astype(jnp.bfloat16).reshape(local_rows, HEADS, HEAD_DIM)
    )

    def attend_backward(item):
        query_group, key_group, value_group, grad_group, peak, total = item
        scores = scores_of(query_group, key_group)
        probs = jnp.exp(scores - peak) / total
        weights = probs.astype(jnp.bfloat16)
        value_part = jnp.einsum(
            "hqk,qhd->khd", weights, grad_group, preferred_element_type=jnp.float32
        )
        probs_grad = jnp.einsum(
            "qhd,khd->hqk", grad_group, value_group, preferred_element_type=jnp.float32
        )
        inner = jnp.sum(probs * probs_grad, axis=-1, keepdims=True)
        score_grad = (probs * (probs_grad - inner)).astype(jnp.bfloat16)
        query_part = (
            jnp.einsum("hqk,khd->qhd", score_grad, key_group, preferred_element_type=jnp.float32)
            * score_scale
        )
        key_part = (
            jnp.einsum("hqk,qhd->khd", score_grad, query_group, preferred_element_type=jnp.float32)
            * score_scale
        )
        return (query_part, key_part, value_part)

    query_parts, key_parts_grad, value_parts_grad = lax.map(
        attend_backward,
        (query_groups, key_groups, value_groups, by_group(mixed_grad), peaks, totals),
    )
    query_row_grad = from_group(query_parts)
    key_all_grad = from_group(key_parts_grad)
    value_all_grad = from_group(value_parts_grad)
    own_keys = key_all_grad[reach * local_rows :]
    own_values = value_all_grad[reach * local_rows :]
    for back in range(1, reach + 1):
        start = (reach - back) * local_rows
        moved = from_behind(
            (key_all_grad[start : start + local_rows], value_all_grad[start : start + local_rows]),
            "ep",
            -back,
        )
        own_keys = own_keys + moved[0]
        own_values = own_values + moved[1]
    query_turned = rotate_back(
        rounded(query_row_grad).reshape(local_rows, HEADS, HEAD_DIM), cosine, sine
    ).reshape(local_rows, width)
    key_turned = rotate_back(
        rounded(own_keys).reshape(local_rows, HEADS, HEAD_DIM), cosine, sine
    ).reshape(local_rows, width)
    query_lin_grad, q_gain_local = norm_back(query_lin, scale_query, gain_query, query_turned)
    key_lin_grad, k_gain_local = norm_back(key_lin, scale_key, gain_key, key_turned)
    query_lin_grad = query_lin_grad.astype(jnp.bfloat16)
    key_lin_grad = key_lin_grad.astype(jnp.bfloat16)
    value_row_grad = own_values.astype(jnp.bfloat16)
    query_local = matmul(normed.T, query_lin_grad)
    key_local = matmul(normed.T, key_lin_grad)
    value_local = matmul(normed.T, value_row_grad)
    normed_grad = (
        matmul(query_lin_grad, weight_query.T)
        + matmul(key_lin_grad, weight_key.T)
        + matmul(value_row_grad, weight_value.T)
    )
    inputs_part, attn_gain_local = norm_back(inputs, scale_attn, gain_attn, normed_grad)
    tokens_grad = residual_grad + inputs_part
    summed = (
        lax.psum_scatter(attn_gain_local, ("rep", "ep"), scatter_dimension=0, tiled=True),
        lax.psum_scatter(q_gain_local, ("rep", "ep"), scatter_dimension=0, tiled=True),
        lax.psum_scatter(k_gain_local, ("rep", "ep"), scatter_dimension=0, tiled=True),
        lax.psum_scatter(moe_gain_local, ("rep", "ep"), scatter_dimension=0, tiled=True),
        lax.psum_scatter(query_local, ("rep", "ep"), scatter_dimension=0, tiled=True),
        lax.psum_scatter(key_local, ("rep", "ep"), scatter_dimension=0, tiled=True),
        lax.psum_scatter(value_local, ("rep", "ep"), scatter_dimension=0, tiled=True),
        lax.psum_scatter(out_local, ("rep", "ep"), scatter_dimension=0, tiled=True),
        lax.psum_scatter(router_local, ("rep", "ep"), scatter_dimension=0, tiled=True),
    )
    expert_summed = (
        lax.psum_scatter(gate_local[None], "rep", scatter_dimension=1, tiled=True),
        lax.psum_scatter(up_local[None], "rep", scatter_dimension=1, tiled=True),
        lax.psum_scatter(down_local[None], "rep", scatter_dimension=1, tiled=True),
    )
    return (
        output,
        loss,
        tokens_grad,
        summed[0],
        summed[1],
        summed[2],
        summed[3],
        summed[4],
        summed[5],
        summed[6],
        summed[7],
        summed[8],
        expert_summed[0],
        expert_summed[1],
        expert_summed[2],
    )


def dot_t(left, right):
    return lax.dot_general(left, right, (((1,), (1,)), ((), ())), preferred_element_type=jnp.float32)


def t_dot(left, right):
    return lax.dot_general(left, right, (((0,), (0,)), ((), ())), preferred_element_type=jnp.float32)


def kernel_call(kernel, **options):
    return pl.pallas_call(
        kernel,
        compiler_params=pltpu.CompilerParams(vmem_limit_bytes=VMEM_LIMIT),
        **options,
    )


def turn(value, cosine, sine):
    return value * cosine + pltpu.roll(value, HEAD_DIM // 2, 1) * sine


def code_of(place, blocks):
    return place % (blocks // 2) * 2 + place // (blocks // 2)


def place_of(code, blocks):
    return code % 2 * (blocks // 2) + code // 2


def norm_kernel(rank, *refs, codes, tiles):
    gain_ref, o_ref, scale_ref, x_ref = refs[-4:]
    for k, ref in enumerate(refs[:-4]):

        @pl.when(pl.program_id(0) // tiles == k)
        def _(ref=ref):
            x_ref[...] = ref[...].astype(jnp.float32)

    value = x_ref[...]
    scale = lax.rsqrt(jnp.mean(value * value, axis=1, keepdims=True) + norm_eps)
    scale_ref[...] = scale
    half = len(codes) // 2
    block = x_ref.shape[1] // len(codes)
    for place, code in enumerate(codes):
        columns = dynamic_block(rank[0] ^ code, block)
        piece = x_ref[:, columns] * scale * gain_ref[:, columns]
        at = place % half * block
        o_ref[place // half, :, at : at + block] = piece.astype(jnp.bfloat16)


def norm_rows(rank, parts, gain, codes):
    rows, width = parts[0].shape
    tile = 256
    tiles = rows // tile
    rows = rows * len(parts)

    def spec(k):
        return pl.BlockSpec(
            (tile, width), lambda i, rank: (jnp.clip(i - k * tiles, 0, tiles - 1), 0)
        )

    return kernel_call(
        functools.partial(norm_kernel, codes=codes, tiles=tiles),
        grid_spec=pltpu.PrefetchScalarGridSpec(
            num_scalar_prefetch=1,
            grid=(rows // tile,),
            in_specs=[spec(k) for k in range(len(parts))]
            + [pl.BlockSpec((1, width), lambda i, rank: (0, 0))],
            out_specs=[
                pl.BlockSpec((2, tile, width // 2), lambda i, rank: (0, i, 0)),
                pl.BlockSpec((tile, 1), lambda i, rank: (i, 0)),
            ],
            scratch_shapes=[pltpu.VMEM((tile, width), jnp.float32)],
        ),
        out_shape=[
            jax.ShapeDtypeStruct((2, rows, width // 2), jnp.bfloat16),
            jax.ShapeDtypeStruct((rows, 1), jnp.float32),
        ],
    )(rank, *parts, gain[None])


def project_kernel(low_ref, high_ref, a_ref, b_ref, o_ref, s_ref):
    total = matmul(low_ref[0], a_ref[...]) + matmul(high_ref[0], b_ref[...])
    o_ref[...] = total.astype(o_ref.dtype)
    s_ref[...] = jnp.sum(total * total, axis=1, keepdims=True)


def project(halves, a, b, dtype, start=0):
    _, rows, depth = halves.shape
    rows = rows - start
    width = a.shape[1]
    tile = 256
    first = start // tile
    weight = pl.BlockSpec((depth, width), lambda i: (0, 0))
    return kernel_call(
        project_kernel,
        grid=(rows // tile,),
        in_specs=[
            pl.BlockSpec((1, tile, depth), lambda i: (0, i + first, 0)),
            pl.BlockSpec((1, tile, depth), lambda i: (1, i + first, 0)),
            weight,
            weight,
        ],
        out_specs=[
            pl.BlockSpec((tile, width), lambda i: (i, 0)),
            pl.BlockSpec((tile, 1), lambda i: (i, 0)),
        ],
        out_shape=[
            jax.ShapeDtypeStruct((rows, width), dtype),
            jax.ShapeDtypeStruct((rows, 1), jnp.float32),
        ],
    )(halves, halves, a, b)


def project_back_kernel(k_ref, v_ref, w_ref, q_ref, ka, kb, va, vb, qa, qb, o_ref, *, tile):
    j = pl.program_id(0)
    half = pl.num_programs(0) // 2
    half_width = v_ref.shape[1]
    own = k_ref.shape[0] - q_ref.shape[0]

    def part(key, value, query):
        for start in range(0, k_ref.shape[0], tile):
            at = slice(start, start + tile)
            total = dot_t(k_ref[at, :], key[...]) + dot_t(v_ref[at, :], value[:, :half_width])
            total += dot_t(w_ref[at, :], value[:, half_width:])
            if start >= own:
                total += dot_t(q_ref[start - own : start - own + tile, :], query[...])
            o_ref[0, at, :] = total

    @pl.when(j < half)
    def _():
        part(ka, va, qa)

    @pl.when(j >= half)
    def _():
        part(kb, vb, qb)


def project_back(key, value, value_high, query, key_w, value_w, query_w):
    rows, width = key.shape
    depth = value_w[0].shape[0]
    step = 256
    half = depth // step
    whole = lambda value: pl.BlockSpec(value.shape, lambda j: (0, 0), pipeline_mode=pl.Buffered(1))
    low = pl.BlockSpec((step, width), lambda j: (jnp.minimum(j, half - 1), 0))
    high = pl.BlockSpec((step, width), lambda j: (jnp.maximum(j - half, 0), 0))
    return kernel_call(
        functools.partial(project_back_kernel, tile=512),
        grid=(2 * half,),
        in_specs=[whole(key), whole(value), whole(value_high), whole(query)] + [low, high] * 3,
        out_specs=pl.BlockSpec((1, rows, step), lambda j: (j // half, 0, j % half)),
        out_shape=jax.ShapeDtypeStruct((2, rows, depth), jnp.float32),
    )(key, value, value_high, query, *key_w, *value_w, *query_w)


def tokens_back_kernel(
    rank, g_ref, c_ref, x_ref, res_ref, scale_ref, gain_ref, o_ref, *, blocks
):
    scale = scale_ref[...]
    block = x_ref.shape[1] // blocks
    half = blocks // 2

    def pieces(place):
        start = pl.multiple_of((rank[0] ^ code_of(place, blocks)) * block, block)
        at = slice(place % half * block, place % half * block + block)
        grad = g_ref[place // half, :, at] + c_ref[place // half, :, at].astype(jnp.float32)
        columns = pl.ds(start, block)
        return columns, grad, x_ref[:, columns].astype(jnp.float32), gain_ref[:, columns]

    inner = jnp.zeros_like(scale)
    for place in range(blocks):
        columns, grad, value, gain = pieces(place)
        inner += jnp.sum(grad * value * gain, axis=1, keepdims=True)
    inner = inner * (1.0 / x_ref.shape[1]) * (scale * scale * scale)
    for place in range(blocks):
        columns, grad, value, gain = pieces(place)
        o_ref[:, columns] = res_ref[:, columns] + (scale * (grad * gain) - value * inner)


def tokens_back(rank, grad, carried, tokens, residual_grad, scale, gain, blocks):
    rows, width = tokens.shape
    tile = 128
    first = (grad.shape[1] - rows) // tile
    wide = pl.BlockSpec((tile, width), lambda i, rank: (i, 0))
    one = pl.BlockSpec((1, width), lambda i, rank: (0, 0))
    return kernel_call(
        functools.partial(tokens_back_kernel, blocks=blocks),
        grid_spec=pltpu.PrefetchScalarGridSpec(
            num_scalar_prefetch=1,
            grid=(rows // tile,),
            in_specs=[
                pl.BlockSpec((2, tile, width // 2), lambda i, rank: (0, i + first, 0)),
                pl.BlockSpec((2, tile, width // 2), lambda i, rank: (0, i, 0)),
                wide,
                wide,
                pl.BlockSpec((tile, 1), lambda i, rank: (i + first, 0)),
                one,
            ],
            out_specs=wide,
        ),
        out_shape=jax.ShapeDtypeStruct((rows, width), jnp.float32),
    )(rank, grad, carried, tokens, residual_grad, scale, gain[None])


def head_rows(lin, scale, gain, cosine, sine):
    return turn(lin * scale * gain, cosine, sine).astype(jnp.bfloat16)


def moved_head(head, rank):
    place = place_of((head // 2) ^ rank[0], HEADS // 2) * 2 + head % 2
    return place // (HEADS // 2), 0, place % (HEADS // 2)


def attention_specs(rows, all_rows, bias, first=0):
    head = lambda h, rank: (0, h + first)
    fixed = lambda h, rank: (0, 0)
    return [
        pl.BlockSpec((rows, HEAD_DIM), head),
        pl.BlockSpec((all_rows, HEAD_DIM), head),
        pl.BlockSpec((all_rows, HEAD_DIM), head),
        pl.BlockSpec((rows, 1), fixed),
        pl.BlockSpec((all_rows, 1), fixed),
        pl.BlockSpec((1, HEAD_DIM), head),
        pl.BlockSpec((1, HEAD_DIM), head),
        pl.BlockSpec((all_rows, HEAD_DIM), fixed),
        pl.BlockSpec((all_rows, HEAD_DIM), fixed),
        pl.BlockSpec(bias.shape, lambda h, rank: (0, 0, 0)),
    ]


def attend_kernel(
    rank,
    q_ref,
    k_ref,
    v_ref,
    sq_ref,
    sk_ref,
    gq_ref,
    gk_ref,
    cos_ref,
    sin_ref,
    bias_ref,
    *refs,
    behind,
    tile,
    span,
):
    o_ref, lse_ref = refs[-2:]
    rows = q_ref.shape[0]
    cosine, sine = cos_ref[...], sin_ref[...]
    keys = head_rows(k_ref[...], sk_ref[...], gk_ref[...], cosine, sine)
    queries = head_rows(q_ref[...], sq_ref[...], gq_ref[...], cosine[behind:], sine[behind:])
    for t in range(rows // tile):
        at = slice(t * tile, (t + 1) * tile)
        seen = slice(t * tile, t * tile + span)
        scores = dot_t(keys[seen], queries[at])
        scores = scores * HEAD_DIM ** (-0.5) + bias_ref[t].astype(jnp.float32)
        peak = jnp.max(scores, axis=0, keepdims=True)
        shifted = jnp.exp(scores - peak)
        total = jnp.sum(shifted, axis=0, keepdims=True)
        weights = (shifted * (1.0 / total)).astype(jnp.bfloat16)
        o_ref[0, at, :] = t_dot(weights, v_ref[seen, :]).astype(jnp.bfloat16)
        lse_ref[0, :, at] = peak + jnp.log(total)


def attend(rank, operands, bias, first, into=()):
    rows, width = operands[0].shape
    all_rows = operands[1].shape[0]
    tiles, span, tile = bias.shape
    return kernel_call(
        functools.partial(attend_kernel, behind=all_rows - rows, tile=tile, span=span),
        grid_spec=pltpu.PrefetchScalarGridSpec(
            num_scalar_prefetch=1,
            grid=(HEADS // 2,),
            in_specs=attention_specs(rows, all_rows, bias, first)
            + [pl.BlockSpec(memory_space=pl.ANY)] * len(into),
            out_specs=[
                pl.BlockSpec((1, rows, HEAD_DIM), lambda h, rank: moved_head(h + first, rank)),
                pl.BlockSpec((1, 1, rows), lambda h, rank: (h, 0, 0)),
            ],
        ),
        input_output_aliases={2 + len(operands): 0} if into else {},
        out_shape=[
            jax.ShapeDtypeStruct((2, rows, width // 2), jnp.bfloat16),
            jax.ShapeDtypeStruct((HEADS // 2, 1, rows), jnp.float32),
        ],
    )(rank, *operands, bias, *into)


def attend_back_kernel(
    rank,
    q_ref,
    k_ref,
    v_ref,
    sq_ref,
    sk_ref,
    gq_ref,
    gk_ref,
    cos_ref,
    sin_ref,
    bias_ref,
    g_ref,
    lse_ref,
    dq_ref,
    dk_ref,
    dv_ref,
    key_total,
    value_total,
    *,
    behind,
    tile,
    span,
):
    rows = q_ref.shape[0]
    score_scale = HEAD_DIM ** (-0.5)
    cosine, sine = cos_ref[...], sin_ref[...]
    keys = head_rows(k_ref[...], sk_ref[...], gk_ref[...], cosine, sine)
    queries = head_rows(q_ref[...], sq_ref[...], gq_ref[...], cosine[behind:], sine[behind:])
    key_total[...] = jnp.zeros_like(key_total)
    value_total[...] = jnp.zeros_like(value_total)
    for t in range(rows // tile):
        at = slice(t * tile, (t + 1) * tile)
        seen = slice(t * tile, t * tile + span)
        scores = dot_t(keys[seen], queries[at])
        scores = scores * score_scale + bias_ref[t].astype(jnp.float32)
        probs = jnp.exp(scores - lse_ref[0, :, at])
        grad = g_ref[0, at, :]
        value_total[seen, :] += matmul(probs.astype(jnp.bfloat16), grad)
        probs_grad = dot_t(v_ref[seen, :], grad)
        inner = jnp.sum(probs * probs_grad, axis=0, keepdims=True)
        score_grad = (probs * (probs_grad - inner)).astype(jnp.bfloat16)
        dq_ref[at, :] = (t_dot(score_grad, keys[seen]) * score_scale).astype(jnp.bfloat16)
        key_total[seen, :] += matmul(score_grad, queries[at])
    dk_ref[...] = (key_total[...] * score_scale).astype(jnp.bfloat16)
    dv_ref[...] = value_total[...].astype(jnp.bfloat16)


def attend_back(rank, operands, bias, grad, lse, first):
    rows, width = operands[0].shape
    width = width // 2
    all_rows = operands[1].shape[0]
    tiles, span, tile = bias.shape
    head = lambda h, rank: (0, h)
    return kernel_call(
        functools.partial(attend_back_kernel, behind=all_rows - rows, tile=tile, span=span),
        grid_spec=pltpu.PrefetchScalarGridSpec(
            num_scalar_prefetch=1,
            grid=(HEADS // 2,),
            in_specs=attention_specs(rows, all_rows, bias, first)
            + [
                pl.BlockSpec((1, rows, HEAD_DIM), lambda h, rank: moved_head(h + first, rank)),
                pl.BlockSpec((1, 1, rows), lambda h, rank: (h, 0, 0)),
            ],
            out_specs=[
                pl.BlockSpec((rows, HEAD_DIM), head),
                pl.BlockSpec((all_rows, HEAD_DIM), head),
                pl.BlockSpec((all_rows, HEAD_DIM), head),
            ],
            scratch_shapes=[
                pltpu.VMEM((all_rows, HEAD_DIM), jnp.float32),
                pltpu.VMEM((all_rows, HEAD_DIM), jnp.float32),
            ],
        ),
        out_shape=[
            jax.ShapeDtypeStruct((rows, width), jnp.bfloat16),
            jax.ShapeDtypeStruct((all_rows, width), jnp.bfloat16),
            jax.ShapeDtypeStruct((all_rows, width), jnp.bfloat16),
        ],
    )(rank, *operands, bias, grad, lse)


def lin_back_kernel(
    low_ref, high_ref, lin_ref, scale_ref, gain_ref, cos_ref, sin_ref, o_ref, gain_grad_ref, kept
):
    rows = scale_ref.shape[0]
    scale = jnp.broadcast_to(scale_ref[...], (rows, HEAD_DIM))
    cosine, sine = cos_ref[...], -sin_ref[...]

    @pl.when(pl.program_id(0) == 0)
    def _():
        gain_grad_ref[...] = jnp.zeros_like(gain_grad_ref)

    inner = jnp.zeros((rows, HEAD_DIM), jnp.float32)
    for h in range(HEADS):
        at = slice(h * HEAD_DIM, (h + 1) * HEAD_DIM)
        ref = low_ref if h < HEADS // 2 else high_ref
        here = slice(h % (HEADS // 2) * HEAD_DIM, (h % (HEADS // 2) + 1) * HEAD_DIM)
        grad = turn(ref[:, here].astype(jnp.float32), cosine, sine)
        product = grad * lin_ref[:, at]
        gain = gain_ref[:, at]
        gain_grad_ref[:, at] += jnp.sum(product * scale, axis=0, keepdims=True)
        inner += product * gain
        kept[:, at] = grad * gain * scale
    inner = jnp.sum(inner, axis=1, keepdims=True) * (1.0 / (HEADS * HEAD_DIM))
    inner = jnp.broadcast_to(inner, (rows, HEAD_DIM)) * (scale * scale * scale)
    for h in range(HEADS):
        at = slice(h * HEAD_DIM, (h + 1) * HEAD_DIM)
        o_ref[:, at] = (kept[:, at] - lin_ref[:, at] * inner).astype(jnp.bfloat16)


def lin_back(low, high, lin, scale, gain, cosine, sine):
    rows, width = lin.shape
    tile = 256
    wide = pl.BlockSpec((tile, width), lambda i: (i, 0))
    one = pl.BlockSpec((1, width), lambda i: (0, 0))
    half = pl.BlockSpec((tile, width // 2), lambda i: (i, 0))
    table = pl.BlockSpec((tile, HEAD_DIM), lambda i: (i, 0))
    return kernel_call(
        lin_back_kernel,
        grid=(rows // tile,),
        in_specs=[half, half, wide, pl.BlockSpec((tile, 1), lambda i: (i, 0)), one, table, table],
        out_specs=[wide, one],
        scratch_shapes=[pltpu.VMEM((tile, width), jnp.float32)],
        out_shape=[
            jax.ShapeDtypeStruct((rows, width), jnp.bfloat16),
            jax.ShapeDtypeStruct((1, width), jnp.float32),
        ],
    )(low, high, lin, scale, gain, cosine, sine)


def flat(ref):
    return ref[...].reshape(-1, ref.shape[-1])


def gu_spec(weights, rows):
    return pl.BlockSpec((2, rows, weights.shape[2]), lambda i, *_: (0, 0, 0))


def d_spec(weights, rows):
    last = weights.shape[1] // rows - 1
    return pl.BlockSpec((2, rows, weights.shape[2]), lambda i, *_: (0, last, 0))


def dynamic_block(index, block):
    return pl.ds(pl.multiple_of(index * block, block), block)


def experts_up_kernel(rank, x_ref, z_ref, ga, gb, ua, ub, g_ref, u_ref, my_ref, mx_ref, middle_ref):
    gate = matmul(x_ref[0], flat(ga)) + matmul(x_ref[1], flat(gb))
    up = matmul(z_ref[0], flat(ua)) + matmul(z_ref[1], flat(ub))
    g_ref[...] = gate
    u_ref[...] = up
    middle_ref[...] = (gate * jax.nn.sigmoid(gate) * up).astype(jnp.bfloat16)
    block = gate.shape[1] // 4
    for j in range(4):
        piece = middle_ref[:, dynamic_block(rank[0] ^ j, block)]
        dy, dx = j // 2, j % 2
        my_ref[dy, :, dx * block : (dx + 1) * block] = piece
        mx_ref[dx, :, dy * block : (dy + 1) * block] = piece


def experts_up(rank, by_y, by_x, weights):
    _, rows, depth = by_y.shape
    hidden = weights[0].shape[2]
    tile = 256
    x_spec = pl.BlockSpec((2, tile, depth), lambda i, rank: (0, i, 0))
    w_specs = [gu_spec(weight, depth // 2) for weight in weights]
    wide = pl.BlockSpec((tile, hidden), lambda i, rank: (i, 0))
    half = pl.BlockSpec((2, tile, hidden // 2), lambda i, rank: (0, i, 0))
    return kernel_call(
        experts_up_kernel,
        grid_spec=pltpu.PrefetchScalarGridSpec(
            num_scalar_prefetch=1,
            grid=(rows // tile,),
            in_specs=[x_spec, x_spec] + w_specs,
            out_specs=[wide, wide, half, half],
            scratch_shapes=[pltpu.VMEM((tile, hidden), jnp.bfloat16)],
        ),
        out_shape=[jax.ShapeDtypeStruct((rows, hidden), jnp.float32)] * 2
        + [jax.ShapeDtypeStruct((2, rows, hidden // 2), jnp.bfloat16)] * 2,
    )(rank, by_y, by_x, *weights)


def experts_down_kernel(*refs):
    gates, slots, outs = refs[:2], (refs[2:8], refs[8:14]), refs[14:]
    half = outs[0].shape[1] // 2
    mixtures = []
    for side in range(2):
        at = slice(side * half, (side + 1) * half)
        mixture = 0.0
        for slot, (my, mx, la, lb, ra, rb) in enumerate(slots):
            if side == 0:
                out = matmul(my[0], flat(la)) + matmul(my[1], flat(lb))
            else:
                out = matmul(mx[0], flat(ra)) + matmul(mx[1], flat(rb))
            out = out.astype(jnp.bfloat16)
            outs[slot][:, at] = out
            mixture += gates[slot][...] * out.astype(jnp.float32)
        mixtures.append(mixture)

    @pl.when(pl.program_id(0) < pl.num_programs(0) // 2)
    def _():
        outs[2][:, :half], outs[2][:, half:] = mixtures

    @pl.when(pl.program_id(0) >= pl.num_programs(0) // 2)
    def _():
        outs[3][:, :half], outs[3][:, half:] = mixtures


def experts_down(gates, slots):
    _, rows, depth = slots[0][0].shape
    half = slots[0][2].shape[2]
    tile = 256
    x_spec = pl.BlockSpec((2, tile, depth), lambda i: (0, i, 0))
    w_specs = [d_spec(weight, depth // 2) for weight in slots[0][2:]]
    wide = pl.BlockSpec((tile, 2 * half), lambda i: (i, 0))
    column = pl.BlockSpec((tile, 1), lambda i: (i, 0))
    steps = rows // tile // 2
    return kernel_call(
        experts_down_kernel,
        grid=(rows // tile,),
        in_specs=[column] * 2 + ([x_spec] * 2 + w_specs) * 2,
        out_specs=[
            wide,
            wide,
            pl.BlockSpec((tile, 2 * half), lambda i: (jnp.minimum(i, steps - 1), 0)),
            pl.BlockSpec((tile, 2 * half), lambda i: (jnp.maximum(i - steps, 0), 0)),
        ],
        out_shape=[
            jax.ShapeDtypeStruct((rows, 2 * half), jnp.bfloat16),
            jax.ShapeDtypeStruct((rows, 2 * half), jnp.bfloat16),
            jax.ShapeDtypeStruct((rows // 2, 2 * half), jnp.float32),
            jax.ShapeDtypeStruct((rows // 2, 2 * half), jnp.float32),
        ],
    )(*gates, *slots[0], *slots[1])


def experts_back_kernel(
    rank, own_ref, other_ref, out_ref, gate_ref, g_ref, u_ref, la, lb, ra, rb, p_ref, dg_ref, du_ref, gg_ref
):
    own = pl.program_id(0) < pl.num_programs(0) // 2
    grad = jnp.where(own, own_ref[...], other_ref[...])
    gg_ref[...] = jnp.sum(grad * out_ref[...].astype(jnp.float32), axis=1, keepdims=True)
    p_ref[...] = (gate_ref[...] * grad).astype(jnp.bfloat16)
    half = grad.shape[1] // 2
    left, right = p_ref[:, :half], p_ref[:, half:]
    block = la.shape[1]
    for j in range(4):
        dy, dx = j // 2, j % 2
        left_w = (la, lb)[dy][dx]
        right_w = (ra, rb)[dx][dy]
        middle_grad = dot_t(left, left_w) + dot_t(right, right_w)
        at = dynamic_block(rank[0] ^ j, block)
        gate_pre, up_pre = g_ref[:, at], u_ref[:, at]
        sigma = jax.nn.sigmoid(gate_pre)
        change = middle_grad * up_pre * sigma * (1.0 + gate_pre * (1.0 - sigma))
        dg_ref[:, at] = change.astype(jnp.bfloat16)
        du_ref[:, at] = (middle_grad * (gate_pre * sigma)).astype(jnp.bfloat16)


def experts_back(rank, own, other, out, gate, gate_pre, up_pre, weights):
    rows, width = out.shape
    hidden = gate_pre.shape[1]
    tile = 256
    wide = pl.BlockSpec((tile, width), lambda i, rank: (i, 0))
    narrow = pl.BlockSpec((tile, hidden), lambda i, rank: (i, 0))
    column = pl.BlockSpec((tile, 1), lambda i, rank: (i, 0))
    w_specs = [d_spec(weight, hidden // 4) for weight in weights]
    steps = rows // tile // 2
    return kernel_call(
        experts_back_kernel,
        grid_spec=pltpu.PrefetchScalarGridSpec(
            num_scalar_prefetch=1,
            grid=(rows // tile,),
            in_specs=[
                pl.BlockSpec((tile, width), lambda i, rank: (jnp.minimum(i, steps - 1), 0)),
                pl.BlockSpec((tile, width), lambda i, rank: (jnp.maximum(i - steps, 0), 0)),
                wide, column, narrow, narrow
            ] + w_specs,
            out_specs=[wide, narrow, narrow, column],
        ),
        out_shape=[
            jax.ShapeDtypeStruct((rows, width), jnp.bfloat16),
            jax.ShapeDtypeStruct((rows, hidden), jnp.bfloat16),
            jax.ShapeDtypeStruct((rows, hidden), jnp.bfloat16),
            jax.ShapeDtypeStruct((rows, 1), jnp.float32),
        ],
    )(rank, own, other, out, gate, gate_pre, up_pre, *weights)


def experts_input_kernel(*refs):
    totals = []
    for j in range(4):
        dy, dx = j // 2, j % 2
        total = 0.0
        for dg, du, ga, gb, ua, ub in (refs[:6], refs[6:12]):
            gate_w = (ga, gb)[dy][dx]
            up_w = (ua, ub)[dx][dy]
            part = dot_t(dg[...], gate_w) + dot_t(du[...], up_w)
            total += part.astype(jnp.bfloat16).astype(jnp.float32)
        totals.append(total)

    @pl.when(pl.program_id(0) < pl.num_programs(0) // 2)
    def _():
        for j in range(4):
            refs[-2][j] = totals[j]

    @pl.when(pl.program_id(0) >= pl.num_programs(0) // 2)
    def _():
        for j in range(4):
            refs[-1][j] = totals[j]


def experts_input(slots):
    rows, hidden = slots[0][0].shape
    depth = slots[0][2].shape[1] // 3 * 2
    tile = 256
    narrow = pl.BlockSpec((tile, hidden), lambda i: (i, 0))
    w_specs = [gu_spec(weight, depth) for weight in slots[0][2:]]
    steps = rows // tile // 2
    return kernel_call(
        experts_input_kernel,
        grid=(rows // tile,),
        in_specs=([narrow] * 2 + w_specs) * 2,
        out_specs=[
            pl.BlockSpec((4, tile, depth), lambda i: (0, jnp.minimum(i, steps - 1), 0)),
            pl.BlockSpec((4, tile, depth), lambda i: (0, jnp.maximum(i - steps, 0), 0)),
        ],
        out_shape=[jax.ShapeDtypeStruct((4, rows // 2, depth), jnp.float32)] * 2,
    )(*slots[0], *slots[1])


def residual_back_kernel(
    rank, a_ref, b_ref, lg_ref, wr_ref, x_ref, r_ref, scale_ref, gain_ref, o_ref, c_ref, gg_ref
):
    scale = scale_ref[...]
    block = a_ref.shape[2]

    @pl.when(pl.program_id(0) == 0)
    def _():
        gg_ref[...] = jnp.zeros_like(gg_ref)

    inner = jnp.zeros_like(scale)
    for j in range(4):
        at = dynamic_block(rank[0] ^ j, block)
        grad = a_ref[j] + b_ref[j]
        for e in range(wr_ref.shape[0]):
            grad += lg_ref[:, e : e + 1] * wr_ref[e : e + 1, at]
        o_ref[:, at] = grad
        product = grad * x_ref[:, at]
        inner += jnp.sum(product * gain_ref[:, at], axis=1, keepdims=True)
        gg_ref[:, at] += jnp.sum(product * scale, axis=0, keepdims=True)
    inner = inner * (1.0 / x_ref.shape[1]) * (scale * scale * scale)
    for j in range(4):
        at = slice(j * block, (j + 1) * block)
        value = scale * (o_ref[:, at] * gain_ref[:, at]) - x_ref[:, at] * inner
        value = r_ref[:, at] + value
        o_ref[:, at] = value
        c_ref[:, at] = value.astype(jnp.bfloat16)


def residual_back(rank, own, other, logit_grad, router, residual, result_grad, scale, gain):
    rows, width = residual.shape
    tile = 128
    wide = pl.BlockSpec((tile, width), lambda i, rank: (i, 0))
    piece = pl.BlockSpec((4, tile, width // 4), lambda i, rank: (0, i, 0))
    one = pl.BlockSpec((1, width), lambda i, rank: (0, 0))
    experts = logit_grad.shape[1]
    return kernel_call(
        residual_back_kernel,
        grid_spec=pltpu.PrefetchScalarGridSpec(
            num_scalar_prefetch=1,
            grid=(rows // tile,),
            in_specs=[
                piece,
                piece,
                pl.BlockSpec((tile, experts), lambda i, rank: (i, 0)),
                pl.BlockSpec((experts, width), lambda i, rank: (0, 0)),
                wide,
                wide,
                pl.BlockSpec((tile, 1), lambda i, rank: (i, 0)),
                one,
            ],
            out_specs=[wide, wide, one],
        ),
        out_shape=[
            jax.ShapeDtypeStruct((rows, width), jnp.float32),
            jax.ShapeDtypeStruct((rows, width), jnp.bfloat16),
            jax.ShapeDtypeStruct((1, width), jnp.float32),
        ],
    )(rank, own, other, logit_grad, router, residual, result_grad, scale, gain[None])


def experts_grad_kernel(x_ref, d_ref, m_ref, p_ref, *refs):
    o_ref = refs[-1]
    rows, down_rows = x_ref.shape[2], m_ref.shape[2]
    top, bottom = t_dot(x_ref[0], d_ref[...]), t_dot(m_ref[0], p_ref[...])
    if len(refs) == 2:
        top += refs[0][0, :rows].astype(jnp.float32)
        bottom += refs[0][0, rows:].astype(jnp.float32)
    o_ref[0, :rows] = top.astype(jnp.bfloat16)
    o_ref[0, rows:] = bottom.astype(jnp.bfloat16)


def experts_grad(inputs, pre_grad, middle, pair, part, side, got=()):
    _, rows, depth = inputs.shape
    hidden, down = pre_grad.shape[1], middle.shape[2]
    piece = pl.BlockSpec((1, (depth + down) // 2, hidden), lambda q: (q, 0, 0))
    return kernel_call(
        experts_grad_kernel,
        grid=(2,),
        in_specs=[
            pl.BlockSpec((1, rows, depth // 2), lambda q: (part, 0, q)),
            pl.BlockSpec((rows, hidden), lambda q: (0, 0)),
            pl.BlockSpec((1, rows, down // 2), lambda q: (part, 0, q)),
            pl.BlockSpec((rows, hidden), lambda q: (0, side)),
        ]
        + [piece] * len(got),
        out_specs=piece,
        out_shape=jax.ShapeDtypeStruct((2, (depth + down) // 2, hidden), jnp.bfloat16),
    )(inputs, pre_grad, middle, pair, *got)


def chip_grad_kernel(x_ref, *refs, count):
    o_ref = refs[-1]
    width = o_ref.shape[1] // count
    for i in range(count):
        at = slice(i * width, (i + 1) * width)
        total = t_dot(x_ref[0], refs[i][...])
        if len(refs) > count + 1:
            total += refs[count][:, at].astype(jnp.float32)
        o_ref[:, at] = total.astype(jnp.bfloat16)


def chip_grad(halves, part, grads, start=0, got=()):
    depth = halves.shape[2]
    rows = grads[0].shape[0]
    width = sum(grad.shape[1] for grad in grads)
    tile = 256
    piece = pl.BlockSpec((tile, width), lambda i: (i, 0))
    return kernel_call(
        functools.partial(chip_grad_kernel, count=len(grads)),
        grid=(depth // tile,),
        in_specs=[pl.BlockSpec((1, rows, tile), lambda i: (part, start // rows, i))]
        + [pl.BlockSpec(grad.shape, lambda i: (0, 0)) for grad in grads]
        + [piece] * len(got),
        out_specs=piece,
        out_shape=jax.ShapeDtypeStruct((depth, width), jnp.bfloat16),
    )(halves, *grads, *got)


def mixed_back_kernel(g_ref, a_ref, b_ref, o_ref):
    for half, ref in enumerate((a_ref, b_ref)):
        o_ref[half] = dot_t(g_ref[...], ref[...]).astype(jnp.bfloat16)


def mixed_back(grad, weights):
    rows, width = grad.shape
    depth = weights[0].shape[0]
    step = 256
    weight = pl.BlockSpec((step, width), lambda j: (j, 0))
    return kernel_call(
        mixed_back_kernel,
        grid=(depth // step,),
        in_specs=[pl.BlockSpec((rows, width), lambda j: (0, 0)), weight, weight],
        out_specs=pl.BlockSpec((2, rows, step), lambda j: (0, 0, j)),
        out_shape=jax.ShapeDtypeStruct((2, rows, depth), jnp.bfloat16),
    )(grad, *weights)


def across(value, bit):
    count = lax.axis_size("rep")
    return lax.ppermute(value, "rep", [(place, place ^ bit) for place in range(count)])


def along(value, steps):
    count = lax.axis_size("ep")
    return lax.ppermute(value, "ep", [(place, (place + steps) % count) for place in range(count)])


def mirrored(value, moves):
    reps, count = lax.axis_size("rep"), lax.axis_size("ep")
    pairs = []
    for rep in range(reps):
        for source, target in moves:
            if rep % 2:
                source, target = count - 1 - source, count - 1 - target
            pairs.append((rep * count + source, rep * count + target))
    return lax.ppermute(value, ("rep", "ep"), pairs)


def pick(value, index, axis):
    return lax.dynamic_index_in_dim(value, index, axis, keepdims=False)


def in_order(own, other, bit, axis):
    return jnp.where(bit == 1, jnp.stack([other, own], axis), jnp.stack([own, other], axis))


def over_ep(value, place):
    shard = place[3]
    experts = lax.axis_size("ep")
    parts = jnp.zeros((experts,) + value.shape, value.dtype)
    parts = lax.dynamic_update_index_in_dim(parts, value, shard, 0)
    for steps in range(1, experts):
        parts = lax.dynamic_update_index_in_dim(
            parts, along(value, steps), lax.rem(shard - steps + experts, experts), 0
        )
    return parts


def hold(*values):
    return lax.optimization_barrier(values)


def both_ways(value):
    return across(value[0], 2), across(value[1], 4)


def other_ways(first, second):
    return across(first, 4), across(second, 2)


def add(left, right):
    return (left.astype(jnp.float32) + right.astype(jnp.float32)).astype(jnp.bfloat16)


def ep_sum(both):
    return lax.psum_scatter(both, "ep", scatter_dimension=1, tiled=True).astype(jnp.float32)


def body(
    tokens,
    teacher,
    segment_ids,
    valid_mask,
    routes,
    attn_gain,
    q_gain,
    k_gain,
    moe_gain,
    w_query,
    w_key,
    w_value,
    w_out,
    w_router,
    w_gate,
    w_up,
    w_down,
):
    bf16, f32 = jnp.bfloat16, jnp.float32
    local_rows, width = tokens.shape
    experts = lax.axis_size("ep")
    reps = lax.axis_size("rep")
    reach = min(-(-WINDOW // local_rows), experts - 1)
    shard = lax.axis_index("ep")
    rep = lax.axis_index("rep")
    place = (rep // 4, rep // 2 % 2, rep % 2, shard)
    core = rep % 2
    total_tokens = local_rows * reps * experts

    valid = valid_mask.reshape(local_rows).astype(f32)
    own_count = jnp.sum(valid_mask)
    counts = jnp.stack([own_count // 16, own_count % 16]).astype(bf16)
    small = jnp.concatenate(
        [
            jnp.stack([attn_gain, q_gain, k_gain, moe_gain], 1),
            w_router,
            jnp.broadcast_to(counts[None], (attn_gain.shape[0], 2)),
        ],
        1,
    )
    rank = rep.astype(jnp.int32)[None]
    quarter = rep // 2
    quarter_rank = quarter.astype(jnp.int32)[None]
    order = tuple(code_of(j, reps) for j in range(reps))
    half = width // 2
    behind = reach * local_rows
    all_rows = local_rows + behind
    m = jnp.where(core == 0, shard, experts - 1 - shard)
    quarter_rows = w_gate.shape[1] // 4
    quarter_down = w_down.shape[1] // 4

    def own_part(weight, rows):
        return lax.dynamic_slice_in_dim(weight[0], quarter * rows, rows, 0)

    down = own_part(w_down, quarter_down)
    own = jnp.stack(
        [
            jnp.concatenate([own_part(w_gate, quarter_rows), down[:, :half]], 0),
            jnp.concatenate([own_part(w_up, quarter_rows), down[:, half:]], 0),
        ]
    )
    segments = segment_ids.reshape(local_rows)
    shard_rows = w_key.shape[0]
    columns = small.shape[1]
    small = small.T

    small = over_ep(small, place)
    parts = over_ep(jnp.stack([w_key, w_value]), place)
    segments_1 = from_behind(segments, "ep", 1)
    parts, small, own, tokens_1, segments_1 = hold(parts, small, own, tokens, segments_1)
    qo = jnp.stack([w_query, w_out])

    qo, parts = hold(qo, parts)
    qo = lax.all_gather(qo, "ep", axis=0)
    block = shard_rows * experts
    k_w, v_w = parts[:, 0].reshape(block, width), parts[:, 1].reshape(block, width)
    e_1 = mirrored(own, [(0, 1), (1, 2)])
    small = small.reshape(-1)
    small = jnp.pad(small, (0, 16 * width - small.shape[0])).reshape(16, width)
    k_w = jnp.concatenate([k_w, small], 0)
    k_x, v_y = both_ways((k_w, v_w))
    segments_2 = from_behind(segments_1, "ep", 1)
    k_w, k_x, v_w, v_y, tokens_1, segments_2 = hold(k_w, k_x, v_w, v_y, tokens_1, segments_2)

    k_w = jnp.stack([k_w, k_x])
    k_y, v_x = other_ways(k_w, jnp.stack([v_w, v_y]))
    tokens_1 = from_behind(tokens_1, "ep", 1)
    qo, k_w, k_y, v_w, v_y, v_x, tokens_1 = hold(qo, k_w, k_y, v_w, v_y, v_x, tokens_1)

    small = jnp.concatenate([k_w[:, block : block + 2], k_y[:, block : block + 2]], 0)
    small = jnp.pad(small.reshape(-1, width), ((0, 8), (0, 0)))
    k_w = jnp.concatenate([k_w[0, :block], k_w[1, :block], k_y[0, :block], k_y[1, :block], small], 0)
    v_w = jnp.concatenate([v_w, v_x[0], v_y, v_x[1]], 0)
    key_w, value_w = (k_w, across(k_w, 1)), (v_w, across(v_w, 1))
    q_w, o_w = qo[:, 0].reshape(-1, width), qo[:, 1].reshape(-1, width)
    q_x, o_y = both_ways((q_w, o_w))
    tokens_2 = from_behind(tokens_1, "ep", 1)
    key_w, value_w, q_w, q_x, o_w, o_y, tokens_2, tokens_1, e_1, own = hold(
        key_w, value_w, q_w, q_x, o_w, o_y, tokens_2, tokens_1, e_1, own
    )

    q_w = jnp.concatenate([q_w, q_x], 0)
    q_y, o_x = other_ways(q_w, jnp.stack([o_w, o_y]))
    q_w = jnp.concatenate([q_w, q_y], 0)
    o_w = jnp.concatenate([o_w, o_x[0], o_y, o_x[1]], 0)
    e_2 = mirrored(jnp.where(m == 2, e_1, own), [(1, 0), (2, 3)])
    e_3 = mirrored(e_1, [(1, 2)])
    small = jnp.stack([weight[4 * block : 4 * block + 8] for weight in key_w])
    small = small.reshape(2, 2, 2, -1)[..., : experts * columns * shard_rows]
    for axis, bit in enumerate((core, place[0], place[1])):
        small = jnp.where(bit == 1, jnp.flip(small, axis), small)
    small = small.reshape(2, 2, 2, experts, columns, shard_rows)
    small = jnp.transpose(small, (4, 1, 2, 0, 3, 5)).reshape(columns, -1)
    gain_attn, gain_query, gain_key, gain_moe = [small[i].astype(f32) for i in range(4)]
    weight_router = small[4 : 4 + experts].T
    counts = small[4 + experts :, ::shard_rows].astype(f32)
    count = jnp.sum(counts[0]) * 16.0 + jnp.sum(counts[1])
    key_segments = jnp.concatenate([segments_2, segments_1, segments], 0)
    normed, scale_all = norm_rows(rank, (tokens_2, tokens_1, tokens), gain_attn, order)
    key_lin, key_squares = project(normed, *key_w, f32)
    value_all, _ = project(normed, *value_w, bf16)
    q_w, o_w, e_2, e_3, e_1, own, normed, key_lin, value_all = hold(
        q_w, o_w, e_2, e_3, e_1, own, normed, key_lin, value_all
    )

    query_w, out_w = (q_w, across(q_w, 1)), (o_w, across(o_w, 1))
    e_b = jnp.where(m == 1, own, jnp.where(m == 2, e_1, e_2))
    b_x, b_y = both_ways(e_b)
    e_4 = mirrored(e_3, [(2, 3)])
    query_lin, query_squares = project(normed, *query_w, f32, behind)
    scale_key = lax.rsqrt(key_squares / width + norm_eps)
    scale_query = lax.rsqrt(query_squares / width + norm_eps)
    key_positions = (shard - reach) * local_rows + jnp.arange(all_rows, dtype=jnp.int32)
    half_head = HEAD_DIM // 2
    frequency = 10000.0 ** (-jnp.arange(half_head, dtype=f32) * 2.0 / HEAD_DIM)
    angles = key_positions[:, None].astype(f32) * frequency[None, :]
    cosine, sine = jnp.cos(angles), jnp.sin(angles)
    cosine, sine = jnp.concatenate([cosine, cosine], 1), jnp.concatenate([-sine, sine], 1)

    def mask_of(tile):
        span = behind + tile
        parts = []
        for start in range(0, local_rows, tile):
            keys = slice(start, start + span)
            queries = slice(behind + start, behind + start + tile)
            distance = key_positions[None, queries] - key_positions[keys, None]
            allowed = (
                (distance >= 0)
                & (distance < WINDOW)
                & (key_positions[keys, None] >= 0)
                & (key_segments[None, queries] == key_segments[keys, None])
            )
            parts.append(jnp.where(allowed, 0.0, -1e30).astype(f32))
        return jnp.stack(parts)

    operands = (
        query_lin,
        key_lin,
        value_all,
        scale_query,
        scale_key,
        gain_query[None],
        gain_key[None],
        cosine,
        sine,
    )
    bias_small = mask_of(local_rows // 4)
    mixed, lse_0 = attend(rank, operands, bias_small, 0)
    mixed, out_w, e_b, b_x, b_y, e_4, e_3, e_1, own = hold(
        mixed, out_w, e_b, b_x, b_y, e_4, e_3, e_1, own
    )

    b_0, b_1 = jnp.stack([e_b[0], b_x]), jnp.stack([e_b[1], b_y])
    b_2, b_3 = other_ways(b_0[:, :quarter_rows], b_1[:, :quarter_rows])
    mixed, lse_1 = attend(rank, operands, bias_small, HEADS // 2, (mixed,))
    e_a = jnp.where(m == 0, own, jnp.where(m == 1, e_1, jnp.where(m == 2, e_3, e_4)))
    mixed, b_2, b_3, e_a = hold(mixed, b_2, b_3, e_a)
    a_x, a_y = both_ways(e_a)
    branch, _ = project(mixed, *out_w, f32)
    residual = tokens.astype(f32) + branch
    moe, scale_moe = norm_rows(quarter_rank, (residual,), gain_moe, (0, 1, 2, 3))
    moe_y = jnp.concatenate([moe, across(moe, 1)], 1)
    piece = half // 2
    moe_x = jnp.stack(
        [
            jnp.concatenate([moe_y[0, :, i : i + piece], moe_y[1, :, i : i + piece]], 1)
            for i in (0, piece)
        ]
    )
    router_parts = weight_router.reshape(4, -1, experts)
    router_rel = jnp.concatenate([pick(router_parts, quarter ^ j, 0) for j in range(4)], 0)
    router_probs = jax.nn.softmax(
        matmul(moe[0], router_rel[:half]) + matmul(moe[1], router_rel[half:]), axis=-1
    )
    chosen = jnp.sum(
        (routes[:, :, None] == jnp.arange(experts, dtype=jnp.int32)).astype(f32), axis=1
    )
    gates = router_probs * chosen
    gates_both = jnp.concatenate([gates, across(gates, 1)], 0)
    gates_a = jnp.where(core == 0, gates_both[:, :1], gates_both[:, -1:])
    gates_b = jnp.where(core == 0, gates_both[:, 1:2], gates_both[:, -2:-1])
    b_0, b_1, e_a, a_x, a_y, moe_y, moe_x = hold(b_0, b_1, e_a, a_x, a_y, moe_y, moe_x)

    a_0, a_1 = jnp.stack([e_a[0], a_x]), jnp.stack([e_a[1], a_y])
    a_2, a_3 = other_ways(a_0[:, :quarter_rows], a_1[:, :quarter_rows])
    b_4, b_5 = other_ways(b_0[:, quarter_rows:], b_1[:, quarter_rows:])
    up_weights_b, down_weights_b = (b_0, b_2, b_1, b_3), (b_0, b_4, b_1, b_5)
    gate_pre_b, up_pre_b, my_b, mx_b = experts_up(quarter_rank, moe_y, moe_x, up_weights_b)
    a_0, a_1, a_2, a_3, my_b, mx_b = hold(a_0, a_1, a_2, a_3, my_b, mx_b)

    a_4, a_5 = other_ways(a_0[:, quarter_rows:], a_1[:, quarter_rows:])
    up_weights_a, down_weights_a = (a_0, a_2, a_1, a_3), (a_0, a_4, a_1, a_5)
    gate_pre_a, up_pre_a, my_a, mx_a = experts_up(quarter_rank, moe_y, moe_x, up_weights_a)
    expert_out_a, expert_out_b, mixture, mixture_other = experts_down(
        (gates_a, gates_b), ((my_a, mx_a) + down_weights_a, (my_b, mx_b) + down_weights_b)
    )
    result = residual + (mixture + across(mixture_other, 1))
    output = result.astype(bf16)
    error = result - teacher.astype(f32)
    squares = jnp.sum(valid * jnp.sum(error * error, axis=1))
    result_grad = total_tokens / count * valid[:, None] * error
    result_other = across(result_grad, 1)

    pair_b, dg_b, du_b, gate_grad_b = experts_back(
        quarter_rank,
        result_grad,
        result_other,
        expert_out_b,
        gates_b,
        gate_pre_b,
        up_pre_b,
        down_weights_b,
    )
    sent_x = experts_grad(moe_x, dg_b, mx_b, pair_b, 1, 0)
    sent_y = experts_grad(moe_y, du_b, my_b, pair_b, 1, 1)
    sent_x, sent_y, expert_out_a = hold(sent_x, sent_y, expert_out_a)

    b_x, b_y = both_ways((sent_x, sent_y))
    pair_a, dg_a, du_a, gate_grad_a = experts_back(
        quarter_rank,
        result_grad,
        result_other,
        expert_out_a,
        gates_a,
        gate_pre_a,
        up_pre_a,
        down_weights_a,
    )
    sent_x = experts_grad(moe_x, dg_a, mx_a, pair_a, 1, 0)
    sent_y = experts_grad(moe_y, du_a, my_a, pair_a, 1, 1)
    input_grad, input_other = experts_input(
        ((dg_a, du_a) + up_weights_a, (dg_b, du_b) + up_weights_b)
    )
    slot_grads = jnp.concatenate([gate_grad_a, gate_grad_b], 1)
    own_slots, partner_slots = slot_grads[:local_rows], across(slot_grads[local_rows:], 1)
    from_low = jnp.where(core == 0, own_slots, partner_slots)
    from_high = jnp.where(core == 0, partner_slots, own_slots)
    prob_grad = chosen * jnp.concatenate([from_low, from_high[:, ::-1]], 1)
    logit_grad = router_probs * (
        prob_grad - jnp.sum(prob_grad * router_probs, axis=-1, keepdims=True)
    )
    b_x, b_y, sent_x, sent_y, input_grad, input_other, logit_grad = hold(
        b_x, b_y, sent_x, sent_y, input_grad, input_other, logit_grad
    )

    input_other = across(input_other, 1)
    a_x, a_y = both_ways((sent_x, sent_y))
    b_0 = experts_grad(moe_x, dg_b, mx_b, pair_b, 0, 0, (b_x,))
    b_1 = experts_grad(moe_y, du_b, my_b, pair_b, 0, 1, (b_y,))
    router_local = jnp.concatenate(
        [
            jnp.dot(part.T.astype(f32), logit_grad, precision=highest, preferred_element_type=f32)
            for part in (moe[0], moe[1])
        ],
        0,
    )
    router_local = router_local.reshape(4, -1, experts)
    router_local = jnp.concatenate([pick(router_local, quarter ^ j, 0) for j in range(4)], 0)
    residual_grad, branch_grad, moe_gain_local = residual_back(
        quarter_rank,
        input_grad,
        input_other,
        logit_grad,
        weight_router.astype(f32).T,
        residual,
        result_grad,
        scale_moe,
        gain_moe,
    )
    out_sent = across(chip_grad(mixed, 1, (branch_grad,)), 1)
    out_sum = chip_grad(mixed, 0, (branch_grad,), 0, (out_sent,)).reshape(2, 2, -1, width)
    mixed_grad = mixed_back(branch_grad, out_w)
    b_y, b_x = other_ways(b_0[1], b_1[1])
    bias = mask_of(local_rows // 2)
    dq_0, dk_0, dv_0 = attend_back(rank, operands, bias, mixed_grad, lse_0, 0)
    dq_1, dk_1, dv_1 = attend_back(rank, operands, bias, mixed_grad, lse_1, HEADS // 2)
    a_x, a_y, b_0, b_1, b_x, b_y, out_sum, dq_0, dk_0, dv_0, dq_1, dk_1, dv_1 = hold(
        a_x, a_y, b_0, b_1, b_x, b_y, out_sum, dq_0, dk_0, dv_0, dq_1, dk_1, dv_1
    )

    a_0 = experts_grad(moe_x, dg_a, mx_a, pair_a, 0, 0, (a_x,))
    a_1 = experts_grad(moe_y, du_a, my_a, pair_a, 0, 1, (a_y,))
    a_y, a_x = other_ways(a_0[1], a_1[1])
    out_x, out_y = across(out_sum[:, 1, :, :half], 2), across(out_sum[1, :, :, half:], 4)
    b_end = jnp.stack([add(b_0[0], b_y), add(b_1[0], b_x)])
    b_got = mirrored(b_end, [(3, 2), (0, 1)])
    value_sent = chip_grad(normed, 1, (dv_0, dv_1))
    value_got = across(value_sent, 1)
    value_sum = chip_grad(normed, 0, (dv_0, dv_1), 0, (value_got,)).reshape(2, 2, -1, width)
    value_x = across(value_sum[:, 1, :, :half], 2)
    value_y = across(value_sum[1, :, :, half:], 4)
    query_lin_grad, q_gain_local = lin_back(
        dq_0, dq_1, query_lin, scale_query, gain_query[None], cosine[behind:], sine[behind:]
    )
    key_lin_grad, k_gain_local = lin_back(
        dk_0, dk_1, key_lin, scale_key, gain_key[None], cosine, sine
    )
    query_sent = chip_grad(normed, 1, (query_lin_grad,), behind)
    key_sent = chip_grad(normed, 1, (key_lin_grad,))
    packed = jnp.concatenate(
        [
            jnp.broadcast_to(squares, (1, width)),
            q_gain_local,
            k_gain_local,
            moe_gain_local,
            router_local.T,
        ],
        0,
    )
    (
        a_0, a_1, a_x, a_y, out_sum, out_x, out_y, b_end, b_got, query_lin_grad, key_lin_grad,
        value_sum, value_x, value_y, query_sent, key_sent, packed,
    ) = hold(
        a_0, a_1, a_x, a_y, out_sum, out_x, out_y, b_end, b_got, query_lin_grad, key_lin_grad,
        value_sum, value_x, value_y, query_sent, key_sent, packed,
    )

    query_got, key_got = across(query_sent, 1), across(key_sent, 1)
    value_a = add(value_sum[:, 0, :, :half], value_x)
    value_b = add(value_sum[0, :, :, half:], value_y)
    for link in (1, 2, 4):
        packed = packed + across(packed, link)
    out_a, out_b = add(out_sum[:, 0, :, :half], out_x), add(out_sum[0, :, :, half:], out_y)
    value_a, value_b, packed, out_a, out_b = hold(value_a, value_b, packed, out_a, out_b)
    moved_x = across(jnp.stack([value_b[1], out_b[1]]), 2)
    moved_y = across(jnp.stack([value_a[1], out_a[1]]), 4)
    value_x, value_y, out_x, out_y = moved_x[0], moved_y[0], moved_x[1], moved_y[1]
    four = [add(out_a[0], out_y), add(out_b[0], out_x)]
    four += [add(value_a[0], value_y), add(value_b[0], value_x)]
    four = ep_sum(jnp.stack(four))
    out_total, value_total = four[:2], four[2:]
    b_low = add(b_end, b_got)
    b_got_2 = mirrored(b_low, [(2, 1)])
    a_end = jnp.stack([add(a_0[0], a_y), add(a_1[0], a_x)])
    a_got = mirrored(a_end, [(3, 2)])
    normed_grad = project_back(
        key_lin_grad, dv_0, dv_1, query_lin_grad, key_w, value_w, query_w
    )
    query_sum = chip_grad(normed, 0, (query_lin_grad,), behind, (query_got,))
    key_sum = chip_grad(normed, 0, (key_lin_grad,), 0, (key_got,))
    (
        normed_grad, query_sum, key_sum, out_total, value_total, b_got_2, a_end, a_got, packed,
    ) = hold(
        normed_grad, query_sum, key_sum, out_total, value_total, b_got_2, a_end, a_got, packed,
    )

    query_sum = query_sum.reshape(2, 2, -1, width)
    key_sum = key_sum.reshape(2, 2, -1, width)
    query_x, key_y = across(query_sum[:, 1], 2), across(key_sum[1], 4)
    carried = from_behind(normed_grad[:, :local_rows].astype(bf16), "ep", -1)
    a_low = add(a_end, a_got)
    a_got = mirrored(a_low, [(2, 1)])
    b_total = (b_end.astype(f32) + b_got.astype(f32) + b_got_2.astype(f32)).astype(bf16)
    query_sum, key_sum, query_x, key_y, carried, a_low, a_got, packed, b_total = hold(
        query_sum, key_sum, query_x, key_y, carried, a_low, a_got, packed, b_total
    )

    query_sum, key_sum = add(query_sum[:, 0], query_x), add(key_sum[0], key_y)
    query_y, key_x = across(query_sum[1], 4), across(key_sum[1], 2)
    for back in range(1, reach):
        here = normed_grad[:, back * local_rows : (back + 1) * local_rows] + carried.astype(f32)
        carried = from_behind(here.astype(bf16), "ep", -1)
    a_low = add(a_low, a_got)
    a_got = mirrored(a_low, [(1, 0)])
    query_sum, key_sum, query_y, key_x, carried, packed, a_low, a_got = hold(
        query_sum, key_sum, query_y, key_x, carried, packed, a_low, a_got
    )

    qk_total = ep_sum(jnp.stack([add(query_sum[0], query_y), add(key_sum[0], key_x)]))
    packed = jnp.sum(over_ep(packed, place), axis=0)
    tokens_grad = tokens_back(
        rank, normed_grad, carried, tokens, residual_grad, scale_all, gain_attn, reps
    )
    mine = jnp.where(m == 0, add(a_low, a_got), b_total)

    def own_half(piece):
        return piece.reshape(2, 2, -1, piece.shape[2])

    tops, bottoms = own_half(mine[:, :quarter_rows]), own_half(mine[:, quarter_rows:])
    halves = jnp.concatenate([tops, bottoms], 2)
    other = across(pick(halves, 1 - core, 1), 1)
    mine = jnp.where(m < 2, pick(halves, core, 1), other).astype(f32)
    top = quarter_rows // 2
    down_out = jnp.concatenate([mine[0, top:], mine[1, top:]], 1)
    out_out = jnp.concatenate([out_total[0], out_total[1]], 1)
    value_out = jnp.concatenate([value_total[0], value_total[1]], 1)
    loss = packed[0, 0] / (2.0 * count * width)
    attn_gain_out = (
        jnp.sum(w_query.astype(f32) * qk_total[0], axis=1)
        + jnp.sum(w_key.astype(f32) * qk_total[1], axis=1)
        + jnp.sum(w_value.astype(f32) * value_out, axis=1)
    ) / attn_gain.astype(f32)
    shares = lax.dynamic_slice_in_dim(
        packed, (rep * experts + shard) * shard_rows, shard_rows, 1
    )
    return (
        output,
        loss,
        tokens_grad,
        attn_gain_out,
        shares[1],
        shares[2],
        shares[3],
        qk_total[0],
        qk_total[1],
        value_out,
        out_out,
        shares[4:].T,
        mine[0, :top][None],
        mine[1, :top][None],
        down_out[None],
    )


def solution(mesh):
    placed = (
        P(("rep", "ep"), None),
        P(("rep", "ep"), None),
        P("rep", "ep"),
        P("rep", "ep"),
        P(("rep", "ep"), None),
        P(("rep", "ep")),
        P(("rep", "ep")),
        P(("rep", "ep")),
        P(("rep", "ep")),
        P(("rep", "ep"), None),
        P(("rep", "ep"), None),
        P(("rep", "ep"), None),
        P(("rep", "ep"), None),
        P(("rep", "ep"), None),
        P("ep", None, None),
        P("ep", None, None),
        P("ep", None, None),
    )
    chips = mesh.shape["rep"] == 8 and mesh.shape["ep"] == 4
    return jax.shard_map(
        body if chips else body_plain,
        mesh=mesh,
        in_specs=placed,
        out_specs=(
            P(("rep", "ep"), None),
            P(),
            P(("rep", "ep"), None),
            P(("rep", "ep")),
            P(("rep", "ep")),
            P(("rep", "ep")),
            P(("rep", "ep")),
            P(("rep", "ep"), None),
            P(("rep", "ep"), None),
            P(("rep", "ep"), None),
            P(("rep", "ep"), None),
            P(("rep", "ep"), None),
            P("ep", "rep", None),
            P("ep", "rep", None),
            P("ep", "rep", None),
        ),
        check_vma=False,
    )
```
